32 devices in a mesh: section: 2 (over core), mp: 4 (over z), dp: 4 (over y, x).
Axes of the slice: x: 2, y: 2, z: 4, core: 2. Of those that a mesh axis runs over, the one named last changes fastest.
Arguments:
- char_ids: int32 [64, 20, 50], P('dp'), may hold values from 0 to 261
- row_lengths: int32 [64], P('dp'), may hold values from 1 to 20, as said below
- top_grad: bfloat16 [64, 20, 2, 512], P('dp'), may hold values from -6 to 6
- char_table: bfloat16 [262, 16], replicated, may hold values from -6 to 6
- conv_weight: bfloat16 [7, 16, 2048], P(None, None, 'mp'), may hold values from -0.5 to 0.5
- conv_bias: bfloat16 [2048], P('mp'), may hold values from -3 to 3
- highway_weight: bfloat16 [2, 2048, 2, 2048], P(None, None, None, 'mp'), may hold values from -0.125 to 0.125
- highway_bias: bfloat16 [2, 2, 2048], P(None, None, 'mp'), may hold values from -3 to 3
- proj_weight: bfloat16 [2048, 512], replicated, may hold values from -0.125 to 0.125
- proj_bias: bfloat16 [512], replicated, may hold values from -3 to 3
- lstm_input: bfloat16 [2, 2, 512, 4, 4096], P('section', None, None, None, 'mp'), may hold values from -0.25 to 0.25
- lstm_state: bfloat16 [2, 2, 512, 4, 4096], P('section', None, None, None, 'mp'), may hold values from -0.25 to 0.25
- lstm_bias: bfloat16 [2, 2, 4, 4096], P('section', None, None, 'mp'), may hold values from -3 to 3
- lstm_proj: bfloat16 [2, 2, 4096, 512], P('section', None, 'mp'), may hold values from -0.1875 to 0.1875
Outputs:
- char_table_grad: float32 [262, 16], replicated
- conv_weight_grad: float32 [7, 16, 2048], P(None, None, 'mp')
- conv_bias_grad: float32 [2048], P('mp')
- highway_weight_grad: float32 [2, 2048, 2, 2048], P(None, None, None, 'mp')
- highway_bias_grad: float32 [2, 2, 2048], P(None, None, 'mp')
- proj_weight_grad: float32 [2048, 512], replicated
- proj_bias_grad: float32 [512], replicated
- lstm_input_grad: float32 [2, 2, 512, 4, 4096], P('section', None, None, None, 'mp')
- lstm_state_grad: float32 [2, 2, 512, 4, 4096], P('section', None, None, None, 'mp')
- lstm_bias_grad: float32 [2, 2, 4, 4096], P('section', None, None, 'mp')
- lstm_proj_grad: float32 [2, 2, 4096, 512], P('section', None, 'mp')
The draws below stay inside these ranges and needn't reach their ends.
Inputs may be any that keep to these rules, and one draw needn't show every extreme that they name: `row_lengths`: each row's live tokens; positions from it on are padding; some row has exactly 20.
All inputs are finite; a program needn't handle non-finite values.
Results may differ from the reference program's by a relative error of at most 0.019.
Values may be sent and summed in bfloat16 or wider, within the bound.
A program may use at most 384 MiB of HBM per device.

```python
import jax
import jax.numpy as jnp
from jax import lax

EMB = 16
CHARS = 262
CH = 50
FILT = 2048
HWY = 2
CELL = 4096
PROJ = 512
L = 20
MB_ROWS = 8
ROWS = 64


def draw_row_lengths(key, part):
    key = jax.random.fold_in(key, 17)
    first_key, second_key = jax.random.split(key)
    drawn = jax.random.randint(first_key, (ROWS,), 1, L + 1)
    chosen = jax.random.randint(second_key, (), 0, ROWS)
    return jnp.where(jnp.arange(ROWS) == chosen, L, drawn).astype(jnp.int32)


def touch_ends(values, stream_key, low, high):
    index_at = [jax.random.randint(jax.random.fold_in(stream_key, axis), (), 0, length) for axis, length in enumerate(values.shape)]
    main_axis = values.shape.index(max(values.shape))
    next_to = index_at[:main_axis] + [(index_at[main_axis] + 1) % values.shape[main_axis]] + index_at[main_axis + 1:]
    return values.at[tuple(index_at)].set(low).at[tuple(next_to)].set(high)


def shard_levels(key, shape, cuts, least, high):
    factor_of, own = 1.0, jax.random.fold_in(key, 6)
    for position, shards_of in cuts:
        draws = jnp.exp(jax.random.uniform(jax.random.fold_in(own, position), (shards_of,), jnp.float32, least / len(cuts), high / len(cuts)))
        factor_of = factor_of * jnp.repeat(draws, shape[position] // shards_of).reshape([-1 if axis == position else 1 for axis in range(len(shape))])
    return factor_of


def normal_values(own_key, shape, deviation, bound, pieces=(), kind=jnp.bfloat16):
    entries = deviation * jax.random.normal(own_key, shape, jnp.float32)
    if pieces:
        entries = entries * shard_levels(own_key, shape, pieces, -0.22, 0.18)
    return jnp.clip(entries, -bound, bound).astype(kind)


def setup_inputs(seed: int = 0) -> dict:
    key_of = jax.random.split(jax.random.key(seed), 15)
    char_ids = touch_ends(jax.random.randint(key_of[0], (ROWS, L, CH), 0, CHARS), jax.random.fold_in(key_of[0], 1), 0, CHARS - 1).astype(jnp.int32)
    row_lengths = draw_row_lengths(jax.random.fold_in(key_of[14], 71), 0)
    top_grad = normal_values(key_of[2], (ROWS, L, 2, PROJ), 1.0, 6.0, ((0, 4),))
    char_table = normal_values(key_of[3], (CHARS, EMB), 1.0, 6.0)
    conv_weight = normal_values(key_of[4], (7, EMB, FILT), (7 * EMB) ** -0.5, 0.5, ((2, 4),))
    conv_bias = normal_values(key_of[5], (FILT,), 0.5, 3.0, ((0, 4),))
    highway_weight = normal_values(key_of[6], (HWY, FILT, 2, FILT), FILT ** -0.5, 0.125, ((3, 4),))
    highway_bias = normal_values(key_of[7], (HWY, 2, FILT), 0.5, 3.0, ((2, 4),))
    proj_weight = normal_values(key_of[8], (FILT, PROJ), FILT ** -0.5, 0.125)
    proj_bias = normal_values(key_of[9], (PROJ,), 0.5, 3.0)
    lstm_input = normal_values(key_of[10], (2, 2, PROJ, 4, CELL), PROJ ** -0.5, 0.25, ((0, 2), (4, 4)))
    lstm_state = normal_values(key_of[11], (2, 2, PROJ, 4, CELL), PROJ ** -0.5, 0.25, ((0, 2), (4, 4)))
    lstm_bias = normal_values(key_of[12], (2, 2, 4, CELL), 0.5, 3.0, ((0, 2), (3, 4)))
    lstm_proj = normal_values(key_of[13], (2, 2, CELL, PROJ), (CELL // 4) ** -0.5, 0.1875, ((0, 2), (2, 4)))
    return dict(char_ids=char_ids, row_lengths=row_lengths, top_grad=top_grad, char_table=char_table, conv_weight=conv_weight, conv_bias=conv_bias, highway_weight=highway_weight, highway_bias=highway_bias, proj_weight=proj_weight, proj_bias=proj_bias, lstm_input=lstm_input, lstm_state=lstm_state, lstm_bias=lstm_bias, lstm_proj=lstm_proj)


HIGH = lax.Precision.HIGHEST

@jax.custom_vjp
def low(v):
    return lax.optimization_barrier(v.astype(jnp.bfloat16)).astype(jnp.float32)

@jax.custom_vjp
def low_back(v):
    return v

def low_keep(v):
    return (low(v), None)

def low_pass(kept, grad):
    return (grad,)

def back_keep(v):
    return (v, None)

def back_low(kept, grad):
    return (low(grad),)
low.defvjp(low_keep, low_pass)
low_back.defvjp(back_keep, back_low)

def soft_clip(values):
    return 3.0 * jnp.tanh(values / 3.0)

def filter_widths(amount):
    period = amount // 32
    in_period = jnp.arange(amount, dtype=jnp.int32) % period
    widths = jnp.ones((amount,), jnp.int32)
    for exponent in range(6):
        widths = widths + (in_period * 64 >= period * 2 ** exponent).astype(jnp.int32)
    return widths

def cnn_block(char_block, weights):
    char_table, conv_masked, conv_bias, position_keep, positions, highway_weight, highway_bias, proj_weight, proj_bias = weights
    embedded = char_table[char_block]
    padded = jnp.pad(embedded, ((0, 0), (0, 0), (0, 6), (0, 0)))
    taps = jnp.concatenate([padded[:, :, offset:offset + CH, :] for offset in range(7)], axis=3)
    scores = jnp.einsum('rlcq,qf->rlcf', taps, conv_masked, precision=HIGH) + conv_bias
    scores = low_back(scores)
    guarded = jnp.where(position_keep, scores, -1e+30)
    top_score = lax.optimization_barrier(jnp.max(guarded, axis=2, keepdims=True))
    exp_terms = jnp.where(position_keep, jnp.exp(guarded - top_score), 0.0)
    pooled = top_score[:, :, 0, :] + jnp.log(lax.optimization_barrier(jnp.sum(exp_terms, axis=2))) - jnp.log(positions)
    current = jax.nn.softplus(pooled)
    for depth_index in range(HWY):
        mixed_out = jnp.einsum('rlf,fkg->rlkg', low(current), highway_weight[depth_index], precision=HIGH)
        mixed_out = low_back(mixed_out + highway_bias[depth_index])
        gate_value = jax.nn.sigmoid(mixed_out[:, :, 1, :])
        current = gate_value * current + (1.0 - gate_value) * jax.nn.silu(mixed_out[:, :, 0, :])
    return jnp.einsum('rlf,fp->rlp', low(current), proj_weight, precision=HIGH) + proj_bias

def run_direction(inputs, live, input_weight, state_weight, bias_here, proj_here, backward_dir):
    row_count = inputs.shape[0]
    pre_gates = jnp.einsum('rlp,pgc->rlgc', low(inputs), input_weight, precision=HIGH) + bias_here

    def advance(carry, slices):
        cell_prev, state_prev = carry
        pre_now, live_now = slices
        gates = low_back(pre_now + jnp.einsum('rp,pgc->rgc', low(state_prev), state_weight, precision=HIGH))
        in_gate = jax.nn.sigmoid(gates[:, 0])
        forget = jax.nn.sigmoid(gates[:, 1])
        memory = jnp.tanh(gates[:, 2])
        out_gate = jax.nn.sigmoid(gates[:, 3])
        cell_new = soft_clip(in_gate * memory + forget * cell_prev)
        hidden = out_gate * jnp.tanh(cell_new)
        projected = low_back(jnp.dot(low(hidden), proj_here, precision=HIGH))
        state_new = soft_clip(projected)
        live_col = live_now[:, None]
        cell_next = live_col * cell_new + (1.0 - live_col) * cell_prev
        state_next = live_col * state_new + (1.0 - live_col) * state_prev
        return ((cell_next, state_next), live_col * state_new)
    initial = (jnp.zeros((row_count, proj_here.shape[0]), jnp.float32), jnp.zeros((row_count, proj_here.shape[1]), jnp.float32))
    outputs = lax.scan(jax.checkpoint(advance), initial, (jnp.swapaxes(pre_gates, 0, 1), live.T), reverse=backward_dir)[1]
    return jnp.swapaxes(outputs, 0, 1)

def reference(char_ids, row_lengths, top_grad, char_table, conv_weight, conv_bias, highway_weight, highway_bias, proj_weight, proj_bias, lstm_input, lstm_state, lstm_bias, lstm_proj):
    widths = filter_widths(FILT)
    tap_keep = (jnp.arange(7, dtype=jnp.int32)[:, None] < widths[None, :]).astype(jnp.float32)
    position_keep = jnp.arange(CH, dtype=jnp.int32)[:, None] <= (CH - widths)[None, :]
    positions = (CH - widths + 1).astype(jnp.float32)
    live = (jnp.arange(L, dtype=jnp.int32)[None, :] < row_lengths[:, None]).astype(jnp.float32)
    blocks = char_ids.reshape(-1, MB_ROWS, L, CH)

    def forward(table_f, conv_w, conv_b, high_w, high_b, proj_w, proj_b, lstm_in, lstm_st, lstm_bi, lstm_pr):
        conv_masked = (conv_w * tap_keep[:, None, :]).reshape(7 * EMB, FILT)
        weights = (table_f, conv_masked, conv_b, position_keep, positions, high_w, high_b, proj_w, proj_b)

        def one_block(char_block):
            return cnn_block(char_block, weights)
        base = lax.map(jax.checkpoint(one_block), blocks).reshape(ROWS, L, PROJ)
        base = low_back(base)
        first_out = jnp.stack([run_direction(base, live, lstm_in[0, direction], lstm_st[0, direction], lstm_bi[0, direction], lstm_pr[0, direction], direction == 1) for direction in range(2)], axis=2)
        first_out = low(low_back(first_out))
        second_out = jnp.stack([run_direction(first_out[:, :, direction], live, lstm_in[1, direction], lstm_st[1, direction], lstm_bi[1, direction], lstm_pr[1, direction], direction == 1) for direction in range(2)], axis=2)
        return second_out + first_out
    floats = tuple((item.astype(jnp.float32) for item in (char_table, conv_weight, conv_bias, highway_weight, highway_bias, proj_weight, proj_bias, lstm_input, lstm_state, lstm_bias, lstm_proj)))
    _, pullback = jax.vjp(forward, *floats)
    grads = pullback(top_grad.astype(jnp.float32))
    return (grads[0], grads[1], grads[2], grads[3], grads[4], grads[5], grads[6], grads[7], grads[8], grads[9], grads[10])
```

```python
import jax
import jax.numpy as jnp
from jax import lax
from jax.experimental import pallas as pl
from jax.experimental.pallas import tpu as pltpu
from jax.sharding import PartitionSpec as P

F32 = jnp.float32
BF16 = jnp.bfloat16
PERIODS = 32
TAPS = 7
VMEM_LIMIT = 62 * 1024 * 1024


def dot(left, right, left_dim, right_dim):
    return lax.dot_general(
        left, right, (((left_dim,), (right_dim,)), ((), ())), preferred_element_type=F32
    )


def soft_clip(values):
    return 3.0 * jnp.tanh(values / 3.0)


def filter_widths(offset, amount, total):
    period = total // PERIODS
    in_period = (offset + jnp.arange(amount, dtype=jnp.int32)) % period
    widths = jnp.ones((amount,), jnp.int32)
    for exponent in range(6):
        widths = widths + (in_period * 64 >= period * 2**exponent).astype(jnp.int32)
    return widths


def shift_up(values, amount):
    return jnp.pad(values[:, amount:, :], ((0, 0), (0, amount), (0, 0)))


def shift_down(values, amount):
    count = values.shape[1]
    return jnp.pad(values[:, : count - amount, :], ((0, 0), (amount, 0), (0, 0)))


def spread(values):
    return lax.all_gather(values, "mp", axis=1, tiled=True)


def cnn_forward(chars, weights):
    table, conv_weight, conv_bias, high_weight, high_bias, proj_weight, proj_bias = weights
    tokens, per_token = chars.shape
    emb = table.shape[1]
    local = conv_weight.shape[2]
    one_hot = (chars[:, :, None] == jnp.arange(table.shape[0], dtype=jnp.int32)).astype(BF16)
    one_hot = one_hot.reshape(tokens * per_token, -1)
    repeated = jnp.dot(one_hot, jnp.tile(table, (1, TAPS)), preferred_element_type=F32)
    repeated = repeated.astype(BF16).reshape(tokens, per_token, TAPS * emb)
    group = (jnp.arange(TAPS * emb, dtype=jnp.int32) // emb)[None, None, :]
    taps = repeated
    for offset in range(1, TAPS):
        taps = jnp.where(group == offset, shift_up(repeated, offset), taps)
    widths = filter_widths(lax.axis_index("mp") * local, local, local * lax.axis_size("mp"))
    tap_keep = jnp.arange(TAPS, dtype=jnp.int32)[:, None] < widths[None, :]
    position_keep = jnp.arange(per_token, dtype=jnp.int32)[:, None] <= (per_token - widths)[None, :]
    masked = jnp.where(tap_keep[:, None, :], conv_weight, jnp.zeros_like(conv_weight))
    masked = masked.reshape(-1, local)
    scores = jnp.dot(taps.reshape(tokens * per_token, -1), masked, preferred_element_type=F32)
    scores = scores.reshape(tokens, per_token, local) + conv_bias.astype(F32)
    guarded = jnp.where(position_keep[None], scores, -1e30)
    top_score = jnp.max(guarded, axis=1, keepdims=True)
    exp_terms = jnp.where(position_keep[None], jnp.exp(guarded - top_score), 0.0)
    exp_total = jnp.sum(exp_terms, axis=1)
    positions = (per_token - widths + 1).astype(F32)
    pooled = top_score[:, 0, :] + jnp.log(exp_total) - jnp.log(positions)
    current = jax.nn.softplus(pooled)
    layers = []
    for depth in range(high_weight.shape[0]):
        gathered = spread(current.astype(BF16))
        mixed = jnp.dot(
            gathered, high_weight[depth].reshape(gathered.shape[1], -1), preferred_element_type=F32
        )
        mixed = mixed + high_bias[depth].reshape(-1).astype(F32)
        transform = mixed[:, :local]
        gate = jax.nn.sigmoid(mixed[:, local:])
        layers.append((gathered, current, transform, gate))
        current = gate * current + (1.0 - gate) * jax.nn.silu(transform)
    gathered = spread(current.astype(BF16))
    base = jnp.dot(gathered, proj_weight, preferred_element_type=F32) + proj_bias.astype(F32)
    saved = (one_hot, taps, masked, tap_keep, exp_terms, exp_total, pooled, layers, gathered)
    return base.astype(BF16), saved


def cnn_backward(grad_base, saved, weights):
    table, conv_weight, conv_bias, high_weight, high_bias, proj_weight, proj_bias = weights
    one_hot, taps, masked, tap_keep, exp_terms, exp_total, pooled, layers, gathered = saved
    tokens, per_token, width = taps.shape
    local = masked.shape[1]
    own_rows = lax.dynamic_slice_in_dim(proj_weight, lax.axis_index("mp") * local, local, 0)
    grad_current = dot(grad_base, own_rows, 1, 1)
    mixed_grads = []
    for depth in range(len(layers) - 1, -1, -1):
        gathered_in, before, transform, gate = layers[depth]
        slope = jax.nn.sigmoid(transform)
        grad_transform = grad_current * (1.0 - gate) * slope * (1.0 + transform * (1.0 - slope))
        grad_gate = grad_current * (before - transform * slope) * gate * (1.0 - gate)
        grad_mixed = jnp.concatenate([grad_transform, grad_gate], axis=1).astype(BF16)
        mixed_grads.insert(0, grad_mixed)
        weight_here = high_weight[depth].reshape(gathered_in.shape[1], -1)
        back = lax.psum_scatter(
            dot(weight_here, grad_mixed, 1, 1), "mp", scatter_dimension=0, tiled=True
        )
        grad_current = grad_current * gate + back.T
    scale = grad_current * jax.nn.sigmoid(pooled) / exp_total
    grad_scores = (exp_terms * scale[:, None, :]).astype(BF16)
    grad_flat = grad_scores.reshape(tokens * per_token, local)
    conv_grad = dot(taps.reshape(tokens * per_token, width), grad_flat, 0, 0)
    conv_grad = jnp.where(tap_keep[:, None, :], conv_grad.reshape(conv_weight.shape), 0.0)
    conv_bias_grad = jnp.sum(grad_flat.astype(F32), axis=0)
    grad_taps = dot(grad_flat, masked, 1, 1).reshape(tokens, per_token, width)
    emb = width // TAPS
    group = (jnp.arange(width, dtype=jnp.int32) // emb)[None, None, :]
    moved = grad_taps
    for offset in range(1, TAPS):
        moved = jnp.where(group == offset, shift_down(grad_taps, offset), moved)
    moved = moved.astype(BF16).reshape(tokens * per_token, width)
    table_grad = dot(one_hot, moved, 0, 0).reshape(-1, TAPS, emb).sum(axis=1)
    return table_grad, conv_grad, conv_bias_grad, mixed_grads


MESH = pl.DeviceIdType.MESH
VMEM_SPEC = pl.BlockSpec(memory_space=pltpu.VMEM)
ANY_SPEC = pl.BlockSpec(memory_space=pl.ANY)


def recurrence_kernel(
    base_ref,
    live_ref,
    top_ref,
    w_in,
    w_state,
    bias_ref,
    proj_ref,
    w_in_t,
    w_state_t,
    proj_t,
    x_out,
    state_out,
    hidden_out,
    gates_out,
    projected_out,
    input_out,
    acts,
    cells,
    clips,
    pre,
    grad_cell,
    parts,
    back_parts,
    above,
    gate_buf,
    base_sem,
    send_sem,
    recv_sem,
    back_send,
    back_recv,
    x_send,
    x_recv,
    above_send,
    above_recv,
    gate_sem,
):
    count = lax.axis_size("mp")
    me = lax.axis_index("mp")
    section = lax.axis_index("section")
    steps = x_out.shape[1]
    cell_count = proj_ref.shape[1]
    chunk = min(256, cell_count)
    peers = [lax.rem(me + j, count) for j in range(1, count)]

    barrier = pltpu.get_barrier_semaphore()
    for peer in peers:
        pl.semaphore_signal(barrier, inc=1, device_id={"mp": peer}, device_id_type=MESH)
    pl.semaphore_signal(barrier, inc=1, device_id={"section": 1 - section}, device_id_type=MESH)
    pl.semaphore_wait(barrier, count)

    def wide(values, width):
        return jnp.concatenate([values] * (width // values.shape[1]), axis=1)

    def copy_part(buffer, send, recv, d, parity, source, j, target):
        return pltpu.make_async_remote_copy(
            src_ref=buffer.at[d, parity, source],
            dst_ref=buffer.at[d, parity, source],
            send_sem=send.at[d, parity, j],
            recv_sem=recv.at[d, parity, source],
            device_id={"mp": target},
            device_id_type=MESH,
        )

    def exchange_start(buffer, send, recv, d, parity, value):
        buffer[d, parity, me] = value.astype(BF16)
        for j, peer in enumerate(peers):
            copy_part(buffer, send, recv, d, parity, me, j, peer).start()

    def exchange_wait(buffer, send, recv, d, parity):
        for j, peer in enumerate(peers):
            copy_part(buffer, send, recv, d, parity, peer, j, peer).wait_recv()
        total = buffer[d, parity, 0].astype(F32)
        for source in range(1, count):
            total = total + buffer[d, parity, source].astype(F32)
        for j, peer in enumerate(peers):
            copy_part(buffer, send, recv, d, parity, me, j, peer).wait_send()
        return total

    def pass_up(d, k):
        return pltpu.make_async_remote_copy(
            src_ref=state_out.at[d, k + 1],
            dst_ref=x_out.at[d, k],
            send_sem=x_send.at[d],
            recv_sem=x_recv.at[d, k],
            device_id={"section": 1 - section},
            device_id_type=MESH,
        )

    def pass_down(d, k):
        return pltpu.make_async_remote_copy(
            src_ref=above.at[d, k],
            dst_ref=above.at[d, k],
            send_sem=above_send.at[d],
            recv_sem=above_recv.at[d, k],
            device_id={"section": 1 - section},
            device_id_type=MESH,
        )

    def gates_copy(d, k, parity):
        return pltpu.make_async_copy(
            gate_buf.at[d, parity], gates_out.at[d, k], gate_sem.at[d, parity]
        )

    @pl.when(section == 0)
    def _():
        copy = pltpu.make_async_copy(base_ref, x_out, base_sem)
        copy.start()
        copy.wait()

    for d in range(2):
        state_out[d, 0] = jnp.zeros(state_out.shape[2:], BF16)
        cells[d, 0] = jnp.zeros(cells.shape[2:], F32)
        grad_cell[d] = jnp.zeros(grad_cell.shape[1:], F32)

    def input_part(d, k):
        @pl.when(section == 1)
        def _():
            pass_up(d, k).wait_recv()

        x = x_out[d, k]
        for start in range(0, 4 * cell_count, 2 * chunk):
            cols = slice(start, start + 2 * chunk)
            pre[d, :, cols] = bias_ref[d, :, cols] + jnp.dot(
                x, w_in[d, :, cols], preferred_element_type=F32
            )

    def forward_cells(d, k):
        state = state_out[d, k]
        live = live_ref[d, k]
        for start in range(0, cell_count, chunk):
            raw = []
            for block in range(4):
                cols = slice(block * cell_count + start, block * cell_count + start + chunk)
                raw.append(
                    pre[d, :, cols]
                    + jnp.dot(state, w_state[d, :, cols], preferred_element_type=F32)
                )
            own = slice(start, start + chunk)
            in_gate = jax.nn.sigmoid(raw[0])
            forget = jax.nn.sigmoid(raw[1])
            memory = jnp.tanh(raw[2])
            out_gate = jax.nn.sigmoid(raw[3])
            for block, value in enumerate((in_gate, forget, memory, out_gate)):
                acts[d, k, block, :, own] = value
            cell_new = soft_clip(in_gate * memory + forget * cells[d, k, :, own])
            cells[d, k + 1, :, own] = wide(live, chunk) * cell_new
            hidden_out[d, k, :, own] = (out_gate * jnp.tanh(cell_new)).astype(BF16)
        part = jnp.dot(hidden_out[d, k], proj_ref[d], preferred_element_type=F32)
        exchange_start(parts, send_sem, recv_sem, d, lax.rem(k, 2), part)

    def forward_state(d, k):
        total = exchange_wait(parts, send_sem, recv_sem, d, lax.rem(k, 2))
        clip = jnp.tanh(total / 3.0)
        clips[d, k] = clip
        live = wide(live_ref[d, k], clip.shape[1])
        state_out[d, k + 1] = (live * 3.0 * clip).astype(BF16)

        @pl.when(section == 0)
        def _():
            @pl.when(k > 0)
            def _():
                pass_up(d, k - 1).wait_send()

            pass_up(d, k).start()

    for d in range(2):
        input_part(d, 0)
    for d in range(2):
        forward_cells(d, 0)
    for d in range(2):
        input_part(d, 1)

    @pl.loop(1, steps)
    def _(k):
        for d in range(2):
            forward_state(d, k - 1)
            forward_cells(d, k)

        @pl.when(k + 1 < steps)
        def _():
            for d in range(2):
                input_part(d, k + 1)

    for d in range(2):
        forward_state(d, steps - 1)

    @pl.when(section == 0)
    def _():
        for d in range(2):
            pass_up(d, steps - 1).wait_send()

    def back_wait(d, parity):
        return exchange_wait(back_parts, back_send, back_recv, d, parity)

    def back_start(d, parity, value):
        exchange_start(back_parts, back_send, back_recv, d, parity, value)

    def backward_cells(d, k, total):
        parity = lax.rem(k, 2)
        live = live_ref[d, k]
        clip = clips[d, k]
        grad_out = wide(live, clip.shape[1]) * (total + top_ref[d, k].astype(F32))
        grad_projected = (grad_out * (1.0 - clip * clip)).astype(BF16)
        projected_out[d, k] = grad_projected

        @pl.when(k < steps - 2)
        def _():
            gates_copy(d, k + 2, parity).wait()

        for start in range(0, cell_count, chunk):
            own = slice(start, start + chunk)
            grad_hidden = jnp.dot(grad_projected, proj_t[d, :, own], preferred_element_type=F32)
            in_gate, forget, memory, out_gate = [acts[d, k, block, :, own] for block in range(4)]
            cell = cells[d, k, :, own]
            clip_raw = jnp.tanh((in_gate * memory + forget * cell) / 3.0)
            tanh_cell = jnp.tanh(3.0 * clip_raw)
            grad_new = wide(live, chunk) * grad_cell[d, :, own] + grad_hidden * out_gate * (
                1.0 - tanh_cell * tanh_cell
            )
            grad_raw = grad_new * (1.0 - clip_raw * clip_raw)
            grad_cell[d, :, own] = grad_raw * forget
            grads = (
                grad_raw * memory * in_gate * (1.0 - in_gate),
                grad_raw * cell * forget * (1.0 - forget),
                grad_raw * in_gate * (1.0 - memory * memory),
                grad_hidden * tanh_cell * out_gate * (1.0 - out_gate),
            )
            for block, value in enumerate(grads):
                cols = slice(block * cell_count + start, block * cell_count + start + chunk)
                gate_buf[d, parity, :, cols] = value.astype(BF16)
        gates_copy(d, k, parity).start()

    def backward_state(d, k):
        @pl.when(k > 0)
        def _():
            parity = lax.rem(k, 2)
            back = jnp.dot(gate_buf[d, parity], w_state_t[d], preferred_element_type=F32)
            pre[d, :, : back.shape[1]] = back

            @pl.when(section == 0)
            def _():
                pass_down(d, k - 1).wait_recv()
                pre[d, :, : back.shape[1]] = back + above[d, k - 1]

            back_start(d, lax.rem(k - 1, 2), pre[d, :, : back.shape[1]])

    def backward_input(d, k):
        parity = lax.rem(k, 2)
        part = jnp.dot(gate_buf[d, parity], w_in_t[d], preferred_element_type=F32)

        @pl.when(section == 1)
        def _():
            above[d, k] = part

            @pl.when(k < steps - 1)
            def _():
                pass_down(d, k + 1).wait_send()

            pass_down(d, k).start()

        @pl.when(section == 0)
        def _():
            input_out[d, k] = part

    last = steps - 1

    @pl.when(section == 0)
    def _():
        for d in range(2):
            pass_down(d, last).wait_recv()
            back_start(d, lax.rem(last, 2), above[d, last])

    for d in range(2):

        @pl.when(section == 0)
        def _():
            pre[d, :, : clips.shape[3]] = back_wait(d, lax.rem(last, 2))

        @pl.when(section == 1)
        def _():
            pre[d, :, : clips.shape[3]] = jnp.zeros(clips.shape[2:], F32)

        backward_cells(d, last, pre[d, :, : clips.shape[3]])
        backward_state(d, last)
    for d in range(2):
        backward_input(d, last)

    @pl.loop(1, steps)
    def _(tick):
        k = last - tick
        for d in range(2):
            backward_cells(d, k, back_wait(d, lax.rem(k, 2)))
            backward_state(d, k)
        for d in range(2):
            backward_input(d, k)

    for d in range(2):
        for k in range(min(2, steps)):
            gates_copy(d, k, k % 2).wait()

    @pl.when(section == 1)
    def _():
        for d in range(2):
            pass_down(d, 0).wait_send()


def recurrence(base_seq, live_seq, top_seq, layer_weights):
    w_in, w_state, bias, proj = layer_weights
    _, steps, rows, width = base_seq.shape
    cell_count = proj.shape[1]
    count = lax.axis_size("mp")
    weights = (
        w_in,
        w_state,
        bias.astype(F32)[:, None, :],
        proj,
        jnp.swapaxes(w_in, 1, 2),
        jnp.swapaxes(w_state, 1, 2),
        jnp.swapaxes(proj, 1, 2),
    )
    dma = pltpu.SemaphoreType.DMA
    return pl.pallas_call(
        recurrence_kernel,
        out_shape=(
            jax.ShapeDtypeStruct((2, steps, rows, width), BF16),
            jax.ShapeDtypeStruct((2, steps + 1, rows, width), BF16),
            jax.ShapeDtypeStruct((2, steps, rows, cell_count), BF16),
            jax.ShapeDtypeStruct((2, steps, rows, 4 * cell_count), BF16),
            jax.ShapeDtypeStruct((2, steps, rows, width), BF16),
            jax.ShapeDtypeStruct((2, steps, rows, width), F32),
        ),
        in_specs=[ANY_SPEC] + [VMEM_SPEC] * 9,
        out_specs=(VMEM_SPEC, VMEM_SPEC, VMEM_SPEC, ANY_SPEC, VMEM_SPEC, VMEM_SPEC),
        scratch_shapes=[
            pltpu.VMEM((2, steps, 4, rows, cell_count), F32),
            pltpu.VMEM((2, steps + 1, rows, cell_count), F32),
            pltpu.VMEM((2, steps, rows, width), F32),
            pltpu.VMEM((2, rows, 4 * cell_count), F32),
            pltpu.VMEM((2, rows, cell_count), F32),
            pltpu.VMEM((2, 2, count, rows, width), BF16),
            pltpu.VMEM((2, 2, count, rows, width), BF16),
            pltpu.VMEM((2, steps, rows, width), F32),
            pltpu.VMEM((2, 2, rows, 4 * cell_count), BF16),
            dma,
            dma((2, 2, count - 1)),
            dma((2, 2, count)),
            dma((2, 2, count - 1)),
            dma((2, 2, count)),
            dma((2,)),
            dma((2, steps)),
            dma((2,)),
            dma((2, steps)),
            dma((2, 2)),
        ],
        compiler_params=pltpu.CompilerParams(
            collective_id=0, has_side_effects=True, vmem_limit_bytes=VMEM_LIMIT
        ),
        name="recurrence",
    )(base_seq, live_seq, top_seq, *weights)


def on_device(
    char_ids,
    row_lengths,
    top_grad,
    char_table,
    conv_weight,
    conv_bias,
    highway_weight,
    highway_bias,
    proj_weight,
    proj_bias,
    lstm_input,
    lstm_state,
    lstm_bias,
    lstm_proj,
):
    section = lax.axis_index("section")
    rows, steps, per_token = char_ids.shape
    proj_width = proj_weight.shape[1]
    half = rows // 2
    weights = (
        char_table,
        conv_weight,
        conv_bias,
        highway_weight,
        highway_bias,
        proj_weight,
        proj_bias,
    )
    chars = lax.dynamic_slice_in_dim(char_ids, section * half, half, 0)
    base_half, saved = cnn_forward(chars.reshape(half * steps, per_token), weights)
    base = lax.all_gather(base_half.reshape(half, steps, proj_width), "section", axis=0, tiled=True)
    by_step = jnp.transpose(base, (1, 0, 2))
    base_seq = jnp.stack([by_step, jnp.flip(by_step, axis=0)])
    top_step = jnp.transpose(top_grad, (2, 1, 0, 3))
    top_seq = jnp.stack([top_step[0], jnp.flip(top_step[1], axis=0)])
    live = (jnp.arange(steps, dtype=jnp.int32)[:, None] < row_lengths[None, :]).astype(F32)
    live_seq = jnp.stack([live, jnp.flip(live, axis=0)])[..., None]
    live_seq = jnp.broadcast_to(live_seq, (*live_seq.shape[:3], 128))
    layer_weights = (
        lstm_input[0].reshape(2, proj_width, -1),
        lstm_state[0].reshape(2, proj_width, -1),
        lstm_bias[0].reshape(2, -1),
        lstm_proj[0],
    )
    inputs_all, state_all, hidden_all, grad_gates, grad_projected, input_parts = recurrence(
        base_seq, live_seq, top_seq, layer_weights
    )

    state_all = state_all[:, :steps]
    both = input_parts[0] + jnp.flip(input_parts[1], axis=0)
    grad_base = lax.psum(both, "mp").astype(BF16)
    lower, upper = grad_base[:, :half], grad_base[:, half:]
    passed = lax.ppermute(upper, "section", [(0, 1)])
    grad_half = jnp.where(section == 0, lower, passed)
    grad_half = jnp.transpose(grad_half, (1, 0, 2)).reshape(half * steps, proj_width)
    table_grad, conv_grad, conv_bias_grad, mixed_grads = cnn_backward(grad_half, saved, weights)

    def all_rows(values):
        return lax.all_gather(values, "dp", axis=0, tiled=False)

    def weight_grad(left, right):
        return lax.dot_general(
            left, right, (((0, 2, 3), (0, 2, 3)), ((1,), (1,))), preferred_element_type=F32
        )

    all_inputs, all_states, all_hidden, all_gates, all_projected = [
        all_rows(item) for item in (inputs_all, state_all, hidden_all, grad_gates, grad_projected)
    ]
    input_grad = weight_grad(all_inputs, all_gates)
    state_grad = weight_grad(all_states, all_gates)
    proj_grad = weight_grad(all_hidden, all_projected)

    def all_tokens(values):
        return lax.all_gather(values, ("section", "dp"), axis=0, tiled=True)

    layers, gathered_last = saved[7], saved[8]
    high_grad = jnp.stack(
        [
            dot(all_tokens(layer[0]), all_tokens(grad_mixed), 0, 0)
            for layer, grad_mixed in zip(layers, mixed_grads)
        ]
    )
    proj_weight_grad = dot(all_tokens(gathered_last), all_tokens(grad_half), 0, 0)
    small = lax.psum(
        (
            conv_grad,
            conv_bias_grad,
            jnp.stack([jnp.sum(item.astype(F32), axis=0) for item in mixed_grads]),
            jnp.sum(grad_half.astype(F32), axis=0),
        ),
        ("section", "dp"),
    )
    bias_grad = lax.psum(jnp.sum(grad_gates.astype(F32), axis=(1, 2)), "dp")
    table_grad = lax.psum(table_grad, ("section", "mp", "dp"))
    return (
        table_grad,
        small[0],
        small[1],
        high_grad.reshape(highway_weight.shape),
        small[2].reshape(highway_bias.shape),
        proj_weight_grad,
        small[3],
        input_grad.reshape(lstm_input.shape),
        state_grad.reshape(lstm_state.shape),
        bias_grad.reshape(lstm_bias.shape),
        proj_grad.reshape(lstm_proj.shape),
    )


def solution(mesh):
    return jax.shard_map(
        on_device,
        mesh=mesh,
        in_specs=(
            P("dp", None, None),
            P("dp"),
            P("dp", None, None, None),
            P(),
            P(None, None, "mp"),
            P("mp"),
            P(None, None, None, "mp"),
            P(None, None, "mp"),
            P(),
            P(),
            P("section", None, None, None, "mp"),
            P("section", None, None, None, "mp"),
            P("section", None, None, "mp"),
            P("section", None, "mp", None),
        ),
        out_specs=(
            P(),
            P(None, None, "mp"),
            P("mp"),
            P(None, None, None, "mp"),
            P(None, None, "mp"),
            P(),
            P(),
            P("section", None, None, None, "mp"),
            P("section", None, None, None, "mp"),
            P("section", None, None, "mp"),
            P("section", None, "mp", None),
        ),
        check_vma=False,
    )
```

```python
import functools

import jax
import jax.numpy as jnp
from jax import lax
from jax.experimental import pallas as pl
from jax.experimental.pallas import tpu as pltpu
from jax.sharding import PartitionSpec as P

F32 = jnp.float32
BF16 = jnp.bfloat16
PERIODS = 32
TAPS = 7
VMEM_LIMIT = 62 * 1024 * 1024
SLOTS = 4


def dot(left, right, left_dim, right_dim):
    return lax.dot_general(
        left, right, (((left_dim,), (right_dim,)), ((), ())), preferred_element_type=F32
    )


def soft_clip(values):
    return 3.0 * jnp.tanh(values / 3.0)


def filter_widths(offset, amount, total):
    period = total // PERIODS
    in_period = (offset + jnp.arange(amount, dtype=jnp.int32)) % period
    widths = jnp.ones((amount,), jnp.int32)
    for exponent in range(6):
        widths = widths + (in_period * 64 >= period * 2**exponent).astype(jnp.int32)
    return widths


def shift_up(values, amount):
    return jnp.pad(values[:, amount:, :], ((0, 0), (0, amount), (0, 0)))


def shift_down(values, amount):
    count = values.shape[1]
    return jnp.pad(values[:, : count - amount, :], ((0, 0), (amount, 0), (0, 0)))


def spread(values):
    return lax.all_gather(values, "mp", axis=1, tiled=True)


def cnn_forward(chars, weights):
    table, conv_weight, conv_bias, high_weight, high_bias, proj_weight, proj_bias = weights
    tokens, per_token = chars.shape
    emb = table.shape[1]
    local = conv_weight.shape[2]
    one_hot = (chars[:, :, None] == jnp.arange(table.shape[0], dtype=jnp.int32)).astype(BF16)
    one_hot = one_hot.reshape(tokens * per_token, -1)
    repeated = jnp.dot(one_hot, jnp.tile(table, (1, TAPS)), preferred_element_type=F32)
    repeated = repeated.astype(BF16).reshape(tokens, per_token, TAPS * emb)
    group = (jnp.arange(TAPS * emb, dtype=jnp.int32) // emb)[None, None, :]
    taps = repeated
    for offset in range(1, TAPS):
        taps = jnp.where(group == offset, shift_up(repeated, offset), taps)
    widths = filter_widths(lax.axis_index("mp") * local, local, local * lax.axis_size("mp"))
    tap_keep = jnp.arange(TAPS, dtype=jnp.int32)[:, None] < widths[None, :]
    position_keep = jnp.arange(per_token, dtype=jnp.int32)[:, None] <= (per_token - widths)[None, :]
    masked = jnp.where(tap_keep[:, None, :], conv_weight, jnp.zeros_like(conv_weight))
    masked = masked.reshape(-1, local)
    scores = jnp.dot(taps.reshape(tokens * per_token, -1), masked, preferred_element_type=F32)
    scores = scores.reshape(tokens, per_token, local) + conv_bias.astype(F32)
    guarded = jnp.where(position_keep[None], scores, -1e30)
    top_score = jnp.max(guarded, axis=1, keepdims=True)
    exp_terms = jnp.where(position_keep[None], jnp.exp(guarded - top_score), 0.0)
    exp_total = jnp.sum(exp_terms, axis=1)
    positions = (per_token - widths + 1).astype(F32)
    pooled = top_score[:, 0, :] + jnp.log(exp_total) - jnp.log(positions)
    current = jax.nn.softplus(pooled)
    layers = []
    for depth in range(high_weight.shape[0]):
        gathered = spread(current.astype(BF16))
        mixed = jnp.dot(
            gathered, high_weight[depth].reshape(gathered.shape[1], -1), preferred_element_type=F32
        )
        mixed = mixed + high_bias[depth].reshape(-1).astype(F32)
        transform = mixed[:, :local]
        gate = jax.nn.sigmoid(mixed[:, local:])
        layers.append((gathered, current, transform, gate))
        current = gate * current + (1.0 - gate) * jax.nn.silu(transform)
    gathered = spread(current.astype(BF16))
    base = jnp.dot(gathered, proj_weight, preferred_element_type=F32) + proj_bias.astype(F32)
    saved = (one_hot, taps, masked, tap_keep, exp_terms, exp_total, pooled, layers, gathered)
    return base.astype(BF16), saved


def cnn_backward(grad_base, saved, weights):
    table, conv_weight, conv_bias, high_weight, high_bias, proj_weight, proj_bias = weights
    one_hot, taps, masked, tap_keep, exp_terms, exp_total, pooled, layers, gathered = saved
    tokens, per_token, width = taps.shape
    local = masked.shape[1]
    own_rows = lax.dynamic_slice_in_dim(proj_weight, lax.axis_index("mp") * local, local, 0)
    grad_current = dot(grad_base, own_rows, 1, 1)
    mixed_grads = []
    for depth in range(len(layers) - 1, -1, -1):
        gathered_in, before, transform, gate = layers[depth]
        slope = jax.nn.sigmoid(transform)
        grad_transform = grad_current * (1.0 - gate) * slope * (1.0 + transform * (1.0 - slope))
        grad_gate = grad_current * (before - transform * slope) * gate * (1.0 - gate)
        grad_mixed = jnp.concatenate([grad_transform, grad_gate], axis=1).astype(BF16)
        mixed_grads.insert(0, grad_mixed)
        weight_here = high_weight[depth].reshape(gathered_in.shape[1], -1)
        back = lax.psum_scatter(
            dot(weight_here, grad_mixed, 1, 1), "mp", scatter_dimension=0, tiled=True
        )
        grad_current = grad_current * gate + back.T
    scale = grad_current * jax.nn.sigmoid(pooled) / exp_total
    grad_scores = (exp_terms * scale[:, None, :]).astype(BF16)
    grad_flat = grad_scores.reshape(tokens * per_token, local)
    conv_grad = dot(taps.reshape(tokens * per_token, width), grad_flat, 0, 0)
    conv_grad = jnp.where(tap_keep[:, None, :], conv_grad.reshape(conv_weight.shape), 0.0)
    conv_bias_grad = jnp.sum(grad_flat.astype(F32), axis=0)
    grad_taps = dot(grad_flat, masked, 1, 1).reshape(tokens, per_token, width)
    emb = width // TAPS
    group = (jnp.arange(width, dtype=jnp.int32) // emb)[None, None, :]
    moved = grad_taps
    for offset in range(1, TAPS):
        moved = jnp.where(group == offset, shift_down(grad_taps, offset), moved)
    moved = moved.astype(BF16).reshape(tokens * per_token, width)
    table_grad = dot(one_hot, moved, 0, 0).reshape(-1, TAPS, emb).sum(axis=1)
    return table_grad, conv_grad, conv_bias_grad, mixed_grads


MESH = pl.DeviceIdType.MESH
VMEM_SPEC = pl.BlockSpec(memory_space=pltpu.VMEM)
ANY_SPEC = pl.BlockSpec(memory_space=pl.ANY)


def recurrence_kernel(
    base_ref,
    live_ref,
    top_ref,
    w_in,
    w_state,
    bias_ref,
    proj_ref,
    w_in_t,
    w_state_t,
    proj_t,
    x_all,
    state_all,
    hidden_all,
    gates_all,
    projected_all,
    input_out,
    x_out,
    state_out,
    hidden_out,
    projected_out,
    acts,
    cells,
    clips,
    pre,
    grad_cell,
    parts,
    back_parts,
    above,
    gate_buf,
    base_sem,
    send_sem,
    recv_sem,
    back_send,
    back_recv,
    x_send,
    x_recv,
    above_send,
    above_recv,
    gate_sem,
    gate_send,
    own_sem,
    row_send,
    row_recv,
    relay_send,
    relay_recv,
    lift_send,
    lift_recv,
):
    count = lax.axis_size("mp")
    me = lax.axis_index("mp")
    section = lax.axis_index("section")
    steps = x_out.shape[1]
    cell_count = proj_ref.shape[1]
    chunk = min(256, cell_count)
    peers = [lax.rem(me + j, count) for j in range(1, count)]
    groups = lax.axis_size("dp")
    group = lax.axis_index("dp")
    others = [lax.rem(group + j, groups) for j in range(1, groups)]
    relayed = groups == 4
    beside = group + 1 - 2 * lax.rem(group, 2)
    across = lax.rem(group + 2, 4)
    near = [beside, across] if relayed else others

    barrier = pltpu.get_barrier_semaphore()
    for peer in peers:
        pl.semaphore_signal(barrier, inc=1, device_id={"mp": peer}, device_id_type=MESH)
    pl.semaphore_signal(barrier, inc=1, device_id={"section": 1 - section}, device_id_type=MESH)
    for other in others:
        pl.semaphore_signal(barrier, inc=1, device_id={"dp": other}, device_id_type=MESH)
    pl.semaphore_wait(barrier, count + groups - 1)

    def wide(values, width):
        return jnp.concatenate([values] * (width // values.shape[1]), axis=1)

    def copy_part(buffer, send, recv, d, parity, source, j, target):
        return pltpu.make_async_remote_copy(
            src_ref=buffer.at[d, parity, source],
            dst_ref=buffer.at[d, parity, source],
            send_sem=send.at[d, parity, j],
            recv_sem=recv.at[d, parity, source],
            device_id={"mp": target},
            device_id_type=MESH,
        )

    def exchange_start(buffer, send, recv, d, parity, value):
        buffer[d, parity, me] = value.astype(BF16)
        for j, peer in enumerate(peers):
            copy_part(buffer, send, recv, d, parity, me, j, peer).start()

    def exchange_wait(buffer, send, recv, d, parity):
        for j, peer in enumerate(peers):
            copy_part(buffer, send, recv, d, parity, peer, j, peer).wait_recv()
        total = buffer[d, parity, 0].astype(F32)
        for source in range(1, count):
            total = total + buffer[d, parity, source].astype(F32)
        for j, peer in enumerate(peers):
            copy_part(buffer, send, recv, d, parity, me, j, peer).wait_send()
        return total

    def pass_up(d, k):
        return pltpu.make_async_remote_copy(
            src_ref=state_out.at[d, k + 1],
            dst_ref=x_out.at[d, k],
            send_sem=x_send.at[d],
            recv_sem=x_recv.at[d, k],
            device_id={"section": 1 - section},
            device_id_type=MESH,
        )

    def pass_down(d, k):
        return pltpu.make_async_remote_copy(
            src_ref=above.at[d, k],
            dst_ref=above.at[d, k],
            send_sem=above_send.at[d],
            recv_sem=above_recv.at[d, k],
            device_id={"section": 1 - section},
            device_id_type=MESH,
        )

    def gates_copy(d, k, slot):
        return pltpu.make_async_copy(
            gate_buf.at[d, slot], gates_all.at[d, group, k], gate_sem.at[d, slot]
        )

    def gates_row(d, k, slot, j, other):
        return pltpu.make_async_remote_copy(
            src_ref=gate_buf.at[d, slot],
            dst_ref=gates_all.at[d, group, k],
            send_sem=gate_send.at[d, slot, j],
            recv_sem=row_recv.at[0, j],
            device_id={"dp": other},
            device_id_type=MESH,
        )

    def row(kind, source, target, j, other):
        return pltpu.make_async_remote_copy(
            src_ref=source,
            dst_ref=target,
            send_sem=row_send.at[kind, j],
            recv_sem=row_recv.at[kind, j],
            device_id={"dp": other},
            device_id_type=MESH,
        )

    def from_peer(j, targets):
        back = len(targets) - 1 - j
        return targets[j] if relayed and len(targets) == 2 else targets[back]

    def relay(kind, buffer, d):
        source, target = (beside, across) if d == 0 else (across, beside)
        return pltpu.make_async_remote_copy(
            src_ref=buffer.at[d, source],
            dst_ref=buffer.at[d, source],
            send_sem=relay_send.at[kind, d],
            recv_sem=relay_recv.at[kind, d],
            device_id={"dp": target},
            device_id_type=MESH,
        )

    @pl.when(section == 0)
    def _():
        copy = pltpu.make_async_copy(base_ref, x_out, base_sem)
        copy.start()
        copy.wait()
        for j, other in enumerate(others):
            row(1, x_out, x_all.at[:, group], j, other).start()

    for d in range(2):
        state_out[d, 0] = jnp.zeros(state_out.shape[2:], BF16)
        cells[d, 0] = jnp.zeros(cells.shape[2:], F32)
        grad_cell[d] = jnp.zeros(grad_cell.shape[1:], F32)

    def input_part(d, k):
        @pl.when(section == 1)
        def _():
            pass_up(d, k).wait_recv()

        x = x_out[d, k]
        for start in range(0, 4 * cell_count, 2 * chunk):
            cols = slice(start, start + 2 * chunk)
            pre[d, :, cols] = bias_ref[d, :, cols] + jnp.dot(
                x, w_in[d, :, cols], preferred_element_type=F32
            )

    def forward_cells(d, k):
        state = state_out[d, k]
        live = live_ref[d, k]
        for start in range(0, cell_count, chunk):
            raw = []
            for block in range(4):
                cols = slice(block * cell_count + start, block * cell_count + start + chunk)
                raw.append(
                    pre[d, :, cols]
                    + jnp.dot(state, w_state[d, :, cols], preferred_element_type=F32)
                )
            own = slice(start, start + chunk)
            in_gate = jax.nn.sigmoid(raw[0])
            forget = jax.nn.sigmoid(raw[1])
            memory = jnp.tanh(raw[2])
            out_gate = jax.nn.sigmoid(raw[3])
            for block, value in enumerate((in_gate, forget, memory, out_gate)):
                acts[d, k, block, :, own] = value
            cell_new = soft_clip(in_gate * memory + forget * cells[d, k, :, own])
            cells[d, k + 1, :, own] = wide(live, chunk) * cell_new
            hidden_out[d, k, :, own] = (out_gate * jnp.tanh(cell_new)).astype(BF16)
        part = jnp.dot(hidden_out[d, k], proj_ref[d], preferred_element_type=F32)
        exchange_start(parts, send_sem, recv_sem, d, lax.rem(k, 2), part)
        for j, other in enumerate(others):
            row(2, hidden_out.at[d, k], hidden_all.at[d, group, k], j, other).start()

    def forward_state(d, k):
        total = exchange_wait(parts, send_sem, recv_sem, d, lax.rem(k, 2))
        clip = jnp.tanh(total / 3.0)
        clips[d, k] = clip
        live = wide(live_ref[d, k], clip.shape[1])
        state_out[d, k + 1] = (live * 3.0 * clip).astype(BF16)

        @pl.when(section == 0)
        def _():
            @pl.when(k > 0)
            def _():
                pass_up(d, k - 1).wait_send()

            pass_up(d, k).start()

        for j, other in enumerate(others):
            row(3, state_out.at[d, k + 1], state_all.at[d, group, k + 1], j, other).start()

    for d in range(2):
        input_part(d, 0)
    for d in range(2):
        forward_cells(d, 0)
    for d in range(2):
        input_part(d, 1)

    @pl.loop(1, steps)
    def _(k):
        for d in range(2):
            forward_state(d, k - 1)
            forward_cells(d, k)

        @pl.when(k + 1 < steps)
        def _():
            for d in range(2):
                input_part(d, k + 1)

    for d in range(2):
        forward_state(d, steps - 1)

    @pl.when(section == 0)
    def _():
        for d in range(2):
            pass_up(d, steps - 1).wait_send()

    def back_wait(d, parity):
        return exchange_wait(back_parts, back_send, back_recv, d, parity)

    def back_start(d, parity, value):
        exchange_start(back_parts, back_send, back_recv, d, parity, value)

    def backward_cells(d, k, total):
        slot = lax.rem(k, SLOTS)
        live = live_ref[d, k]
        clip = clips[d, k]
        grad_out = wide(live, clip.shape[1]) * (total + top_ref[d, k].astype(F32))
        grad_projected = (grad_out * (1.0 - clip * clip)).astype(BF16)
        projected_out[d, k] = grad_projected

        for j, other in enumerate(near):
            row(
                4, projected_out.at[d, k], projected_all.at[d, group, k], j, other
            ).start()

        @pl.when(k < steps - SLOTS)
        def _():
            gates_copy(d, k + SLOTS, slot).wait()
            for j, other in enumerate(near):
                gates_row(d, k + SLOTS, slot, j, other).wait_send()

        for start in range(0, cell_count, chunk):
            own = slice(start, start + chunk)
            grad_hidden = jnp.dot(grad_projected, proj_t[d, :, own], preferred_element_type=F32)
            in_gate, forget, memory, out_gate = [acts[d, k, block, :, own] for block in range(4)]
            cell = cells[d, k, :, own]
            clip_raw = jnp.tanh((in_gate * memory + forget * cell) / 3.0)
            tanh_cell = jnp.tanh(3.0 * clip_raw)
            grad_new = wide(live, chunk) * grad_cell[d, :, own] + grad_hidden * out_gate * (
                1.0 - tanh_cell * tanh_cell
            )
            grad_raw = grad_new * (1.0 - clip_raw * clip_raw)
            grad_cell[d, :, own] = grad_raw * forget
            grads = (
                grad_raw * memory * in_gate * (1.0 - in_gate),
                grad_raw * cell * forget * (1.0 - forget),
                grad_raw * in_gate * (1.0 - memory * memory),
                grad_hidden * tanh_cell * out_gate * (1.0 - out_gate),
            )
            for block, value in enumerate(grads):
                cols = slice(block * cell_count + start, block * cell_count + start + chunk)
                gate_buf[d, slot, :, cols] = value.astype(BF16)
        gates_copy(d, k, slot).start()

    def gates_send(d, k):
        for j, other in enumerate(near):
            gates_row(d, k, lax.rem(k, SLOTS), j, other).start()

    def backward_state(d, k):
        @pl.when(k > 0)
        def _():
            back = jnp.dot(gate_buf[d, lax.rem(k, SLOTS)], w_state_t[d], preferred_element_type=F32)
            pre[d, :, : back.shape[1]] = back

            @pl.when(section == 0)
            def _():
                pass_down(d, k - 1).wait_recv()
                pre[d, :, : back.shape[1]] = back + above[d, k - 1]

            back_start(d, lax.rem(k - 1, 2), pre[d, :, : back.shape[1]])

    def backward_input(d, k):
        gates_send(d, k)
        part = jnp.dot(gate_buf[d, lax.rem(k, SLOTS)], w_in_t[d], preferred_element_type=F32)

        @pl.when(section == 1)
        def _():
            above[d, k] = part

            @pl.when(k < steps - 1)
            def _():
                pass_down(d, k + 1).wait_send()

            pass_down(d, k).start()

        @pl.when(section == 0)
        def _():
            input_out[d, k] = part

    last = steps - 1

    @pl.when(section == 0)
    def _():
        for d in range(2):
            pass_down(d, last).wait_recv()
            back_start(d, lax.rem(last, 2), above[d, last])

    for d in range(2):

        @pl.when(section == 0)
        def _():
            pre[d, :, : clips.shape[3]] = back_wait(d, lax.rem(last, 2))

        @pl.when(section == 1)
        def _():
            pre[d, :, : clips.shape[3]] = jnp.zeros(clips.shape[2:], F32)

        backward_cells(d, last, pre[d, :, : clips.shape[3]])
        backward_state(d, last)
    for d in range(2):
        backward_input(d, last)

    @pl.loop(1, steps)
    def _(tick):
        k = last - tick
        for d in range(2):
            backward_cells(d, k, back_wait(d, lax.rem(k, 2)))
            backward_state(d, k)
        for d in range(2):
            backward_input(d, k)

    for d in range(2):
        for k in range(min(SLOTS, steps)):
            gates_copy(d, k, k % SLOTS).wait()
            for j, other in enumerate(near):
                gates_row(d, k, k % SLOTS, j, other).wait_send()

    @pl.when(section == 1)
    def _():
        for d in range(2):
            pass_down(d, 0).wait_send()

    own = [
        (hidden_out, hidden_all.at[:, group]),
        (state_out, state_all.at[:, group]),
        (projected_out, projected_all.at[:, group]),
    ]
    for other in others:
        own.append((state_out.at[:, 0], state_all.at[:, other, 0]))
    own = [
        pltpu.make_async_copy(source, target, own_sem.at[i])
        for i, (source, target) in enumerate(own)
    ]
    for copy in own:
        copy.start()

    rest = pl.ds(1, steps)
    for j, other in enumerate(others):
        source = from_peer(j, others)
        hidden_row = row(2, hidden_out, hidden_all.at[:, source], j, other)
        state_row = row(3, state_out.at[:, rest], state_all.at[:, source, rest], j, other)
        for copy in (hidden_row, state_row):
            copy.wait_send()
            copy.wait_recv()

    for copy in own:
        copy.wait()

    @pl.when(section == 0)
    def _():
        mine = pltpu.make_async_copy(x_out, x_all.at[:, group], base_sem)
        mine.start()
        for j, other in enumerate(others):
            copy = row(1, x_out, x_all.at[:, from_peer(j, others)], j, other)
            copy.wait_send()
            copy.wait_recv()
        mine.wait()

    def lift():
        return pltpu.make_async_remote_copy(
            src_ref=state_all.at[:, :, rest],
            dst_ref=x_all,
            send_sem=lift_send,
            recv_sem=lift_recv,
            device_id={"section": 1 - section},
            device_id_type=MESH,
        )

    @pl.when(section == 0)
    def _():
        lift().start()

    for j, other in enumerate(near):
        source = from_peer(j, near)
        pltpu.make_async_remote_copy(
            src_ref=gates_all.at[:, source],
            dst_ref=gates_all.at[:, source],
            send_sem=row_send.at[0, j],
            recv_sem=row_recv.at[0, j],
            device_id={"dp": other},
            device_id_type=MESH,
        ).wait_recv()
        projected_row = row(4, projected_out, projected_all.at[:, source], j, other)
        projected_row.wait_send()
        projected_row.wait_recv()

    if relayed:
        for d in range(2):
            relay(0, gates_all, d).start()
            relay(1, projected_all, d).start()
        for d in range(2):
            for kind, buffer in ((0, gates_all), (1, projected_all)):
                copy = relay(kind, buffer, d)
                copy.wait_send()
                far = 3 - group
                pltpu.make_async_remote_copy(
                    src_ref=buffer.at[d, far],
                    dst_ref=buffer.at[d, far],
                    send_sem=relay_send.at[kind, d],
                    recv_sem=relay_recv.at[kind, d],
                    device_id={"dp": across if d == 0 else beside},
                    device_id_type=MESH,
                ).wait_recv()

    @pl.when(section == 0)
    def _():
        lift().wait_send()

    @pl.when(section == 1)
    def _():
        lift().wait_recv()


def recurrence(base_seq, live_seq, top_seq, layer_weights):
    w_in, w_state, bias, proj = layer_weights
    _, steps, rows, width = base_seq.shape
    cell_count = proj.shape[1]
    count = lax.axis_size("mp")
    groups = lax.axis_size("dp")
    weights = (
        w_in,
        w_state,
        bias.astype(F32)[:, None, :],
        proj,
        jnp.swapaxes(w_in, 1, 2),
        jnp.swapaxes(w_state, 1, 2),
        jnp.swapaxes(proj, 1, 2),
    )
    dma = pltpu.SemaphoreType.DMA
    return pl.pallas_call(
        recurrence_kernel,
        out_shape=(
            jax.ShapeDtypeStruct((2, groups, steps, rows, width), BF16),
            jax.ShapeDtypeStruct((2, groups, steps + 1, rows, width), BF16),
            jax.ShapeDtypeStruct((2, groups, steps, rows, cell_count), BF16),
            jax.ShapeDtypeStruct((2, groups, steps, rows, 4 * cell_count), BF16),
            jax.ShapeDtypeStruct((2, groups, steps, rows, width), BF16),
            jax.ShapeDtypeStruct((2, steps, rows, width), F32),
        ),
        in_specs=[ANY_SPEC] + [VMEM_SPEC] * 9,
        out_specs=(*[ANY_SPEC] * 5, VMEM_SPEC),
        scratch_shapes=[
            pltpu.VMEM((2, steps, rows, width), BF16),
            pltpu.VMEM((2, steps + 1, rows, width), BF16),
            pltpu.VMEM((2, steps, rows, cell_count), BF16),
            pltpu.VMEM((2, steps, rows, width), BF16),
            pltpu.VMEM((2, steps, 4, rows, cell_count), F32),
            pltpu.VMEM((2, steps + 1, rows, cell_count), F32),
            pltpu.VMEM((2, steps, rows, width), F32),
            pltpu.VMEM((2, rows, 4 * cell_count), F32),
            pltpu.VMEM((2, rows, cell_count), F32),
            pltpu.VMEM((2, 2, count, rows, width), BF16),
            pltpu.VMEM((2, 2, count, rows, width), BF16),
            pltpu.VMEM((2, steps, rows, width), F32),
            pltpu.VMEM((2, SLOTS, rows, 4 * cell_count), BF16),
            dma,
            dma((2, 2, count - 1)),
            dma((2, 2, count)),
            dma((2, 2, count - 1)),
            dma((2, 2, count)),
            dma((2,)),
            dma((2, steps)),
            dma((2,)),
            dma((2, steps)),
            dma((2, SLOTS)),
            dma((2, SLOTS, groups - 1)),
            dma((groups + 2,)),
            dma((5, groups - 1)),
            dma((5, groups - 1)),
            dma((2, 2)),
            dma((2, 2)),
            dma,
            dma,
        ],
        compiler_params=pltpu.CompilerParams(
            collective_id=0, has_side_effects=True, vmem_limit_bytes=VMEM_LIMIT
        ),
        name="recurrence",
    )(base_seq, live_seq, top_seq, *weights)


def weight_grads(lefts, right, parts):
    batch, tokens, _ = lefts[0].shape
    sizes = [left.shape[2] for left in lefts]
    columns = right.shape[2] // parts
    block = min(256, columns)
    blocks = columns // block
    chunk = 256

    def kernel(*refs):
        left_refs = refs[: len(lefts)]
        right_refs = refs[len(lefts) : len(lefts) + parts]
        out_refs = refs[len(lefts) + parts : -3]
        bias_out, turned, ones = refs[-3:]

        @pl.when(pl.program_id(1) == 0)
        def _():
            start = 0
            for left, size in zip(left_refs, sizes):
                for offset in range(0, size, chunk):
                    turned[start + offset : start + offset + chunk, :] = left[
                        0, :, offset : offset + chunk
                    ].T
                start += size
            ones[...] = jnp.ones_like(ones)

        start = 0
        for out, size in zip(out_refs, sizes):

            @pl.loop(0, size // chunk)
            def _(i):
                at = pl.multiple_of(start + i * chunk, chunk)
                own = pl.multiple_of(i * chunk, chunk)
                left = turned[pl.ds(at, chunk), :]
                for part in range(parts):
                    out[0, pl.ds(own, chunk), part, :] = jnp.dot(
                        left, right_refs[part][0], preferred_element_type=F32
                    )

            start += size
        for part in range(parts):
            bias_out[0, part : part + 1, :] = jnp.dot(
                ones[...], right_refs[part][0], preferred_element_type=F32
            )[:1]

    return pl.pallas_call(
        kernel,
        out_shape=(
            *[jax.ShapeDtypeStruct((batch, size, parts, columns), F32) for size in sizes],
            jax.ShapeDtypeStruct((batch, parts, columns), F32),
        ),
        grid=(batch, blocks),
        in_specs=[
            *[pl.BlockSpec((1, tokens, size), lambda b, n: (b, 0, 0)) for size in sizes],
            *[
                pl.BlockSpec(
                    (1, tokens, block), functools.partial(lambda g, b, n: (b, 0, g * blocks + n), g)
                )
                for g in range(parts)
            ],
        ],
        out_specs=(
            *[pl.BlockSpec((1, size, parts, block), lambda b, n: (b, 0, 0, n)) for size in sizes],
            pl.BlockSpec((1, parts, block), lambda b, n: (b, 0, n)),
        ),
        scratch_shapes=[
            pltpu.VMEM((sum(sizes), tokens), BF16),
            pltpu.VMEM((16, tokens), BF16),
        ],
        compiler_params=pltpu.CompilerParams(vmem_limit_bytes=VMEM_LIMIT),
        name="weight_grads",
    )(*lefts, *[right] * parts)


def on_device(
    char_ids,
    row_lengths,
    top_grad,
    char_table,
    conv_weight,
    conv_bias,
    highway_weight,
    highway_bias,
    proj_weight,
    proj_bias,
    lstm_input,
    lstm_state,
    lstm_bias,
    lstm_proj,
):
    section = lax.axis_index("section")
    rows, steps, per_token = char_ids.shape
    proj_width = proj_weight.shape[1]
    half = rows // 2
    weights = (
        char_table,
        conv_weight,
        conv_bias,
        highway_weight,
        highway_bias,
        proj_weight,
        proj_bias,
    )
    chars = lax.dynamic_slice_in_dim(char_ids, section * half, half, 0)
    base_half, saved = cnn_forward(chars.reshape(half * steps, per_token), weights)
    base = lax.all_gather(base_half.reshape(half, steps, proj_width), "section", axis=0, tiled=True)
    by_step = jnp.transpose(base, (1, 0, 2))
    base_seq = jnp.stack([by_step, jnp.flip(by_step, axis=0)])
    top_step = jnp.transpose(top_grad, (2, 1, 0, 3))
    top_seq = jnp.stack([top_step[0], jnp.flip(top_step[1], axis=0)])
    live = (jnp.arange(steps, dtype=jnp.int32)[:, None] < row_lengths[None, :]).astype(F32)
    live_seq = jnp.stack([live, jnp.flip(live, axis=0)])[..., None]
    live_seq = jnp.broadcast_to(live_seq, (*live_seq.shape[:3], 128))
    layer_weights = (
        lstm_input[0].reshape(2, proj_width, -1),
        lstm_state[0].reshape(2, proj_width, -1),
        lstm_bias[0].reshape(2, -1),
        lstm_proj[0],
    )
    all_inputs, all_states, all_hidden, all_gates, all_projected, input_parts = recurrence(
        base_seq, live_seq, top_seq, layer_weights
    )
    both = input_parts[0] + jnp.flip(input_parts[1], axis=0)
    grad_base = lax.psum(both, "mp").astype(BF16)
    lower, upper = grad_base[:, :half], grad_base[:, half:]
    passed = lax.ppermute(upper, "section", [(0, 1)])
    grad_half = jnp.where(section == 0, lower, passed)
    grad_half = jnp.transpose(grad_half, (1, 0, 2)).reshape(half * steps, proj_width)
    table_grad, conv_grad, conv_bias_grad, mixed_grads = cnn_backward(grad_half, saved, weights)

    def flat(values):
        return values.reshape(2, -1, values.shape[4])

    input_grad, state_grad, bias_grad = weight_grads(
        [flat(all_inputs), flat(all_states[:, :, :steps])], flat(all_gates), 4
    )
    proj_grad = lax.dot_general(
        flat(all_hidden),
        flat(all_projected),
        (((1,), (1,)), ((0,), (0,))),
        preferred_element_type=F32,
    )

    def all_tokens(values):
        return lax.all_gather(values, ("section", "dp"), axis=values.ndim - 2, tiled=True)

    layers, gathered_last = saved[7], saved[8]
    high_grad, high_bias_grad = weight_grads(
        [all_tokens(jnp.stack([layer[0] for layer in layers]))],
        all_tokens(jnp.stack(mixed_grads)),
        2,
    )
    all_base = all_tokens(grad_half)
    proj_weight_grad = dot(all_tokens(gathered_last), all_base, 0, 0)
    small = lax.psum((conv_grad, conv_bias_grad), ("section", "dp"))
    table_grad = lax.psum(table_grad, ("section", "mp", "dp"))
    return (
        table_grad,
        small[0],
        small[1],
        high_grad,
        high_bias_grad,
        proj_weight_grad,
        jnp.sum(all_base.astype(F32), axis=0),
        input_grad.reshape(lstm_input.shape),
        state_grad.reshape(lstm_state.shape),
        bias_grad.reshape(lstm_bias.shape),
        proj_grad.reshape(lstm_proj.shape),
    )


def solution(mesh):
    return jax.shard_map(
        on_device,
        mesh=mesh,
        in_specs=(
            P("dp", None, None),
            P("dp"),
            P("dp", None, None, None),
            P(),
            P(None, None, "mp"),
            P("mp"),
            P(None, None, None, "mp"),
            P(None, None, "mp"),
            P(),
            P(),
            P("section", None, None, None, "mp"),
            P("section", None, None, None, "mp"),
            P("section", None, None, "mp"),
            P("section", None, "mp", None),
        ),
        out_specs=(
            P(),
            P(None, None, "mp"),
            P("mp"),
            P(None, None, None, "mp"),
            P(None, None, "mp"),
            P(),
            P(),
            P("section", None, None, None, "mp"),
            P("section", None, None, None, "mp"),
            P("section", None, None, "mp"),
            P("section", None, "mp", None),
        ),
        check_vma=False,
    )
```

```python
import functools

import jax
import jax.numpy as jnp
from jax import lax
from jax.experimental import pallas as pl
from jax.experimental.pallas import tpu as pltpu
from jax.sharding import PartitionSpec as P

F32 = jnp.float32
BF16 = jnp.bfloat16
PERIODS = 32
TAPS = 7
VMEM_LIMIT = 62 * 1024 * 1024
SLOTS = 4
CHUNK = 16
TURN = 128
RELAY_SHARE = 4
PER_TOKEN = 50
CHARS = 262


def dot(left, right, left_dim, right_dim):
    return lax.dot_general(
        left, right, (((left_dim,), (right_dim,)), ((), ())), preferred_element_type=F32
    )


def soft_clip(values):
    return 3.0 * jnp.tanh(values / 3.0)


def filter_widths(offset, amount, total):
    period = total // PERIODS
    in_period = (offset + jnp.arange(amount, dtype=jnp.int32)) % period
    widths = jnp.ones((amount,), jnp.int32)
    for exponent in range(6):
        widths = widths + (in_period * 64 >= period * 2**exponent).astype(jnp.int32)
    return widths


MESH = pl.DeviceIdType.MESH
VMEM_SPEC = pl.BlockSpec(memory_space=pltpu.VMEM)
ANY_SPEC = pl.BlockSpec(memory_space=pl.ANY)


def column_peers():
    count = lax.axis_size("mp")
    me = lax.axis_index("mp")
    return [lax.rem(me + j, count) for j in range(1, count)]


def greet(devices):
    barrier = pltpu.get_barrier_semaphore()
    for device in devices:
        pl.semaphore_signal(barrier, inc=1, device_id=device, device_id_type=MESH)
    pl.semaphore_wait(barrier, len(devices))


def remote(source, target, send, recv, device):
    return pltpu.make_async_remote_copy(
        src_ref=source,
        dst_ref=target,
        send_sem=send,
        recv_sem=recv,
        device_id=device,
        device_id_type=MESH,
    )


def one_hot_columns(ids, vocabulary):
    symbols = lax.broadcasted_iota(jnp.int32, (vocabulary, ids.shape[1]), 0)
    return (symbols == ids).astype(F32).astype(BF16)


def cnn_forward_kernel(
    ids_ref,
    table_ref,
    flags_ref,
    masked_ref,
    log_positions,
    w_high,
    b_high,
    w_proj,
    b_proj,
    input_ref,
    state_ref,
    base_out,
    taps_out,
    peak_out,
    pooled_out,
    features,
    current_out,
    transform_out,
    gate_out,
    features_all,
    input_out,
    state_out,
    raw,
    turned,
    send_sem,
    recv_sem,
    base_send,
    base_recv,
    row_send,
    row_recv,
    own_sem,
    relay_send,
    relay_recv,
    raw_sem,
    turned_sem,
):
    count = lax.axis_size("mp")
    me = lax.axis_index("mp")
    section = lax.axis_index("section")
    peers = column_peers()
    depth_count, tokens, local = current_out.shape
    chunk_rows = ids_ref.shape[2]
    padded = chunk_rows // CHUNK
    half = tokens // 2
    emb = 16
    block = min(256, local)
    groups = lax.axis_size("dp")
    group = lax.axis_index("dp")
    others = [lax.rem(group + j, groups) for j in range(1, groups)]
    relayed = groups == 4
    beside = group + 1 - 2 * lax.rem(group, 2)
    across = lax.rem(group + 2, 4)
    far = 3 - group
    near = [beside, across] if relayed else others
    origin = near if relayed else others[::-1]
    greet(
        [{"mp": peer} for peer in peers]
        + [{"section": 1 - section}]
        + [{"dp": other} for other in others]
    )

    def relay_rows(depth, way, slot):
        pieces = pl.ds(way * (count // 2), count // 2)
        return remote(
            features_all.at[depth, section, slot, pieces],
            features_all.at[depth, section, slot, pieces],
            relay_send.at[depth, way],
            relay_recv.at[depth, way],
            {"dp": across if way == 0 else beside},
        )

    def pass_rows(depth):
        for j in range(len(near)):
            give_rows(depth, j, origin[j]).wait_recv()
        if relayed and depth + 1 < depth_count:
            for way in range(2):
                relay_rows(depth, way, beside if way == 0 else across).start()

    blocks = input_out.shape[2] // TURN
    units = 4 * blocks

    def fetch(unit, start):
        slot = lax.rem(unit, 2)
        d = lax.rem(unit, 2 * blocks) // blocks
        rows = pl.ds(pl.multiple_of(lax.rem(unit, blocks) * TURN, TURN), TURN)
        for which, source in enumerate((input_ref, state_ref)):

            @pl.when(unit // (2 * blocks) == which)
            def _():
                copy = pltpu.make_async_copy(source.at[d, rows], raw.at[slot], raw_sem.at[slot])
                copy.start() if start else copy.wait()

    def deliver(unit, start):
        slot = lax.rem(unit, 2)
        d = lax.rem(unit, 2 * blocks) // blocks
        rows = pl.ds(pl.multiple_of(lax.rem(unit, blocks) * TURN, TURN), TURN)
        for which, target in enumerate((input_out, state_out)):

            @pl.when(unit // (2 * blocks) == which)
            def _():
                copy = pltpu.make_async_copy(
                    turned.at[slot], target.at[d, :, rows], turned_sem.at[slot]
                )
                copy.start() if start else copy.wait()

    def turn_units(first, last):
        @pl.loop(first, last)
        def _(unit):
            slot = lax.rem(unit, 2)
            fetch(unit, False)

            @pl.when(unit + 1 < units)
            def _():
                fetch(unit + 1, True)

            @pl.when(unit >= 2)
            def _():
                deliver(unit - 2, False)

            for g in range(4):
                turned[slot, g] = raw[slot, :, g, :]
            deliver(unit, True)

    fetch(0, True)

    def own_rows(depth):
        return pltpu.make_async_copy(
            features.at[depth], features_all.at[depth, section, group], own_sem.at[depth]
        )

    def give_rows(depth, j, slot):
        return remote(
            features.at[depth],
            features_all.at[depth, section, slot],
            row_send.at[depth, j],
            row_recv.at[depth, j],
            {"dp": near[j]},
        )

    def send(depth, part, rows, start):
        for j, peer in enumerate(peers):
            copy = remote(
                features.at[depth, me, rows],
                features.at[depth, me, rows],
                send_sem.at[depth, part, j],
                recv_sem.at[depth, part, me],
                {"mp": peer},
            )
            if start:
                copy.start()
            else:
                copy.wait_send()

    def receive(depth, part):
        rows = pl.ds(part * half, half)
        for j, peer in enumerate(peers):
            remote(
                features.at[depth, peer, rows],
                features.at[depth, peer, rows],
                send_sem.at[depth, part, j],
                recv_sem.at[depth, part, peer],
                {"mp": peer},
            ).wait_recv()

    lane_group = lax.broadcasted_iota(jnp.int32, (chunk_rows, 128), 1) // emb

    def pool_chunk(c):
        hot = one_hot_columns(ids_ref[c], table_ref.shape[0])
        embedded = lax.dot_general(
            hot, table_ref[...], (((0,), (0,)), ((), ())), preferred_element_type=F32
        )
        taps = embedded + flags_ref[...]
        for offset in range(1, TAPS):
            rolled = pltpu.roll(embedded, chunk_rows - offset, 0)
            taps = jnp.where(lane_group == offset, rolled, taps)
        taps = taps.astype(BF16)
        taps_out[c] = taps
        rows = pl.ds(pl.multiple_of(c * CHUNK, CHUNK), CHUNK)
        for start in range(0, local, block):
            cols = slice(start, start + block)
            scores = jnp.dot(taps, masked_ref[:, cols], preferred_element_type=F32)
            scores = scores.reshape(CHUNK, padded, block)
            top = jnp.max(scores, axis=1, keepdims=True)
            total = jnp.sum(jnp.exp(scores - top), axis=1, keepdims=True)
            peak = top + jnp.log(total)
            peak_out[rows, :, cols] = peak
            pooled = jnp.sum(peak, axis=1) - log_positions[:, cols]
            pooled_out[rows, cols] = pooled
            current = jnp.maximum(pooled, 0.0) + jnp.log1p(jnp.exp(-jnp.abs(pooled)))
            current_out[0, rows, cols] = current
            features[0, me, rows, cols] = current.astype(BF16)
        return rows

    for part in range(2):

        @pl.loop(0, half // CHUNK)
        def _(i):
            rows = pool_chunk(part * (half // CHUNK) + i)
            send(0, part, rows, True)

    for depth in range(depth_count):
        for part in range(2):
            rows = pl.ds(part * half, half)
            receive(depth, part)
            if part == 1:
                own_rows(depth).start()
                for j in range(len(near)):
                    give_rows(depth, j, group).start()
            mixed = []
            for g in range(2):
                total = jnp.broadcast_to(b_high[depth, g : g + 1, :], (half, local))
                for p in range(count):
                    total = total + jnp.dot(
                        features[depth, p, rows, :],
                        w_high[depth, g, p * local : (p + 1) * local, :],
                        preferred_element_type=F32,
                    )
                mixed.append(total)
            transform = mixed[0]
            gate = jax.nn.sigmoid(mixed[1])
            transform_out[depth, rows, :] = transform
            gate_out[depth, rows, :] = gate
            current = gate * current_out[depth, rows, :] + (1.0 - gate) * (
                transform * jax.nn.sigmoid(transform)
            )
            if depth + 1 < depth_count:
                current_out[depth + 1, rows, :] = current
            features[depth + 1, me, rows, :] = current.astype(BF16)
            send(depth + 1, part, rows, True)
        if depth >= 1:
            pass_rows(depth - 1)
        turn_units(depth * units * 3 // (4 * depth_count), (depth + 1) * units * 3 // (4 * depth_count))

    def give():
        return remote(
            base_out.at[section],
            base_out.at[section],
            base_send,
            base_recv,
            {"section": 1 - section},
        )

    for part in range(2):
        rows = pl.ds(part * half, half)
        receive(depth_count, part)
        total = jnp.broadcast_to(b_proj[...], (half, w_proj.shape[1]))
        for p in range(count):
            total = total + jnp.dot(
                features[depth_count, p, rows, :],
                w_proj[p * local : (p + 1) * local, :],
                preferred_element_type=F32,
            )
        base_out[section, rows, :] = total
    give().start()
    turn_units(units * 3 // 4, units)
    pass_rows(depth_count - 1)
    for depth in range(depth_count + 1):
        for part in range(2):
            send(depth, part, pl.ds(part * half, half), False)
    give().wait_send()
    remote(
        base_out.at[1 - section],
        base_out.at[1 - section],
        base_send,
        base_recv,
        {"section": 1 - section},
    ).wait_recv()
    for depth in range(depth_count):
        own_rows(depth).wait()
        for j in range(len(near)):
            give_rows(depth, j, group).wait_send()
        if relayed and depth + 1 < depth_count:
            for way in range(2):
                relay_rows(depth, way, beside if way == 0 else across).wait_send()
                relay_rows(depth, way, far).wait_recv()
    for unit in range(units - 2, units):
        deliver(unit, False)


def cnn_forward(ids, weights, lstm_input, lstm_state):
    table, masked, log_positions, w_high, b_high, w_proj, b_proj = weights
    chunks, _, chunk_rows = ids.shape
    tokens = chunks * CHUNK
    depth_count, _, total, local = w_high.shape
    count = lax.axis_size("mp")
    groups = lax.axis_size("dp")
    directions, in_width, gate_blocks, cell_columns = lstm_input.shape
    padded = chunk_rows // CHUNK
    position = jnp.tile(jnp.arange(padded, dtype=jnp.int32), CHUNK)[:, None]
    lane = jnp.arange(128, dtype=jnp.int32)[None, :]
    width = lane - 16 * TAPS
    flags = (lane == 16 * TAPS) | ((width >= 1) & (width <= TAPS) & (position > PER_TOKEN - width))
    dma = pltpu.SemaphoreType.DMA
    return pl.pallas_call(
        cnn_forward_kernel,
        out_shape=(
            jax.ShapeDtypeStruct((2, tokens, w_proj.shape[1]), F32),
            jax.ShapeDtypeStruct((chunks, chunk_rows, 128), BF16),
            jax.ShapeDtypeStruct((tokens, 1, local), F32),
            jax.ShapeDtypeStruct((tokens, local), F32),
            jax.ShapeDtypeStruct((depth_count + 1, count, tokens, local), BF16),
            jax.ShapeDtypeStruct((depth_count, tokens, local), F32),
            jax.ShapeDtypeStruct((depth_count, tokens, local), F32),
            jax.ShapeDtypeStruct((depth_count, tokens, local), F32),
            jax.ShapeDtypeStruct((depth_count, 2, groups, count, tokens, local), BF16),
            jax.ShapeDtypeStruct((directions, gate_blocks, in_width, cell_columns), BF16),
            jax.ShapeDtypeStruct((directions, gate_blocks, in_width, cell_columns), BF16),
        ),
        in_specs=[VMEM_SPEC] * 9 + [ANY_SPEC] * 2,
        out_specs=(*[VMEM_SPEC] * 8, *[ANY_SPEC] * 3),
        scratch_shapes=[
            pltpu.VMEM((2, TURN, gate_blocks, cell_columns), BF16),
            pltpu.VMEM((2, gate_blocks, TURN, cell_columns), BF16),
            dma((depth_count + 1, 2, count - 1)),
            dma((depth_count + 1, 2, count)),
            dma,
            dma,
            dma((depth_count, groups - 1)),
            dma((depth_count, groups - 1)),
            dma((depth_count,)),
            dma((depth_count, 2)),
            dma((depth_count, 2)),
            dma((2,)),
            dma((2,)),
        ],
        compiler_params=pltpu.CompilerParams(
            collective_id=1, has_side_effects=True, vmem_limit_bytes=VMEM_LIMIT
        ),
        name="cnn_forward",
    )(
        ids,
        table,
        flags.astype(F32),
        masked,
        log_positions,
        w_high,
        b_high,
        w_proj,
        b_proj,
        lstm_input,
        lstm_state,
    )


def cnn_backward_kernel(
    base_ref,
    own_ref,
    w_high,
    current_ref,
    transform_ref,
    gate_ref,
    peak_ref,
    pooled_ref,
    taps_ref,
    masked_ref,
    masked_t,
    ids_ref,
    gates_in,
    projected_in,
    x_in,
    state_all,
    gates_all,
    projected_all,
    x_all,
    base_full,
    mixed_all,
    late_first,
    late_second,
    conv_out,
    table_out,
    mixed_out,
    late_buf,
    base_all,
    table_sum,
    table_all,
    grad_current,
    outgoing,
    incoming,
    base_send,
    base_recv,
    sum_send,
    sum_recv,
    own_sem,
    relay_send,
    relay_recv,
    lift_send,
    lift_recv,
    row_send,
    row_recv,
    full_sem,
    share_send,
    share_recv,
    table_send,
    table_recv,
    mixed_sem,
    mixed_send,
    mixed_recv,
    mixed_share,
    mixed_shared,
    late_sem,
):
    count = lax.axis_size("mp")
    me = lax.axis_index("mp")
    section = lax.axis_index("section")
    groups = lax.axis_size("dp")
    group = lax.axis_index("dp")
    peers = column_peers()
    depth_count, tokens, local = current_ref.shape
    steps = x_all.shape[2]
    chunks, chunk_rows, _ = taps_ref.shape
    padded = chunk_rows // CHUNK
    emb = 16
    vocabulary = -(-CHARS // 8) * 8
    relayed = groups == 4
    beside = group + 1 - 2 * lax.rem(group, 2)
    across = lax.rem(group + 2, 4)
    far = 3 - group
    greet(
        [{"mp": peer} for peer in peers]
        + [{"section": 1 - section, "mp": peer} for peer in [*peers, me]]
        + [{"dp": lax.rem(group + j, groups)} for j in range(1, groups)]
    )

    def lift():
        return remote(
            state_all.at[:, :, pl.ds(1, steps)],
            x_all,
            lift_send,
            lift_recv,
            {"section": 1 - section},
        )

    def relay(kind, buffer, d, slot):
        early = pl.ds(0, steps if kind == 0 else steps // RELAY_SHARE)
        return remote(
            buffer.at[d, slot, early],
            buffer.at[d, slot, early],
            relay_send.at[kind, d],
            relay_recv.at[kind, d],
            {"dp": across if d == 0 else beside},
        )

    buffers = ((0, projected_all), (1, gates_all))

    early = steps // RELAY_SHARE
    late = pl.ds(early, steps - early)
    late_loads = [
        pltpu.make_async_copy(gates_all.at[d, slot, late], late_buf.at[d], late_sem.at[d])
        for d, slot in ((0, beside), (1, across))
    ]
    late_stores = [
        pltpu.make_async_copy(late_buf.at[d], target, late_sem.at[d])
        for d, target in ((0, late_first), (1, late_second))
    ]
    if relayed:
        for copy in late_loads:
            copy.start()

    def spread_base(half, target_section, peer, j):
        return remote(
            base_ref.at[half],
            base_all.at[me],
            base_send.at[half, j],
            base_recv.at[me],
            {"section": target_section, "mp": peer},
        )

    everyone = [*peers, me]

    @pl.when(section == 0)
    def _():
        for j, peer in enumerate(peers):
            spread_base(0, 0, peer, j).start()
        for j, peer in enumerate(everyone):
            spread_base(1, 1, peer, j).start()
        lift().start()
        own = pltpu.make_async_copy(base_ref.at[0], base_all.at[me], own_sem)
        own.start()
        own.wait()

    def base_arrival(source):
        return remote(
            base_ref.at[0],
            base_all.at[source],
            base_send.at[0, 0],
            base_recv.at[source],
            {"section": 1 - section},
        )

    for peer in peers:
        base_arrival(peer).wait_recv()

    @pl.when(section == 1)
    def _():
        base_arrival(me).wait_recv()

    others = [lax.rem(group + j, groups) for j in range(1, groups)]
    keep = pltpu.make_async_copy(base_all, base_full.at[section, group], full_sem)
    keep.start()

    def base_row(j, slot):
        return remote(
            base_all,
            base_full.at[section, slot],
            row_send.at[j],
            row_recv.at[j],
            {"dp": others[j]},
        )

    def share_base(owner):
        return remote(
            base_full.at[owner],
            base_full.at[owner],
            share_send,
            share_recv,
            {"section": 1 - section},
        )

    for j in range(groups - 1):
        base_row(j, group).start()

    def keep_mixed(depth):
        return pltpu.make_async_copy(
            mixed_out.at[depth], mixed_all.at[depth, section, group], mixed_sem.at[depth]
        )

    def mixed_row(depth, j, slot):
        return remote(
            mixed_out.at[depth],
            mixed_all.at[depth, section, slot],
            mixed_send.at[depth, j],
            mixed_recv.at[depth, j],
            {"dp": others[j]},
        )

    def share_mixed(depth, owner):
        return remote(
            mixed_all.at[depth, owner],
            mixed_all.at[depth, owner],
            mixed_share.at[depth],
            mixed_shared.at[depth],
            {"section": 1 - section},
        )

    def collect_mixed(depth):
        keep_mixed(depth).wait()
        for j in range(groups - 1):
            mixed_row(depth, j, others[groups - 2 - j]).wait_recv()
        share_mixed(depth, section).start()

    wide = base_all.shape[2]
    total = jnp.zeros((tokens, local), F32)
    for p in range(count):
        total = total + jnp.dot(
            base_all[p], own_ref[p * wide : (p + 1) * wide, :], preferred_element_type=F32
        )
    grad_current[...] = total

    def send_sum(depth, peer, j):
        return remote(
            outgoing.at[depth, j],
            incoming.at[depth, me],
            sum_send.at[depth, j],
            sum_recv.at[depth, me],
            {"mp": peer},
        )

    def back(depth, owner):
        rows = pl.ds(pl.multiple_of(owner * local, local), local)
        parts = [
            lax.dot_general(
                mixed_out[depth, :, g * local : (g + 1) * local],
                w_high[depth, g, rows, :],
                (((1,), (1,)), ((), ())),
                preferred_element_type=F32,
            )
            for g in range(2)
        ]
        return parts[0] + parts[1]

    for depth in range(depth_count - 1, -1, -1):
        transform = transform_ref[depth]
        gate = gate_ref[depth]
        grad = grad_current[...]
        slope = jax.nn.sigmoid(transform)
        mixed_out[depth, :, :local] = (
            grad * (1.0 - gate) * slope * (1.0 + transform * (1.0 - slope))
        ).astype(BF16)
        mixed_out[depth, :, local:] = (
            grad * (current_ref[depth] - transform * slope) * gate * (1.0 - gate)
        ).astype(BF16)
        keep_mixed(depth).start()
        for j in range(groups - 1):
            mixed_row(depth, j, group).start()
        if relayed and depth == depth_count - 1:
            for kind, buffer in buffers:
                for d in range(2):
                    relay(kind, buffer, d, beside if d == 0 else across).start()
        for j, peer in enumerate(peers):
            outgoing[depth, j] = back(depth, peer).astype(BF16)
            send_sum(depth, peer, j).start()
        total = grad * gate + back(depth, me)
        for j, peer in enumerate(peers):
            remote(
                outgoing.at[depth, j],
                incoming.at[depth, peer],
                sum_send.at[depth, j],
                sum_recv.at[depth, peer],
                {"mp": peer},
            ).wait_recv()
            total = total + incoming[depth, peer].astype(F32)
        grad_current[...] = total

    if relayed:
        for load, store in zip(late_loads, late_stores):
            load.wait()
            store.start()
    for depth in range(depth_count - 1, 0, -1):
        collect_mixed(depth)
    grad_current[...] = grad_current[...] * jax.nn.sigmoid(pooled_ref[...])
    conv_out[...] = jnp.zeros_like(conv_out)
    table_sum[...] = jnp.zeros_like(table_sum)
    lane_group = lax.broadcasted_iota(jnp.int32, (chunk_rows, 128), 1) // emb

    @pl.loop(0, chunks)
    def _(c):
        rows = pl.ds(pl.multiple_of(c * CHUNK, CHUNK), CHUNK)
        taps = taps_ref[c]
        scores = jnp.dot(taps, masked_ref[...], preferred_element_type=F32)
        scores = scores.reshape(CHUNK, padded, local)
        share = jnp.exp(scores - peak_ref[rows])
        grads = share * grad_current[rows, :][:, None, :]
        grads = grads.reshape(chunk_rows, local).astype(BF16)
        conv_out[...] += lax.dot_general(
            taps, grads, (((0,), (0,)), ((), ())), preferred_element_type=F32
        )
        back_taps = jnp.dot(grads, masked_t[...], preferred_element_type=F32)
        moved = back_taps
        for offset in range(1, TAPS):
            moved = jnp.where(lane_group == offset, pltpu.roll(back_taps, offset, 0), moved)
        hot = one_hot_columns(ids_ref[c], vocabulary)
        table_sum[:vocabulary, :] += jnp.dot(
            hot, moved.astype(BF16), preferred_element_type=F32
        )

    columns = table_sum[...].T
    folded = columns[:emb]
    for offset in range(1, TAPS):
        folded = folded + columns[offset * emb : (offset + 1) * emb]
    table_all[me] = folded

    def table_copy(j, slot):
        return remote(
            table_all.at[slot],
            table_all.at[slot],
            table_send.at[j],
            table_recv.at[slot],
            {"mp": peers[j]},
        )

    for j in range(count - 1):
        table_copy(j, me).start()

    for j in range(count - 1):
        table_copy(j, peers[j]).wait_recv()
    folded = table_all[0]
    for p in range(1, count):
        folded = folded + table_all[p]
    table_out[...] = folded
    for j in range(count - 1):
        table_copy(j, me).wait_send()
    keep.wait()
    for j in range(groups - 1):
        base_row(j, others[groups - 2 - j]).wait_recv()
    share_base(section).start()
    collect_mixed(0)
    for j in range(groups - 1):
        base_row(j, group).wait_send()
        for depth in range(depth_count):
            mixed_row(depth, j, group).wait_send()
    for depth in range(depth_count):
        for j, peer in enumerate(peers):
            send_sum(depth, peer, j).wait_send()

    @pl.when(section == 0)
    def _():
        for j, peer in enumerate(peers):
            spread_base(0, 0, peer, j).wait_send()
        for j, peer in enumerate(everyone):
            spread_base(1, 1, peer, j).wait_send()
        lift().wait_send()

    @pl.when(section == 1)
    def _():
        lift().wait_recv()

    if relayed:
        for kind, buffer in buffers:
            for d in range(2):
                relay(kind, buffer, d, beside if d == 0 else across).wait_send()
                relay(kind, buffer, d, far).wait_recv()
        for copy in late_stores:
            copy.wait()

    share_base(section).wait_send()
    share_base(1 - section).wait_recv()
    for depth in range(depth_count):
        share_mixed(depth, section).wait_send()
        share_mixed(depth, 1 - section).wait_recv()


def cnn_backward(base_shards, saved, weights, rows_all):
    own_rows, w_high, masked, ids = weights
    taps, peak, pooled, current, transform, gate = saved
    gates_all, projected_all, x_all, state_all = rows_all
    depth_count, tokens, local = current.shape
    count = lax.axis_size("mp")
    groups = lax.axis_size("dp")
    vocabulary = -(-CHARS // 128) * 128
    steps = gates_all.shape[2]
    late = steps - steps // RELAY_SHARE
    dma = pltpu.SemaphoreType.DMA
    return pl.pallas_call(
        cnn_backward_kernel,
        out_shape=(
            jax.ShapeDtypeStruct(gates_all.shape, BF16),
            jax.ShapeDtypeStruct(projected_all.shape, BF16),
            jax.ShapeDtypeStruct(x_all.shape, BF16),
            jax.ShapeDtypeStruct((2, groups, count, tokens, base_shards.shape[2]), BF16),
            jax.ShapeDtypeStruct((depth_count, 2, groups, tokens, 2 * local), BF16),
            jax.ShapeDtypeStruct((late, *gates_all.shape[3:]), BF16),
            jax.ShapeDtypeStruct((late, *gates_all.shape[3:]), BF16),
            jax.ShapeDtypeStruct((128, local), F32),
            jax.ShapeDtypeStruct((16, vocabulary), F32),
        ),
        in_specs=[VMEM_SPEC] * 12 + [ANY_SPEC] * 4,
        out_specs=(*[ANY_SPEC] * 7, *[VMEM_SPEC] * 2),
        input_output_aliases={12: 0, 13: 1, 14: 2},
        scratch_shapes=[
            pltpu.VMEM((depth_count, tokens, 2 * local), BF16),
            pltpu.VMEM((2, late, *gates_all.shape[3:]), BF16),
            pltpu.VMEM((count, tokens, base_shards.shape[2]), BF16),
            pltpu.VMEM((vocabulary, 128), F32),
            pltpu.VMEM((count, 16, vocabulary), F32),
            pltpu.VMEM((tokens, local), F32),
            pltpu.VMEM((depth_count, count - 1, tokens, local), BF16),
            pltpu.VMEM((depth_count, count, tokens, local), BF16),
            dma((2, count)),
            dma((count,)),
            dma((depth_count, count - 1)),
            dma((depth_count, count)),
            dma,
            dma((2, 2)),
            dma((2, 2)),
            dma,
            dma,
            dma((groups - 1,)),
            dma((groups - 1,)),
            dma,
            dma,
            dma,
            dma((count - 1,)),
            dma((count,)),
            dma((depth_count,)),
            dma((depth_count, groups - 1)),
            dma((depth_count, groups - 1)),
            dma((depth_count,)),
            dma((depth_count,)),
            dma((2,)),
        ],
        compiler_params=pltpu.CompilerParams(
            collective_id=2, has_side_effects=True, vmem_limit_bytes=VMEM_LIMIT
        ),
        name="cnn_backward",
    )(
        base_shards,
        own_rows,
        w_high,
        current,
        transform,
        gate,
        peak,
        pooled,
        taps,
        masked,
        jnp.pad(masked[: 16 * TAPS], ((0, 128 - 16 * TAPS), (0, 0))).T,
        ids,
        gates_all,
        projected_all,
        x_all,
        state_all,
    )


def recurrence_kernel(
    base_ref,
    live_ref,
    top_ref,
    w_in,
    w_state,
    bias_ref,
    proj_ref,
    features_in,
    x_all,
    state_all,
    hidden_all,
    gates_all,
    projected_all,
    base_out,
    features_all,
    x_out,
    state_out,
    hidden_out,
    projected_out,
    acts,
    cells,
    clips,
    pre,
    grad_cell,
    parts,
    back_parts,
    above,
    gate_buf,
    base_sem,
    send_sem,
    recv_sem,
    back_send,
    back_recv,
    x_send,
    x_recv,
    above_send,
    above_recv,
    gate_sem,
    gate_send,
    own_sem,
    row_send,
    row_recv,
    w_in_t,
    w_state_t,
    proj_t,
    input_parts,
    input_sums,
    input_send,
    input_recv,
    base_sum,
    share_send,
    share_recv,
    relay_send,
    relay_recv,
):
    count = lax.axis_size("mp")
    me = lax.axis_index("mp")
    section = lax.axis_index("section")
    steps = x_out.shape[1]
    cell_count = proj_ref.shape[1]
    chunk = min(256, cell_count)
    peers = [lax.rem(me + j, count) for j in range(1, count)]
    groups = lax.axis_size("dp")
    group = lax.axis_index("dp")
    others = [lax.rem(group + j, groups) for j in range(1, groups)]
    relayed = groups == 4
    beside = group + 1 - 2 * lax.rem(group, 2)
    across = lax.rem(group + 2, 4)
    near = [beside, across] if relayed else others

    barrier = pltpu.get_barrier_semaphore()
    for peer in peers:
        pl.semaphore_signal(barrier, inc=1, device_id={"mp": peer}, device_id_type=MESH)
    pl.semaphore_signal(barrier, inc=1, device_id={"section": 1 - section}, device_id_type=MESH)
    for other in others:
        pl.semaphore_signal(barrier, inc=1, device_id={"dp": other}, device_id_type=MESH)
    pl.semaphore_wait(barrier, count + groups - 1)

    def share_features(owner):
        return remote(
            features_all.at[:, owner],
            features_all.at[:, owner],
            share_send,
            share_recv,
            {"section": 1 - section},
        )

    pieces = features_all.shape[3]

    def relay_features(way, slot):
        half = pl.ds(way * (pieces // 2), pieces // 2)
        depth = features_all.shape[0] - 1
        return remote(
            features_all.at[depth, section, slot, half],
            features_all.at[depth, section, slot, half],
            relay_send.at[way],
            relay_recv.at[way],
            {"dp": across if way == 0 else beside},
        )

    if relayed:
        for way in range(2):
            relay_features(way, beside if way == 0 else across).start()

    def wide(values, width):
        return jnp.concatenate([values] * (width // values.shape[1]), axis=1)

    def copy_part(buffer, send, recv, d, parity, source, j, target):
        return pltpu.make_async_remote_copy(
            src_ref=buffer.at[d, parity, source],
            dst_ref=buffer.at[d, parity, source],
            send_sem=send.at[d, parity, j],
            recv_sem=recv.at[d, parity, source],
            device_id={"mp": target},
            device_id_type=MESH,
        )

    ordered = peers
    if count == 4:
        ordered = [3 - me, lax.rem(me + 2, 4), me + 1 - 2 * lax.rem(me, 2)]

    def exchange_start(buffer, send, recv, d, parity, value):
        buffer[d, parity, me] = value.astype(BF16)
        for j, peer in enumerate(ordered):
            copy_part(buffer, send, recv, d, parity, me, j, peer).start()

    def exchange_wait(buffer, send, recv, d, parity):
        for j, peer in enumerate(ordered):
            copy_part(buffer, send, recv, d, parity, peer, j, peer).wait_recv()
        total = buffer[d, parity, 0].astype(F32)
        for source in range(1, count):
            total = total + buffer[d, parity, source].astype(F32)
        for j, peer in enumerate(ordered):
            copy_part(buffer, send, recv, d, parity, me, j, peer).wait_send()
        return total

    def pass_up(d, k):
        return pltpu.make_async_remote_copy(
            src_ref=state_out.at[d, k + 1],
            dst_ref=x_out.at[d, k],
            send_sem=x_send.at[d],
            recv_sem=x_recv.at[d, k],
            device_id={"section": 1 - section},
            device_id_type=MESH,
        )

    def pass_down(d, k):
        return pltpu.make_async_remote_copy(
            src_ref=above.at[d, k],
            dst_ref=above.at[d, k],
            send_sem=above_send.at[d],
            recv_sem=above_recv.at[d, k],
            device_id={"section": 1 - section},
            device_id_type=MESH,
        )

    def gates_copy(d, k, slot):
        return pltpu.make_async_copy(
            gate_buf.at[d, slot], gates_all.at[d, group, k], gate_sem.at[d, slot]
        )

    def gates_row(d, k, slot, j, other):
        return pltpu.make_async_remote_copy(
            src_ref=gate_buf.at[d, slot],
            dst_ref=gates_all.at[d, group, k],
            send_sem=gate_send.at[d, slot, j],
            recv_sem=row_recv.at[0, j],
            device_id={"dp": other},
            device_id_type=MESH,
        )

    def row(kind, source, target, j, other):
        return pltpu.make_async_remote_copy(
            src_ref=source,
            dst_ref=target,
            send_sem=row_send.at[kind, j],
            recv_sem=row_recv.at[kind, j],
            device_id={"dp": other},
            device_id_type=MESH,
        )

    def from_peer(j, targets):
        back = len(targets) - 1 - j
        return targets[j] if relayed and len(targets) == 2 else targets[back]

    def time_of(d, k):
        return k if d == 0 else steps - 1 - k

    @pl.when(section == 0)
    def _():
        part_rows = base_ref.shape[1] // steps

        @pl.loop(0, steps)
        def _(t):
            at = pl.ds(pl.multiple_of(t * part_rows, part_rows), part_rows)
            x = jnp.concatenate([base_ref[0, at, :], base_ref[1, at, :]], axis=0).astype(BF16)
            for d in range(2):
                x_out[d, time_of(d, t)] = x

        for j, other in enumerate(others):
            row(1, x_out, x_all.at[:, group], j, other).start()

    for d in range(2):
        state_out[d, 0] = jnp.zeros(state_out.shape[2:], BF16)
        cells[d, 0] = jnp.zeros(cells.shape[2:], F32)
        grad_cell[d] = jnp.zeros(grad_cell.shape[1:], F32)

    def input_part(d, k):
        @pl.when(section == 1)
        def _():
            pass_up(d, k).wait_recv()

        x = x_out[d, k]
        for block in range(4):
            for start in range(0, cell_count, chunk):
                cols = slice(block * cell_count + start, block * cell_count + start + chunk)
                pre[d, :, cols] = bias_ref[d, :, cols] + jnp.dot(
                    x, w_in[d, block, :, start : start + chunk], preferred_element_type=F32
                )

    def turn_weights(unit):
        per_block = cell_count // chunk
        block = unit // per_block
        cols = pl.ds(pl.multiple_of(lax.rem(unit, per_block) * chunk, chunk), chunk)
        rows_t = pl.ds(pl.multiple_of(unit * chunk, chunk), chunk)
        for d in range(2):
            w_in_t[d, rows_t, :] = w_in[d, block, :, cols].T
            w_state_t[d, rows_t, :] = w_state[d, block, :, cols].T

    def turn_proj(unit):
        cols = pl.ds(pl.multiple_of(unit * 128, 128), 128)
        for d in range(2):
            proj_t[d, :, cols] = proj_ref[d, cols, :].T

    def forward_cells(d, k):
        state = state_out[d, k]
        live = live_ref[time_of(d, k)]
        for start in range(0, cell_count, chunk):
            raw = []
            for block in range(4):
                cols = slice(block * cell_count + start, block * cell_count + start + chunk)
                raw.append(
                    pre[d, :, cols]
                    + jnp.dot(
                        state, w_state[d, block, :, start : start + chunk], preferred_element_type=F32
                    )
                )
            own = slice(start, start + chunk)
            in_gate = jax.nn.sigmoid(raw[0])
            forget = jax.nn.sigmoid(raw[1])
            memory = jnp.tanh(raw[2])
            out_gate = jax.nn.sigmoid(raw[3])
            for block, value in enumerate((in_gate, forget, memory, out_gate)):
                acts[d, k, block, :, own] = value
            cell_new = soft_clip(in_gate * memory + forget * cells[d, k, :, own])
            cells[d, k + 1, :, own] = wide(live, chunk) * cell_new
            hidden_out[d, k, :, own] = (out_gate * jnp.tanh(cell_new)).astype(BF16)
        part = jnp.dot(hidden_out[d, k], proj_ref[d], preferred_element_type=F32)
        exchange_start(parts, send_sem, recv_sem, d, lax.rem(k, 2), part)
        for j, other in enumerate(others):
            row(2, hidden_out.at[d, k], hidden_all.at[d, group, k], j, other).start()

    def forward_state(d, k):
        total = exchange_wait(parts, send_sem, recv_sem, d, lax.rem(k, 2))
        clip = jnp.tanh(total / 3.0)
        clips[d, k] = clip
        live = wide(live_ref[time_of(d, k)], clip.shape[1])
        state_out[d, k + 1] = (live * 3.0 * clip).astype(BF16)

        @pl.when(section == 0)
        def _():
            @pl.when(k > 0)
            def _():
                pass_up(d, k - 1).wait_send()

            pass_up(d, k).start()

        for j, other in enumerate(others):
            row(3, state_out.at[d, k + 1], state_all.at[d, group, k + 1], j, other).start()

    units = 4 * cell_count // chunk
    for d in range(2):
        input_part(d, 0)
    for d in range(2):
        forward_cells(d, 0)
    for d in range(2):
        input_part(d, 1)

    @pl.loop(1, steps)
    def _(k):
        for d in range(2):
            forward_state(d, k - 1)
            forward_cells(d, k)

        @pl.when(k + 1 < steps)
        def _():
            for d in range(2):
                input_part(d, k + 1)

        @pl.when(k <= units)
        def _():
            turn_weights(k - 1)

        @pl.when(k <= cell_count // 128)
        def _():
            turn_proj(k - 1)

    for unit in range(steps - 1, units):
        turn_weights(unit)
    for d in range(2):
        forward_state(d, steps - 1)
    if relayed:
        for way in range(2):
            relay_features(way, beside if way == 0 else across).wait_send()
            relay_features(way, 3 - group).wait_recv()
    share_features(section).start()

    @pl.when(section == 0)
    def _():
        for d in range(2):
            pass_up(d, steps - 1).wait_send()

    def back_wait(d, parity):
        return exchange_wait(back_parts, back_send, back_recv, d, parity)

    def back_start(d, parity, value):
        exchange_start(back_parts, back_send, back_recv, d, parity, value)

    def backward_cells(d, k, total):
        slot = lax.rem(k, SLOTS)
        live = live_ref[time_of(d, k)]
        clip = clips[d, k]
        grad_out = wide(live, clip.shape[1]) * (total + top_ref[d, time_of(d, k)].astype(F32))
        grad_projected = (grad_out * (1.0 - clip * clip)).astype(BF16)
        projected_out[d, k] = grad_projected

        for j, other in enumerate(near):
            row(
                4, projected_out.at[d, k], projected_all.at[d, group, k], j, other
            ).start()

        @pl.when(k < steps - SLOTS)
        def _():
            gates_copy(d, k + SLOTS, slot).wait()
            for j, other in enumerate(near):
                gates_row(d, k + SLOTS, slot, j, other).wait_send()

        for start in range(0, cell_count, chunk):
            own = slice(start, start + chunk)
            grad_hidden = jnp.dot(grad_projected, proj_t[d, :, own], preferred_element_type=F32)
            in_gate, forget, memory, out_gate = [acts[d, k, block, :, own] for block in range(4)]
            cell = cells[d, k, :, own]
            clip_raw = jnp.tanh((in_gate * memory + forget * cell) / 3.0)
            tanh_cell = jnp.tanh(3.0 * clip_raw)
            grad_new = wide(live, chunk) * grad_cell[d, :, own] + grad_hidden * out_gate * (
                1.0 - tanh_cell * tanh_cell
            )
            grad_raw = grad_new * (1.0 - clip_raw * clip_raw)
            grad_cell[d, :, own] = grad_raw * forget
            grads = (
                grad_raw * memory * in_gate * (1.0 - in_gate),
                grad_raw * cell * forget * (1.0 - forget),
                grad_raw * in_gate * (1.0 - memory * memory),
                grad_hidden * tanh_cell * out_gate * (1.0 - out_gate),
            )
            for block, value in enumerate(grads):
                cols = slice(block * cell_count + start, block * cell_count + start + chunk)
                gate_buf[d, slot, :, cols] = value.astype(BF16)
        gates_copy(d, k, slot).start()

    def gates_send(d, k):
        for j, other in enumerate(near):
            gates_row(d, k, lax.rem(k, SLOTS), j, other).start()

    def backward_state(d, k):
        @pl.when(k > 0)
        def _():
            back = jnp.dot(gate_buf[d, lax.rem(k, SLOTS)], w_state_t[d], preferred_element_type=F32)
            pre[d, :, : back.shape[1]] = back

            @pl.when(section == 0)
            def _():
                pass_down(d, k - 1).wait_recv()
                pre[d, :, : back.shape[1]] = back + above[d, k - 1]

            back_start(d, lax.rem(k - 1, 2), pre[d, :, : back.shape[1]])

    share = base_out.shape[2]

    def input_copy(source, target, j, peer):
        return remote(source, target, input_send.at[j], input_recv.at[j], {"mp": peer})

    def backward_input(d, k):
        gates_send(d, k)
        part = jnp.dot(gate_buf[d, lax.rem(k, SLOTS)], w_in_t[d], preferred_element_type=F32)

        @pl.when(section == 1)
        def _():
            above[d, k] = part

            @pl.when(k < steps - 1)
            def _():
                pass_down(d, k + 1).wait_send()

            pass_down(d, k).start()

        @pl.when(section == 0)
        def _():
            for p in range(count):
                input_parts[d, k, p] = part[:, p * share : (p + 1) * share].astype(BF16)
            for j, peer in enumerate(peers):
                input_copy(input_parts.at[d, k, peer], input_sums.at[d, k, me], j, peer).start()

    last = steps - 1

    @pl.when(section == 0)
    def _():
        for d in range(2):
            pass_down(d, last).wait_recv()
            back_start(d, lax.rem(last, 2), above[d, last])

    for d in range(2):

        @pl.when(section == 0)
        def _():
            pre[d, :, : clips.shape[3]] = back_wait(d, lax.rem(last, 2))

        @pl.when(section == 1)
        def _():
            pre[d, :, : clips.shape[3]] = jnp.zeros(clips.shape[2:], F32)

        backward_cells(d, last, pre[d, :, : clips.shape[3]])
        backward_state(d, last)
    for d in range(2):
        backward_input(d, last)

    @pl.loop(1, steps)
    def _(tick):
        k = last - tick
        for d in range(2):
            backward_cells(d, k, back_wait(d, lax.rem(k, 2)))
            backward_state(d, k)
        for d in range(2):
            backward_input(d, k)

    for d in range(2):
        for k in range(min(SLOTS, steps)):
            gates_copy(d, k, k % SLOTS).wait()
            for j, other in enumerate(near):
                gates_row(d, k, k % SLOTS, j, other).wait_send()

    @pl.when(section == 1)
    def _():
        for d in range(2):
            pass_down(d, 0).wait_send()

    own = [
        (hidden_out, hidden_all.at[:, group]),
        (state_out, state_all.at[:, group]),
        (projected_out, projected_all.at[:, group]),
    ]
    for other in others:
        own.append((state_out.at[:, 0], state_all.at[:, other, 0]))
    own = [
        pltpu.make_async_copy(source, target, own_sem.at[i])
        for i, (source, target) in enumerate(own)
    ]
    for copy in own:
        copy.start()

    rest = pl.ds(1, steps)
    for j, other in enumerate(others):
        source = from_peer(j, others)
        hidden_row = row(2, hidden_out, hidden_all.at[:, source], j, other)
        state_row = row(3, state_out.at[:, rest], state_all.at[:, source, rest], j, other)
        for copy in (hidden_row, state_row):
            copy.wait_send()
            copy.wait_recv()

    for copy in own:
        copy.wait()

    @pl.when(section == 0)
    def _():
        mine = pltpu.make_async_copy(x_out, x_all.at[:, group], base_sem)
        mine.start()
        for j, other in enumerate(others):
            copy = row(1, x_out, x_all.at[:, from_peer(j, others)], j, other)
            copy.wait_send()
            copy.wait_recv()
        mine.wait()

    @pl.when(section == 0)
    def _():
        for j, peer in enumerate(peers):
            source = peers[count - 2 - j]
            copy = input_copy(input_parts.at[:, :, peer], input_sums.at[:, :, source], j, peer)
            copy.wait_send()
            copy.wait_recv()
        rows_half = base_out.shape[1] // steps

        @pl.loop(0, steps)
        def _(t):
            total = input_parts[0, t, me].astype(F32) + input_parts[1, steps - 1 - t, me].astype(F32)
            for peer in peers:
                total = total + input_sums[0, t, peer].astype(F32)
                total = total + input_sums[1, steps - 1 - t, peer].astype(F32)
            at = pl.ds(pl.multiple_of(t * rows_half, rows_half), rows_half)
            for half in range(2):
                base_sum[half, at, :] = total[half * rows_half : (half + 1) * rows_half]

        base_out[...] = base_sum[...].astype(BF16)

    share_features(section).wait_send()
    share_features(1 - section).wait_recv()

    for j, other in enumerate(near):
        source = from_peer(j, near)
        pltpu.make_async_remote_copy(
            src_ref=gates_all.at[:, source],
            dst_ref=gates_all.at[:, source],
            send_sem=row_send.at[0, j],
            recv_sem=row_recv.at[0, j],
            device_id={"dp": other},
            device_id_type=MESH,
        ).wait_recv()
        projected_row = row(4, projected_out, projected_all.at[:, source], j, other)
        projected_row.wait_send()
        projected_row.wait_recv()


def recurrence(base_seq, live_seq, top_seq, layer_weights, features_all):
    w_in, w_state, bias, proj = layer_weights
    _, steps, rows, width = top_seq.shape
    cell_count = proj.shape[1]
    count = lax.axis_size("mp")
    groups = lax.axis_size("dp")
    weights = (
        w_in,
        w_state,
        bias.astype(F32)[:, None, :],
        proj,
    )
    dma = pltpu.SemaphoreType.DMA
    return pl.pallas_call(
        recurrence_kernel,
        out_shape=(
            jax.ShapeDtypeStruct((2, groups, steps, rows, width), BF16),
            jax.ShapeDtypeStruct((2, groups, steps + 1, rows, width), BF16),
            jax.ShapeDtypeStruct((2, groups, steps, rows, cell_count), BF16),
            jax.ShapeDtypeStruct((2, groups, steps, rows, 4 * cell_count), BF16),
            jax.ShapeDtypeStruct((2, groups, steps, rows, width), BF16),
            jax.ShapeDtypeStruct((2, steps * rows // 2, width // count), BF16),
            jax.ShapeDtypeStruct(features_all.shape, BF16),
        ),
        in_specs=[VMEM_SPEC] * 7 + [ANY_SPEC],
        out_specs=(*[ANY_SPEC] * 5, VMEM_SPEC, ANY_SPEC),
        input_output_aliases={7: 6},
        scratch_shapes=[
            pltpu.VMEM((2, steps, rows, width), BF16),
            pltpu.VMEM((2, steps + 1, rows, width), BF16),
            pltpu.VMEM((2, steps, rows, cell_count), BF16),
            pltpu.VMEM((2, steps, rows, width), BF16),
            pltpu.VMEM((2, steps, 4, rows, cell_count), F32),
            pltpu.VMEM((2, steps + 1, rows, cell_count), F32),
            pltpu.VMEM((2, steps, rows, width), F32),
            pltpu.VMEM((2, rows, 4 * cell_count), F32),
            pltpu.VMEM((2, rows, cell_count), F32),
            pltpu.VMEM((2, 2, count, rows, width), BF16),
            pltpu.VMEM((2, 2, count, rows, width), BF16),
            pltpu.VMEM((2, steps, rows, width), F32),
            pltpu.VMEM((2, SLOTS, rows, 4 * cell_count), BF16),
            dma,
            dma((2, 2, count - 1)),
            dma((2, 2, count)),
            dma((2, 2, count - 1)),
            dma((2, 2, count)),
            dma((2,)),
            dma((2, steps)),
            dma((2,)),
            dma((2, steps)),
            dma((2, SLOTS)),
            dma((2, SLOTS, groups - 1)),
            dma((groups + 2,)),
            dma((5, groups - 1)),
            dma((5, groups - 1)),
            pltpu.VMEM((2, 4 * cell_count, width), BF16),
            pltpu.VMEM((2, 4 * cell_count, width), BF16),
            pltpu.VMEM((2, width, cell_count), BF16),
            pltpu.VMEM((2, steps, count, rows, width // count), BF16),
            pltpu.VMEM((2, steps, count, rows, width // count), BF16),
            dma((count - 1,)),
            dma((count - 1,)),
            pltpu.VMEM((2, steps * rows // 2, width // count), F32),
            dma,
            dma,
            dma((2,)),
            dma((2,)),
        ],
        compiler_params=pltpu.CompilerParams(
            collective_id=0, has_side_effects=True, vmem_limit_bytes=VMEM_LIMIT
        ),
        name="recurrence",
    )(base_seq, live_seq, top_seq, *weights, features_all)


def weight_grads(lefts, right, parts):
    batch, outer, pieces, inner, size = lefts[0].shape
    tokens = right.shape[1]
    inner = tokens // outer
    columns = right.shape[2] // parts
    block = min(512, columns)
    blocks = columns // block
    chunk = min(512, size)
    total = size * len(lefts)
    single = parts == 1

    def kernel(*refs):
        left_refs = refs[: len(lefts)]
        right_refs = refs[len(lefts) : len(lefts) + parts]
        out_refs = refs[len(lefts) + parts : -3]
        bias_out, turned, ones = refs[-3:]

        @pl.when(pl.program_id(2) == 0)
        def _():
            for i, left in enumerate(left_refs):
                for offset in range(0, size, chunk):
                    at = i * size + offset
                    turned[at : at + chunk, :] = (
                        left[0, :, 0, :, offset : offset + chunk].reshape(tokens, chunk).T
                    )
            ones[...] = jnp.ones_like(ones)

        for i, out in enumerate(out_refs):

            @pl.loop(0, size // chunk)
            def _(step):
                at = pl.multiple_of(i * size + step * chunk, chunk)
                own = pl.multiple_of(step * chunk, chunk)
                left = turned[pl.ds(at, chunk), :]
                for part in range(parts):
                    value = jnp.dot(left, right_refs[part][0], preferred_element_type=F32)
                    if single:
                        out[0, pl.ds(own, chunk), :] = value
                    else:
                        out[0, pl.ds(own, chunk), part, :] = value

        for part in range(parts):
            bias_out[0, part : part + 1, :] = jnp.dot(
                ones[...], right_refs[part][0], preferred_element_type=F32
            )[:1]

    outputs = 4 * batch * pieces * total * parts * columns
    return pl.pallas_call(
        kernel,
        out_shape=(
            *[
                jax.ShapeDtypeStruct(
                    (batch, pieces * size, *((parts,) * (not single)), columns), F32
                )
                for _ in lefts
            ],
            jax.ShapeDtypeStruct((batch, parts, columns), F32),
        ),
        grid=(batch, pieces, blocks),
        in_specs=[
            *[
                pl.BlockSpec((1, outer, 1, inner, size), lambda b, p, n: (b, 0, p, 0, 0))
                for _ in lefts
            ],
            *[
                pl.BlockSpec(
                    (1, tokens, block),
                    functools.partial(lambda g, b, p, n: (b, 0, g * blocks + n), g),
                )
                for g in range(parts)
            ],
        ],
        out_specs=(
            *[
                pl.BlockSpec((1, size, block), lambda b, p, n: (b, p, n))
                if single
                else pl.BlockSpec((1, size, parts, block), lambda b, p, n: (b, p, 0, n))
                for _ in lefts
            ],
            pl.BlockSpec((1, parts, block), lambda b, p, n: (b, 0, n)),
        ),
        scratch_shapes=[
            pltpu.VMEM((total, tokens), BF16),
            pltpu.VMEM((16, tokens), BF16),
        ],
        compiler_params=pltpu.CompilerParams(vmem_limit_bytes=VMEM_LIMIT),
        cost_estimate=pl.CostEstimate(
            flops=2 * batch * pieces * total * tokens * parts * columns,
            bytes_accessed=outputs + 2 * right.size + 2 * batch * pieces * total * tokens,
            transcendentals=0,
        ),
        name="weight_grads",
    )(*lefts, *[right] * parts)


def merge_kernel(first_ref, second_ref, gates_in, gates_all, staged, sems):
    far = 3 - lax.axis_index("dp")
    late = first_ref.shape[0]
    half = late // 2
    pieces = [pl.ds(0, half), pl.ds(half, late - half)]
    start = gates_all.shape[2] - late
    loads, stores = [], []
    for d, source in enumerate((first_ref, second_ref)):
        for i, piece in enumerate(pieces):
            target = gates_all.at[d, far, pl.ds(start + i * half, piece.size)]
            buffer = staged.at[d, piece]
            loads.append(pltpu.make_async_copy(source.at[piece], buffer, sems.at[d, i]))
            stores.append(pltpu.make_async_copy(buffer, target, sems.at[d, i]))
    for load in loads:
        load.start()
    for load, store in zip(loads, stores):
        load.wait()
        store.start()
    for store in stores:
        store.wait()


def send_late(late):
    beside = [(i, i + 1 - 2 * (i % 2)) for i in range(4)]
    across = [(i, (i + 2) % 4) for i in range(4)]
    return lax.ppermute(late[0], "dp", across), lax.ppermute(late[1], "dp", beside)


def merge_late(gates_all, moved):
    return pl.pallas_call(
        merge_kernel,
        out_shape=jax.ShapeDtypeStruct(gates_all.shape, BF16),
        in_specs=[ANY_SPEC] * 3,
        out_specs=ANY_SPEC,
        input_output_aliases={2: 0},
        scratch_shapes=[pltpu.VMEM((2, *moved[0].shape), BF16), pltpu.SemaphoreType.DMA((2, 2))],
        compiler_params=pltpu.CompilerParams(vmem_limit_bytes=VMEM_LIMIT),
        name="merge_late",
    )(*moved, gates_all)


def on_device(
    char_ids,
    row_lengths,
    top_grad,
    char_table,
    conv_weight,
    conv_bias,
    highway_weight,
    highway_bias,
    proj_weight,
    proj_bias,
    lstm_input,
    lstm_state,
    lstm_bias,
    lstm_proj,
):
    section = lax.axis_index("section")
    rows, steps, per_token = char_ids.shape
    proj_width = proj_weight.shape[1]
    half = rows // 2
    tokens = half * steps
    local = conv_weight.shape[2]
    emb = char_table.shape[1]
    padded = -(-(per_token + TAPS - 1) // 8) * 8
    vocabulary = -(-char_table.shape[0] // 8) * 8
    chars = lax.dynamic_slice_in_dim(char_ids, section * half, half, 0)
    chars = jnp.transpose(chars, (1, 0, 2)).reshape(tokens, per_token)
    ids = jnp.pad(chars, ((0, 0), (0, padded - per_token)), constant_values=-1)
    ids = ids.reshape(tokens // CHUNK, 1, CHUNK * padded)
    table = jnp.pad(
        jnp.tile(char_table, (1, TAPS)),
        ((0, vocabulary - char_table.shape[0]), (0, 128 - TAPS * emb)),
    )
    widths = filter_widths(lax.axis_index("mp") * local, local, local * lax.axis_size("mp"))
    tap_keep = jnp.arange(TAPS, dtype=jnp.int32)[:, None] < widths[None, :]
    masked = jnp.where(tap_keep[:, None, :], conv_weight, jnp.zeros_like(conv_weight))
    excluded = jnp.arange(1, TAPS + 1, dtype=jnp.int32)[:, None] == widths[None, :]
    masked = jnp.concatenate(
        [
            masked.reshape(TAPS * emb, local),
            conv_bias[None, :],
            jnp.where(excluded, -1e30, 0.0).astype(BF16),
            jnp.zeros((128 - TAPS * emb - 1 - TAPS, local), BF16),
        ]
    )
    log_positions = jnp.log((per_token - widths + 1).astype(F32))[None, :]
    w_high = jnp.transpose(highway_weight, (0, 2, 1, 3))
    b_high = highway_bias.astype(F32)
    (
        base_pair,
        taps,
        peak,
        pooled,
        features,
        current,
        transform,
        gate,
        features_all,
        w_input,
        w_state,
    ) = cnn_forward(
        ids,
        (table, masked, log_positions, w_high, b_high, proj_weight, proj_bias.astype(F32)[None]),
        lstm_input[0],
        lstm_state[0],
    )
    depth_count = highway_weight.shape[0]

    def all_tokens(values):
        return lax.all_gather(values, ("section", "dp"), axis=values.ndim - 2, tiled=True)

    last_features = all_tokens(
        lax.dynamic_index_in_dim(features[depth_count], lax.axis_index("mp"), 0, False)
    )
    top_seq = jnp.transpose(top_grad, (2, 1, 0, 3))
    live = (jnp.arange(steps, dtype=jnp.int32)[:, None] < row_lengths[None, :]).astype(F32)
    live_seq = jnp.broadcast_to(live[..., None], (steps, rows, 128))
    layer_weights = (
        w_input,
        w_state,
        lstm_bias[0].reshape(2, -1),
        lstm_proj[0],
    )
    (
        x_all,
        all_states,
        all_hidden,
        gates_all,
        projected_all,
        base_shards,
        high_features,
    ) = recurrence(base_pair, live_seq, top_seq, layer_weights, features_all)
    own_rows = lax.dynamic_slice_in_dim(proj_weight, lax.axis_index("mp") * local, local, 0).T
    (
        all_gates,
        all_projected,
        all_inputs,
        base_full,
        all_mixed,
        late_first,
        late_second,
        conv_grad,
        table_grad,
    ) = (
        cnn_backward(
            base_shards,
            (taps, peak, pooled, current, transform, gate),
            (own_rows, w_high, masked, ids),
            (gates_all, projected_all, x_all, all_states),
        )
    )
    relayed = lax.axis_size("dp") == 4
    moved = send_late((late_first, late_second)) if relayed else None
    table_flat = table_grad.reshape(-1)
    table_rows = -(-(-(-table_flat.shape[0] // local)) // 16) * 16
    table_flat = jnp.pad(table_flat, (0, table_rows * local - table_flat.shape[0]))
    small = jnp.concatenate([conv_grad, table_flat.reshape(table_rows, local)]).astype(BF16)
    small = lax.all_gather(small, ("section", "dp"), axis=0)
    small = jnp.sum(small.astype(F32), axis=0)
    conv_weight_grad = jnp.where(
        tap_keep[:, None, :], small[: TAPS * emb].reshape(conv_weight.shape), 0.0
    )
    table_grad = small[128:].reshape(-1)[: table_grad.size].reshape(table_grad.shape)
    table_grad = table_grad[:, : char_table.shape[0]].T
    all_base = jnp.transpose(base_full, (0, 1, 3, 2, 4)).reshape(-1, proj_width)

    def flat(values):
        return values.reshape(2, -1, values.shape[4])

    def one_piece(values):
        batch, groups, _, _, width = values.shape
        return values.reshape(batch, groups, 1, -1, width)

    proj_weight_grad = lax.all_gather(
        dot(last_features, all_base, 0, 0).astype(BF16), "mp", axis=0, tiled=True
    ).astype(F32)
    proj_grad = weight_grads([one_piece(all_hidden)], flat(all_projected), 1)[0]
    batch, _, groups, count, _, _ = high_features.shape
    high_grad, high_bias_grad = weight_grads(
        [high_features.reshape(batch, 2 * groups, count, tokens, local)],
        all_mixed.reshape(batch, -1, 2 * local),
        2,
    )
    if relayed:
        moved, high_grad, proj_grad = lax.optimization_barrier((moved, high_grad, proj_grad))
        all_gates = merge_late(all_gates, moved)
    input_grad, state_grad, bias_grad = weight_grads(
        [one_piece(all_inputs), one_piece(all_states)], flat(all_gates), 4
    )
    return (
        table_grad,
        conv_weight_grad,
        small[TAPS * emb],
        high_grad,
        high_bias_grad,
        proj_weight_grad,
        jnp.sum(all_base.astype(F32), axis=0),
        input_grad.reshape(lstm_input.shape),
        state_grad.reshape(lstm_state.shape),
        bias_grad.reshape(lstm_bias.shape),
        proj_grad.reshape(lstm_proj.shape),
    )


def solution(mesh):
    return jax.shard_map(
        on_device,
        mesh=mesh,
        in_specs=(
            P("dp", None, None),
            P("dp"),
            P("dp", None, None, None),
            P(),
            P(None, None, "mp"),
            P("mp"),
            P(None, None, None, "mp"),
            P(None, None, "mp"),
            P(),
            P(),
            P("section", None, None, None, "mp"),
            P("section", None, None, None, "mp"),
            P("section", None, None, "mp"),
            P("section", None, "mp", None),
        ),
        out_specs=(
            P(),
            P(None, None, "mp"),
            P("mp"),
            P(None, None, None, "mp"),
            P(None, None, "mp"),
            P(),
            P(),
            P("section", None, None, None, "mp"),
            P("section", None, None, None, "mp"),
            P("section", None, None, "mp"),
            P("section", None, "mp", None),
        ),
        check_vma=False,
    )
```

```python
import functools

import jax
import jax.numpy as jnp
import numpy as np
from jax import lax
from jax.experimental import pallas as pl
from jax.experimental.pallas import tpu as pltpu
from jax.sharding import PartitionSpec as P

F32 = jnp.float32
BF16 = jnp.bfloat16
PERIODS = 32
TAPS = 7
VMEM_LIMIT = 62 * 1024 * 1024
SLOTS = 4
DEFER = 3
CHUNK = 16
TURN = 128
PER_TOKEN = 50
CHARS = 262


def dot(left, right, left_dim, right_dim):
    return lax.dot_general(
        left, right, (((left_dim,), (right_dim,)), ((), ())), preferred_element_type=F32
    )


def soft_clip(values):
    return 3.0 * jnp.tanh(values / 3.0)


def filter_widths(offset, amount, total):
    period = total // PERIODS
    in_period = (offset + jnp.arange(amount, dtype=jnp.int32)) % period
    widths = jnp.ones((amount,), jnp.int32)
    for exponent in range(6):
        widths = widths + (in_period * 64 >= period * 2**exponent).astype(jnp.int32)
    return widths


MESH = pl.DeviceIdType.MESH
VMEM_SPEC = pl.BlockSpec(memory_space=pltpu.VMEM)
ANY_SPEC = pl.BlockSpec(memory_space=pl.ANY)


def column_peers():
    count = lax.axis_size("mp")
    me = lax.axis_index("mp")
    return [lax.rem(me + j, count) for j in range(1, count)]


def greet(devices):
    barrier = pltpu.get_barrier_semaphore()
    for device in devices:
        pl.semaphore_signal(barrier, inc=1, device_id=device, device_id_type=MESH)
    pl.semaphore_wait(barrier, len(devices))


def remote(source, target, send, recv, device):
    return pltpu.make_async_remote_copy(
        src_ref=source,
        dst_ref=target,
        send_sem=send,
        recv_sem=recv,
        device_id=device,
        device_id_type=MESH,
    )


def one_hot_columns(ids, vocabulary):
    symbols = lax.broadcasted_iota(jnp.int32, (vocabulary, ids.shape[1]), 0)
    return (symbols == ids).astype(F32).astype(BF16)


def cnn_forward_kernel(
    ids_ref,
    table_ref,
    flags_ref,
    masked_ref,
    log_positions,
    w_high,
    b_high,
    w_proj,
    b_proj,
    input_ref,
    state_ref,
    base_out,
    taps_out,
    peak_out,
    pooled_out,
    current_out,
    transform_out,
    gate_out,
    features_all,
    last_out,
    input_out,
    state_out,
    features,
    raw,
    turned,
    send_sem,
    recv_sem,
    base_send,
    base_recv,
    row_send,
    row_recv,
    own_sem,
    relay_send,
    relay_recv,
    raw_sem,
    turned_sem,
):
    count = lax.axis_size("mp")
    me = lax.axis_index("mp")
    section = lax.axis_index("section")
    peers = column_peers()
    depth_count, tokens, local = current_out.shape
    chunk_rows = ids_ref.shape[2]
    padded = chunk_rows // CHUNK
    half = tokens // 2
    emb = 16
    block = min(256, local)
    groups = lax.axis_size("dp")
    group = lax.axis_index("dp")
    others = [lax.rem(group + j, groups) for j in range(1, groups)]
    relayed = groups == 4
    beside = group + 1 - 2 * lax.rem(group, 2)
    across = lax.rem(group + 2, 4)
    far = 3 - group
    near = [beside, across] if relayed else others
    origin = near if relayed else others[::-1]
    greet(
        [{"mp": peer} for peer in peers]
        + [{"section": 1 - section}]
        + [{"dp": other} for other in others]
    )

    def relay_rows(depth, way, slot):
        pieces = pl.ds(way * (count // 2), count // 2)
        return remote(
            features_all.at[depth, section, slot, pieces],
            features_all.at[depth, section, slot, pieces],
            relay_send.at[depth, way],
            relay_recv.at[depth, way],
            {"dp": across if way == 0 else beside},
        )

    def pass_rows(depth):
        for j in range(len(near)):
            give_rows(depth, j, origin[j]).wait_recv()
        if relayed and depth + 1 < depth_count:
            for way in range(2):
                relay_rows(depth, way, beside if way == 0 else across).start()

    blocks = input_out.shape[2] // TURN
    units = 4 * blocks

    def fetch(unit, start):
        slot = lax.rem(unit, 2)
        d = lax.rem(unit, 2 * blocks) // blocks
        rows = pl.ds(pl.multiple_of(lax.rem(unit, blocks) * TURN, TURN), TURN)
        for which, source in enumerate((input_ref, state_ref)):

            @pl.when(unit // (2 * blocks) == which)
            def _():
                copy = pltpu.make_async_copy(source.at[d, rows], raw.at[slot], raw_sem.at[slot])
                copy.start() if start else copy.wait()

    def deliver(unit, start):
        slot = lax.rem(unit, 2)
        d = lax.rem(unit, 2 * blocks) // blocks
        rows = pl.ds(pl.multiple_of(lax.rem(unit, blocks) * TURN, TURN), TURN)
        for which, target in enumerate((input_out, state_out)):

            @pl.when(unit // (2 * blocks) == which)
            def _():
                copy = pltpu.make_async_copy(
                    turned.at[slot], target.at[d, :, rows], turned_sem.at[slot]
                )
                copy.start() if start else copy.wait()

    def turn_units(first, last):
        @pl.loop(first, last)
        def _(unit):
            slot = lax.rem(unit, 2)
            fetch(unit, False)

            @pl.when(unit + 1 < units)
            def _():
                fetch(unit + 1, True)

            @pl.when(unit >= 2)
            def _():
                deliver(unit - 2, False)

            for g in range(4):
                turned[slot, g] = raw[slot, :, g, :]
            deliver(unit, True)

    fetch(0, True)

    def own_rows(depth):
        return pltpu.make_async_copy(
            features.at[depth], features_all.at[depth, section, group], own_sem.at[depth]
        )

    def give_rows(depth, j, slot):
        return remote(
            features.at[depth],
            features_all.at[depth, section, slot],
            row_send.at[depth, j],
            row_recv.at[depth, j],
            {"dp": near[j]},
        )

    def send(depth, part, rows, start):
        for j, peer in enumerate(peers):
            copy = remote(
                features.at[depth, me, rows],
                features.at[depth, me, rows],
                send_sem.at[depth, part, j],
                recv_sem.at[depth, part, me],
                {"mp": peer},
            )
            if start:
                copy.start()
            else:
                copy.wait_send()

    def receive(depth, part):
        rows = pl.ds(part * half, half)
        for j, peer in enumerate(peers):
            remote(
                features.at[depth, peer, rows],
                features.at[depth, peer, rows],
                send_sem.at[depth, part, j],
                recv_sem.at[depth, part, peer],
                {"mp": peer},
            ).wait_recv()

    lane_group = lax.broadcasted_iota(jnp.int32, (chunk_rows, 128), 1) // emb

    def pool_chunk(c):
        hot = one_hot_columns(ids_ref[c], table_ref.shape[0])
        embedded = lax.dot_general(
            hot, table_ref[...], (((0,), (0,)), ((), ())), preferred_element_type=F32
        )
        taps = embedded + flags_ref[...]
        for offset in range(1, TAPS):
            rolled = pltpu.roll(embedded, chunk_rows - offset, 0)
            taps = jnp.where(lane_group == offset, rolled, taps)
        taps = taps.astype(BF16)
        taps_out[c] = taps
        rows = pl.ds(pl.multiple_of(c * CHUNK, CHUNK), CHUNK)
        for start in range(0, local, block):
            cols = slice(start, start + block)
            scores = jnp.dot(taps, masked_ref[:, cols], preferred_element_type=F32)
            scores = scores.reshape(CHUNK, padded, block)
            top = jnp.max(scores, axis=1, keepdims=True)
            total = jnp.sum(jnp.exp(scores - top), axis=1, keepdims=True)
            peak = top + jnp.log(total)
            peak_out[rows, :, cols] = peak
            pooled = jnp.sum(peak, axis=1) - log_positions[:, cols]
            pooled_out[rows, cols] = pooled
            current = jnp.maximum(pooled, 0.0) + jnp.log1p(jnp.exp(-jnp.abs(pooled)))
            current_out[0, rows, cols] = current
            features[0, me, rows, cols] = current.astype(BF16)
        return rows

    for part in range(2):

        @pl.loop(0, half // CHUNK)
        def _(i):
            rows = pool_chunk(part * (half // CHUNK) + i)
            send(0, part, rows, True)

    for depth in range(depth_count):
        for part in range(2):
            rows = pl.ds(part * half, half)
            receive(depth, part)
            if part == 1:
                own_rows(depth).start()
                for j in range(len(near)):
                    give_rows(depth, j, group).start()
            mixed = []
            for g in range(2):
                total = jnp.broadcast_to(b_high[depth, g : g + 1, :].astype(F32), (half, local))
                for p in range(count):
                    total = total + jnp.dot(
                        features[depth, p, rows, :],
                        w_high[depth, g, p * local : (p + 1) * local, :],
                        preferred_element_type=F32,
                    )
                mixed.append(total)
            transform = mixed[0]
            gate = jax.nn.sigmoid(mixed[1])
            transform_out[depth, rows, :] = transform
            gate_out[depth, rows, :] = gate
            current = gate * current_out[depth, rows, :] + (1.0 - gate) * (
                transform * jax.nn.sigmoid(transform)
            )
            if depth + 1 < depth_count:
                current_out[depth + 1, rows, :] = current
            else:
                last_out[rows, :] = current.astype(BF16)
            features[depth + 1, me, rows, :] = current.astype(BF16)
            send(depth + 1, part, rows, True)
        if depth >= 1:
            pass_rows(depth - 1)
        turn_units(depth * units * 3 // (4 * depth_count), (depth + 1) * units * 3 // (4 * depth_count))

    def give():
        return remote(
            base_out.at[section],
            base_out.at[section],
            base_send,
            base_recv,
            {"section": 1 - section},
        )

    for part in range(2):
        rows = pl.ds(part * half, half)
        receive(depth_count, part)
        total = jnp.broadcast_to(b_proj[...].astype(F32), (half, w_proj.shape[1]))
        for p in range(count):
            total = total + jnp.dot(
                features[depth_count, p, rows, :],
                w_proj[p * local : (p + 1) * local, :],
                preferred_element_type=F32,
            )
        base_out[section, rows, :] = total
    give().start()
    turn_units(units * 3 // 4, units)
    pass_rows(depth_count - 1)
    for depth in range(depth_count + 1):
        for part in range(2):
            send(depth, part, pl.ds(part * half, half), False)
    give().wait_send()
    remote(
        base_out.at[1 - section],
        base_out.at[1 - section],
        base_send,
        base_recv,
        {"section": 1 - section},
    ).wait_recv()
    for depth in range(depth_count):
        own_rows(depth).wait()
        for j in range(len(near)):
            give_rows(depth, j, group).wait_send()
        if relayed and depth + 1 < depth_count:
            for way in range(2):
                relay_rows(depth, way, beside if way == 0 else across).wait_send()
                relay_rows(depth, way, far).wait_recv()
    for unit in range(units - 2, units):
        deliver(unit, False)


def cnn_forward(ids, weights, lstm_input, lstm_state):
    table, masked, log_positions, w_high, b_high, w_proj, b_proj = weights
    chunks, _, chunk_rows = ids.shape
    tokens = chunks * CHUNK
    depth_count, _, total, local = w_high.shape
    count = lax.axis_size("mp")
    groups = lax.axis_size("dp")
    directions, in_width, gate_blocks, cell_columns = lstm_input.shape
    padded = chunk_rows // CHUNK
    position = np.tile(np.arange(padded), CHUNK)[:, None]
    lane = np.arange(128)[None, :]
    excluded = lane - 16 * TAPS
    flags = (lane == 16 * TAPS) | (
        (excluded >= 1) & (excluded <= TAPS) & (position > PER_TOKEN - excluded)
    )
    dma = pltpu.SemaphoreType.DMA
    return pl.pallas_call(
        cnn_forward_kernel,
        out_shape=(
            jax.ShapeDtypeStruct((2, tokens, w_proj.shape[1]), F32),
            jax.ShapeDtypeStruct((chunks, chunk_rows, 128), BF16),
            jax.ShapeDtypeStruct((tokens, 1, local), F32),
            jax.ShapeDtypeStruct((tokens, local), F32),
            jax.ShapeDtypeStruct((depth_count, tokens, local), F32),
            jax.ShapeDtypeStruct((depth_count, tokens, local), F32),
            jax.ShapeDtypeStruct((depth_count, tokens, local), F32),
            jax.ShapeDtypeStruct((depth_count, 2, groups, count, tokens, local), BF16),
            jax.ShapeDtypeStruct((tokens, local), BF16),
            jax.ShapeDtypeStruct((directions, gate_blocks, in_width, cell_columns), BF16),
            jax.ShapeDtypeStruct((directions, gate_blocks, in_width, cell_columns), BF16),
        ),
        in_specs=[VMEM_SPEC] * 9 + [ANY_SPEC] * 2,
        out_specs=(*[VMEM_SPEC] * 7, ANY_SPEC, VMEM_SPEC, *[ANY_SPEC] * 2),
        scratch_shapes=[
            pltpu.VMEM((depth_count + 1, count, tokens, local), BF16),
            pltpu.VMEM((2, TURN, gate_blocks, cell_columns), BF16),
            pltpu.VMEM((2, gate_blocks, TURN, cell_columns), BF16),
            dma((depth_count + 1, 2, count - 1)),
            dma((depth_count + 1, 2, count)),
            dma,
            dma,
            dma((depth_count, groups - 1)),
            dma((depth_count, groups - 1)),
            dma((depth_count,)),
            dma((depth_count, 2)),
            dma((depth_count, 2)),
            dma((2,)),
            dma((2,)),
        ],
        compiler_params=pltpu.CompilerParams(
            collective_id=1, has_side_effects=True, vmem_limit_bytes=VMEM_LIMIT
        ),
        name="cnn_forward",
    )(
        ids,
        table,
        jnp.asarray(flags.astype(np.float32)),
        masked,
        log_positions,
        w_high,
        b_high,
        w_proj,
        b_proj,
        lstm_input,
        lstm_state,
    )


def cnn_backward_kernel(
    base_ref,
    own_ref,
    w_high,
    current_ref,
    transform_ref,
    gate_ref,
    peak_ref,
    pooled_ref,
    taps_ref,
    masked_ref,
    masked_t,
    ids_ref,
    gates_in,
    projected_in,
    x_in,
    state_all,
    gates_all,
    projected_all,
    x_all,
    base_full,
    mixed_all,
    late_a,
    late_b,
    late_c,
    late_d,
    small_out,
    conv_out,
    mixed_out,
    late_buf,
    base_all,
    table_sum,
    table_all,
    grad_current,
    outgoing,
    incoming,
    base_send,
    base_recv,
    sum_send,
    sum_recv,
    own_sem,
    relay_send,
    relay_recv,
    lift_send,
    lift_recv,
    row_send,
    row_recv,
    full_sem,
    share_send,
    share_recv,
    table_send,
    table_recv,
    mixed_sem,
    mixed_send,
    mixed_recv,
    mixed_share,
    mixed_shared,
    late_sem,
    defer_send,
    defer_recv,
):
    count = lax.axis_size("mp")
    me = lax.axis_index("mp")
    section = lax.axis_index("section")
    groups = lax.axis_size("dp")
    group = lax.axis_index("dp")
    peers = column_peers()
    depth_count, tokens, local = current_ref.shape
    steps = x_all.shape[2]
    chunks, chunk_rows, _ = taps_ref.shape
    padded = chunk_rows // CHUNK
    emb = 16
    vocabulary = -(-CHARS // 8) * 8
    relayed = groups == 4
    beside = group + 1 - 2 * lax.rem(group, 2)
    across = lax.rem(group + 2, 4)
    far = 3 - group
    greet(
        [{"mp": peer} for peer in peers]
        + [{"section": 1 - section, "mp": peer} for peer in [*peers, me]]
        + [{"dp": lax.rem(group + j, groups)} for j in range(1, groups)]
    )

    def lift():
        return remote(
            state_all.at[:, :, pl.ds(1, steps)],
            x_all,
            lift_send,
            lift_recv,
            {"section": 1 - section},
        )

    half_steps = steps // 2
    others = [lax.rem(group + j, groups) for j in range(1, groups)]
    near = [beside, across] if relayed else others
    origin = near if relayed else others[::-1]

    def relay(way, slot):
        return remote(
            projected_all.at[way, slot],
            projected_all.at[way, slot],
            relay_send.at[way],
            relay_recv.at[way],
            {"dp": across if way == 0 else beside},
        )

    def deferred(j, slot):
        return remote(
            gates_all.at[:, slot, pl.ds(0, DEFER)],
            gates_all.at[:, slot, pl.ds(0, DEFER)],
            defer_send.at[j],
            defer_recv.at[j],
            {"dp": near[j]},
        )

    for j in range(len(near)):
        deferred(j, group).start()


    late_loads, late_stores = [], []
    for i, target in enumerate((late_a, late_b, late_c, late_d)):
        d, way = i // 2, i % 2
        rows = pl.ds(way * half_steps, half_steps)
        source = gates_all.at[d, (beside, across)[way], rows]
        late_loads.append(pltpu.make_async_copy(source, late_buf.at[i], late_sem.at[i]))
        late_stores.append(pltpu.make_async_copy(late_buf.at[i], target, late_sem.at[i]))

    def spread_base(half, target_section, peer, j):
        return remote(
            base_ref.at[half],
            base_all.at[me],
            base_send.at[half, j],
            base_recv.at[me],
            {"section": target_section, "mp": peer},
        )

    everyone = [*peers, me]

    @pl.when(section == 0)
    def _():
        for j, peer in enumerate(peers):
            spread_base(0, 0, peer, j).start()
        for j, peer in enumerate(everyone):
            spread_base(1, 1, peer, j).start()
        lift().start()
        own = pltpu.make_async_copy(base_ref.at[0], base_all.at[me], own_sem)
        own.start()
        own.wait()

    def base_arrival(source):
        return remote(
            base_ref.at[0],
            base_all.at[source],
            base_send.at[0, 0],
            base_recv.at[source],
            {"section": 1 - section},
        )

    for peer in peers:
        base_arrival(peer).wait_recv()

    @pl.when(section == 1)
    def _():
        base_arrival(me).wait_recv()

    keep = pltpu.make_async_copy(base_all, base_full.at[section, group], full_sem)
    keep.start()

    def base_row(j, slot):
        return remote(
            base_all,
            base_full.at[section, slot],
            row_send.at[j],
            row_recv.at[j],
            {"dp": others[j]},
        )

    def share_base(owner):
        return remote(
            base_full.at[owner],
            base_full.at[owner],
            share_send,
            share_recv,
            {"section": 1 - section},
        )

    for j in range(groups - 1):
        base_row(j, group).start()

    def keep_mixed(depth):
        return pltpu.make_async_copy(
            mixed_out.at[depth], mixed_all.at[depth, section, group], mixed_sem.at[depth]
        )

    def mixed_row(depth, j, slot):
        return remote(
            mixed_out.at[depth],
            mixed_all.at[depth, section, slot],
            mixed_send.at[depth, j],
            mixed_recv.at[depth, j],
            {"dp": others[j]},
        )

    def share_mixed(depth, owner):
        return remote(
            mixed_all.at[depth, owner],
            mixed_all.at[depth, owner],
            mixed_share.at[depth],
            mixed_shared.at[depth],
            {"section": 1 - section},
        )

    def collect_mixed(depth):
        keep_mixed(depth).wait()
        for j in range(groups - 1):
            mixed_row(depth, j, others[groups - 2 - j]).wait_recv()
        share_mixed(depth, section).start()

    wide = base_all.shape[2]
    own_rows = pl.ds(pl.multiple_of(me * local, local), local)
    total = jnp.zeros((tokens, local), F32)
    for p in range(count):
        total = total + lax.dot_general(
            base_all[p],
            own_ref[own_rows, p * wide : (p + 1) * wide],
            (((1,), (1,)), ((), ())),
            preferred_element_type=F32,
        )
    grad_current[...] = total

    def send_sum(depth, peer, j):
        return remote(
            outgoing.at[depth, j],
            incoming.at[depth, me],
            sum_send.at[depth, j],
            sum_recv.at[depth, me],
            {"mp": peer},
        )

    def back(depth, owner):
        rows = pl.ds(pl.multiple_of(owner * local, local), local)
        parts = [
            lax.dot_general(
                mixed_out[depth, :, g * local : (g + 1) * local],
                w_high[depth, g, rows, :],
                (((1,), (1,)), ((), ())),
                preferred_element_type=F32,
            )
            for g in range(2)
        ]
        return parts[0] + parts[1]

    for depth in range(depth_count - 1, -1, -1):
        transform = transform_ref[depth]
        gate = gate_ref[depth]
        grad = grad_current[...]
        slope = jax.nn.sigmoid(transform)
        mixed_out[depth, :, :local] = (
            grad * (1.0 - gate) * slope * (1.0 + transform * (1.0 - slope))
        ).astype(BF16)
        mixed_out[depth, :, local:] = (
            grad * (current_ref[depth] - transform * slope) * gate * (1.0 - gate)
        ).astype(BF16)
        keep_mixed(depth).start()
        for j in range(groups - 1):
            mixed_row(depth, j, group).start()
        if relayed and depth == depth_count - 1:
            for way in range(2):
                relay(way, beside if way == 0 else across).start()
        for j, peer in enumerate(peers):
            outgoing[depth, j] = back(depth, peer).astype(BF16)
            send_sum(depth, peer, j).start()
        total = grad * gate + back(depth, me)
        for j, peer in enumerate(peers):
            remote(
                outgoing.at[depth, j],
                incoming.at[depth, peer],
                sum_send.at[depth, j],
                sum_recv.at[depth, peer],
                {"mp": peer},
            ).wait_recv()
            total = total + incoming[depth, peer].astype(F32)
        grad_current[...] = total

    for j in range(len(near)):
        deferred(j, group).wait_send()
        deferred(j, origin[j]).wait_recv()
    if relayed:
        for load in late_loads:
            load.start()
    for depth in range(depth_count - 1, 0, -1):
        collect_mixed(depth)
    if relayed:
        for load, store in zip(late_loads, late_stores):
            load.wait()
            store.start()
    grad_current[...] = grad_current[...] * jax.nn.sigmoid(pooled_ref[...])
    conv_out[...] = jnp.zeros_like(conv_out)
    small_out[...] = jnp.zeros_like(small_out)
    table_sum[...] = jnp.zeros_like(table_sum)
    lane_group = lax.broadcasted_iota(jnp.int32, (chunk_rows, 128), 1) // emb

    @pl.loop(0, chunks)
    def _(c):
        rows = pl.ds(pl.multiple_of(c * CHUNK, CHUNK), CHUNK)
        taps = taps_ref[c]
        scores = jnp.dot(taps, masked_ref[...], preferred_element_type=F32)
        scores = scores.reshape(CHUNK, padded, local)
        share = jnp.exp(scores - peak_ref[rows])
        grads = share * grad_current[rows, :][:, None, :]
        grads = grads.reshape(chunk_rows, local).astype(BF16)
        conv_out[...] += lax.dot_general(
            taps, grads, (((0,), (0,)), ((), ())), preferred_element_type=F32
        )
        back_taps = jnp.dot(grads, masked_t[...], preferred_element_type=F32)
        moved = back_taps
        for offset in range(1, TAPS):
            moved = jnp.where(lane_group == offset, pltpu.roll(back_taps, offset, 0), moved)
        hot = one_hot_columns(ids_ref[c], vocabulary)
        table_sum[:vocabulary, :] += jnp.dot(
            hot, moved.astype(BF16), preferred_element_type=F32
        )

    columns = table_sum[...].T
    folded = columns[:emb]
    for offset in range(1, TAPS):
        folded = folded + columns[offset * emb : (offset + 1) * emb]
    table_all[me] = folded

    def table_copy(j, slot):
        return remote(
            table_all.at[slot],
            table_all.at[slot],
            table_send.at[j],
            table_recv.at[slot],
            {"mp": peers[j]},
        )

    for j in range(count - 1):
        table_copy(j, me).start()

    for j in range(count - 1):
        table_copy(j, peers[j]).wait_recv()
    folded = table_all[0]
    for p in range(1, count):
        folded = folded + table_all[p]
    small_out[:128, :] = conv_out[...].astype(BF16)
    span = min(local, folded.shape[1])
    for i in range(folded.shape[1] // span):
        at = 128 + i * emb
        small_out[at : at + emb, :span] = folded[:, i * span : (i + 1) * span].astype(BF16)
    for j in range(count - 1):
        table_copy(j, me).wait_send()
    keep.wait()
    for j in range(groups - 1):
        base_row(j, others[groups - 2 - j]).wait_recv()
    share_base(section).start()
    collect_mixed(0)
    for j in range(groups - 1):
        base_row(j, group).wait_send()
        for depth in range(depth_count):
            mixed_row(depth, j, group).wait_send()
    for depth in range(depth_count):
        for j, peer in enumerate(peers):
            send_sum(depth, peer, j).wait_send()

    @pl.when(section == 0)
    def _():
        for j, peer in enumerate(peers):
            spread_base(0, 0, peer, j).wait_send()
        for j, peer in enumerate(everyone):
            spread_base(1, 1, peer, j).wait_send()
        lift().wait_send()

    @pl.when(section == 1)
    def _():
        lift().wait_recv()

    if relayed:
        for way in range(2):
            relay(way, beside if way == 0 else across).wait_send()
            relay(way, far).wait_recv()
        for copy in late_stores:
            copy.wait()

    share_base(section).wait_send()
    share_base(1 - section).wait_recv()
    for depth in range(depth_count):
        share_mixed(depth, section).wait_send()
        share_mixed(depth, 1 - section).wait_recv()


def cnn_backward(base_shards, saved, weights, rows_all):
    w_proj, w_high, masked, ids = weights
    taps, peak, pooled, current, transform, gate = saved
    gates_all, projected_all, x_all, state_all = rows_all
    depth_count, tokens, local = current.shape
    count = lax.axis_size("mp")
    groups = lax.axis_size("dp")
    vocabulary = -(-CHARS // 128) * 128
    half_steps = gates_all.shape[2] // 2
    late = (half_steps, *gates_all.shape[3:])
    dma = pltpu.SemaphoreType.DMA
    return pl.pallas_call(
        cnn_backward_kernel,
        out_shape=(
            jax.ShapeDtypeStruct(gates_all.shape, BF16),
            jax.ShapeDtypeStruct(projected_all.shape, BF16),
            jax.ShapeDtypeStruct(x_all.shape, BF16),
            jax.ShapeDtypeStruct((2, groups, count, tokens, base_shards.shape[2]), BF16),
            jax.ShapeDtypeStruct((depth_count, 2, groups, tokens, 2 * local), BF16),
            *[jax.ShapeDtypeStruct(late, BF16)] * 4,
            jax.ShapeDtypeStruct((128 + 16 * max(1, vocabulary // local), local), BF16),
        ),
        in_specs=[VMEM_SPEC] * 12 + [ANY_SPEC] * 4,
        out_specs=(*[ANY_SPEC] * 9, VMEM_SPEC),
        input_output_aliases={12: 0, 13: 1, 14: 2},
        scratch_shapes=[
            pltpu.VMEM((128, local), F32),
            pltpu.VMEM((depth_count, tokens, 2 * local), BF16),
            pltpu.VMEM((4, *late), BF16),
            pltpu.VMEM((count, tokens, base_shards.shape[2]), BF16),
            pltpu.VMEM((vocabulary, 128), F32),
            pltpu.VMEM((count, 16, vocabulary), F32),
            pltpu.VMEM((tokens, local), F32),
            pltpu.VMEM((depth_count, count - 1, tokens, local), BF16),
            pltpu.VMEM((depth_count, count, tokens, local), BF16),
            dma((2, count)),
            dma((count,)),
            dma((depth_count, count - 1)),
            dma((depth_count, count)),
            dma,
            dma((2,)),
            dma((2,)),
            dma,
            dma,
            dma((groups - 1,)),
            dma((groups - 1,)),
            dma,
            dma,
            dma,
            dma((count - 1,)),
            dma((count,)),
            dma((depth_count,)),
            dma((depth_count, groups - 1)),
            dma((depth_count, groups - 1)),
            dma((depth_count,)),
            dma((depth_count,)),
            dma((4,)),
            dma((groups - 1,)),
            dma((groups - 1,)),
        ],
        compiler_params=pltpu.CompilerParams(
            collective_id=2, has_side_effects=True, vmem_limit_bytes=VMEM_LIMIT
        ),
        name="cnn_backward",
    )(
        base_shards,
        w_proj,
        w_high,
        current,
        transform,
        gate,
        peak,
        pooled,
        taps,
        masked,
        jnp.pad(masked[: 16 * TAPS], ((0, 128 - 16 * TAPS), (0, 0))).T,
        ids,
        gates_all,
        projected_all,
        x_all,
        state_all,
    )


def recurrence_kernel(
    base_ref,
    live_ref,
    top_ref,
    w_in,
    w_state,
    bias_ref,
    proj_ref,
    features_in,
    x_all,
    state_all,
    hidden_all,
    gates_all,
    projected_all,
    base_out,
    features_all,
    x_out,
    state_out,
    hidden_out,
    projected_out,
    acts,
    cells,
    clips,
    pre,
    grad_cell,
    parts,
    back_parts,
    above,
    gate_buf,
    base_sem,
    send_sem,
    recv_sem,
    back_send,
    back_recv,
    x_send,
    x_recv,
    above_send,
    above_recv,
    gate_sem,
    gate_send,
    own_sem,
    row_send,
    row_recv,
    w_in_t,
    w_state_t,
    proj_t,
    input_parts,
    input_sums,
    input_send,
    input_recv,
    base_sum,
    share_send,
    share_recv,
    relay_send,
    relay_recv,
):
    count = lax.axis_size("mp")
    me = lax.axis_index("mp")
    section = lax.axis_index("section")
    steps = x_out.shape[1]
    cell_count = proj_ref.shape[1]
    chunk = min(256, cell_count)
    peers = [lax.rem(me + j, count) for j in range(1, count)]
    groups = lax.axis_size("dp")
    group = lax.axis_index("dp")
    others = [lax.rem(group + j, groups) for j in range(1, groups)]
    relayed = groups == 4
    beside = group + 1 - 2 * lax.rem(group, 2)
    across = lax.rem(group + 2, 4)
    near = [beside, across] if relayed else others

    barrier = pltpu.get_barrier_semaphore()
    for peer in peers:
        pl.semaphore_signal(barrier, inc=1, device_id={"mp": peer}, device_id_type=MESH)
    pl.semaphore_signal(barrier, inc=1, device_id={"section": 1 - section}, device_id_type=MESH)
    for other in others:
        pl.semaphore_signal(barrier, inc=1, device_id={"dp": other}, device_id_type=MESH)
    pl.semaphore_wait(barrier, count + groups - 1)

    def share_features(owner):
        return remote(
            features_all.at[:, owner],
            features_all.at[:, owner],
            share_send,
            share_recv,
            {"section": 1 - section},
        )

    pieces = features_all.shape[3]

    def relay_features(way, slot):
        half = pl.ds(way * (pieces // 2), pieces // 2)
        depth = features_all.shape[0] - 1
        return remote(
            features_all.at[depth, section, slot, half],
            features_all.at[depth, section, slot, half],
            relay_send.at[way],
            relay_recv.at[way],
            {"dp": across if way == 0 else beside},
        )

    if relayed:
        for way in range(2):
            relay_features(way, beside if way == 0 else across).start()

    def wide(values, width):
        return jnp.concatenate([values] * (width // values.shape[1]), axis=1)

    def copy_part(buffer, send, recv, d, parity, source, j, target):
        return pltpu.make_async_remote_copy(
            src_ref=buffer.at[d, parity, source],
            dst_ref=buffer.at[d, parity, source],
            send_sem=send.at[d, parity, j],
            recv_sem=recv.at[d, parity, source],
            device_id={"mp": target},
            device_id_type=MESH,
        )

    ordered = peers
    if count == 4:
        ordered = [3 - me, lax.rem(me + 2, 4), me + 1 - 2 * lax.rem(me, 2)]

    def exchange_start(buffer, send, recv, d, parity, value):
        buffer[d, parity, me] = value.astype(BF16)
        for j, peer in enumerate(ordered):
            copy_part(buffer, send, recv, d, parity, me, j, peer).start()

    def exchange_wait(buffer, send, recv, d, parity):
        for j, peer in enumerate(ordered):
            copy_part(buffer, send, recv, d, parity, peer, j, peer).wait_recv()
        total = buffer[d, parity, 0].astype(F32)
        for source in range(1, count):
            total = total + buffer[d, parity, source].astype(F32)
        for j, peer in enumerate(ordered):
            copy_part(buffer, send, recv, d, parity, me, j, peer).wait_send()
        return total

    def pass_up(d, k):
        return pltpu.make_async_remote_copy(
            src_ref=state_out.at[d, k + 1],
            dst_ref=x_out.at[d, k],
            send_sem=x_send.at[d],
            recv_sem=x_recv.at[d, k],
            device_id={"section": 1 - section},
            device_id_type=MESH,
        )

    def pass_down(d, k):
        return pltpu.make_async_remote_copy(
            src_ref=above.at[d, k],
            dst_ref=above.at[d, k],
            send_sem=above_send.at[d],
            recv_sem=above_recv.at[d, k],
            device_id={"section": 1 - section},
            device_id_type=MESH,
        )

    def gates_copy(d, k, slot):
        return pltpu.make_async_copy(
            gate_buf.at[d, slot], gates_all.at[d, group, k], gate_sem.at[d, slot]
        )

    def gates_row(d, k, slot, j, other):
        return pltpu.make_async_remote_copy(
            src_ref=gate_buf.at[d, slot],
            dst_ref=gates_all.at[d, group, k],
            send_sem=gate_send.at[d, slot, j],
            recv_sem=row_recv.at[0, j],
            device_id={"dp": other},
            device_id_type=MESH,
        )

    def row(kind, source, target, j, other):
        return pltpu.make_async_remote_copy(
            src_ref=source,
            dst_ref=target,
            send_sem=row_send.at[kind, j],
            recv_sem=row_recv.at[kind, j],
            device_id={"dp": other},
            device_id_type=MESH,
        )

    def from_peer(j, targets):
        back = len(targets) - 1 - j
        return targets[j] if relayed and len(targets) == 2 else targets[back]

    def time_of(d, k):
        return k if d == 0 else steps - 1 - k

    @pl.when(section == 0)
    def _():
        part_rows = base_ref.shape[1] // steps

        @pl.loop(0, steps)
        def _(t):
            at = pl.ds(pl.multiple_of(t * part_rows, part_rows), part_rows)
            x = jnp.concatenate([base_ref[0, at, :], base_ref[1, at, :]], axis=0).astype(BF16)
            for d in range(2):
                x_out[d, time_of(d, t)] = x

        for j, other in enumerate(others):
            row(1, x_out, x_all.at[:, group], j, other).start()

    for d in range(2):
        state_out[d, 0] = jnp.zeros(state_out.shape[2:], BF16)
        cells[d, 0] = jnp.zeros(cells.shape[2:], F32)
        grad_cell[d] = jnp.zeros(grad_cell.shape[1:], F32)

    def input_part(d, k):
        @pl.when(section == 1)
        def _():
            pass_up(d, k).wait_recv()

        x = x_out[d, k]
        for block in range(4):
            for start in range(0, cell_count, chunk):
                cols = slice(block * cell_count + start, block * cell_count + start + chunk)
                bias = bias_ref[d, block : block + 1, start : start + chunk].astype(F32)
                pre[d, :, cols] = bias + jnp.dot(
                    x, w_in[d, block, :, start : start + chunk], preferred_element_type=F32
                )

    def turn_weights(unit):
        per_block = cell_count // chunk
        block = unit // per_block
        cols = pl.ds(pl.multiple_of(lax.rem(unit, per_block) * chunk, chunk), chunk)
        rows_t = pl.ds(pl.multiple_of(unit * chunk, chunk), chunk)
        for d in range(2):
            w_in_t[d, rows_t, :] = w_in[d, block, :, cols].T
            w_state_t[d, rows_t, :] = w_state[d, block, :, cols].T

    def turn_proj(unit):
        cols = pl.ds(pl.multiple_of(unit * 128, 128), 128)
        for d in range(2):
            proj_t[d, :, cols] = proj_ref[d, cols, :].T

    def forward_cells(d, k):
        state = state_out[d, k]
        live = live_ref[time_of(d, k)]
        for start in range(0, cell_count, chunk):
            raw = []
            for block in range(4):
                cols = slice(block * cell_count + start, block * cell_count + start + chunk)
                raw.append(
                    pre[d, :, cols]
                    + jnp.dot(
                        state, w_state[d, block, :, start : start + chunk], preferred_element_type=F32
                    )
                )
            own = slice(start, start + chunk)
            in_gate = jax.nn.sigmoid(raw[0])
            forget = jax.nn.sigmoid(raw[1])
            memory = jnp.tanh(raw[2])
            out_gate = jax.nn.sigmoid(raw[3])
            for block, value in enumerate((in_gate, forget, memory, out_gate)):
                acts[d, k, block, :, own] = value
            cell_new = soft_clip(in_gate * memory + forget * cells[d, k, :, own])
            cells[d, k + 1, :, own] = wide(live, chunk) * cell_new
            hidden_out[d, k, :, own] = (out_gate * jnp.tanh(cell_new)).astype(BF16)
        part = jnp.dot(hidden_out[d, k], proj_ref[d], preferred_element_type=F32)
        exchange_start(parts, send_sem, recv_sem, d, lax.rem(k, 2), part)
        for j, other in enumerate(others):
            row(2, hidden_out.at[d, k], hidden_all.at[d, group, k], j, other).start()

    def forward_state(d, k):
        total = exchange_wait(parts, send_sem, recv_sem, d, lax.rem(k, 2))
        clip = jnp.tanh(total / 3.0)
        clips[d, k] = clip
        live = wide(live_ref[time_of(d, k)], clip.shape[1])
        state_out[d, k + 1] = (live * 3.0 * clip).astype(BF16)

        @pl.when(section == 0)
        def _():
            @pl.when(k > 0)
            def _():
                pass_up(d, k - 1).wait_send()

            pass_up(d, k).start()

        for j, other in enumerate(others):
            row(3, state_out.at[d, k + 1], state_all.at[d, group, k + 1], j, other).start()

    units = 4 * cell_count // chunk
    for d in range(2):
        input_part(d, 0)
    for d in range(2):
        forward_cells(d, 0)
    for d in range(2):
        input_part(d, 1)

    @pl.loop(1, steps)
    def _(k):
        for d in range(2):
            forward_state(d, k - 1)
            forward_cells(d, k)

        @pl.when(k + 1 < steps)
        def _():
            for d in range(2):
                input_part(d, k + 1)

        @pl.when(k <= units)
        def _():
            turn_weights(k - 1)

        @pl.when(k <= cell_count // 128)
        def _():
            turn_proj(k - 1)

    for unit in range(steps - 1, units):
        turn_weights(unit)
    for d in range(2):
        forward_state(d, steps - 1)
    if relayed:
        for way in range(2):
            relay_features(way, beside if way == 0 else across).wait_send()
            relay_features(way, 3 - group).wait_recv()
    share_features(section).start()

    @pl.when(section == 0)
    def _():
        for d in range(2):
            pass_up(d, steps - 1).wait_send()

    def back_wait(d, parity):
        return exchange_wait(back_parts, back_send, back_recv, d, parity)

    def back_start(d, parity, value):
        exchange_start(back_parts, back_send, back_recv, d, parity, value)

    def backward_cells(d, k, total):
        slot = lax.rem(k, SLOTS)
        live = live_ref[time_of(d, k)]
        clip = clips[d, k]
        grad_out = wide(live, clip.shape[1]) * (total + top_ref[d, time_of(d, k)].astype(F32))
        grad_projected = (grad_out * (1.0 - clip * clip)).astype(BF16)
        projected_out[d, k] = grad_projected

        for j, other in enumerate(near):
            row(
                4, projected_out.at[d, k], projected_all.at[d, group, k], j, other
            ).start()

        @pl.when(k < steps - SLOTS)
        def _():
            gates_copy(d, k + SLOTS, slot).wait()
            for j, other in enumerate(near):
                gates_row(d, k + SLOTS, slot, j, other).wait_send()

        for start in range(0, cell_count, chunk):
            own = slice(start, start + chunk)
            grad_hidden = jnp.dot(grad_projected, proj_t[d, :, own], preferred_element_type=F32)
            in_gate, forget, memory, out_gate = [acts[d, k, block, :, own] for block in range(4)]
            cell = cells[d, k, :, own]
            clip_raw = jnp.tanh((in_gate * memory + forget * cell) / 3.0)
            tanh_cell = jnp.tanh(3.0 * clip_raw)
            grad_new = wide(live, chunk) * grad_cell[d, :, own] + grad_hidden * out_gate * (
                1.0 - tanh_cell * tanh_cell
            )
            grad_raw = grad_new * (1.0 - clip_raw * clip_raw)
            grad_cell[d, :, own] = grad_raw * forget
            grads = (
                grad_raw * memory * in_gate * (1.0 - in_gate),
                grad_raw * cell * forget * (1.0 - forget),
                grad_raw * in_gate * (1.0 - memory * memory),
                grad_hidden * tanh_cell * out_gate * (1.0 - out_gate),
            )
            for block, value in enumerate(grads):
                cols = slice(block * cell_count + start, block * cell_count + start + chunk)
                gate_buf[d, slot, :, cols] = value.astype(BF16)
        gates_copy(d, k, slot).start()

    def gates_send(d, k):
        @pl.when(k >= DEFER)
        def _():
            for j, other in enumerate(near):
                gates_row(d, k, lax.rem(k, SLOTS), j, other).start()

    def backward_state(d, k):
        @pl.when(k > 0)
        def _():
            back = jnp.dot(gate_buf[d, lax.rem(k, SLOTS)], w_state_t[d], preferred_element_type=F32)
            pre[d, :, : back.shape[1]] = back

            @pl.when(section == 0)
            def _():
                pass_down(d, k - 1).wait_recv()
                pre[d, :, : back.shape[1]] = back + above[d, k - 1]

            back_start(d, lax.rem(k - 1, 2), pre[d, :, : back.shape[1]])

    share = base_out.shape[2]

    def input_copy(source, target, j, peer):
        return remote(source, target, input_send.at[j], input_recv.at[j], {"mp": peer})

    def backward_input(d, k):
        gates_send(d, k)
        part = jnp.dot(gate_buf[d, lax.rem(k, SLOTS)], w_in_t[d], preferred_element_type=F32)

        @pl.when(section == 1)
        def _():
            above[d, k] = part

            @pl.when(k < steps - 1)
            def _():
                pass_down(d, k + 1).wait_send()

            pass_down(d, k).start()

        @pl.when(section == 0)
        def _():
            for p in range(count):
                input_parts[d, k, p] = part[:, p * share : (p + 1) * share].astype(BF16)
            for j, peer in enumerate(peers):
                input_copy(input_parts.at[d, k, peer], input_sums.at[d, k, me], j, peer).start()

    last = steps - 1

    @pl.when(section == 0)
    def _():
        for d in range(2):
            pass_down(d, last).wait_recv()
            back_start(d, lax.rem(last, 2), above[d, last])

    for d in range(2):

        @pl.when(section == 0)
        def _():
            pre[d, :, : clips.shape[3]] = back_wait(d, lax.rem(last, 2))

        @pl.when(section == 1)
        def _():
            pre[d, :, : clips.shape[3]] = jnp.zeros(clips.shape[2:], F32)

        backward_cells(d, last, pre[d, :, : clips.shape[3]])
        backward_state(d, last)
    for d in range(2):
        backward_input(d, last)

    @pl.loop(1, steps)
    def _(tick):
        k = last - tick
        for d in range(2):
            backward_cells(d, k, back_wait(d, lax.rem(k, 2)))
            backward_state(d, k)
        for d in range(2):
            backward_input(d, k)

    for d in range(2):
        for k in range(min(SLOTS, steps)):
            gates_copy(d, k, k % SLOTS).wait()
            for j, other in enumerate(near):
                if k >= DEFER:
                    gates_row(d, k, k % SLOTS, j, other).wait_send()

    @pl.when(section == 1)
    def _():
        for d in range(2):
            pass_down(d, 0).wait_send()

    own = [
        (hidden_out, hidden_all.at[:, group]),
        (state_out, state_all.at[:, group]),
        (projected_out, projected_all.at[:, group]),
    ]
    for other in others:
        own.append((state_out.at[:, 0], state_all.at[:, other, 0]))
    own = [
        pltpu.make_async_copy(source, target, own_sem.at[i])
        for i, (source, target) in enumerate(own)
    ]
    for copy in own:
        copy.start()

    rest = pl.ds(1, steps)
    for j, other in enumerate(others):
        source = from_peer(j, others)
        hidden_row = row(2, hidden_out, hidden_all.at[:, source], j, other)
        state_row = row(3, state_out.at[:, rest], state_all.at[:, source, rest], j, other)
        for copy in (hidden_row, state_row):
            copy.wait_send()
            copy.wait_recv()

    for copy in own:
        copy.wait()

    @pl.when(section == 0)
    def _():
        mine = pltpu.make_async_copy(x_out, x_all.at[:, group], base_sem)
        mine.start()
        for j, other in enumerate(others):
            copy = row(1, x_out, x_all.at[:, from_peer(j, others)], j, other)
            copy.wait_send()
            copy.wait_recv()
        mine.wait()

    @pl.when(section == 0)
    def _():
        for j, peer in enumerate(peers):
            source = peers[count - 2 - j]
            copy = input_copy(input_parts.at[:, :, peer], input_sums.at[:, :, source], j, peer)
            copy.wait_send()
            copy.wait_recv()
        rows_half = base_out.shape[1] // steps

        @pl.loop(0, steps)
        def _(t):
            total = input_parts[0, t, me].astype(F32) + input_parts[1, steps - 1 - t, me].astype(F32)
            for peer in peers:
                total = total + input_sums[0, t, peer].astype(F32)
                total = total + input_sums[1, steps - 1 - t, peer].astype(F32)
            at = pl.ds(pl.multiple_of(t * rows_half, rows_half), rows_half)
            for half in range(2):
                base_sum[half, at, :] = total[half * rows_half : (half + 1) * rows_half]

        base_out[...] = base_sum[...].astype(BF16)

    share_features(section).wait_send()
    share_features(1 - section).wait_recv()

    for j, other in enumerate(near):
        source = from_peer(j, near)
        pltpu.make_async_remote_copy(
            src_ref=gates_all.at[:, source, pl.ds(DEFER, steps - DEFER)],
            dst_ref=gates_all.at[:, source, pl.ds(DEFER, steps - DEFER)],
            send_sem=row_send.at[0, j],
            recv_sem=row_recv.at[0, j],
            device_id={"dp": other},
            device_id_type=MESH,
        ).wait_recv()
        projected_row = row(4, projected_out, projected_all.at[:, source], j, other)
        projected_row.wait_send()
        projected_row.wait_recv()


def recurrence(base_seq, live_seq, top_seq, layer_weights, features_all):
    w_in, w_state, bias, proj = layer_weights
    _, steps, rows, width = top_seq.shape
    cell_count = proj.shape[1]
    count = lax.axis_size("mp")
    groups = lax.axis_size("dp")
    weights = (
        w_in,
        w_state,
        bias,
        proj,
    )
    dma = pltpu.SemaphoreType.DMA
    return pl.pallas_call(
        recurrence_kernel,
        out_shape=(
            jax.ShapeDtypeStruct((2, groups, steps, rows, width), BF16),
            jax.ShapeDtypeStruct((2, groups, steps + 1, rows, width), BF16),
            jax.ShapeDtypeStruct((2, groups, steps, rows, cell_count), BF16),
            jax.ShapeDtypeStruct((2, groups, steps, rows, 4 * cell_count), BF16),
            jax.ShapeDtypeStruct((2, groups, steps, rows, width), BF16),
            jax.ShapeDtypeStruct((2, steps * rows // 2, width // count), BF16),
            jax.ShapeDtypeStruct(features_all.shape, BF16),
        ),
        in_specs=[VMEM_SPEC] * 7 + [ANY_SPEC],
        out_specs=(*[ANY_SPEC] * 5, VMEM_SPEC, ANY_SPEC),
        input_output_aliases={7: 6},
        scratch_shapes=[
            pltpu.VMEM((2, steps, rows, width), BF16),
            pltpu.VMEM((2, steps + 1, rows, width), BF16),
            pltpu.VMEM((2, steps, rows, cell_count), BF16),
            pltpu.VMEM((2, steps, rows, width), BF16),
            pltpu.VMEM((2, steps, 4, rows, cell_count), F32),
            pltpu.VMEM((2, steps + 1, rows, cell_count), F32),
            pltpu.VMEM((2, steps, rows, width), F32),
            pltpu.VMEM((2, rows, 4 * cell_count), F32),
            pltpu.VMEM((2, rows, cell_count), F32),
            pltpu.VMEM((2, 2, count, rows, width), BF16),
            pltpu.VMEM((2, 2, count, rows, width), BF16),
            pltpu.VMEM((2, steps, rows, width), F32),
            pltpu.VMEM((2, SLOTS, rows, 4 * cell_count), BF16),
            dma,
            dma((2, 2, count - 1)),
            dma((2, 2, count)),
            dma((2, 2, count - 1)),
            dma((2, 2, count)),
            dma((2,)),
            dma((2, steps)),
            dma((2,)),
            dma((2, steps)),
            dma((2, SLOTS)),
            dma((2, SLOTS, groups - 1)),
            dma((groups + 2,)),
            dma((5, groups - 1)),
            dma((5, groups - 1)),
            pltpu.VMEM((2, 4 * cell_count, width), BF16),
            pltpu.VMEM((2, 4 * cell_count, width), BF16),
            pltpu.VMEM((2, width, cell_count), BF16),
            pltpu.VMEM((2, steps, count, rows, width // count), BF16),
            pltpu.VMEM((2, steps, count, rows, width // count), BF16),
            dma((count - 1,)),
            dma((count - 1,)),
            pltpu.VMEM((2, steps * rows // 2, width // count), F32),
            dma,
            dma,
            dma((2,)),
            dma((2,)),
        ],
        compiler_params=pltpu.CompilerParams(
            collective_id=0, has_side_effects=True, vmem_limit_bytes=VMEM_LIMIT
        ),
        name="recurrence",
    )(base_seq, live_seq, top_seq, *weights, features_all)


def weight_grads(lefts, right, parts, only=None, done=()):
    batch, outer, pieces, inner, size = lefts[0].shape
    tokens = right.shape[1]
    inner = tokens // outer
    columns = right.shape[2] // parts
    block = min(512, columns)
    blocks = columns // block
    chunk = min(512, size)
    total = size * len(lefts)
    single = parts == 1
    chosen = 1 if only is not None else batch

    def entry(b):
        return b if only is None else only


    def kernel(*refs):
        left_refs = refs[: len(lefts)]
        right_refs = refs[len(lefts) : len(lefts) + parts]
        out_refs = refs[len(lefts) + parts + len(done) : -3]
        bias_out, turned, ones = refs[-3:]

        @pl.when(pl.program_id(2) == 0)
        def _():
            for i, left in enumerate(left_refs):
                for offset in range(0, size, chunk):
                    at = i * size + offset
                    turned[at : at + chunk, :] = (
                        left[0, :, 0, :, offset : offset + chunk].reshape(tokens, chunk).T
                    )
            ones[...] = jnp.ones_like(ones)

        for i, out in enumerate(out_refs):

            @pl.loop(0, size // chunk)
            def _(step):
                at = pl.multiple_of(i * size + step * chunk, chunk)
                own = pl.multiple_of(step * chunk, chunk)
                left = turned[pl.ds(at, chunk), :]
                for part in range(parts):
                    value = jnp.dot(left, right_refs[part][0], preferred_element_type=F32)
                    if single:
                        out[0, pl.ds(own, chunk), :] = value
                    else:
                        out[0, pl.ds(own, chunk), part, :] = value

        for part in range(parts):
            bias_out[0, part : part + 1, :] = jnp.dot(
                ones[...], right_refs[part][0], preferred_element_type=F32
            )[:1]

    outputs = 4 * chosen * pieces * total * parts * columns
    return pl.pallas_call(
        kernel,
        out_shape=(
            *[
                jax.ShapeDtypeStruct(
                    (batch, pieces * size, *((parts,) * (not single)), columns), F32
                )
                for _ in lefts
            ],
            jax.ShapeDtypeStruct((batch, parts, columns), F32),
        ),
        grid=(chosen, pieces, blocks),
        in_specs=[
            *[
                pl.BlockSpec((1, outer, 1, inner, size), lambda b, p, n: (entry(b), 0, p, 0, 0))
                for _ in lefts
            ],
            *[
                pl.BlockSpec(
                    (1, tokens, block),
                    functools.partial(lambda g, b, p, n: (entry(b), 0, g * blocks + n), g),
                )
                for g in range(parts)
            ],
            *[ANY_SPEC] * len(done),
        ],
        input_output_aliases={len(lefts) + parts + i: i for i in range(len(done))},
        out_specs=(
            *[
                pl.BlockSpec((1, size, block), lambda b, p, n: (entry(b), p, n))
                if single
                else pl.BlockSpec((1, size, parts, block), lambda b, p, n: (entry(b), p, 0, n))
                for _ in lefts
            ],
            pl.BlockSpec((1, parts, block), lambda b, p, n: (entry(b), 0, n)),
        ),
        scratch_shapes=[
            pltpu.VMEM((total, tokens), BF16),
            pltpu.VMEM((16, tokens), BF16),
        ],
        compiler_params=pltpu.CompilerParams(vmem_limit_bytes=VMEM_LIMIT),
        cost_estimate=pl.CostEstimate(
            flops=2 * chosen * pieces * total * tokens * parts * columns,
            bytes_accessed=outputs + 2 * right.size + 2 * batch * pieces * total * tokens,
            transcendentals=0,
        ),
        name="weight_grads",
    )(*lefts, *[right] * parts, *done)


def merge_kernel(d, first_ref, second_ref, gates_in, gates_all, staged, sems):
    far = 3 - lax.axis_index("dp")
    late = first_ref.shape[0]
    half_steps = gates_all.shape[2] // 2
    loads, stores = [], []
    for way, source in enumerate((first_ref, second_ref)):
        rows = pl.ds((way + 1) * half_steps - late, late)
        buffer = staged.at[way]
        loads.append(pltpu.make_async_copy(source, buffer, sems.at[way]))
        stores.append(pltpu.make_async_copy(buffer, gates_all.at[d, far, rows], sems.at[way]))
    for load in loads:
        load.start()
    for load, store in zip(loads, stores):
        load.wait()
        store.start()
    for store in stores:
        store.wait()


def send_late(late):
    beside = [(i, i + 1 - 2 * (i % 2)) for i in range(4)]
    across = [(i, (i + 2) % 4) for i in range(4)]
    return lax.ppermute(late[0], "dp", across), lax.ppermute(late[1], "dp", beside)


def merge_late(d, gates_all, moved):
    return pl.pallas_call(
        functools.partial(merge_kernel, d),
        out_shape=jax.ShapeDtypeStruct(gates_all.shape, BF16),
        in_specs=[ANY_SPEC] * 3,
        out_specs=ANY_SPEC,
        input_output_aliases={2: 0},
        scratch_shapes=[pltpu.VMEM((2, *moved[0].shape), BF16), pltpu.SemaphoreType.DMA((2,))],
        compiler_params=pltpu.CompilerParams(vmem_limit_bytes=VMEM_LIMIT),
        name="merge_late",
    )(*moved, gates_all)


def on_device(
    char_ids,
    row_lengths,
    top_grad,
    char_table,
    conv_weight,
    conv_bias,
    highway_weight,
    highway_bias,
    proj_weight,
    proj_bias,
    lstm_input,
    lstm_state,
    lstm_bias,
    lstm_proj,
):
    section = lax.axis_index("section")
    rows, steps, per_token = char_ids.shape
    proj_width = proj_weight.shape[1]
    half = rows // 2
    tokens = half * steps
    local = conv_weight.shape[2]
    emb = char_table.shape[1]
    padded = -(-(per_token + TAPS - 1) // 8) * 8
    vocabulary = -(-char_table.shape[0] // 8) * 8
    chars = lax.dynamic_slice_in_dim(char_ids, section * half, half, 0)
    chars = jnp.transpose(chars, (1, 0, 2)).reshape(tokens, per_token)
    ids = jnp.pad(chars, ((0, 0), (0, padded - per_token)), constant_values=-1)
    ids = ids.reshape(tokens // CHUNK, 1, CHUNK * padded)
    table = jnp.pad(
        jnp.tile(char_table, (1, TAPS)),
        ((0, vocabulary - char_table.shape[0]), (0, 128 - TAPS * emb)),
    )
    widths = filter_widths(lax.axis_index("mp") * local, local, local * lax.axis_size("mp"))
    tap_keep = jnp.arange(TAPS, dtype=jnp.int32)[:, None] < widths[None, :]
    row = jnp.arange(128, dtype=jnp.int32)[:, None]
    taps_padded = jnp.pad(
        conv_weight.reshape(TAPS * emb, local), ((0, 128 - TAPS * emb), (0, 0))
    )
    masked = jnp.where(
        row < emb * widths[None, :],
        taps_padded,
        jnp.where(
            row == TAPS * emb,
            conv_bias[None, :],
            jnp.where(row == TAPS * emb + widths[None, :], -1e30, 0.0).astype(BF16),
        ),
    )
    log_positions = jnp.log((per_token - widths + 1).astype(F32))[None, :]
    w_high = jnp.transpose(highway_weight, (0, 2, 1, 3))
    (
        base_pair,
        taps,
        peak,
        pooled,
        current,
        transform,
        gate,
        features_all,
        last_own,
        w_input,
        w_state,
    ) = cnn_forward(
        ids,
        (table, masked, log_positions, w_high, highway_bias, proj_weight, proj_bias[None]),
        lstm_input[0],
        lstm_state[0],
    )
    depth_count = highway_weight.shape[0]

    def all_tokens(values):
        return lax.all_gather(values, ("section", "dp"), axis=values.ndim - 2, tiled=True)

    last_features = all_tokens(last_own)
    top_seq = jnp.transpose(top_grad, (2, 1, 0, 3))
    live = (jnp.arange(steps, dtype=jnp.int32)[:, None] < row_lengths[None, :]).astype(F32)
    live_seq = jnp.broadcast_to(live[..., None], (steps, rows, 128))
    layer_weights = (
        w_input,
        w_state,
        lstm_bias[0],
        lstm_proj[0],
    )
    (
        x_all,
        all_states,
        all_hidden,
        gates_all,
        projected_all,
        base_shards,
        high_features,
    ) = recurrence(base_pair, live_seq, top_seq, layer_weights, features_all)
    (
        all_gates,
        all_projected,
        all_inputs,
        base_full,
        all_mixed,
        *late,
        small,
    ) = (
        cnn_backward(
            base_shards,
            (taps, peak, pooled, current, transform, gate),
            (proj_weight, w_high, masked, ids),
            (gates_all, projected_all, x_all, all_states),
        )
    )
    relayed = lax.axis_size("dp") == 4
    if relayed:
        moved_first = send_late(late[:2])
        moved_second = send_late(late[2:])
    small = lax.all_gather(small, ("section", "dp"), axis=0)
    small = jnp.sum(small.astype(F32), axis=0)
    conv_weight_grad = jnp.where(
        tap_keep[:, None, :], small[: TAPS * emb].reshape(conv_weight.shape), 0.0
    )
    table_grad = small[128:].reshape(-1, emb, local)
    table_grad = jnp.transpose(table_grad, (0, 2, 1)).reshape(-1, emb)[: char_table.shape[0]]
    all_base = jnp.transpose(base_full, (0, 1, 3, 2, 4)).reshape(-1, proj_width)

    def flat(values):
        return values.reshape(2, -1, values.shape[4])

    def one_piece(values):
        batch, groups, _, _, width = values.shape
        return values.reshape(batch, groups, 1, -1, width)

    proj_weight_grad = lax.all_gather(
        dot(last_features, all_base, 0, 0).astype(BF16), "mp", axis=0, tiled=True
    ).astype(F32)
    proj_grad = weight_grads([one_piece(all_hidden)], flat(all_projected), 1)[0]
    batch, _, groups, count, _, _ = high_features.shape
    high_grad, high_bias_grad = weight_grads(
        [high_features.reshape(batch, 2 * groups, count, tokens, local)],
        all_mixed.reshape(batch, -1, 2 * local),
        2,
    )
    lefts = [one_piece(all_inputs), one_piece(all_states)]
    if relayed:
        moved_first, high_grad, proj_grad, conv_weight_grad, table_grad = lax.optimization_barrier(
            (moved_first, high_grad, proj_grad, conv_weight_grad, table_grad)
        )
        all_gates = merge_late(0, all_gates, moved_first)
        done = weight_grads(lefts, flat(all_gates), 4, only=0)
        done, moved_second, all_gates = lax.optimization_barrier((done, moved_second, all_gates))
        all_gates = merge_late(1, all_gates, moved_second)
        input_grad, state_grad, bias_grad = weight_grads(
            lefts, flat(all_gates), 4, only=1, done=done
        )
    else:
        input_grad, state_grad, bias_grad = weight_grads(lefts, flat(all_gates), 4)
    return (
        table_grad,
        conv_weight_grad,
        small[TAPS * emb],
        high_grad,
        high_bias_grad,
        proj_weight_grad,
        jnp.sum(all_base.astype(F32), axis=0),
        input_grad.reshape(lstm_input.shape),
        state_grad.reshape(lstm_state.shape),
        bias_grad.reshape(lstm_bias.shape),
        proj_grad.reshape(lstm_proj.shape),
    )


def solution(mesh):
    return jax.shard_map(
        on_device,
        mesh=mesh,
        in_specs=(
            P("dp", None, None),
            P("dp"),
            P("dp", None, None, None),
            P(),
            P(None, None, "mp"),
            P("mp"),
            P(None, None, None, "mp"),
            P(None, None, "mp"),
            P(),
            P(),
            P("section", None, None, None, "mp"),
            P("section", None, None, None, "mp"),
            P("section", None, None, "mp"),
            P("section", None, "mp", None),
        ),
        out_specs=(
            P(),
            P(None, None, "mp"),
            P("mp"),
            P(None, None, None, "mp"),
            P(None, None, "mp"),
            P(),
            P(),
            P("section", None, None, None, "mp"),
            P("section", None, None, None, "mp"),
            P("section", None, None, "mp"),
            P("section", None, "mp", None),
        ),
        check_vma=False,
    )
```

```python
import functools

import jax
import jax.numpy as jnp
import numpy as np
from jax import lax
from jax.experimental import pallas as pl
from jax.experimental.pallas import tpu as pltpu
from jax.sharding import PartitionSpec as P

F32 = jnp.float32
BF16 = jnp.bfloat16
PERIODS = 32
TAPS = 7
VMEM_LIMIT = 62 * 1024 * 1024
SLOTS = 4
DEFER = 3
CHUNK = 16
TURN = 128
PER_TOKEN = 50
CHARS = 262


def dot(left, right, left_dim, right_dim):
    return lax.dot_general(
        left, right, (((left_dim,), (right_dim,)), ((), ())), preferred_element_type=F32
    )


def soft_clip(values):
    return 3.0 * jnp.tanh(values / 3.0)


def filter_widths(offset, amount, total):
    period = total // PERIODS
    in_period = (offset + jnp.arange(amount, dtype=jnp.int32)) % period
    widths = jnp.ones((amount,), jnp.int32)
    for exponent in range(6):
        widths = widths + (in_period * 64 >= period * 2**exponent).astype(jnp.int32)
    return widths


MESH = pl.DeviceIdType.MESH
VMEM_SPEC = pl.BlockSpec(memory_space=pltpu.VMEM)
ANY_SPEC = pl.BlockSpec(memory_space=pl.ANY)


def column_peers():
    count = lax.axis_size("mp")
    me = lax.axis_index("mp")
    return [lax.rem(me + j, count) for j in range(1, count)]


def greet(devices):
    barrier = pltpu.get_barrier_semaphore()
    for device in devices:
        pl.semaphore_signal(barrier, inc=1, device_id=device, device_id_type=MESH)
    pl.semaphore_wait(barrier, len(devices))


def remote(source, target, send, recv, device):
    return pltpu.make_async_remote_copy(
        src_ref=source,
        dst_ref=target,
        send_sem=send,
        recv_sem=recv,
        device_id=device,
        device_id_type=MESH,
    )


def one_hot_columns(ids, vocabulary):
    symbols = lax.broadcasted_iota(jnp.int32, (vocabulary, ids.shape[1]), 0)
    return (symbols == ids).astype(F32).astype(BF16)


def cnn_forward_kernel(
    ids_ref,
    table_ref,
    flags_ref,
    masked_ref,
    log_positions,
    b_high,
    b_proj,
    high_ref,
    proj_ref,
    input_ref,
    state_ref,
    base_out,
    taps_out,
    peak_out,
    pooled_out,
    current_out,
    transform_out,
    gate_out,
    features_all,
    last_out,
    input_out,
    state_out,
    features,
    w_high,
    w_proj,
    raw,
    turned,
    send_sem,
    recv_sem,
    base_send,
    base_recv,
    row_send,
    row_recv,
    own_sem,
    raw_sem,
    turned_sem,
    load_sem,
    relay_send,
    relay_recv,
):
    count = lax.axis_size("mp")
    me = lax.axis_index("mp")
    section = lax.axis_index("section")
    peers = column_peers()
    depth_count, tokens, local = current_out.shape
    chunk_rows = ids_ref.shape[2]
    padded = chunk_rows // CHUNK
    half = tokens // 2
    emb = 16
    block = min(256, local)
    loads = [
        pltpu.make_async_copy(high_ref, w_high, load_sem.at[0]),
        pltpu.make_async_copy(proj_ref, w_proj, load_sem.at[1]),
    ]
    for load in loads:
        load.start()
    groups = lax.axis_size("dp")
    group = lax.axis_index("dp")
    others = [lax.rem(group + j, groups) for j in range(1, groups)]
    relayed = groups == 4
    beside = group + 1 - 2 * lax.rem(group, 2)
    across = lax.rem(group + 2, 4)
    far = 3 - group
    near = [beside, across] if relayed else others
    origin = near if relayed else others[::-1]
    greet(
        [{"mp": peer} for peer in peers]
        + [{"section": 1 - section}]
        + [{"dp": other} for other in others]
    )

    def relay_rows(depth, way, slot):
        pieces = pl.ds(way * (count // 2), count // 2)
        return remote(
            features_all.at[depth, section, slot, pieces],
            features_all.at[depth, section, slot, pieces],
            relay_send.at[depth, way],
            relay_recv.at[depth, way],
            {"dp": across if way == 0 else beside},
        )

    def pass_rows(depth):
        for j in range(len(near)):
            give_rows(depth, j, origin[j]).wait_recv()
        if relayed:
            for way in range(2):
                relay_rows(depth, way, beside if way == 0 else across).start()

    blocks = input_out.shape[2] // TURN
    units = 4 * blocks

    def fetch(unit, start):
        slot = lax.rem(unit, 2)
        d = lax.rem(unit, 2 * blocks) // blocks
        rows = pl.ds(pl.multiple_of(lax.rem(unit, blocks) * TURN, TURN), TURN)
        for which, source in enumerate((input_ref, state_ref)):

            @pl.when(unit // (2 * blocks) == which)
            def _():
                copy = pltpu.make_async_copy(source.at[d, rows], raw.at[slot], raw_sem.at[slot])
                copy.start() if start else copy.wait()

    def deliver(unit, start):
        slot = lax.rem(unit, 2)
        d = lax.rem(unit, 2 * blocks) // blocks
        rows = pl.ds(pl.multiple_of(lax.rem(unit, blocks) * TURN, TURN), TURN)
        for which, target in enumerate((input_out, state_out)):

            @pl.when(unit // (2 * blocks) == which)
            def _():
                copy = pltpu.make_async_copy(
                    turned.at[slot], target.at[d, :, rows], turned_sem.at[slot]
                )
                copy.start() if start else copy.wait()

    def turn_units(first, last):
        @pl.loop(first, last)
        def _(unit):
            slot = lax.rem(unit, 2)
            fetch(unit, False)

            @pl.when(unit + 1 < units)
            def _():
                fetch(unit + 1, True)

            @pl.when(unit >= 2)
            def _():
                deliver(unit - 2, False)

            for g in range(4):
                turned[slot, g] = raw[slot, :, g, :]
            deliver(unit, True)

    fetch(0, True)

    def own_rows(depth):
        return pltpu.make_async_copy(
            features.at[depth], features_all.at[depth, section, group], own_sem.at[depth]
        )

    def give_rows(depth, j, slot):
        return remote(
            features.at[depth],
            features_all.at[depth, section, slot],
            row_send.at[depth, j],
            row_recv.at[depth, j],
            {"dp": near[j]},
        )

    def send(depth, part, rows, start):
        for j, peer in enumerate(peers):
            copy = remote(
                features.at[depth, me, rows],
                features.at[depth, me, rows],
                send_sem.at[depth, part, j],
                recv_sem.at[depth, part, me],
                {"mp": peer},
            )
            if start:
                copy.start()
            else:
                copy.wait_send()

    def receive(depth, part):
        rows = pl.ds(part * half, half)
        for j, peer in enumerate(peers):
            remote(
                features.at[depth, peer, rows],
                features.at[depth, peer, rows],
                send_sem.at[depth, part, j],
                recv_sem.at[depth, part, peer],
                {"mp": peer},
            ).wait_recv()

    lane_group = lax.broadcasted_iota(jnp.int32, (chunk_rows, 128), 1) // emb

    def pool_chunk(c):
        hot = one_hot_columns(ids_ref[c], table_ref.shape[0])
        embedded = lax.dot_general(
            hot, table_ref[...], (((0,), (0,)), ((), ())), preferred_element_type=F32
        )
        taps = embedded + flags_ref[...]
        for offset in range(1, TAPS):
            rolled = pltpu.roll(embedded, chunk_rows - offset, 0)
            taps = jnp.where(lane_group == offset, rolled, taps)
        taps = taps.astype(BF16)
        taps_out[c] = taps
        rows = pl.ds(pl.multiple_of(c * CHUNK, CHUNK), CHUNK)
        for start in range(0, local, block):
            cols = slice(start, start + block)
            scores = jnp.dot(taps, masked_ref[:, cols], preferred_element_type=F32)
            scores = scores.reshape(CHUNK, padded, block)
            top = jnp.max(scores, axis=1, keepdims=True)
            total = jnp.sum(jnp.exp(scores - top), axis=1, keepdims=True)
            peak = top + jnp.log(total)
            peak_out[rows, :, cols] = peak
            pooled = jnp.sum(peak, axis=1) - log_positions[:, cols]
            pooled_out[rows, cols] = pooled
            current = jnp.maximum(pooled, 0.0) + jnp.log1p(jnp.exp(-jnp.abs(pooled)))
            current_out[0, rows, cols] = current
            features[0, me, rows, cols] = current.astype(BF16)
        return rows

    for part in range(2):

        @pl.loop(0, half // CHUNK)
        def _(i):
            rows = pool_chunk(part * (half // CHUNK) + i)
            send(0, part, rows, True)

    for load in loads:
        load.wait()
    stops = [2, 2, 6, 9, 13, 16]
    turned_to = [0]

    def turn_some():
        stop = units * stops[min(turn_count[0], len(stops) - 1)] // 16
        turn_count[0] += 1
        if stop > turned_to[0]:
            turn_units(turned_to[0], stop)
            turned_to[0] = stop

    turn_count = [0]
    for depth in range(depth_count):
        for part in range(2):
            rows = pl.ds(part * half, half)
            turn_some()
            receive(depth, part)
            if part == 1:
                own_rows(depth).start()
                if depth + 1 < depth_count:
                    for j in range(len(near)):
                        give_rows(depth, j, group).start()
            mixed = []
            for g in range(2):
                total = jnp.broadcast_to(b_high[depth, g : g + 1, :].astype(F32), (half, local))
                for p in range(count):
                    total = total + jnp.dot(
                        features[depth, p, rows, :],
                        w_high[depth, g, p * local : (p + 1) * local, :],
                        preferred_element_type=F32,
                    )
                mixed.append(total)
            transform = mixed[0]
            gate = jax.nn.sigmoid(mixed[1])
            transform_out[depth, rows, :] = transform
            gate_out[depth, rows, :] = gate
            current = gate * current_out[depth, rows, :] + (1.0 - gate) * (
                transform * jax.nn.sigmoid(transform)
            )
            if depth + 1 < depth_count:
                current_out[depth + 1, rows, :] = current
            else:
                last_out[rows, :] = current.astype(BF16)
            features[depth + 1, me, rows, :] = current.astype(BF16)
            send(depth + 1, part, rows, True)
        if depth >= 1:
            pass_rows(depth - 1)

    def give():
        return remote(
            base_out.at[section],
            base_out.at[section],
            base_send,
            base_recv,
            {"section": 1 - section},
        )

    for part in range(2):
        rows = pl.ds(part * half, half)
        turn_some()
        receive(depth_count, part)
        total = jnp.broadcast_to(b_proj[...].astype(F32), (half, w_proj.shape[1]))
        for p in range(count):
            total = total + jnp.dot(
                features[depth_count, p, rows, :],
                w_proj[p * local : (p + 1) * local, :],
                preferred_element_type=F32,
            )
        base_out[section, rows, :] = total
    give().start()
    turn_units(turned_to[0], units)
    for depth in range(depth_count + 1):
        for part in range(2):
            send(depth, part, pl.ds(part * half, half), False)
    give().wait_send()
    remote(
        base_out.at[1 - section],
        base_out.at[1 - section],
        base_send,
        base_recv,
        {"section": 1 - section},
    ).wait_recv()
    for depth in range(depth_count):
        own_rows(depth).wait()
        if depth + 1 < depth_count:
            for j in range(len(near)):
                give_rows(depth, j, group).wait_send()
            if relayed:
                for way in range(2):
                    relay_rows(depth, way, beside if way == 0 else across).wait_send()
                    relay_rows(depth, way, far).wait_recv()
    for unit in range(units - 2, units):
        deliver(unit, False)


def cnn_forward(ids, weights, lstm_input, lstm_state):
    table, masked, log_positions, w_high, b_high, w_proj, b_proj = weights
    chunks, _, chunk_rows = ids.shape
    tokens = chunks * CHUNK
    depth_count, _, total, local = w_high.shape
    count = lax.axis_size("mp")
    groups = lax.axis_size("dp")
    directions, in_width, gate_blocks, cell_columns = lstm_input.shape
    padded = chunk_rows // CHUNK
    position = np.tile(np.arange(padded), CHUNK)[:, None]
    lane = np.arange(128)[None, :]
    excluded = lane - 16 * TAPS
    flags = (lane == 16 * TAPS) | (
        (excluded >= 1) & (excluded <= TAPS) & (position > PER_TOKEN - excluded)
    )
    dma = pltpu.SemaphoreType.DMA
    return pl.pallas_call(
        cnn_forward_kernel,
        out_shape=(
            jax.ShapeDtypeStruct((2, tokens, w_proj.shape[1]), F32),
            jax.ShapeDtypeStruct((chunks, chunk_rows, 128), BF16),
            jax.ShapeDtypeStruct((tokens, 1, local), F32),
            jax.ShapeDtypeStruct((tokens, local), F32),
            jax.ShapeDtypeStruct((depth_count, tokens, local), F32),
            jax.ShapeDtypeStruct((depth_count, tokens, local), F32),
            jax.ShapeDtypeStruct((depth_count, tokens, local), F32),
            jax.ShapeDtypeStruct((depth_count, 2, groups, count, tokens, local), BF16),
            jax.ShapeDtypeStruct((tokens, local), BF16),
            jax.ShapeDtypeStruct((directions, gate_blocks, in_width, cell_columns), BF16),
            jax.ShapeDtypeStruct((directions, gate_blocks, in_width, cell_columns), BF16),
        ),
        in_specs=[VMEM_SPEC] * 7 + [ANY_SPEC] * 4,
        out_specs=(*[VMEM_SPEC] * 7, ANY_SPEC, VMEM_SPEC, *[ANY_SPEC] * 2),
        scratch_shapes=[
            pltpu.VMEM((depth_count + 1, count, tokens, local), BF16),
            pltpu.VMEM(w_high.shape, BF16),
            pltpu.VMEM(w_proj.shape, BF16),
            pltpu.VMEM((2, TURN, gate_blocks, cell_columns), BF16),
            pltpu.VMEM((2, gate_blocks, TURN, cell_columns), BF16),
            dma((depth_count + 1, 2, count - 1)),
            dma((depth_count + 1, 2, count)),
            dma,
            dma,
            dma((depth_count, groups - 1)),
            dma((depth_count, groups - 1)),
            dma((depth_count,)),
            dma((2,)),
            dma((2,)),
            dma((2,)),
            dma((depth_count, 2)),
            dma((depth_count, 2)),
        ],
        compiler_params=pltpu.CompilerParams(
            collective_id=1, has_side_effects=True, vmem_limit_bytes=VMEM_LIMIT
        ),
        name="cnn_forward",
    )(
        ids,
        table,
        jnp.asarray(flags.astype(np.float32)),
        masked,
        log_positions,
        b_high,
        b_proj,
        w_high,
        w_proj,
        lstm_input,
        lstm_state,
    )


def cnn_backward_kernel(
    base_ref,
    own_ref,
    current_ref,
    transform_ref,
    gate_ref,
    peak_ref,
    pooled_ref,
    masked_ref,
    masked_t,
    ids_ref,
    high_ref,
    taps_hbm,
    gates_in,
    projected_in,
    x_in,
    hidden_in,
    state_all,
    gates_all,
    projected_all,
    x_all,
    hidden_all,
    base_full,
    mixed_all,
    late_a,
    late_b,
    late_c,
    late_d,
    small_out,
    w_high,
    taps_ref,
    load_sem,
    conv_out,
    mixed_out,
    late_buf,
    base_all,
    base_rows,
    table_sum,
    table_all,
    grad_current,
    outgoing,
    incoming,
    base_send,
    base_recv,
    sum_send,
    sum_recv,
    own_sem,
    relay_send,
    relay_recv,
    lift_send,
    lift_recv,
    row_send,
    row_recv,
    full_sem,
    share_send,
    share_recv,
    table_send,
    table_recv,
    mixed_sem,
    mixed_send,
    mixed_recv,
    mixed_share,
    mixed_shared,
    late_sem,
    defer_send,
    defer_recv,
):
    count = lax.axis_size("mp")
    me = lax.axis_index("mp")
    section = lax.axis_index("section")
    groups = lax.axis_size("dp")
    group = lax.axis_index("dp")
    peers = column_peers()
    depth_count, tokens, local = current_ref.shape
    steps = x_all.shape[2]
    chunks, chunk_rows, _ = taps_ref.shape
    loads = [
        pltpu.make_async_copy(high_ref, w_high, load_sem.at[0]),
        pltpu.make_async_copy(taps_hbm, taps_ref, load_sem.at[1]),
    ]
    for load in loads:
        load.start()
    padded = chunk_rows // CHUNK
    emb = 16
    vocabulary = -(-CHARS // 8) * 8
    relayed = groups == 4
    beside = group + 1 - 2 * lax.rem(group, 2)
    across = lax.rem(group + 2, 4)
    far = 3 - group
    greet(
        [{"mp": peer} for peer in peers]
        + [{"section": 1 - section, "mp": peer} for peer in [*peers, me]]
        + [{"dp": lax.rem(group + j, groups)} for j in range(1, groups)]
    )

    def lift():
        return remote(
            state_all.at[:, :, pl.ds(1, steps)],
            x_all,
            lift_send,
            lift_recv,
            {"section": 1 - section},
        )

    half_steps = steps // 2
    others = [lax.rem(group + j, groups) for j in range(1, groups)]
    near = [beside, across] if relayed else others
    origin = near if relayed else others[::-1]

    def relay(kind, way, slot):
        head = steps * 7 // 10
        if kind == 0:
            block = projected_all.at[way, slot]
        else:
            block = hidden_all.at[way, slot, pl.ds(head, steps - head)]
        return remote(
            block,
            block,
            relay_send.at[kind, way],
            relay_recv.at[kind, way],
            {"dp": across if way == 0 else beside},
        )

    def deferred(j, slot):
        return remote(
            gates_all.at[:, slot, pl.ds(0, DEFER)],
            gates_all.at[:, slot, pl.ds(0, DEFER)],
            defer_send.at[j],
            defer_recv.at[j],
            {"dp": near[j]},
        )

    for j in range(len(near)):
        deferred(j, group).start()


    late_loads, late_stores = [], []
    for i, target in enumerate((late_a, late_b, late_c, late_d)):
        d, way = i // 2, i % 2
        rows = pl.ds(way * half_steps, half_steps)
        source = gates_all.at[d, (beside, across)[way], rows]
        late_loads.append(pltpu.make_async_copy(source, late_buf.at[i], late_sem.at[i]))
        late_stores.append(pltpu.make_async_copy(late_buf.at[i], target, late_sem.at[i]))

    def spread_base(half, target_section, peer, j):
        return remote(
            base_ref.at[half],
            base_all.at[me],
            base_send.at[half, j],
            base_recv.at[me],
            {"section": target_section, "mp": peer},
        )

    everyone = [*peers, me]

    @pl.when(section == 0)
    def _():
        for j, peer in enumerate(peers):
            spread_base(0, 0, peer, j).start()
        for j, peer in enumerate(everyone):
            spread_base(1, 1, peer, j).start()
        lift().start()
        own = pltpu.make_async_copy(base_ref.at[0], base_all.at[me], own_sem)
        own.start()
        own.wait()

    def base_arrival(source):
        return remote(
            base_ref.at[0],
            base_all.at[source],
            base_send.at[0, 0],
            base_recv.at[source],
            {"section": 1 - section},
        )

    for peer in peers:
        base_arrival(peer).wait_recv()

    @pl.when(section == 1)
    def _():
        base_arrival(me).wait_recv()

    wide = base_all.shape[2]
    for p in range(count):
        base_rows[:, p * wide : (p + 1) * wide] = base_all[p]
    keep = pltpu.make_async_copy(base_rows, base_full.at[section, group], full_sem)
    keep.start()

    def base_row(j, slot):
        return remote(
            base_rows,
            base_full.at[section, slot],
            row_send.at[j],
            row_recv.at[j],
            {"dp": others[j]},
        )

    def share_base(owner):
        return remote(
            base_full.at[owner],
            base_full.at[owner],
            share_send,
            share_recv,
            {"section": 1 - section},
        )

    for j in range(groups - 1):
        base_row(j, group).start()

    def keep_mixed(depth):
        return pltpu.make_async_copy(
            mixed_out.at[depth], mixed_all.at[depth, section, group], mixed_sem.at[depth]
        )

    def mixed_row(depth, j, slot):
        return remote(
            mixed_out.at[depth],
            mixed_all.at[depth, section, slot],
            mixed_send.at[depth, j],
            mixed_recv.at[depth, j],
            {"dp": others[j]},
        )

    def share_mixed(depth, owner):
        return remote(
            mixed_all.at[depth, owner],
            mixed_all.at[depth, owner],
            mixed_share.at[depth],
            mixed_shared.at[depth],
            {"section": 1 - section},
        )

    def collect_mixed(depth):
        keep_mixed(depth).wait()
        for j in range(groups - 1):
            mixed_row(depth, j, others[groups - 2 - j]).wait_recv()
        share_mixed(depth, section).start()

    own_rows = pl.ds(pl.multiple_of(me * local, local), local)
    total = jnp.zeros((tokens, local), F32)
    for p in range(count):
        total = total + lax.dot_general(
            base_all[p],
            own_ref[own_rows, p * wide : (p + 1) * wide],
            (((1,), (1,)), ((), ())),
            preferred_element_type=F32,
        )
    grad_current[...] = total

    def send_sum(depth, peer, j):
        return remote(
            outgoing.at[depth, j],
            incoming.at[depth, me],
            sum_send.at[depth, j],
            sum_recv.at[depth, me],
            {"mp": peer},
        )

    def back(depth, owner):
        rows = pl.ds(pl.multiple_of(owner * local, local), local)
        parts = [
            lax.dot_general(
                mixed_out[depth, :, g * local : (g + 1) * local],
                w_high[depth, g, rows, :],
                (((1,), (1,)), ((), ())),
                preferred_element_type=F32,
            )
            for g in range(2)
        ]
        return parts[0] + parts[1]

    for load in loads:
        load.wait()
    for depth in range(depth_count - 1, -1, -1):
        transform = transform_ref[depth]
        gate = gate_ref[depth]
        grad = grad_current[...]
        slope = jax.nn.sigmoid(transform)
        mixed_out[depth, :, :local] = (
            grad * (1.0 - gate) * slope * (1.0 + transform * (1.0 - slope))
        ).astype(BF16)
        mixed_out[depth, :, local:] = (
            grad * (current_ref[depth] - transform * slope) * gate * (1.0 - gate)
        ).astype(BF16)
        keep_mixed(depth).start()
        for j in range(groups - 1):
            mixed_row(depth, j, group).start()
        if relayed and depth == depth_count - 1:
            for kind in range(2):
                for way in range(2):
                    relay(kind, way, beside if way == 0 else across).start()
        for j, peer in enumerate(peers):
            outgoing[depth, j] = back(depth, peer).astype(BF16)
            send_sum(depth, peer, j).start()
        total = grad * gate + back(depth, me)
        for j, peer in enumerate(peers):
            remote(
                outgoing.at[depth, j],
                incoming.at[depth, peer],
                sum_send.at[depth, j],
                sum_recv.at[depth, peer],
                {"mp": peer},
            ).wait_recv()
            total = total + incoming[depth, peer].astype(F32)
        grad_current[...] = total

    for j in range(len(near)):
        deferred(j, group).wait_send()
        deferred(j, origin[j]).wait_recv()
    if relayed:
        for load in late_loads:
            load.start()
    for depth in range(depth_count - 1, 0, -1):
        collect_mixed(depth)
    if relayed:
        for load, store in zip(late_loads, late_stores):
            load.wait()
            store.start()
    grad_current[...] = grad_current[...] * jax.nn.sigmoid(pooled_ref[...])
    conv_out[...] = jnp.zeros_like(conv_out)
    small_out[...] = jnp.zeros_like(small_out)
    table_sum[...] = jnp.zeros_like(table_sum)
    lane_group = lax.broadcasted_iota(jnp.int32, (chunk_rows, 128), 1) // emb

    @pl.loop(0, chunks)
    def _(c):
        rows = pl.ds(pl.multiple_of(c * CHUNK, CHUNK), CHUNK)
        taps = taps_ref[c]
        scores = jnp.dot(taps, masked_ref[...], preferred_element_type=F32)
        scores = scores.reshape(CHUNK, padded, local)
        share = jnp.exp(scores - peak_ref[rows])
        grads = share * grad_current[rows, :][:, None, :]
        grads = grads.reshape(chunk_rows, local).astype(BF16)
        conv_out[...] += lax.dot_general(
            taps, grads, (((0,), (0,)), ((), ())), preferred_element_type=F32
        )
        back_taps = jnp.dot(grads, masked_t[...], preferred_element_type=F32)
        moved = back_taps
        for offset in range(1, TAPS):
            moved = jnp.where(lane_group == offset, pltpu.roll(back_taps, offset, 0), moved)
        hot = one_hot_columns(ids_ref[c], vocabulary)
        table_sum[:vocabulary, :] += jnp.dot(
            hot, moved.astype(BF16), preferred_element_type=F32
        )

    columns = table_sum[...].T
    folded = columns[:emb]
    for offset in range(1, TAPS):
        folded = folded + columns[offset * emb : (offset + 1) * emb]
    table_all[me] = folded

    def table_copy(j, slot):
        return remote(
            table_all.at[slot],
            table_all.at[slot],
            table_send.at[j],
            table_recv.at[slot],
            {"mp": peers[j]},
        )

    for j in range(count - 1):
        table_copy(j, me).start()

    for j in range(count - 1):
        table_copy(j, peers[j]).wait_recv()
    folded = table_all[0]
    for p in range(1, count):
        folded = folded + table_all[p]
    small_out[:128, :] = conv_out[...].astype(BF16)
    span = min(local, folded.shape[1])
    for i in range(folded.shape[1] // span):
        at = 128 + i * emb
        small_out[at : at + emb, :span] = folded[:, i * span : (i + 1) * span].astype(BF16)
    for j in range(count - 1):
        table_copy(j, me).wait_send()
    keep.wait()
    for j in range(groups - 1):
        base_row(j, others[groups - 2 - j]).wait_recv()
    share_base(section).start()
    collect_mixed(0)
    for j in range(groups - 1):
        base_row(j, group).wait_send()
        for depth in range(depth_count):
            mixed_row(depth, j, group).wait_send()
    for depth in range(depth_count):
        for j, peer in enumerate(peers):
            send_sum(depth, peer, j).wait_send()

    @pl.when(section == 0)
    def _():
        for j, peer in enumerate(peers):
            spread_base(0, 0, peer, j).wait_send()
        for j, peer in enumerate(everyone):
            spread_base(1, 1, peer, j).wait_send()
        lift().wait_send()

    @pl.when(section == 1)
    def _():
        lift().wait_recv()

    if relayed:
        for kind in range(2):
            for way in range(2):
                relay(kind, way, beside if way == 0 else across).wait_send()
                relay(kind, way, far).wait_recv()
        for copy in late_stores:
            copy.wait()

    share_base(section).wait_send()
    share_base(1 - section).wait_recv()
    for depth in range(depth_count):
        share_mixed(depth, section).wait_send()
        share_mixed(depth, 1 - section).wait_recv()


def cnn_backward(base_shards, saved, weights, rows_all):
    w_proj, w_high, masked, ids = weights
    taps, peak, pooled, current, transform, gate = saved
    gates_all, projected_all, x_all, hidden_all, state_all = rows_all
    depth_count, tokens, local = current.shape
    count = lax.axis_size("mp")
    groups = lax.axis_size("dp")
    vocabulary = -(-CHARS // 128) * 128
    half_steps = gates_all.shape[2] // 2
    late = (half_steps, *gates_all.shape[3:])
    dma = pltpu.SemaphoreType.DMA
    return pl.pallas_call(
        cnn_backward_kernel,
        out_shape=(
            jax.ShapeDtypeStruct(gates_all.shape, BF16),
            jax.ShapeDtypeStruct(projected_all.shape, BF16),
            jax.ShapeDtypeStruct(x_all.shape, BF16),
            jax.ShapeDtypeStruct(hidden_all.shape, BF16),
            jax.ShapeDtypeStruct((2, groups, tokens, count * base_shards.shape[2]), BF16),
            jax.ShapeDtypeStruct((depth_count, 2, groups, tokens, 2 * local), BF16),
            *[jax.ShapeDtypeStruct(late, BF16)] * 4,
            jax.ShapeDtypeStruct((128 + 16 * max(1, vocabulary // local), local), BF16),
        ),
        in_specs=[VMEM_SPEC] * 10 + [ANY_SPEC] * 7,
        out_specs=(*[ANY_SPEC] * 10, VMEM_SPEC),
        input_output_aliases={12: 0, 13: 1, 14: 2, 15: 3},
        scratch_shapes=[
            pltpu.VMEM(w_high.shape, BF16),
            pltpu.VMEM(taps.shape, BF16),
            dma((2,)),
            pltpu.VMEM((128, local), F32),
            pltpu.VMEM((depth_count, tokens, 2 * local), BF16),
            pltpu.VMEM((4, *late), BF16),
            pltpu.VMEM((count, tokens, base_shards.shape[2]), BF16),
            pltpu.VMEM((tokens, count * base_shards.shape[2]), BF16),
            pltpu.VMEM((vocabulary, 128), F32),
            pltpu.VMEM((count, 16, vocabulary), F32),
            pltpu.VMEM((tokens, local), F32),
            pltpu.VMEM((depth_count, count - 1, tokens, local), BF16),
            pltpu.VMEM((depth_count, count, tokens, local), BF16),
            dma((2, count)),
            dma((count,)),
            dma((depth_count, count - 1)),
            dma((depth_count, count)),
            dma,
            dma((2, 2)),
            dma((2, 2)),
            dma,
            dma,
            dma((groups - 1,)),
            dma((groups - 1,)),
            dma,
            dma,
            dma,
            dma((count - 1,)),
            dma((count,)),
            dma((depth_count,)),
            dma((depth_count, groups - 1)),
            dma((depth_count, groups - 1)),
            dma((depth_count,)),
            dma((depth_count,)),
            dma((4,)),
            dma((groups - 1,)),
            dma((groups - 1,)),
        ],
        compiler_params=pltpu.CompilerParams(
            collective_id=2, has_side_effects=True, vmem_limit_bytes=VMEM_LIMIT
        ),
        name="cnn_backward",
    )(
        base_shards,
        w_proj,
        current,
        transform,
        gate,
        peak,
        pooled,
        masked,
        jnp.pad(masked[: 16 * TAPS], ((0, 128 - 16 * TAPS), (0, 0))).T,
        ids,
        w_high,
        taps,
        gates_all,
        projected_all,
        x_all,
        hidden_all,
        state_all,
    )


def recurrence_kernel(
    base_ref,
    live_ref,
    top_ref,
    bias_ref,
    proj_ref,
    in_ref,
    state_ref,
    features_in,
    x_all,
    state_all,
    hidden_all,
    gates_all,
    projected_all,
    base_out,
    features_all,
    x_out,
    state_out,
    hidden_out,
    projected_out,
    acts,
    cells,
    clips,
    pre,
    grad_cell,
    parts,
    back_parts,
    above,
    gate_buf,
    base_sem,
    send_sem,
    recv_sem,
    back_send,
    back_recv,
    x_send,
    x_recv,
    above_send,
    above_recv,
    gate_sem,
    gate_send,
    own_sem,
    row_send,
    row_recv,
    w_in,
    w_state,
    load_sem,
    w_in_t,
    w_state_t,
    proj_t,
    input_parts,
    input_sums,
    input_send,
    input_recv,
    base_sum,
    share_send,
    share_recv,
    relay_send,
    relay_recv,
    feature_send,
    feature_recv,
    hidden_send,
    hidden_recv,
):
    count = lax.axis_size("mp")
    me = lax.axis_index("mp")
    section = lax.axis_index("section")
    steps = x_out.shape[1]
    cell_count = proj_ref.shape[1]
    chunk = min(256, cell_count)
    peers = [lax.rem(me + j, count) for j in range(1, count)]
    groups = lax.axis_size("dp")
    group = lax.axis_index("dp")
    others = [lax.rem(group + j, groups) for j in range(1, groups)]
    relayed = groups == 4
    beside = group + 1 - 2 * lax.rem(group, 2)
    across = lax.rem(group + 2, 4)
    near = [beside, across] if relayed else others
    loads = [
        [pltpu.make_async_copy(source.at[d], target.at[d], load_sem.at[i, d]) for d in range(2)]
        for i, (source, target) in enumerate(((in_ref, w_in), (state_ref, w_state)))
    ]
    for d in range(2):
        loads[0][d].start()
    for d in range(2):
        loads[1][d].start()

    barrier = pltpu.get_barrier_semaphore()
    for peer in peers:
        pl.semaphore_signal(barrier, inc=1, device_id={"mp": peer}, device_id_type=MESH)
    pl.semaphore_signal(barrier, inc=1, device_id={"section": 1 - section}, device_id_type=MESH)
    for other in others:
        pl.semaphore_signal(barrier, inc=1, device_id={"dp": other}, device_id_type=MESH)
    pl.semaphore_wait(barrier, count + groups - 1)

    def share_features(owner):
        return remote(
            features_all.at[:, owner],
            features_all.at[:, owner],
            share_send,
            share_recv,
            {"section": 1 - section},
        )

    pieces = features_all.shape[3]

    last_depth = features_all.shape[0] - 1

    def give_features(j, slot):
        return remote(
            features_all.at[last_depth, section, slot],
            features_all.at[last_depth, section, slot],
            feature_send.at[j],
            feature_recv.at[j],
            {"dp": near[j]},
        )

    def relay_features(way, slot):
        half = pl.ds(way * (pieces // 2), pieces // 2)
        block = features_all.at[last_depth, section, slot, half]
        return remote(
            block,
            block,
            relay_send.at[way],
            relay_recv.at[way],
            {"dp": across if way == 0 else beside},
        )

    def start_relays():
        if relayed:
            for way in range(2):
                relay_features(way, beside if way == 0 else across).start()

    def finish_relays():
        if relayed:
            for way in range(2):
                relay_features(way, beside if way == 0 else across).wait_send()
                relay_features(way, 3 - group).wait_recv()

    for j in range(len(near)):
        give_features(j, group).start()

    def wide(values, width):
        return jnp.concatenate([values] * (width // values.shape[1]), axis=1)

    def copy_part(buffer, send, recv, d, parity, source, j, target):
        return pltpu.make_async_remote_copy(
            src_ref=buffer.at[d, parity, source],
            dst_ref=buffer.at[d, parity, source],
            send_sem=send.at[d, parity, j],
            recv_sem=recv.at[d, parity, source],
            device_id={"mp": target},
            device_id_type=MESH,
        )

    ordered = peers
    if count == 4:
        ordered = [3 - me, lax.rem(me + 2, 4), me + 1 - 2 * lax.rem(me, 2)]

    def exchange_start(buffer, send, recv, d, parity, value):
        buffer[d, parity, me] = value.astype(BF16)
        for j, peer in enumerate(ordered):
            copy_part(buffer, send, recv, d, parity, me, j, peer).start()

    def exchange_wait(buffer, send, recv, d, parity):
        for j, peer in enumerate(ordered):
            copy_part(buffer, send, recv, d, parity, peer, j, peer).wait_recv()
        total = buffer[d, parity, 0].astype(F32)
        for source in range(1, count):
            total = total + buffer[d, parity, source].astype(F32)
        for j, peer in enumerate(ordered):
            copy_part(buffer, send, recv, d, parity, me, j, peer).wait_send()
        return total

    def pass_up(d, k):
        return pltpu.make_async_remote_copy(
            src_ref=state_out.at[d, k + 1],
            dst_ref=x_out.at[d, k],
            send_sem=x_send.at[d],
            recv_sem=x_recv.at[d, k],
            device_id={"section": 1 - section},
            device_id_type=MESH,
        )

    def pass_down(d, k):
        return pltpu.make_async_remote_copy(
            src_ref=above.at[d, k],
            dst_ref=above.at[d, k],
            send_sem=above_send.at[d],
            recv_sem=above_recv.at[d, k],
            device_id={"section": 1 - section},
            device_id_type=MESH,
        )

    def gates_copy(d, k, slot):
        return pltpu.make_async_copy(
            gate_buf.at[d, slot], gates_all.at[d, group, k], gate_sem.at[d, slot]
        )

    def gates_row(d, k, slot, j, other):
        return pltpu.make_async_remote_copy(
            src_ref=gate_buf.at[d, slot],
            dst_ref=gates_all.at[d, group, k],
            send_sem=gate_send.at[d, slot, j],
            recv_sem=row_recv.at[0, j],
            device_id={"dp": other},
            device_id_type=MESH,
        )

    def row(kind, source, target, j, other):
        return pltpu.make_async_remote_copy(
            src_ref=source,
            dst_ref=target,
            send_sem=row_send.at[kind, j],
            recv_sem=row_recv.at[kind, j],
            device_id={"dp": other},
            device_id_type=MESH,
        )

    def from_peer(j, targets):
        back = len(targets) - 1 - j
        return targets[j] if relayed and len(targets) == 2 else targets[back]

    head = steps * 7 // 10

    def relay_hidden(way, slot):
        block = hidden_all.at[way, slot, pl.ds(0, head)]
        return remote(
            block,
            block,
            hidden_send.at[way],
            hidden_recv.at[way],
            {"dp": across if way == 0 else beside},
        )

    def finish_hidden(kind, some):
        for j, other in enumerate(near):
            target = hidden_all.at[:, from_peer(j, near), some]
            copy = row(kind, hidden_out.at[:, some], target, j, other)
            copy.wait_send()
            copy.wait_recv()

    def time_of(d, k):
        return k if d == 0 else steps - 1 - k

    @pl.when(section == 0)
    def _():
        part_rows = base_ref.shape[1] // steps

        @pl.loop(0, steps)
        def _(t):
            at = pl.ds(pl.multiple_of(t * part_rows, part_rows), part_rows)
            x = jnp.concatenate([base_ref[0, at, :], base_ref[1, at, :]], axis=0).astype(BF16)
            for d in range(2):
                x_out[d, time_of(d, t)] = x

        for j, other in enumerate(others):
            row(1, x_out.at[0], x_all.at[0, group], j, other).start()

    for d in range(2):
        state_out[d, 0] = jnp.zeros(state_out.shape[2:], BF16)
        cells[d, 0] = jnp.zeros(cells.shape[2:], F32)
        grad_cell[d] = jnp.zeros(grad_cell.shape[1:], F32)

    def input_part(d, k):
        @pl.when(section == 1)
        def _():
            pass_up(d, k).wait_recv()

        x = x_out[d, k]
        for block in range(4):
            for start in range(0, cell_count, chunk):
                cols = slice(block * cell_count + start, block * cell_count + start + chunk)
                bias = bias_ref[d, block : block + 1, start : start + chunk].astype(F32)
                pre[d, :, cols] = bias + jnp.dot(
                    x, w_in[d, block, :, start : start + chunk], preferred_element_type=F32
                )

    def turn_weights(unit):
        per_block = cell_count // chunk
        block = unit // per_block
        cols = pl.ds(pl.multiple_of(lax.rem(unit, per_block) * chunk, chunk), chunk)
        rows_t = pl.ds(pl.multiple_of(unit * chunk, chunk), chunk)
        for d in range(2):
            w_in_t[d, rows_t, :] = w_in[d, block, :, cols].T
            w_state_t[d, rows_t, :] = w_state[d, block, :, cols].T

    def turn_proj(unit):
        cols = pl.ds(pl.multiple_of(unit * 128, 128), 128)
        for d in range(2):
            proj_t[d, :, cols] = proj_ref[d, cols, :].T

    def forward_cells(d, k):
        state = state_out[d, k]
        live = live_ref[time_of(d, k)]
        for start in range(0, cell_count, chunk):
            raw = []
            for block in range(4):
                cols = slice(block * cell_count + start, block * cell_count + start + chunk)
                raw.append(
                    pre[d, :, cols]
                    + jnp.dot(
                        state, w_state[d, block, :, start : start + chunk], preferred_element_type=F32
                    )
                )
            own = slice(start, start + chunk)
            in_gate = jax.nn.sigmoid(raw[0])
            forget = jax.nn.sigmoid(raw[1])
            memory = jnp.tanh(raw[2])
            out_gate = jax.nn.sigmoid(raw[3])
            for block, value in enumerate((in_gate, forget, memory, out_gate)):
                acts[d, k, block, :, own] = value
            cell_new = soft_clip(in_gate * memory + forget * cells[d, k, :, own])
            cells[d, k + 1, :, own] = wide(live, chunk) * cell_new
            hidden_out[d, k, :, own] = (out_gate * jnp.tanh(cell_new)).astype(BF16)
        part = jnp.dot(hidden_out[d, k], proj_ref[d], preferred_element_type=F32)
        exchange_start(parts, send_sem, recv_sem, d, lax.rem(k, 2), part)
        for j, other in enumerate(near):
            kind = 2 + 3 * (k // head)
            row(kind, hidden_out.at[d, k], hidden_all.at[d, group, k], j, other).start()

    def forward_state(d, k):
        total = exchange_wait(parts, send_sem, recv_sem, d, lax.rem(k, 2))
        clip = jnp.tanh(total / 3.0)
        clips[d, k] = clip
        live = wide(live_ref[time_of(d, k)], clip.shape[1])
        state_out[d, k + 1] = (live * 3.0 * clip).astype(BF16)

        @pl.when(section == 0)
        def _():
            @pl.when(k > 0)
            def _():
                pass_up(d, k - 1).wait_send()

            pass_up(d, k).start()

        for j, other in enumerate(others):
            row(3, state_out.at[d, k + 1], state_all.at[d, group, k + 1], j, other).start()

    units = 4 * cell_count // chunk
    for d in range(2):
        loads[0][d].wait()
        input_part(d, 0)
    for d in range(2):
        loads[1][d].wait()
        forward_cells(d, 0)
    for d in range(2):
        input_part(d, 1)

    @pl.loop(1, steps)
    def _(k):
        for d in range(2):
            forward_state(d, k - 1)
            forward_cells(d, k)

        @pl.when(k + 1 < steps)
        def _():
            for d in range(2):
                input_part(d, k + 1)

        @pl.when(k <= units)
        def _():
            turn_weights(k - 1)

        @pl.when(k == steps - 3)
        def _():
            finish_hidden(2, pl.ds(0, head))
            if relayed:
                for way in range(2):
                    relay_hidden(way, beside if way == 0 else across).start()

        @pl.when(k == steps - 5)
        def _():
            for j in range(len(near)):
                give_features(j, group).wait_send()
                give_features(j, from_peer(j, near)).wait_recv()
            start_relays()

        @pl.when(k <= cell_count // 128)
        def _():
            turn_proj(k - 1)

    for unit in range(steps - 1, units):
        turn_weights(unit)
    for d in range(2):
        forward_state(d, steps - 1)

    @pl.when(section == 0)
    def _():
        for d in range(2):
            pass_up(d, steps - 1).wait_send()

    def back_wait(d, parity):
        return exchange_wait(back_parts, back_send, back_recv, d, parity)

    def back_start(d, parity, value):
        exchange_start(back_parts, back_send, back_recv, d, parity, value)

    def backward_cells(d, k, total):
        slot = lax.rem(k, SLOTS)
        live = live_ref[time_of(d, k)]
        clip = clips[d, k]
        grad_out = wide(live, clip.shape[1]) * (total + top_ref[d, time_of(d, k)].astype(F32))
        grad_projected = (grad_out * (1.0 - clip * clip)).astype(BF16)
        projected_out[d, k] = grad_projected

        for j, other in enumerate(near):
            row(
                4, projected_out.at[d, k], projected_all.at[d, group, k], j, other
            ).start()

        @pl.when(k < steps - SLOTS)
        def _():
            gates_copy(d, k + SLOTS, slot).wait()
            for j, other in enumerate(near):
                gates_row(d, k + SLOTS, slot, j, other).wait_send()

        for start in range(0, cell_count, chunk):
            own = slice(start, start + chunk)
            grad_hidden = jnp.dot(grad_projected, proj_t[d, :, own], preferred_element_type=F32)
            in_gate, forget, memory, out_gate = [acts[d, k, block, :, own] for block in range(4)]
            cell = cells[d, k, :, own]
            clip_raw = jnp.tanh((in_gate * memory + forget * cell) / 3.0)
            tanh_cell = jnp.tanh(3.0 * clip_raw)
            grad_new = wide(live, chunk) * grad_cell[d, :, own] + grad_hidden * out_gate * (
                1.0 - tanh_cell * tanh_cell
            )
            grad_raw = grad_new * (1.0 - clip_raw * clip_raw)
            grad_cell[d, :, own] = grad_raw * forget
            grads = (
                grad_raw * memory * in_gate * (1.0 - in_gate),
                grad_raw * cell * forget * (1.0 - forget),
                grad_raw * in_gate * (1.0 - memory * memory),
                grad_hidden * tanh_cell * out_gate * (1.0 - out_gate),
            )
            for block, value in enumerate(grads):
                cols = slice(block * cell_count + start, block * cell_count + start + chunk)
                gate_buf[d, slot, :, cols] = value.astype(BF16)
        gates_copy(d, k, slot).start()

    def gates_send(d, k):
        @pl.when(k >= DEFER)
        def _():
            for j, other in enumerate(near):
                gates_row(d, k, lax.rem(k, SLOTS), j, other).start()

    def backward_state(d, k):
        @pl.when(k > 0)
        def _():
            back = jnp.dot(gate_buf[d, lax.rem(k, SLOTS)], w_state_t[d], preferred_element_type=F32)
            pre[d, :, : back.shape[1]] = back

            @pl.when(section == 0)
            def _():
                pass_down(d, k - 1).wait_recv()
                pre[d, :, : back.shape[1]] = back + above[d, k - 1]

            back_start(d, lax.rem(k - 1, 2), pre[d, :, : back.shape[1]])

    share = base_out.shape[2]

    def input_copy(source, target, j, peer):
        return remote(source, target, input_send.at[j], input_recv.at[j], {"mp": peer})

    def backward_input(d, k):
        gates_send(d, k)
        part = jnp.dot(gate_buf[d, lax.rem(k, SLOTS)], w_in_t[d], preferred_element_type=F32)

        @pl.when(section == 1)
        def _():
            above[d, k] = part

            @pl.when(k < steps - 1)
            def _():
                pass_down(d, k + 1).wait_send()

            pass_down(d, k).start()

        @pl.when(section == 0)
        def _():
            for p in range(count):
                input_parts[d, k, p] = part[:, p * share : (p + 1) * share].astype(BF16)
            for j, peer in enumerate(peers):
                input_copy(input_parts.at[d, k, peer], input_sums.at[d, k, me], j, peer).start()

    last = steps - 1

    @pl.when(section == 0)
    def _():
        for d in range(2):
            pass_down(d, last).wait_recv()
            back_start(d, lax.rem(last, 2), above[d, last])

    for d in range(2):

        @pl.when(section == 0)
        def _():
            pre[d, :, : clips.shape[3]] = back_wait(d, lax.rem(last, 2))

        @pl.when(section == 1)
        def _():
            pre[d, :, : clips.shape[3]] = jnp.zeros(clips.shape[2:], F32)

        backward_cells(d, last, pre[d, :, : clips.shape[3]])
        backward_state(d, last)
    for d in range(2):
        backward_input(d, last)

    @pl.loop(1, steps)
    def _(tick):
        k = last - tick
        for d in range(2):
            backward_cells(d, k, back_wait(d, lax.rem(k, 2)))
            backward_state(d, k)
        for d in range(2):
            backward_input(d, k)

        @pl.when(tick == 5)
        def _():
            finish_relays()
            share_features(section).start()
            if relayed:
                for way in range(2):
                    relay_hidden(way, beside if way == 0 else across).wait_send()
                    relay_hidden(way, 3 - group).wait_recv()

    for d in range(2):
        for k in range(min(SLOTS, steps)):
            gates_copy(d, k, k % SLOTS).wait()
            for j, other in enumerate(near):
                if k >= DEFER:
                    gates_row(d, k, k % SLOTS, j, other).wait_send()

    @pl.when(section == 1)
    def _():
        for d in range(2):
            pass_down(d, 0).wait_send()

    own = [
        (hidden_out, hidden_all.at[:, group]),
        (state_out, state_all.at[:, group]),
        (projected_out, projected_all.at[:, group]),
    ]
    for other in others:
        own.append((state_out.at[:, 0], state_all.at[:, other, 0]))
    own = [
        pltpu.make_async_copy(source, target, own_sem.at[i])
        for i, (source, target) in enumerate(own)
    ]
    for copy in own:
        copy.start()

    rest = pl.ds(1, steps)
    for j, other in enumerate(others):
        source = from_peer(j, others)
        state_row = row(3, state_out.at[:, rest], state_all.at[:, source, rest], j, other)
        state_row.wait_send()
        state_row.wait_recv()

    finish_hidden(5, pl.ds(head, steps - head))

    for copy in own:
        copy.wait()

    @pl.when(section == 0)
    def _():
        mine = pltpu.make_async_copy(x_out.at[0], x_all.at[0, group], base_sem)
        mine.start()
        for j, other in enumerate(others):
            copy = row(1, x_out.at[0], x_all.at[0, from_peer(j, others)], j, other)
            copy.wait_send()
            copy.wait_recv()
        mine.wait()

    @pl.when(section == 0)
    def _():
        for j, peer in enumerate(peers):
            source = peers[count - 2 - j]
            copy = input_copy(input_parts.at[:, :, peer], input_sums.at[:, :, source], j, peer)
            copy.wait_send()
            copy.wait_recv()
        rows_half = base_out.shape[1] // steps

        @pl.loop(0, steps)
        def _(t):
            total = input_parts[0, t, me].astype(F32) + input_parts[1, steps - 1 - t, me].astype(F32)
            for peer in peers:
                total = total + input_sums[0, t, peer].astype(F32)
                total = total + input_sums[1, steps - 1 - t, peer].astype(F32)
            at = pl.ds(pl.multiple_of(t * rows_half, rows_half), rows_half)
            for half in range(2):
                base_sum[half, at, :] = total[half * rows_half : (half + 1) * rows_half]

        base_out[...] = base_sum[...].astype(BF16)

    share_features(section).wait_send()
    share_features(1 - section).wait_recv()

    for j, other in enumerate(near):
        source = from_peer(j, near)
        pltpu.make_async_remote_copy(
            src_ref=gates_all.at[:, source, pl.ds(DEFER, steps - DEFER)],
            dst_ref=gates_all.at[:, source, pl.ds(DEFER, steps - DEFER)],
            send_sem=row_send.at[0, j],
            recv_sem=row_recv.at[0, j],
            device_id={"dp": other},
            device_id_type=MESH,
        ).wait_recv()
        projected_row = row(4, projected_out, projected_all.at[:, source], j, other)
        projected_row.wait_send()
        projected_row.wait_recv()


def recurrence(base_seq, live_seq, top_seq, layer_weights, features_all):
    w_in, w_state, bias, proj = layer_weights
    _, steps, rows, width = top_seq.shape
    cell_count = proj.shape[1]
    count = lax.axis_size("mp")
    groups = lax.axis_size("dp")
    weights = (bias, proj, w_in, w_state)
    dma = pltpu.SemaphoreType.DMA
    return pl.pallas_call(
        recurrence_kernel,
        out_shape=(
            jax.ShapeDtypeStruct((2, groups, steps, rows, width), BF16),
            jax.ShapeDtypeStruct((2, groups, steps + 1, rows, width), BF16),
            jax.ShapeDtypeStruct((2, groups, steps, rows, cell_count), BF16),
            jax.ShapeDtypeStruct((2, groups, steps, rows, 4 * cell_count), BF16),
            jax.ShapeDtypeStruct((2, groups, steps, rows, width), BF16),
            jax.ShapeDtypeStruct((2, steps * rows // 2, width // count), BF16),
            jax.ShapeDtypeStruct(features_all.shape, BF16),
        ),
        in_specs=[VMEM_SPEC] * 5 + [ANY_SPEC] * 3,
        out_specs=(*[ANY_SPEC] * 5, VMEM_SPEC, ANY_SPEC),
        input_output_aliases={7: 6},
        scratch_shapes=[
            pltpu.VMEM((2, steps, rows, width), BF16),
            pltpu.VMEM((2, steps + 1, rows, width), BF16),
            pltpu.VMEM((2, steps, rows, cell_count), BF16),
            pltpu.VMEM((2, steps, rows, width), BF16),
            pltpu.VMEM((2, steps, 4, rows, cell_count), F32),
            pltpu.VMEM((2, steps + 1, rows, cell_count), F32),
            pltpu.VMEM((2, steps, rows, width), F32),
            pltpu.VMEM((2, rows, 4 * cell_count), F32),
            pltpu.VMEM((2, rows, cell_count), F32),
            pltpu.VMEM((2, 2, count, rows, width), BF16),
            pltpu.VMEM((2, 2, count, rows, width), BF16),
            pltpu.VMEM((2, steps, rows, width), F32),
            pltpu.VMEM((2, SLOTS, rows, 4 * cell_count), BF16),
            dma,
            dma((2, 2, count - 1)),
            dma((2, 2, count)),
            dma((2, 2, count - 1)),
            dma((2, 2, count)),
            dma((2,)),
            dma((2, steps)),
            dma((2,)),
            dma((2, steps)),
            dma((2, SLOTS)),
            dma((2, SLOTS, groups - 1)),
            dma((groups + 2,)),
            dma((6, groups - 1)),
            dma((6, groups - 1)),
            pltpu.VMEM(w_in.shape, BF16),
            pltpu.VMEM(w_state.shape, BF16),
            dma((2, 2)),
            pltpu.VMEM((2, 4 * cell_count, width), BF16),
            pltpu.VMEM((2, 4 * cell_count, width), BF16),
            pltpu.VMEM((2, width, cell_count), BF16),
            pltpu.VMEM((2, steps, count, rows, width // count), BF16),
            pltpu.VMEM((2, steps, count, rows, width // count), BF16),
            dma((count - 1,)),
            dma((count - 1,)),
            pltpu.VMEM((2, steps * rows // 2, width // count), F32),
            dma,
            dma,
            dma((2,)),
            dma((2,)),
            dma((groups - 1,)),
            dma((groups - 1,)),
            dma((2,)),
            dma((2,)),
        ],
        compiler_params=pltpu.CompilerParams(
            collective_id=0, has_side_effects=True, vmem_limit_bytes=VMEM_LIMIT
        ),
        name="recurrence",
    )(base_seq, live_seq, top_seq, *weights, features_all)


def weight_grads(lefts, right, parts, only=None, done=()):
    _, outer, pieces, inner, size = lefts[0].shape
    batch = right.shape[0]
    tokens = right.shape[1]
    inner = tokens // outer
    columns = right.shape[2] // parts
    block = min(512, columns)
    blocks = columns // block
    chunk = min(512, size)
    total = size * len(lefts)
    single = parts == 1
    chosen = 1 if only is not None else batch

    def entry(b):
        return b if only is None else only

    def left_entry(left, b):
        return entry(b) if left.shape[0] == batch else 0


    def kernel(*refs):
        left_refs = refs[: len(lefts)]
        right_refs = refs[len(lefts) : len(lefts) + parts]
        out_refs = refs[len(lefts) + parts + len(done) : -3]
        bias_out, turned, ones = refs[-3:]

        @pl.when(pl.program_id(2) == 0)
        def _():
            for i, left in enumerate(left_refs):
                for offset in range(0, size, chunk):
                    at = i * size + offset
                    turned[at : at + chunk, :] = (
                        left[0, :, 0, :, offset : offset + chunk].reshape(tokens, chunk).T
                    )
            ones[...] = jnp.ones_like(ones)

        for i, out in enumerate(out_refs):

            @pl.loop(0, size // chunk)
            def _(step):
                at = pl.multiple_of(i * size + step * chunk, chunk)
                own = pl.multiple_of(step * chunk, chunk)
                left = turned[pl.ds(at, chunk), :]
                for part in range(parts):
                    value = jnp.dot(left, right_refs[part][0], preferred_element_type=F32)
                    if single:
                        out[0, pl.ds(own, chunk), :] = value
                    else:
                        out[0, pl.ds(own, chunk), part, :] = value

        for part in range(parts):
            bias_out[0, part : part + 1, :] = jnp.dot(
                ones[...], right_refs[part][0], preferred_element_type=F32
            )[:1]

    outputs = 4 * chosen * pieces * total * parts * columns
    return pl.pallas_call(
        kernel,
        out_shape=(
            *[
                jax.ShapeDtypeStruct(
                    (batch, pieces * size, *((parts,) * (not single)), columns), F32
                )
                for _ in lefts
            ],
            jax.ShapeDtypeStruct((batch, parts, columns), F32),
        ),
        grid=(chosen, pieces, blocks),
        in_specs=[
            *[
                pl.BlockSpec(
                    (1, outer, 1, inner, size),
                    functools.partial(
                        lambda left, b, p, n: (left_entry(left, b), 0, p, 0, 0), left
                    ),
                )
                for left in lefts
            ],
            *[
                pl.BlockSpec(
                    (1, tokens, block),
                    functools.partial(lambda g, b, p, n: (entry(b), 0, g * blocks + n), g),
                )
                for g in range(parts)
            ],
            *[ANY_SPEC] * len(done),
        ],
        input_output_aliases={len(lefts) + parts + i: i for i in range(len(done))},
        out_specs=(
            *[
                pl.BlockSpec((1, size, block), lambda b, p, n: (entry(b), p, n))
                if single
                else pl.BlockSpec((1, size, parts, block), lambda b, p, n: (entry(b), p, 0, n))
                for _ in lefts
            ],
            pl.BlockSpec((1, parts, block), lambda b, p, n: (entry(b), 0, n)),
        ),
        scratch_shapes=[
            pltpu.VMEM((total, tokens), BF16),
            pltpu.VMEM((16, tokens), BF16),
        ],
        compiler_params=pltpu.CompilerParams(vmem_limit_bytes=VMEM_LIMIT),
        cost_estimate=pl.CostEstimate(
            flops=2 * chosen * pieces * total * tokens * parts * columns,
            bytes_accessed=outputs + 2 * right.size + 2 * batch * pieces * total * tokens,
            transcendentals=0,
        ),
        name="weight_grads",
    )(*lefts, *[right] * parts, *done)


def merge_kernel(d, first_ref, second_ref, gates_in, gates_all, staged, sems):
    far = 3 - lax.axis_index("dp")
    late = first_ref.shape[0]
    half_steps = gates_all.shape[2] // 2
    loads, stores = [], []
    for way, source in enumerate((first_ref, second_ref)):
        rows = pl.ds((way + 1) * half_steps - late, late)
        buffer = staged.at[way]
        loads.append(pltpu.make_async_copy(source, buffer, sems.at[way]))
        stores.append(pltpu.make_async_copy(buffer, gates_all.at[d, far, rows], sems.at[way]))
    for load in loads:
        load.start()
    for load, store in zip(loads, stores):
        load.wait()
        store.start()
    for store in stores:
        store.wait()


def send_late(late):
    beside = [(i, i + 1 - 2 * (i % 2)) for i in range(4)]
    across = [(i, (i + 2) % 4) for i in range(4)]
    return lax.ppermute(late[0], "dp", across), lax.ppermute(late[1], "dp", beside)


def merge_late(d, gates_all, moved):
    return pl.pallas_call(
        functools.partial(merge_kernel, d),
        out_shape=jax.ShapeDtypeStruct(gates_all.shape, BF16),
        in_specs=[ANY_SPEC] * 3,
        out_specs=ANY_SPEC,
        input_output_aliases={2: 0},
        scratch_shapes=[pltpu.VMEM((2, *moved[0].shape), BF16), pltpu.SemaphoreType.DMA((2,))],
        compiler_params=pltpu.CompilerParams(vmem_limit_bytes=VMEM_LIMIT),
        name="merge_late",
    )(*moved, gates_all)


def on_device(
    char_ids,
    row_lengths,
    top_grad,
    char_table,
    conv_weight,
    conv_bias,
    highway_weight,
    highway_bias,
    proj_weight,
    proj_bias,
    lstm_input,
    lstm_state,
    lstm_bias,
    lstm_proj,
):
    section = lax.axis_index("section")
    rows, steps, per_token = char_ids.shape
    proj_width = proj_weight.shape[1]
    half = rows // 2
    tokens = half * steps
    local = conv_weight.shape[2]
    emb = char_table.shape[1]
    padded = -(-(per_token + TAPS - 1) // 8) * 8
    vocabulary = -(-char_table.shape[0] // 8) * 8
    chars = lax.dynamic_slice_in_dim(char_ids, section * half, half, 0)
    chars = jnp.transpose(chars, (1, 0, 2)).reshape(tokens, per_token)
    ids = jnp.pad(chars, ((0, 0), (0, padded - per_token)), constant_values=-1)
    ids = ids.reshape(tokens // CHUNK, 1, CHUNK * padded)
    table = jnp.pad(
        jnp.tile(char_table, (1, TAPS)),
        ((0, vocabulary - char_table.shape[0]), (0, 128 - TAPS * emb)),
    )
    widths = filter_widths(lax.axis_index("mp") * local, local, local * lax.axis_size("mp"))
    tap_keep = jnp.arange(TAPS, dtype=jnp.int32)[:, None] < widths[None, :]
    row = jnp.arange(128, dtype=jnp.int32)[:, None]
    taps_padded = jnp.pad(
        conv_weight.reshape(TAPS * emb, local), ((0, 128 - TAPS * emb), (0, 0))
    )
    masked = jnp.where(
        row < emb * widths[None, :],
        taps_padded,
        jnp.where(
            row == TAPS * emb,
            conv_bias[None, :],
            jnp.where(row == TAPS * emb + widths[None, :], -1e30, 0.0).astype(BF16),
        ),
    )
    log_positions = jnp.log((per_token - widths + 1).astype(F32))[None, :]
    w_high = jnp.transpose(highway_weight, (0, 2, 1, 3))
    (
        base_pair,
        taps,
        peak,
        pooled,
        current,
        transform,
        gate,
        features_all,
        last_own,
        w_input,
        w_state,
    ) = cnn_forward(
        ids,
        (table, masked, log_positions, w_high, highway_bias, proj_weight, proj_bias[None]),
        lstm_input[0],
        lstm_state[0],
    )
    depth_count = highway_weight.shape[0]

    def all_tokens(values):
        return lax.all_gather(values, ("section", "dp"), axis=values.ndim - 2, tiled=True)

    last_features = all_tokens(last_own)
    top_seq = jnp.transpose(top_grad, (2, 1, 0, 3))
    live = (jnp.arange(steps, dtype=jnp.int32)[:, None] < row_lengths[None, :]).astype(F32)
    live_seq = jnp.broadcast_to(live[..., None], (steps, rows, 128))
    layer_weights = (
        w_input,
        w_state,
        lstm_bias[0],
        lstm_proj[0],
    )
    (
        x_all,
        all_states,
        hidden_all,
        gates_all,
        projected_all,
        base_shards,
        high_features,
    ) = recurrence(base_pair, live_seq, top_seq, layer_weights, features_all)
    (
        all_gates,
        all_projected,
        all_inputs,
        all_hidden,
        base_full,
        all_mixed,
        *late,
        small,
    ) = (
        cnn_backward(
            base_shards,
            (taps, peak, pooled, current, transform, gate),
            (proj_weight, w_high, masked, ids),
            (gates_all, projected_all, x_all, hidden_all, all_states),
        )
    )
    relayed = lax.axis_size("dp") == 4
    if relayed:
        moved_first = send_late(late[:2])
        moved_second = send_late(late[2:])
    small = lax.all_gather(small, ("section", "dp"), axis=0)
    small = jnp.sum(small.astype(F32), axis=0)
    conv_weight_grad = jnp.where(
        tap_keep[:, None, :], small[: TAPS * emb].reshape(conv_weight.shape), 0.0
    )
    table_grad = small[128:].reshape(-1, emb, local)
    table_grad = jnp.transpose(table_grad, (0, 2, 1)).reshape(-1, emb)[: char_table.shape[0]]
    all_base = base_full.reshape(-1, proj_width)

    def flat(values):
        return values.reshape(2, -1, values.shape[4])

    def one_piece(values):
        batch, groups, _, _, width = values.shape
        return values.reshape(batch, groups, 1, -1, width)

    proj_weight_grad = lax.all_gather(
        dot(last_features, all_base, 0, 0).astype(BF16), "mp", axis=0, tiled=True
    ).astype(F32)
    proj_grad = weight_grads([one_piece(all_hidden)], flat(all_projected), 1)[0]
    batch, _, groups, count, _, _ = high_features.shape
    high_grad, high_bias_grad = weight_grads(
        [high_features.reshape(batch, 2 * groups, count, tokens, local)],
        all_mixed.reshape(batch, -1, 2 * local),
        2,
    )
    states = one_piece(all_states)
    turned_inputs = jnp.where(section == 0, jnp.flip(all_inputs[0], axis=1), all_inputs[1])[None]
    if relayed:
        moved_first, high_grad, proj_grad, conv_weight_grad, table_grad, turned_inputs = (
            lax.optimization_barrier(
                (moved_first, high_grad, proj_grad, conv_weight_grad, table_grad, turned_inputs)
            )
        )
        all_gates = merge_late(0, all_gates, moved_first)
        done = weight_grads([one_piece(all_inputs), states], flat(all_gates), 4, only=0)
        done, moved_second, all_gates = lax.optimization_barrier((done, moved_second, all_gates))
        all_gates = merge_late(1, all_gates, moved_second)
        input_grad, state_grad, bias_grad = weight_grads(
            [one_piece(turned_inputs), states], flat(all_gates), 4, only=1, done=done
        )
    else:
        both = jnp.concatenate([all_inputs[:1], turned_inputs])
        input_grad, state_grad, bias_grad = weight_grads(
            [one_piece(both), states], flat(all_gates), 4
        )
    return (
        table_grad,
        conv_weight_grad,
        small[TAPS * emb],
        high_grad,
        high_bias_grad,
        proj_weight_grad,
        jnp.sum(all_base.astype(F32), axis=0),
        input_grad.reshape(lstm_input.shape),
        state_grad.reshape(lstm_state.shape),
        bias_grad.reshape(lstm_bias.shape),
        proj_grad.reshape(lstm_proj.shape),
    )


def solution(mesh):
    return jax.shard_map(
        on_device,
        mesh=mesh,
        in_specs=(
            P("dp", None, None),
            P("dp"),
            P("dp", None, None, None),
            P(),
            P(None, None, "mp"),
            P("mp"),
            P(None, None, None, "mp"),
            P(None, None, "mp"),
            P(),
            P(),
            P("section", None, None, None, "mp"),
            P("section", None, None, None, "mp"),
            P("section", None, None, "mp"),
            P("section", None, "mp", None),
        ),
        out_specs=(
            P(),
            P(None, None, "mp"),
            P("mp"),
            P(None, None, None, "mp"),
            P(None, None, "mp"),
            P(),
            P(),
            P("section", None, None, None, "mp"),
            P("section", None, None, None, "mp"),
            P("section", None, None, "mp"),
            P("section", None, "mp", None),
        ),
        check_vma=False,
    )
```

```python
import functools

import jax
import jax.numpy as jnp
import numpy as np
from jax import lax
from jax.experimental import pallas as pl
from jax.experimental.pallas import tpu as pltpu
from jax.sharding import PartitionSpec as P

F32 = jnp.float32
BF16 = jnp.bfloat16
PERIODS = 32
TAPS = 7
VMEM_LIMIT = 62 * 1024 * 1024
SLOTS = 4
DEFER = 3
CHUNK = 16
TURN = 128
PER_TOKEN = 50
CHARS = 262


def dot(left, right, left_dim, right_dim):
    return lax.dot_general(
        left, right, (((left_dim,), (right_dim,)), ((), ())), preferred_element_type=F32
    )


def soft_clip(values):
    return 3.0 * jnp.tanh(values / 3.0)


def filter_widths(offset, amount, total):
    period = total // PERIODS
    in_period = (offset + jnp.arange(amount, dtype=jnp.int32)) % period
    widths = jnp.ones((amount,), jnp.int32)
    for exponent in range(6):
        widths = widths + (in_period * 64 >= period * 2**exponent).astype(jnp.int32)
    return widths


MESH = pl.DeviceIdType.MESH
VMEM_SPEC = pl.BlockSpec(memory_space=pltpu.VMEM)
ANY_SPEC = pl.BlockSpec(memory_space=pl.ANY)


def column_peers():
    count = lax.axis_size("mp")
    me = lax.axis_index("mp")
    return [lax.rem(me + j, count) for j in range(1, count)]


def greet(devices):
    barrier = pltpu.get_barrier_semaphore()
    for device in devices:
        pl.semaphore_signal(barrier, inc=1, device_id=device, device_id_type=MESH)
    pl.semaphore_wait(barrier, len(devices))


def remote(source, target, send, recv, device):
    return pltpu.make_async_remote_copy(
        src_ref=source,
        dst_ref=target,
        send_sem=send,
        recv_sem=recv,
        device_id=device,
        device_id_type=MESH,
    )


def one_hot_columns(ids, vocabulary):
    symbols = lax.broadcasted_iota(jnp.int32, (vocabulary, ids.shape[1]), 0)
    return (symbols == ids).astype(F32).astype(BF16)


def cnn_forward_kernel(
    ids_ref,
    table_ref,
    flags_ref,
    masked_ref,
    log_positions,
    b_high,
    b_proj,
    high_ref,
    proj_ref,
    input_ref,
    state_ref,
    base_out,
    taps_out,
    peak_out,
    pooled_out,
    current_out,
    transform_out,
    gate_out,
    features_all,
    last_out,
    input_out,
    state_out,
    features,
    w_high,
    w_proj,
    raw,
    turned,
    send_sem,
    recv_sem,
    base_send,
    base_recv,
    row_send,
    row_recv,
    own_sem,
    raw_sem,
    turned_sem,
    load_sem,
    relay_send,
    relay_recv,
):
    count = lax.axis_size("mp")
    me = lax.axis_index("mp")
    section = lax.axis_index("section")
    peers = column_peers()
    depth_count, tokens, local = current_out.shape
    chunk_rows = ids_ref.shape[2]
    padded = chunk_rows // CHUNK
    half = tokens // 2
    emb = 16
    block = min(256, local)
    loads = [
        pltpu.make_async_copy(high_ref, w_high, load_sem.at[0]),
        pltpu.make_async_copy(proj_ref, w_proj, load_sem.at[1]),
    ]
    for load in loads:
        load.start()
    groups = lax.axis_size("dp")
    group = lax.axis_index("dp")
    others = [lax.rem(group + j, groups) for j in range(1, groups)]
    relayed = groups == 4
    beside = group + 1 - 2 * lax.rem(group, 2)
    across = lax.rem(group + 2, 4)
    far = 3 - group
    near = [beside, across] if relayed else others
    origin = near if relayed else others[::-1]
    greet(
        [{"mp": peer} for peer in peers]
        + [{"section": 1 - section}]
        + [{"dp": other} for other in others]
    )

    def relay_rows(depth, way, slot):
        pieces = pl.ds(way * (count // 2), count // 2)
        return remote(
            features_all.at[depth, section, slot, pieces],
            features_all.at[depth, section, slot, pieces],
            relay_send.at[depth, way],
            relay_recv.at[depth, way],
            {"dp": across if way == 0 else beside},
        )

    def pass_rows(depth):
        for j in range(len(near)):
            give_rows(depth, j, origin[j]).wait_recv()
        if relayed:
            for way in range(2):
                relay_rows(depth, way, beside if way == 0 else across).start()

    blocks = input_out.shape[2] // TURN
    units = 4 * blocks

    def fetch(unit, start):
        slot = lax.rem(unit, 2)
        d = lax.rem(unit, 2 * blocks) // blocks
        rows = pl.ds(pl.multiple_of(lax.rem(unit, blocks) * TURN, TURN), TURN)
        for which, source in enumerate((input_ref, state_ref)):

            @pl.when(unit // (2 * blocks) == which)
            def _():
                copy = pltpu.make_async_copy(source.at[d, rows], raw.at[slot], raw_sem.at[slot])
                copy.start() if start else copy.wait()

    def deliver(unit, start):
        slot = lax.rem(unit, 2)
        d = lax.rem(unit, 2 * blocks) // blocks
        rows = pl.ds(pl.multiple_of(lax.rem(unit, blocks) * TURN, TURN), TURN)
        for which, target in enumerate((input_out, state_out)):

            @pl.when(unit // (2 * blocks) == which)
            def _():
                copy = pltpu.make_async_copy(
                    turned.at[slot], target.at[d, :, rows], turned_sem.at[slot]
                )
                copy.start() if start else copy.wait()

    def turn_units(first, last):
        @pl.loop(first, last)
        def _(unit):
            slot = lax.rem(unit, 2)
            fetch(unit, False)

            @pl.when(unit + 1 < units)
            def _():
                fetch(unit + 1, True)

            @pl.when(unit >= 2)
            def _():
                deliver(unit - 2, False)

            for g in range(4):
                turned[slot, g] = raw[slot, :, g, :]
            deliver(unit, True)

    fetch(0, True)

    def own_rows(depth):
        return pltpu.make_async_copy(
            features.at[depth], features_all.at[depth, section, group], own_sem.at[depth]
        )

    def give_rows(depth, j, slot):
        return remote(
            features.at[depth],
            features_all.at[depth, section, slot],
            row_send.at[depth, j],
            row_recv.at[depth, j],
            {"dp": near[j]},
        )

    def send(depth, part, rows, start):
        for j, peer in enumerate(peers):
            copy = remote(
                features.at[depth, me, rows],
                features.at[depth, me, rows],
                send_sem.at[depth, part, j],
                recv_sem.at[depth, part, me],
                {"mp": peer},
            )
            if start:
                copy.start()
            else:
                copy.wait_send()

    def receive(depth, part):
        rows = pl.ds(part * half, half)
        for j, peer in enumerate(peers):
            remote(
                features.at[depth, peer, rows],
                features.at[depth, peer, rows],
                send_sem.at[depth, part, j],
                recv_sem.at[depth, part, peer],
                {"mp": peer},
            ).wait_recv()

    lane_group = lax.broadcasted_iota(jnp.int32, (chunk_rows, 128), 1) // emb

    def pool_chunk(c):
        hot = one_hot_columns(ids_ref[c], table_ref.shape[0])
        embedded = lax.dot_general(
            hot, table_ref[...], (((0,), (0,)), ((), ())), preferred_element_type=F32
        )
        taps = embedded + flags_ref[...]
        for offset in range(1, TAPS):
            rolled = pltpu.roll(embedded, chunk_rows - offset, 0)
            taps = jnp.where(lane_group == offset, rolled, taps)
        taps = taps.astype(BF16)
        taps_out[c] = taps
        rows = pl.ds(pl.multiple_of(c * CHUNK, CHUNK), CHUNK)
        for start in range(0, local, block):
            cols = slice(start, start + block)
            scores = jnp.dot(taps, masked_ref[:, cols], preferred_element_type=F32)
            scores = scores.reshape(CHUNK, padded, block)
            top = jnp.max(scores, axis=1, keepdims=True)
            total = jnp.sum(jnp.exp(scores - top), axis=1, keepdims=True)
            peak = top + jnp.log(total)
            peak_out[rows, :, cols] = peak
            pooled = jnp.sum(peak, axis=1) - log_positions[:, cols]
            pooled_out[rows, cols] = pooled
            current = jnp.maximum(pooled, 0.0) + jnp.log1p(jnp.exp(-jnp.abs(pooled)))
            current_out[0, rows, cols] = current
            features[0, me, rows, cols] = current.astype(BF16)
        return rows

    for part in range(2):

        @pl.loop(0, half // CHUNK)
        def _(i):
            rows = pool_chunk(part * (half // CHUNK) + i)
            send(0, part, rows, True)

    for load in loads:
        load.wait()
    stops = [2, 2, 6, 9, 13, 16]
    turned_to = [0]

    def turn_some():
        stop = units * stops[min(turn_count[0], len(stops) - 1)] // 16
        turn_count[0] += 1
        if stop > turned_to[0]:
            turn_units(turned_to[0], stop)
            turned_to[0] = stop

    turn_count = [0]
    for depth in range(depth_count):
        for part in range(2):
            rows = pl.ds(part * half, half)
            turn_some()
            receive(depth, part)
            if part == 1:
                own_rows(depth).start()
                if depth + 1 < depth_count:
                    for j in range(len(near)):
                        give_rows(depth, j, group).start()
            mixed = []
            for g in range(2):
                total = jnp.broadcast_to(b_high[depth, g : g + 1, :].astype(F32), (half, local))
                for p in range(count):
                    total = total + jnp.dot(
                        features[depth, p, rows, :],
                        w_high[depth, g, p * local : (p + 1) * local, :],
                        preferred_element_type=F32,
                    )
                mixed.append(total)
            transform = mixed[0]
            gate = jax.nn.sigmoid(mixed[1])
            transform_out[depth, rows, :] = transform
            gate_out[depth, rows, :] = gate
            current = gate * current_out[depth, rows, :] + (1.0 - gate) * (
                transform * jax.nn.sigmoid(transform)
            )
            if depth + 1 < depth_count:
                current_out[depth + 1, rows, :] = current
            else:
                last_out[rows, :] = current.astype(BF16)
            features[depth + 1, me, rows, :] = current.astype(BF16)
            send(depth + 1, part, rows, True)
        if depth >= 1:
            pass_rows(depth - 1)

    def give():
        return remote(
            base_out.at[section],
            base_out.at[section],
            base_send,
            base_recv,
            {"section": 1 - section},
        )

    for part in range(2):
        rows = pl.ds(part * half, half)
        turn_some()
        receive(depth_count, part)
        total = jnp.broadcast_to(b_proj[...].astype(F32), (half, w_proj.shape[1]))
        for p in range(count):
            total = total + jnp.dot(
                features[depth_count, p, rows, :],
                w_proj[p * local : (p + 1) * local, :],
                preferred_element_type=F32,
            )
        base_out[section, rows, :] = total
    give().start()
    turn_units(turned_to[0], units)
    for depth in range(depth_count + 1):
        for part in range(2):
            send(depth, part, pl.ds(part * half, half), False)
    give().wait_send()
    remote(
        base_out.at[1 - section],
        base_out.at[1 - section],
        base_send,
        base_recv,
        {"section": 1 - section},
    ).wait_recv()
    for depth in range(depth_count):
        own_rows(depth).wait()
        if depth + 1 < depth_count:
            for j in range(len(near)):
                give_rows(depth, j, group).wait_send()
            if relayed:
                for way in range(2):
                    relay_rows(depth, way, beside if way == 0 else across).wait_send()
                    relay_rows(depth, way, far).wait_recv()
    for unit in range(units - 2, units):
        deliver(unit, False)


def cnn_forward(ids, weights, lstm_input, lstm_state):
    table, masked, log_positions, w_high, b_high, w_proj, b_proj = weights
    chunks, _, chunk_rows = ids.shape
    tokens = chunks * CHUNK
    depth_count, _, total, local = w_high.shape
    count = lax.axis_size("mp")
    groups = lax.axis_size("dp")
    directions, in_width, gate_blocks, cell_columns = lstm_input.shape
    padded = chunk_rows // CHUNK
    position = np.tile(np.arange(padded), CHUNK)[:, None]
    lane = np.arange(128)[None, :]
    excluded = lane - 16 * TAPS
    flags = (lane == 16 * TAPS) | (
        (excluded >= 1) & (excluded <= TAPS) & (position > PER_TOKEN - excluded)
    )
    dma = pltpu.SemaphoreType.DMA
    return pl.pallas_call(
        cnn_forward_kernel,
        out_shape=(
            jax.ShapeDtypeStruct((2, tokens, w_proj.shape[1]), F32),
            jax.ShapeDtypeStruct((chunks, chunk_rows, 128), BF16),
            jax.ShapeDtypeStruct((tokens, 1, local), F32),
            jax.ShapeDtypeStruct((tokens, local), F32),
            jax.ShapeDtypeStruct((depth_count, tokens, local), F32),
            jax.ShapeDtypeStruct((depth_count, tokens, local), F32),
            jax.ShapeDtypeStruct((depth_count, tokens, local), F32),
            jax.ShapeDtypeStruct((depth_count, 2, groups, count, tokens, local), BF16),
            jax.ShapeDtypeStruct((tokens, local), BF16),
            jax.ShapeDtypeStruct((directions, gate_blocks, in_width, cell_columns), BF16),
            jax.ShapeDtypeStruct((directions, gate_blocks, in_width, cell_columns), BF16),
        ),
        in_specs=[VMEM_SPEC] * 7 + [ANY_SPEC] * 4,
        out_specs=(*[VMEM_SPEC] * 7, ANY_SPEC, VMEM_SPEC, *[ANY_SPEC] * 2),
        scratch_shapes=[
            pltpu.VMEM((depth_count + 1, count, tokens, local), BF16),
            pltpu.VMEM(w_high.shape, BF16),
            pltpu.VMEM(w_proj.shape, BF16),
            pltpu.VMEM((2, TURN, gate_blocks, cell_columns), BF16),
            pltpu.VMEM((2, gate_blocks, TURN, cell_columns), BF16),
            dma((depth_count + 1, 2, count - 1)),
            dma((depth_count + 1, 2, count)),
            dma,
            dma,
            dma((depth_count, groups - 1)),
            dma((depth_count, groups - 1)),
            dma((depth_count,)),
            dma((2,)),
            dma((2,)),
            dma((2,)),
            dma((depth_count, 2)),
            dma((depth_count, 2)),
        ],
        compiler_params=pltpu.CompilerParams(
            collective_id=1, has_side_effects=True, vmem_limit_bytes=VMEM_LIMIT
        ),
        name="cnn_forward",
    )(
        ids,
        table,
        jnp.asarray(flags.astype(np.float32)),
        masked,
        log_positions,
        b_high,
        b_proj,
        w_high,
        w_proj,
        lstm_input,
        lstm_state,
    )


def cnn_backward_kernel(
    base_ref,
    own_ref,
    current_ref,
    transform_ref,
    gate_ref,
    peak_ref,
    pooled_ref,
    masked_ref,
    masked_t,
    ids_ref,
    high_ref,
    taps_hbm,
    gates_in,
    projected_in,
    x_in,
    hidden_in,
    state_all,
    gates_all,
    projected_all,
    x_all,
    hidden_all,
    base_full,
    mixed_all,
    late_a,
    late_b,
    late_c,
    late_d,
    small_out,
    w_high,
    taps_ref,
    load_sem,
    conv_out,
    mixed_out,
    late_buf,
    base_all,
    base_rows,
    table_sum,
    table_all,
    grad_current,
    outgoing,
    incoming,
    base_send,
    base_recv,
    sum_send,
    sum_recv,
    own_sem,
    relay_send,
    relay_recv,
    lift_send,
    lift_recv,
    row_send,
    row_recv,
    full_sem,
    share_send,
    share_recv,
    table_send,
    table_recv,
    mixed_sem,
    mixed_send,
    mixed_recv,
    mixed_share,
    mixed_shared,
    late_sem,
    defer_send,
    defer_recv,
    x_buf,
    flip_sem,
):
    count = lax.axis_size("mp")
    me = lax.axis_index("mp")
    section = lax.axis_index("section")
    groups = lax.axis_size("dp")
    group = lax.axis_index("dp")
    peers = column_peers()
    depth_count, tokens, local = current_ref.shape
    steps = x_all.shape[2]
    chunks, chunk_rows, _ = taps_ref.shape
    loads = [
        pltpu.make_async_copy(high_ref, w_high, load_sem.at[0]),
        pltpu.make_async_copy(taps_hbm, taps_ref, load_sem.at[1]),
    ]
    for load in loads:
        load.start()
    padded = chunk_rows // CHUNK
    emb = 16
    vocabulary = -(-CHARS // 8) * 8
    relayed = groups == 4
    beside = group + 1 - 2 * lax.rem(group, 2)
    across = lax.rem(group + 2, 4)
    far = 3 - group
    greet(
        [{"mp": peer} for peer in peers]
        + [{"section": 1 - section, "mp": peer} for peer in [*peers, me]]
        + [{"dp": lax.rem(group + j, groups)} for j in range(1, groups)]
    )

    def lift():
        return remote(
            state_all.at[:, :, pl.ds(1, steps)],
            x_all,
            lift_send,
            lift_recv,
            {"section": 1 - section},
        )

    half_steps = steps // 2
    others = [lax.rem(group + j, groups) for j in range(1, groups)]
    near = [beside, across] if relayed else others
    origin = near if relayed else others[::-1]

    def relay(kind, way, slot):
        head = steps * 7 // 10
        if kind == 0:
            block = projected_all.at[way, slot]
        else:
            block = hidden_all.at[way, slot, pl.ds(head, steps - head)]
        return remote(
            block,
            block,
            relay_send.at[kind, way],
            relay_recv.at[kind, way],
            {"dp": across if way == 0 else beside},
        )

    def deferred(j, slot):
        return remote(
            gates_all.at[:, slot, pl.ds(0, DEFER)],
            gates_all.at[:, slot, pl.ds(0, DEFER)],
            defer_send.at[j],
            defer_recv.at[j],
            {"dp": near[j]},
        )

    for j in range(len(near)):
        deferred(j, group).start()


    late_loads, late_stores = [], []
    for i, target in enumerate((late_a, late_b, late_c, late_d)):
        d, way = i // 2, i % 2
        rows = pl.ds(way * half_steps, half_steps)
        source = gates_all.at[d, (beside, across)[way], rows]
        late_loads.append(pltpu.make_async_copy(source, late_buf.at[i], late_sem.at[i]))
        late_stores.append(pltpu.make_async_copy(late_buf.at[i], target, late_sem.at[i]))

    def spread_base(half, target_section, peer, j):
        return remote(
            base_ref.at[half],
            base_all.at[me],
            base_send.at[half, j],
            base_recv.at[me],
            {"section": target_section, "mp": peer},
        )

    everyone = [*peers, me]

    x_load = pltpu.make_async_copy(x_all.at[0], x_buf, flip_sem.at[0])

    @pl.when(section == 0)
    def _():
        x_load.start()
        for j, peer in enumerate(peers):
            spread_base(0, 0, peer, j).start()
        for j, peer in enumerate(everyone):
            spread_base(1, 1, peer, j).start()
        lift().start()
        own = pltpu.make_async_copy(base_ref.at[0], base_all.at[me], own_sem)
        own.start()
        own.wait()

    def base_arrival(source):
        return remote(
            base_ref.at[0],
            base_all.at[source],
            base_send.at[0, 0],
            base_recv.at[source],
            {"section": 1 - section},
        )

    for peer in peers:
        base_arrival(peer).wait_recv()

    @pl.when(section == 1)
    def _():
        base_arrival(me).wait_recv()

    wide = base_all.shape[2]
    for p in range(count):
        base_rows[:, p * wide : (p + 1) * wide] = base_all[p]
    keep = pltpu.make_async_copy(base_rows, base_full.at[section, group], full_sem)
    keep.start()

    def base_row(j, slot):
        return remote(
            base_rows,
            base_full.at[section, slot],
            row_send.at[j],
            row_recv.at[j],
            {"dp": others[j]},
        )

    def share_base(owner):
        return remote(
            base_full.at[owner],
            base_full.at[owner],
            share_send,
            share_recv,
            {"section": 1 - section},
        )

    for j in range(groups - 1):
        base_row(j, group).start()

    def keep_mixed(depth):
        return pltpu.make_async_copy(
            mixed_out.at[depth], mixed_all.at[depth, section, group], mixed_sem.at[depth]
        )

    def mixed_row(depth, j, slot):
        return remote(
            mixed_out.at[depth],
            mixed_all.at[depth, section, slot],
            mixed_send.at[depth, j],
            mixed_recv.at[depth, j],
            {"dp": others[j]},
        )

    def share_mixed(depth, owner):
        return remote(
            mixed_all.at[depth, owner],
            mixed_all.at[depth, owner],
            mixed_share.at[depth],
            mixed_shared.at[depth],
            {"section": 1 - section},
        )

    def collect_mixed(depth):
        keep_mixed(depth).wait()
        for j in range(groups - 1):
            mixed_row(depth, j, others[groups - 2 - j]).wait_recv()
        share_mixed(depth, section).start()

    own_rows = pl.ds(pl.multiple_of(me * local, local), local)
    total = jnp.zeros((tokens, local), F32)
    for p in range(count):
        total = total + lax.dot_general(
            base_all[p],
            own_ref[own_rows, p * wide : (p + 1) * wide],
            (((1,), (1,)), ((), ())),
            preferred_element_type=F32,
        )
    grad_current[...] = total

    def send_sum(depth, peer, j):
        return remote(
            outgoing.at[depth, j],
            incoming.at[depth, me],
            sum_send.at[depth, j],
            sum_recv.at[depth, me],
            {"mp": peer},
        )

    def back(depth, owner):
        rows = pl.ds(pl.multiple_of(owner * local, local), local)
        parts = [
            lax.dot_general(
                mixed_out[depth, :, g * local : (g + 1) * local],
                w_high[depth, g, rows, :],
                (((1,), (1,)), ((), ())),
                preferred_element_type=F32,
            )
            for g in range(2)
        ]
        return parts[0] + parts[1]

    for load in loads:
        load.wait()
    for depth in range(depth_count - 1, -1, -1):
        transform = transform_ref[depth]
        gate = gate_ref[depth]
        grad = grad_current[...]
        slope = jax.nn.sigmoid(transform)
        mixed_out[depth, :, :local] = (
            grad * (1.0 - gate) * slope * (1.0 + transform * (1.0 - slope))
        ).astype(BF16)
        mixed_out[depth, :, local:] = (
            grad * (current_ref[depth] - transform * slope) * gate * (1.0 - gate)
        ).astype(BF16)
        keep_mixed(depth).start()
        for j in range(groups - 1):
            mixed_row(depth, j, group).start()
        if relayed and depth == depth_count - 1:
            for kind in range(2):
                for way in range(2):
                    relay(kind, way, beside if way == 0 else across).start()
        for j, peer in enumerate(peers):
            outgoing[depth, j] = back(depth, peer).astype(BF16)
            send_sum(depth, peer, j).start()
        total = grad * gate + back(depth, me)
        for j, peer in enumerate(peers):
            remote(
                outgoing.at[depth, j],
                incoming.at[depth, peer],
                sum_send.at[depth, j],
                sum_recv.at[depth, peer],
                {"mp": peer},
            ).wait_recv()
            total = total + incoming[depth, peer].astype(F32)
        grad_current[...] = total

    for j in range(len(near)):
        deferred(j, group).wait_send()
        deferred(j, origin[j]).wait_recv()
    if relayed:
        for load in late_loads:
            load.start()
    for depth in range(depth_count - 1, 0, -1):
        collect_mixed(depth)
    if relayed:
        for load, store in zip(late_loads, late_stores):
            load.wait()
            store.start()
    @pl.when(section == 0)
    def _():
        x_load.wait()

        @pl.loop(0, steps)
        def _(t):
            for q in range(groups):
                pltpu.make_async_copy(
                    x_buf.at[q, t], x_all.at[1, q, steps - 1 - t], flip_sem.at[1]
                ).start()

    grad_current[...] = grad_current[...] * jax.nn.sigmoid(pooled_ref[...])
    conv_out[...] = jnp.zeros_like(conv_out)
    small_out[...] = jnp.zeros_like(small_out)
    table_sum[...] = jnp.zeros_like(table_sum)
    lane_group = lax.broadcasted_iota(jnp.int32, (chunk_rows, 128), 1) // emb

    @pl.loop(0, chunks)
    def _(c):
        rows = pl.ds(pl.multiple_of(c * CHUNK, CHUNK), CHUNK)
        taps = taps_ref[c]
        scores = jnp.dot(taps, masked_ref[...], preferred_element_type=F32)
        scores = scores.reshape(CHUNK, padded, local)
        share = jnp.exp(scores - peak_ref[rows])
        grads = share * grad_current[rows, :][:, None, :]
        grads = grads.reshape(chunk_rows, local).astype(BF16)
        conv_out[...] += lax.dot_general(
            taps, grads, (((0,), (0,)), ((), ())), preferred_element_type=F32
        )
        back_taps = jnp.dot(grads, masked_t[...], preferred_element_type=F32)
        moved = back_taps
        for offset in range(1, TAPS):
            moved = jnp.where(lane_group == offset, pltpu.roll(back_taps, offset, 0), moved)
        hot = one_hot_columns(ids_ref[c], vocabulary)
        table_sum[:vocabulary, :] += jnp.dot(
            hot, moved.astype(BF16), preferred_element_type=F32
        )

    columns = table_sum[...].T
    folded = columns[:emb]
    for offset in range(1, TAPS):
        folded = folded + columns[offset * emb : (offset + 1) * emb]
    table_all[me] = folded

    def table_copy(j, slot):
        return remote(
            table_all.at[slot],
            table_all.at[slot],
            table_send.at[j],
            table_recv.at[slot],
            {"mp": peers[j]},
        )

    for j in range(count - 1):
        table_copy(j, me).start()

    for j in range(count - 1):
        table_copy(j, peers[j]).wait_recv()
    folded = table_all[0]
    for p in range(1, count):
        folded = folded + table_all[p]
    small_out[:128, :] = conv_out[...].astype(BF16)
    span = min(local, folded.shape[1])
    for i in range(folded.shape[1] // span):
        at = 128 + i * emb
        small_out[at : at + emb, :span] = folded[:, i * span : (i + 1) * span].astype(BF16)
    for j in range(count - 1):
        table_copy(j, me).wait_send()
    keep.wait()
    for j in range(groups - 1):
        base_row(j, others[groups - 2 - j]).wait_recv()
    share_base(section).start()
    collect_mixed(0)
    for j in range(groups - 1):
        base_row(j, group).wait_send()
        for depth in range(depth_count):
            mixed_row(depth, j, group).wait_send()
    for depth in range(depth_count):
        for j, peer in enumerate(peers):
            send_sum(depth, peer, j).wait_send()

    @pl.when(section == 0)
    def _():
        for j, peer in enumerate(peers):
            spread_base(0, 0, peer, j).wait_send()
        for j, peer in enumerate(everyone):
            spread_base(1, 1, peer, j).wait_send()
        lift().wait_send()
        pltpu.make_async_copy(x_buf, x_all.at[1], flip_sem.at[1]).wait()

    @pl.when(section == 1)
    def _():
        lift().wait_recv()

    if relayed:
        for kind in range(2):
            for way in range(2):
                relay(kind, way, beside if way == 0 else across).wait_send()
                relay(kind, way, far).wait_recv()
        for copy in late_stores:
            copy.wait()

    share_base(section).wait_send()
    share_base(1 - section).wait_recv()
    for depth in range(depth_count):
        share_mixed(depth, section).wait_send()
        share_mixed(depth, 1 - section).wait_recv()


def cnn_backward(base_shards, saved, weights, rows_all):
    w_proj, w_high, masked, ids = weights
    taps, peak, pooled, current, transform, gate = saved
    gates_all, projected_all, x_all, hidden_all, state_all = rows_all
    depth_count, tokens, local = current.shape
    count = lax.axis_size("mp")
    groups = lax.axis_size("dp")
    vocabulary = -(-CHARS // 128) * 128
    half_steps = gates_all.shape[2] // 2
    late = (half_steps, *gates_all.shape[3:])
    dma = pltpu.SemaphoreType.DMA
    return pl.pallas_call(
        cnn_backward_kernel,
        out_shape=(
            jax.ShapeDtypeStruct(gates_all.shape, BF16),
            jax.ShapeDtypeStruct(projected_all.shape, BF16),
            jax.ShapeDtypeStruct(x_all.shape, BF16),
            jax.ShapeDtypeStruct(hidden_all.shape, BF16),
            jax.ShapeDtypeStruct((2, groups, tokens, count * base_shards.shape[2]), BF16),
            jax.ShapeDtypeStruct((depth_count, 2, groups, tokens, 2 * local), BF16),
            *[jax.ShapeDtypeStruct(late, BF16)] * 4,
            jax.ShapeDtypeStruct((128 + 16 * max(1, vocabulary // local), local), BF16),
        ),
        in_specs=[VMEM_SPEC] * 10 + [ANY_SPEC] * 7,
        out_specs=(*[ANY_SPEC] * 10, VMEM_SPEC),
        input_output_aliases={12: 0, 13: 1, 14: 2, 15: 3},
        scratch_shapes=[
            pltpu.VMEM(w_high.shape, BF16),
            pltpu.VMEM(taps.shape, BF16),
            dma((2,)),
            pltpu.VMEM((128, local), F32),
            pltpu.VMEM((depth_count, tokens, 2 * local), BF16),
            pltpu.VMEM((4, *late), BF16),
            pltpu.VMEM((count, tokens, base_shards.shape[2]), BF16),
            pltpu.VMEM((tokens, count * base_shards.shape[2]), BF16),
            pltpu.VMEM((vocabulary, 128), F32),
            pltpu.VMEM((count, 16, vocabulary), F32),
            pltpu.VMEM((tokens, local), F32),
            pltpu.VMEM((depth_count, count - 1, tokens, local), BF16),
            pltpu.VMEM((depth_count, count, tokens, local), BF16),
            dma((2, count)),
            dma((count,)),
            dma((depth_count, count - 1)),
            dma((depth_count, count)),
            dma,
            dma((2, 2)),
            dma((2, 2)),
            dma,
            dma,
            dma((groups - 1,)),
            dma((groups - 1,)),
            dma,
            dma,
            dma,
            dma((count - 1,)),
            dma((count,)),
            dma((depth_count,)),
            dma((depth_count, groups - 1)),
            dma((depth_count, groups - 1)),
            dma((depth_count,)),
            dma((depth_count,)),
            dma((4,)),
            dma((groups - 1,)),
            dma((groups - 1,)),
            pltpu.VMEM(x_all.shape[1:], BF16),
            dma((2,)),
        ],
        compiler_params=pltpu.CompilerParams(
            collective_id=2, has_side_effects=True, vmem_limit_bytes=VMEM_LIMIT
        ),
        name="cnn_backward",
    )(
        base_shards,
        w_proj,
        current,
        transform,
        gate,
        peak,
        pooled,
        masked,
        jnp.pad(masked[: 16 * TAPS], ((0, 128 - 16 * TAPS), (0, 0))).T,
        ids,
        w_high,
        taps,
        gates_all,
        projected_all,
        x_all,
        hidden_all,
        state_all,
    )


def recurrence_kernel(
    base_ref,
    live_ref,
    top_ref,
    bias_ref,
    proj_ref,
    in_ref,
    state_ref,
    features_in,
    x_all,
    state_all,
    hidden_all,
    gates_all,
    projected_all,
    base_out,
    features_all,
    x_out,
    state_out,
    hidden_out,
    projected_out,
    acts,
    cells,
    clips,
    pre,
    grad_cell,
    parts,
    back_parts,
    above,
    gate_buf,
    base_sem,
    send_sem,
    recv_sem,
    back_send,
    back_recv,
    x_send,
    x_recv,
    above_send,
    above_recv,
    gate_sem,
    gate_send,
    own_sem,
    row_send,
    row_recv,
    w_in,
    w_state,
    load_sem,
    w_in_t,
    w_state_t,
    proj_t,
    input_parts,
    input_sums,
    input_send,
    input_recv,
    base_sum,
    share_send,
    share_recv,
    relay_send,
    relay_recv,
    feature_send,
    feature_recv,
    hidden_send,
    hidden_recv,
):
    count = lax.axis_size("mp")
    me = lax.axis_index("mp")
    section = lax.axis_index("section")
    steps = x_out.shape[1]
    cell_count = proj_ref.shape[1]
    chunk = min(256, cell_count)
    peers = [lax.rem(me + j, count) for j in range(1, count)]
    groups = lax.axis_size("dp")
    group = lax.axis_index("dp")
    others = [lax.rem(group + j, groups) for j in range(1, groups)]
    relayed = groups == 4
    beside = group + 1 - 2 * lax.rem(group, 2)
    across = lax.rem(group + 2, 4)
    near = [beside, across] if relayed else others
    loads = [
        [pltpu.make_async_copy(source.at[d], target.at[d], load_sem.at[i, d]) for d in range(2)]
        for i, (source, target) in enumerate(((in_ref, w_in), (state_ref, w_state)))
    ]
    for d in range(2):
        loads[0][d].start()
    for d in range(2):
        loads[1][d].start()

    barrier = pltpu.get_barrier_semaphore()
    for peer in peers:
        pl.semaphore_signal(barrier, inc=1, device_id={"mp": peer}, device_id_type=MESH)
    pl.semaphore_signal(barrier, inc=1, device_id={"section": 1 - section}, device_id_type=MESH)
    for other in others:
        pl.semaphore_signal(barrier, inc=1, device_id={"dp": other}, device_id_type=MESH)
    pl.semaphore_wait(barrier, count + groups - 1)

    def share_features(owner):
        return remote(
            features_all.at[:, owner],
            features_all.at[:, owner],
            share_send,
            share_recv,
            {"section": 1 - section},
        )

    pieces = features_all.shape[3]

    last_depth = features_all.shape[0] - 1

    def give_features(j, slot):
        return remote(
            features_all.at[last_depth, section, slot],
            features_all.at[last_depth, section, slot],
            feature_send.at[j],
            feature_recv.at[j],
            {"dp": near[j]},
        )

    def relay_features(way, slot):
        half = pl.ds(way * (pieces // 2), pieces // 2)
        block = features_all.at[last_depth, section, slot, half]
        return remote(
            block,
            block,
            relay_send.at[way],
            relay_recv.at[way],
            {"dp": across if way == 0 else beside},
        )

    def start_relays():
        if relayed:
            for way in range(2):
                relay_features(way, beside if way == 0 else across).start()

    def finish_relays():
        if relayed:
            for way in range(2):
                relay_features(way, beside if way == 0 else across).wait_send()
                relay_features(way, 3 - group).wait_recv()

    for j in range(len(near)):
        give_features(j, group).start()

    def wide(values, width):
        return jnp.concatenate([values] * (width // values.shape[1]), axis=1)

    def copy_part(buffer, send, recv, d, parity, source, j, target):
        return pltpu.make_async_remote_copy(
            src_ref=buffer.at[d, parity, source],
            dst_ref=buffer.at[d, parity, source],
            send_sem=send.at[d, parity, j],
            recv_sem=recv.at[d, parity, source],
            device_id={"mp": target},
            device_id_type=MESH,
        )

    ordered = peers
    if count == 4:
        ordered = [3 - me, lax.rem(me + 2, 4), me + 1 - 2 * lax.rem(me, 2)]

    def exchange_start(buffer, send, recv, d, parity, value):
        buffer[d, parity, me] = value.astype(BF16)
        for j, peer in enumerate(ordered):
            copy_part(buffer, send, recv, d, parity, me, j, peer).start()

    def exchange_wait(buffer, send, recv, d, parity):
        for j, peer in enumerate(ordered):
            copy_part(buffer, send, recv, d, parity, peer, j, peer).wait_recv()
        total = buffer[d, parity, 0].astype(F32)
        for source in range(1, count):
            total = total + buffer[d, parity, source].astype(F32)
        for j, peer in enumerate(ordered):
            copy_part(buffer, send, recv, d, parity, me, j, peer).wait_send()
        return total

    def pass_up(d, k):
        return pltpu.make_async_remote_copy(
            src_ref=state_out.at[d, k + 1],
            dst_ref=x_out.at[d, k],
            send_sem=x_send.at[d],
            recv_sem=x_recv.at[d, k],
            device_id={"section": 1 - section},
            device_id_type=MESH,
        )

    def pass_down(d, k):
        return pltpu.make_async_remote_copy(
            src_ref=above.at[d, k],
            dst_ref=above.at[d, k],
            send_sem=above_send.at[d],
            recv_sem=above_recv.at[d, k],
            device_id={"section": 1 - section},
            device_id_type=MESH,
        )

    def gates_copy(d, k, slot):
        return pltpu.make_async_copy(
            gate_buf.at[d, slot], gates_all.at[d, group, k], gate_sem.at[d, slot]
        )

    def gates_row(d, k, slot, j, other):
        return pltpu.make_async_remote_copy(
            src_ref=gate_buf.at[d, slot],
            dst_ref=gates_all.at[d, group, k],
            send_sem=gate_send.at[d, slot, j],
            recv_sem=row_recv.at[0, j],
            device_id={"dp": other},
            device_id_type=MESH,
        )

    def row(kind, source, target, j, other):
        return pltpu.make_async_remote_copy(
            src_ref=source,
            dst_ref=target,
            send_sem=row_send.at[kind, j],
            recv_sem=row_recv.at[kind, j],
            device_id={"dp": other},
            device_id_type=MESH,
        )

    def from_peer(j, targets):
        back = len(targets) - 1 - j
        return targets[j] if relayed and len(targets) == 2 else targets[back]

    head = steps * 7 // 10

    def relay_hidden(way, slot):
        block = hidden_all.at[way, slot, pl.ds(0, head)]
        return remote(
            block,
            block,
            hidden_send.at[way],
            hidden_recv.at[way],
            {"dp": across if way == 0 else beside},
        )

    def finish_hidden(kind, some):
        for j, other in enumerate(near):
            target = hidden_all.at[:, from_peer(j, near), some]
            copy = row(kind, hidden_out.at[:, some], target, j, other)
            copy.wait_send()
            copy.wait_recv()

    def time_of(d, k):
        return k if d == 0 else steps - 1 - k

    @pl.when(section == 0)
    def _():
        part_rows = base_ref.shape[1] // steps

        @pl.loop(0, steps)
        def _(t):
            at = pl.ds(pl.multiple_of(t * part_rows, part_rows), part_rows)
            x = jnp.concatenate([base_ref[0, at, :], base_ref[1, at, :]], axis=0).astype(BF16)
            for d in range(2):
                x_out[d, time_of(d, t)] = x

        for j, other in enumerate(others):
            row(1, x_out.at[0], x_all.at[0, group], j, other).start()

    for d in range(2):
        state_out[d, 0] = jnp.zeros(state_out.shape[2:], BF16)
        cells[d, 0] = jnp.zeros(cells.shape[2:], F32)
        grad_cell[d] = jnp.zeros(grad_cell.shape[1:], F32)

    def input_part(d, k):
        @pl.when(section == 1)
        def _():
            pass_up(d, k).wait_recv()

        x = x_out[d, k]
        for block in range(4):
            for start in range(0, cell_count, chunk):
                cols = slice(block * cell_count + start, block * cell_count + start + chunk)
                bias = bias_ref[d, block : block + 1, start : start + chunk].astype(F32)
                pre[d, :, cols] = bias + jnp.dot(
                    x, w_in[d, block, :, start : start + chunk], preferred_element_type=F32
                )

    def turn_weights(unit):
        per_block = cell_count // chunk
        block = unit // per_block
        cols = pl.ds(pl.multiple_of(lax.rem(unit, per_block) * chunk, chunk), chunk)
        rows_t = pl.ds(pl.multiple_of(unit * chunk, chunk), chunk)
        for d in range(2):
            w_in_t[d, rows_t, :] = w_in[d, block, :, cols].T
            w_state_t[d, rows_t, :] = w_state[d, block, :, cols].T

    def turn_proj(unit):
        cols = pl.ds(pl.multiple_of(unit * 128, 128), 128)
        for d in range(2):
            proj_t[d, :, cols] = proj_ref[d, cols, :].T

    def forward_cells(d, k):
        state = state_out[d, k]
        live = live_ref[time_of(d, k)]
        for start in range(0, cell_count, chunk):
            raw = []
            for block in range(4):
                cols = slice(block * cell_count + start, block * cell_count + start + chunk)
                raw.append(
                    pre[d, :, cols]
                    + jnp.dot(
                        state, w_state[d, block, :, start : start + chunk], preferred_element_type=F32
                    )
                )
            own = slice(start, start + chunk)
            in_gate = jax.nn.sigmoid(raw[0])
            forget = jax.nn.sigmoid(raw[1])
            memory = jnp.tanh(raw[2])
            out_gate = jax.nn.sigmoid(raw[3])
            for block, value in enumerate((in_gate, forget, memory, out_gate)):
                acts[d, k, block, :, own] = value
            cell_new = soft_clip(in_gate * memory + forget * cells[d, k, :, own])
            cells[d, k + 1, :, own] = wide(live, chunk) * cell_new
            hidden_out[d, k, :, own] = (out_gate * jnp.tanh(cell_new)).astype(BF16)
        part = jnp.dot(hidden_out[d, k], proj_ref[d], preferred_element_type=F32)
        exchange_start(parts, send_sem, recv_sem, d, lax.rem(k, 2), part)
        for j, other in enumerate(near):
            kind = 2 + 3 * (k // head)
            row(kind, hidden_out.at[d, k], hidden_all.at[d, group, k], j, other).start()

    def forward_state(d, k):
        total = exchange_wait(parts, send_sem, recv_sem, d, lax.rem(k, 2))
        clip = jnp.tanh(total / 3.0)
        clips[d, k] = clip
        live = wide(live_ref[time_of(d, k)], clip.shape[1])
        state_out[d, k + 1] = (live * 3.0 * clip).astype(BF16)

        @pl.when(section == 0)
        def _():
            @pl.when(k > 0)
            def _():
                pass_up(d, k - 1).wait_send()

            pass_up(d, k).start()

        for j, other in enumerate(others):
            row(3, state_out.at[d, k + 1], state_all.at[d, group, k + 1], j, other).start()

    units = 4 * cell_count // chunk
    for d in range(2):
        loads[0][d].wait()
        input_part(d, 0)
    for d in range(2):
        loads[1][d].wait()
        forward_cells(d, 0)
    for d in range(2):
        input_part(d, 1)

    @pl.loop(1, steps)
    def _(k):
        for d in range(2):
            forward_state(d, k - 1)
            forward_cells(d, k)

        @pl.when(k + 1 < steps)
        def _():
            for d in range(2):
                input_part(d, k + 1)

        @pl.when(k <= units)
        def _():
            turn_weights(k - 1)

        @pl.when(k == steps - 3)
        def _():
            finish_hidden(2, pl.ds(0, head))
            if relayed:
                for way in range(2):
                    relay_hidden(way, beside if way == 0 else across).start()

        @pl.when(k == steps - 5)
        def _():
            for j in range(len(near)):
                give_features(j, group).wait_send()
                give_features(j, from_peer(j, near)).wait_recv()
            start_relays()

        @pl.when(k <= cell_count // 128)
        def _():
            turn_proj(k - 1)

    for unit in range(steps - 1, units):
        turn_weights(unit)
    for d in range(2):
        forward_state(d, steps - 1)

    @pl.when(section == 0)
    def _():
        for d in range(2):
            pass_up(d, steps - 1).wait_send()

    def back_wait(d, parity):
        return exchange_wait(back_parts, back_send, back_recv, d, parity)

    def back_start(d, parity, value):
        exchange_start(back_parts, back_send, back_recv, d, parity, value)

    def backward_cells(d, k, total):
        slot = lax.rem(k, SLOTS)
        live = live_ref[time_of(d, k)]
        clip = clips[d, k]
        grad_out = wide(live, clip.shape[1]) * (total + top_ref[d, time_of(d, k)].astype(F32))
        grad_projected = (grad_out * (1.0 - clip * clip)).astype(BF16)
        projected_out[d, k] = grad_projected

        for j, other in enumerate(near):
            row(
                4, projected_out.at[d, k], projected_all.at[d, group, k], j, other
            ).start()

        @pl.when(k < steps - SLOTS)
        def _():
            gates_copy(d, k + SLOTS, slot).wait()
            for j, other in enumerate(near):
                gates_row(d, k + SLOTS, slot, j, other).wait_send()

        for start in range(0, cell_count, chunk):
            own = slice(start, start + chunk)
            grad_hidden = jnp.dot(grad_projected, proj_t[d, :, own], preferred_element_type=F32)
            in_gate, forget, memory, out_gate = [acts[d, k, block, :, own] for block in range(4)]
            cell = cells[d, k, :, own]
            clip_raw = jnp.tanh((in_gate * memory + forget * cell) / 3.0)
            tanh_cell = jnp.tanh(3.0 * clip_raw)
            grad_new = wide(live, chunk) * grad_cell[d, :, own] + grad_hidden * out_gate * (
                1.0 - tanh_cell * tanh_cell
            )
            grad_raw = grad_new * (1.0 - clip_raw * clip_raw)
            grad_cell[d, :, own] = grad_raw * forget
            grads = (
                grad_raw * memory * in_gate * (1.0 - in_gate),
                grad_raw * cell * forget * (1.0 - forget),
                grad_raw * in_gate * (1.0 - memory * memory),
                grad_hidden * tanh_cell * out_gate * (1.0 - out_gate),
            )
            for block, value in enumerate(grads):
                cols = slice(block * cell_count + start, block * cell_count + start + chunk)
                gate_buf[d, slot, :, cols] = value.astype(BF16)
        gates_copy(d, k, slot).start()

    def gates_send(d, k):
        @pl.when(k >= DEFER)
        def _():
            for j, other in enumerate(near):
                gates_row(d, k, lax.rem(k, SLOTS), j, other).start()

    def backward_state(d, k):
        @pl.when(k > 0)
        def _():
            back = jnp.dot(gate_buf[d, lax.rem(k, SLOTS)], w_state_t[d], preferred_element_type=F32)
            pre[d, :, : back.shape[1]] = back

            @pl.when(section == 0)
            def _():
                pass_down(d, k - 1).wait_recv()
                pre[d, :, : back.shape[1]] = back + above[d, k - 1]

            back_start(d, lax.rem(k - 1, 2), pre[d, :, : back.shape[1]])

    share = base_out.shape[2]

    def input_copy(source, target, j, peer):
        return remote(source, target, input_send.at[j], input_recv.at[j], {"mp": peer})

    def backward_input(d, k):
        gates_send(d, k)
        part = jnp.dot(gate_buf[d, lax.rem(k, SLOTS)], w_in_t[d], preferred_element_type=F32)

        @pl.when(section == 1)
        def _():
            above[d, k] = part

            @pl.when(k < steps - 1)
            def _():
                pass_down(d, k + 1).wait_send()

            pass_down(d, k).start()

        @pl.when(section == 0)
        def _():
            for p in range(count):
                input_parts[d, k, p] = part[:, p * share : (p + 1) * share].astype(BF16)
            for j, peer in enumerate(peers):
                input_copy(input_parts.at[d, k, peer], input_sums.at[d, k, me], j, peer).start()

    last = steps - 1

    @pl.when(section == 0)
    def _():
        for d in range(2):
            pass_down(d, last).wait_recv()
            back_start(d, lax.rem(last, 2), above[d, last])

    for d in range(2):

        @pl.when(section == 0)
        def _():
            pre[d, :, : clips.shape[3]] = back_wait(d, lax.rem(last, 2))

        @pl.when(section == 1)
        def _():
            pre[d, :, : clips.shape[3]] = jnp.zeros(clips.shape[2:], F32)

        backward_cells(d, last, pre[d, :, : clips.shape[3]])
        backward_state(d, last)
    for d in range(2):
        backward_input(d, last)

    @pl.loop(1, steps)
    def _(tick):
        k = last - tick
        for d in range(2):
            backward_cells(d, k, back_wait(d, lax.rem(k, 2)))
            backward_state(d, k)
        for d in range(2):
            backward_input(d, k)

        @pl.when(tick == 5)
        def _():
            finish_relays()
            share_features(section).start()
            if relayed:
                for way in range(2):
                    relay_hidden(way, beside if way == 0 else across).wait_send()
                    relay_hidden(way, 3 - group).wait_recv()

    for d in range(2):
        for k in range(min(SLOTS, steps)):
            gates_copy(d, k, k % SLOTS).wait()
            for j, other in enumerate(near):
                if k >= DEFER:
                    gates_row(d, k, k % SLOTS, j, other).wait_send()

    @pl.when(section == 1)
    def _():
        for d in range(2):
            pass_down(d, 0).wait_send()

    own = [
        (hidden_out, hidden_all.at[:, group]),
        (state_out, state_all.at[:, group]),
        (projected_out, projected_all.at[:, group]),
    ]
    for other in others:
        own.append((state_out.at[:, 0], state_all.at[:, other, 0]))
    own = [
        pltpu.make_async_copy(source, target, own_sem.at[i])
        for i, (source, target) in enumerate(own)
    ]
    for copy in own:
        copy.start()

    rest = pl.ds(1, steps)
    for j, other in enumerate(others):
        source = from_peer(j, others)
        state_row = row(3, state_out.at[:, rest], state_all.at[:, source, rest], j, other)
        state_row.wait_send()
        state_row.wait_recv()

    finish_hidden(5, pl.ds(head, steps - head))

    for copy in own:
        copy.wait()

    @pl.when(section == 0)
    def _():
        mine = pltpu.make_async_copy(x_out.at[0], x_all.at[0, group], base_sem)
        mine.start()
        for j, other in enumerate(others):
            copy = row(1, x_out.at[0], x_all.at[0, from_peer(j, others)], j, other)
            copy.wait_send()
            copy.wait_recv()
        mine.wait()

    @pl.when(section == 0)
    def _():
        for j, peer in enumerate(peers):
            source = peers[count - 2 - j]
            copy = input_copy(input_parts.at[:, :, peer], input_sums.at[:, :, source], j, peer)
            copy.wait_send()
            copy.wait_recv()
        rows_half = base_out.shape[1] // steps

        @pl.loop(0, steps)
        def _(t):
            total = input_parts[0, t, me].astype(F32) + input_parts[1, steps - 1 - t, me].astype(F32)
            for peer in peers:
                total = total + input_sums[0, t, peer].astype(F32)
                total = total + input_sums[1, steps - 1 - t, peer].astype(F32)
            at = pl.ds(pl.multiple_of(t * rows_half, rows_half), rows_half)
            for half in range(2):
                base_sum[half, at, :] = total[half * rows_half : (half + 1) * rows_half]

        base_out[...] = base_sum[...].astype(BF16)

    share_features(section).wait_send()
    share_features(1 - section).wait_recv()

    for j, other in enumerate(near):
        source = from_peer(j, near)
        pltpu.make_async_remote_copy(
            src_ref=gates_all.at[:, source, pl.ds(DEFER, steps - DEFER)],
            dst_ref=gates_all.at[:, source, pl.ds(DEFER, steps - DEFER)],
            send_sem=row_send.at[0, j],
            recv_sem=row_recv.at[0, j],
            device_id={"dp": other},
            device_id_type=MESH,
        ).wait_recv()
        projected_row = row(4, projected_out, projected_all.at[:, source], j, other)
        projected_row.wait_send()
        projected_row.wait_recv()


def recurrence(base_seq, live_seq, top_seq, layer_weights, features_all):
    w_in, w_state, bias, proj = layer_weights
    _, steps, rows, width = top_seq.shape
    cell_count = proj.shape[1]
    count = lax.axis_size("mp")
    groups = lax.axis_size("dp")
    weights = (bias, proj, w_in, w_state)
    dma = pltpu.SemaphoreType.DMA
    return pl.pallas_call(
        recurrence_kernel,
        out_shape=(
            jax.ShapeDtypeStruct((2, groups, steps, rows, width), BF16),
            jax.ShapeDtypeStruct((2, groups, steps + 1, rows, width), BF16),
            jax.ShapeDtypeStruct((2, groups, steps, rows, cell_count), BF16),
            jax.ShapeDtypeStruct((2, groups, steps, rows, 4 * cell_count), BF16),
            jax.ShapeDtypeStruct((2, groups, steps, rows, width), BF16),
            jax.ShapeDtypeStruct((2, steps * rows // 2, width // count), BF16),
            jax.ShapeDtypeStruct(features_all.shape, BF16),
        ),
        in_specs=[VMEM_SPEC] * 5 + [ANY_SPEC] * 3,
        out_specs=(*[ANY_SPEC] * 5, VMEM_SPEC, ANY_SPEC),
        input_output_aliases={7: 6},
        scratch_shapes=[
            pltpu.VMEM((2, steps, rows, width), BF16),
            pltpu.VMEM((2, steps + 1, rows, width), BF16),
            pltpu.VMEM((2, steps, rows, cell_count), BF16),
            pltpu.VMEM((2, steps, rows, width), BF16),
            pltpu.VMEM((2, steps, 4, rows, cell_count), F32),
            pltpu.VMEM((2, steps + 1, rows, cell_count), F32),
            pltpu.VMEM((2, steps, rows, width), F32),
            pltpu.VMEM((2, rows, 4 * cell_count), F32),
            pltpu.VMEM((2, rows, cell_count), F32),
            pltpu.VMEM((2, 2, count, rows, width), BF16),
            pltpu.VMEM((2, 2, count, rows, width), BF16),
            pltpu.VMEM((2, steps, rows, width), F32),
            pltpu.VMEM((2, SLOTS, rows, 4 * cell_count), BF16),
            dma,
            dma((2, 2, count - 1)),
            dma((2, 2, count)),
            dma((2, 2, count - 1)),
            dma((2, 2, count)),
            dma((2,)),
            dma((2, steps)),
            dma((2,)),
            dma((2, steps)),
            dma((2, SLOTS)),
            dma((2, SLOTS, groups - 1)),
            dma((groups + 2,)),
            dma((6, groups - 1)),
            dma((6, groups - 1)),
            pltpu.VMEM(w_in.shape, BF16),
            pltpu.VMEM(w_state.shape, BF16),
            dma((2, 2)),
            pltpu.VMEM((2, 4 * cell_count, width), BF16),
            pltpu.VMEM((2, 4 * cell_count, width), BF16),
            pltpu.VMEM((2, width, cell_count), BF16),
            pltpu.VMEM((2, steps, count, rows, width // count), BF16),
            pltpu.VMEM((2, steps, count, rows, width // count), BF16),
            dma((count - 1,)),
            dma((count - 1,)),
            pltpu.VMEM((2, steps * rows // 2, width // count), F32),
            dma,
            dma,
            dma((2,)),
            dma((2,)),
            dma((groups - 1,)),
            dma((groups - 1,)),
            dma((2,)),
            dma((2,)),
        ],
        compiler_params=pltpu.CompilerParams(
            collective_id=0, has_side_effects=True, vmem_limit_bytes=VMEM_LIMIT
        ),
        name="recurrence",
    )(base_seq, live_seq, top_seq, *weights, features_all)


def weight_grads(lefts, right, parts, only=None, done=()):
    _, outer, pieces, inner, size = lefts[0].shape
    batch = right.shape[0]
    tokens = right.shape[1]
    inner = tokens // outer
    columns = right.shape[2] // parts
    block = min(512, columns)
    blocks = columns // block
    chunk = min(512, size)
    total = size * len(lefts)
    single = parts == 1
    chosen = 1 if only is not None else batch

    def entry(b):
        return b if only is None else only

    def left_entry(left, b):
        return entry(b) if left.shape[0] == batch else 0


    def kernel(*refs):
        left_refs = refs[: len(lefts)]
        right_refs = refs[len(lefts) : len(lefts) + parts]
        out_refs = refs[len(lefts) + parts + len(done) : -3]
        bias_out, turned, ones = refs[-3:]

        @pl.when(pl.program_id(2) == 0)
        def _():
            for i, left in enumerate(left_refs):
                for offset in range(0, size, chunk):
                    at = i * size + offset
                    turned[at : at + chunk, :] = (
                        left[0, :, 0, :, offset : offset + chunk].reshape(tokens, chunk).T
                    )
            ones[...] = jnp.ones_like(ones)

        for i, out in enumerate(out_refs):

            @pl.loop(0, size // chunk)
            def _(step):
                at = pl.multiple_of(i * size + step * chunk, chunk)
                own = pl.multiple_of(step * chunk, chunk)
                left = turned[pl.ds(at, chunk), :]
                for part in range(parts):
                    value = jnp.dot(left, right_refs[part][0], preferred_element_type=F32)
                    if single:
                        out[0, pl.ds(own, chunk), :] = value
                    else:
                        out[0, pl.ds(own, chunk), part, :] = value

        for part in range(parts):
            bias_out[0, part : part + 1, :] = jnp.dot(
                ones[...], right_refs[part][0], preferred_element_type=F32
            )[:1]

    outputs = 4 * chosen * pieces * total * parts * columns
    return pl.pallas_call(
        kernel,
        out_shape=(
            *[
                jax.ShapeDtypeStruct(
                    (batch, pieces * size, *((parts,) * (not single)), columns), F32
                )
                for _ in lefts
            ],
            jax.ShapeDtypeStruct((batch, parts, columns), F32),
        ),
        grid=(chosen, pieces, blocks),
        in_specs=[
            *[
                pl.BlockSpec(
                    (1, outer, 1, inner, size),
                    functools.partial(
                        lambda left, b, p, n: (left_entry(left, b), 0, p, 0, 0), left
                    ),
                )
                for left in lefts
            ],
            *[
                pl.BlockSpec(
                    (1, tokens, block),
                    functools.partial(lambda g, b, p, n: (entry(b), 0, g * blocks + n), g),
                )
                for g in range(parts)
            ],
            *[ANY_SPEC] * len(done),
        ],
        input_output_aliases={len(lefts) + parts + i: i for i in range(len(done))},
        out_specs=(
            *[
                pl.BlockSpec((1, size, block), lambda b, p, n: (entry(b), p, n))
                if single
                else pl.BlockSpec((1, size, parts, block), lambda b, p, n: (entry(b), p, 0, n))
                for _ in lefts
            ],
            pl.BlockSpec((1, parts, block), lambda b, p, n: (entry(b), 0, n)),
        ),
        scratch_shapes=[
            pltpu.VMEM((total, tokens), BF16),
            pltpu.VMEM((16, tokens), BF16),
        ],
        compiler_params=pltpu.CompilerParams(vmem_limit_bytes=VMEM_LIMIT),
        cost_estimate=pl.CostEstimate(
            flops=2 * chosen * pieces * total * tokens * parts * columns,
            bytes_accessed=outputs + 2 * right.size + 2 * batch * pieces * total * tokens,
            transcendentals=0,
        ),
        name="weight_grads",
    )(*lefts, *[right] * parts, *done)


def merge_kernel(d, first_ref, second_ref, gates_in, gates_all, staged, sems):
    far = 3 - lax.axis_index("dp")
    late = first_ref.shape[0]
    half_steps = gates_all.shape[2] // 2
    loads, stores = [], []
    for way, source in enumerate((first_ref, second_ref)):
        rows = pl.ds((way + 1) * half_steps - late, late)
        buffer = staged.at[way]
        loads.append(pltpu.make_async_copy(source, buffer, sems.at[way]))
        stores.append(pltpu.make_async_copy(buffer, gates_all.at[d, far, rows], sems.at[way]))
    for load in loads:
        load.start()
    for load, store in zip(loads, stores):
        load.wait()
        store.start()
    for store in stores:
        store.wait()


def send_late(late):
    beside = [(i, i + 1 - 2 * (i % 2)) for i in range(4)]
    across = [(i, (i + 2) % 4) for i in range(4)]
    return lax.ppermute(late[0], "dp", across), lax.ppermute(late[1], "dp", beside)


def merge_late(d, gates_all, moved):
    return pl.pallas_call(
        functools.partial(merge_kernel, d),
        out_shape=jax.ShapeDtypeStruct(gates_all.shape, BF16),
        in_specs=[ANY_SPEC] * 3,
        out_specs=ANY_SPEC,
        input_output_aliases={2: 0},
        scratch_shapes=[pltpu.VMEM((2, *moved[0].shape), BF16), pltpu.SemaphoreType.DMA((2,))],
        compiler_params=pltpu.CompilerParams(vmem_limit_bytes=VMEM_LIMIT),
        name="merge_late",
    )(*moved, gates_all)


def on_device(
    char_ids,
    row_lengths,
    top_grad,
    char_table,
    conv_weight,
    conv_bias,
    highway_weight,
    highway_bias,
    proj_weight,
    proj_bias,
    lstm_input,
    lstm_state,
    lstm_bias,
    lstm_proj,
):
    section = lax.axis_index("section")
    rows, steps, per_token = char_ids.shape
    proj_width = proj_weight.shape[1]
    half = rows // 2
    tokens = half * steps
    local = conv_weight.shape[2]
    emb = char_table.shape[1]
    padded = -(-(per_token + TAPS - 1) // 8) * 8
    vocabulary = -(-char_table.shape[0] // 8) * 8
    chars = lax.dynamic_slice_in_dim(char_ids, section * half, half, 0)
    chars = jnp.transpose(chars, (1, 0, 2)).reshape(tokens, per_token)
    ids = jnp.pad(chars, ((0, 0), (0, padded - per_token)), constant_values=-1)
    ids = ids.reshape(tokens // CHUNK, 1, CHUNK * padded)
    table = jnp.pad(
        jnp.tile(char_table, (1, TAPS)),
        ((0, vocabulary - char_table.shape[0]), (0, 128 - TAPS * emb)),
    )
    widths = filter_widths(lax.axis_index("mp") * local, local, local * lax.axis_size("mp"))
    tap_keep = jnp.arange(TAPS, dtype=jnp.int32)[:, None] < widths[None, :]
    row = jnp.arange(128, dtype=jnp.int32)[:, None]
    taps_padded = jnp.pad(
        conv_weight.reshape(TAPS * emb, local), ((0, 128 - TAPS * emb), (0, 0))
    )
    masked = jnp.where(
        row < emb * widths[None, :],
        taps_padded,
        jnp.where(
            row == TAPS * emb,
            conv_bias[None, :],
            jnp.where(row == TAPS * emb + widths[None, :], -1e30, 0.0).astype(BF16),
        ),
    )
    log_positions = jnp.log((per_token - widths + 1).astype(F32))[None, :]
    w_high = jnp.transpose(highway_weight, (0, 2, 1, 3))
    (
        base_pair,
        taps,
        peak,
        pooled,
        current,
        transform,
        gate,
        features_all,
        last_own,
        w_input,
        w_state,
    ) = cnn_forward(
        ids,
        (table, masked, log_positions, w_high, highway_bias, proj_weight, proj_bias[None]),
        lstm_input[0],
        lstm_state[0],
    )
    depth_count = highway_weight.shape[0]

    def all_tokens(values):
        return lax.all_gather(values, ("section", "dp"), axis=values.ndim - 2, tiled=True)

    last_features = all_tokens(last_own)
    top_seq = jnp.transpose(top_grad, (2, 1, 0, 3))
    live = (jnp.arange(steps, dtype=jnp.int32)[:, None] < row_lengths[None, :]).astype(F32)
    live_seq = jnp.broadcast_to(live[..., None], (steps, rows, 128))
    layer_weights = (
        w_input,
        w_state,
        lstm_bias[0],
        lstm_proj[0],
    )
    (
        x_all,
        all_states,
        hidden_all,
        gates_all,
        projected_all,
        base_shards,
        high_features,
    ) = recurrence(base_pair, live_seq, top_seq, layer_weights, features_all)
    (
        all_gates,
        all_projected,
        all_inputs,
        all_hidden,
        base_full,
        all_mixed,
        *late,
        small,
    ) = (
        cnn_backward(
            base_shards,
            (taps, peak, pooled, current, transform, gate),
            (proj_weight, w_high, masked, ids),
            (gates_all, projected_all, x_all, hidden_all, all_states),
        )
    )
    relayed = lax.axis_size("dp") == 4
    if relayed:
        moved_first = send_late(late[:2])
        moved_second = send_late(late[2:])
    small = lax.all_gather(small, ("section", "dp"), axis=0)
    small = jnp.sum(small.astype(F32), axis=0)
    conv_weight_grad = jnp.where(
        tap_keep[:, None, :], small[: TAPS * emb].reshape(conv_weight.shape), 0.0
    )
    table_grad = small[128:].reshape(-1, emb, local)
    table_grad = jnp.transpose(table_grad, (0, 2, 1)).reshape(-1, emb)[: char_table.shape[0]]
    all_base = base_full.reshape(-1, proj_width)

    def flat(values):
        return values.reshape(2, -1, values.shape[4])

    def one_piece(values):
        batch, groups, _, _, width = values.shape
        return values.reshape(batch, groups, 1, -1, width)

    proj_weight_grad = lax.all_gather(
        dot(last_features, all_base, 0, 0).astype(BF16), "mp", axis=0, tiled=True
    ).astype(F32)
    proj_grad = weight_grads([one_piece(all_hidden)], flat(all_projected), 1)[0]
    batch, _, groups, count, _, _ = high_features.shape
    high_grad, high_bias_grad = weight_grads(
        [high_features.reshape(batch, 2 * groups, count, tokens, local)],
        all_mixed.reshape(batch, -1, 2 * local),
        2,
    )
    states = one_piece(all_states)
    inputs = one_piece(all_inputs)
    if relayed:
        moved_first, high_grad, proj_grad, conv_weight_grad, table_grad = lax.optimization_barrier(
            (moved_first, high_grad, proj_grad, conv_weight_grad, table_grad)
        )
        all_gates = merge_late(0, all_gates, moved_first)
        done = weight_grads([inputs, states], flat(all_gates), 4, only=0)
        done, moved_second, all_gates = lax.optimization_barrier((done, moved_second, all_gates))
        all_gates = merge_late(1, all_gates, moved_second)
        input_grad, state_grad, bias_grad = weight_grads(
            [inputs, states], flat(all_gates), 4, only=1, done=done
        )
    else:
        input_grad, state_grad, bias_grad = weight_grads([inputs, states], flat(all_gates), 4)
    return (
        table_grad,
        conv_weight_grad,
        small[TAPS * emb],
        high_grad,
        high_bias_grad,
        proj_weight_grad,
        jnp.sum(all_base.astype(F32), axis=0),
        input_grad.reshape(lstm_input.shape),
        state_grad.reshape(lstm_state.shape),
        bias_grad.reshape(lstm_bias.shape),
        proj_grad.reshape(lstm_proj.shape),
    )


def solution(mesh):
    return jax.shard_map(
        on_device,
        mesh=mesh,
        in_specs=(
            P("dp", None, None),
            P("dp"),
            P("dp", None, None, None),
            P(),
            P(None, None, "mp"),
            P("mp"),
            P(None, None, None, "mp"),
            P(None, None, "mp"),
            P(),
            P(),
            P("section", None, None, None, "mp"),
            P("section", None, None, None, "mp"),
            P("section", None, None, "mp"),
            P("section", None, "mp", None),
        ),
        out_specs=(
            P(),
            P(None, None, "mp"),
            P("mp"),
            P(None, None, None, "mp"),
            P(None, None, "mp"),
            P(),
            P(),
            P("section", None, None, None, "mp"),
            P("section", None, None, None, "mp"),
            P("section", None, None, "mp"),
            P("section", None, "mp", None),
        ),
        check_vma=False,
    )
```

```python
import functools

import jax
import jax.numpy as jnp
import numpy as np
from jax import lax
from jax.experimental import pallas as pl
from jax.experimental.pallas import tpu as pltpu
from jax.sharding import PartitionSpec as P

F32 = jnp.float32
BF16 = jnp.bfloat16
PERIODS = 32
TAPS = 7
VMEM_LIMIT = 62 * 1024 * 1024
SLOTS = 4
DEFER = 3
CHUNK = 16
TURN = 128
PER_TOKEN = 50
CHARS = 262


def dot(left, right, left_dim, right_dim):
    return lax.dot_general(
        left, right, (((left_dim,), (right_dim,)), ((), ())), preferred_element_type=F32
    )


def soft_clip(values):
    return 3.0 * jnp.tanh(values / 3.0)


def filter_widths(offset, amount, total):
    period = total // PERIODS
    in_period = (offset + jnp.arange(amount, dtype=jnp.int32)) % period
    widths = jnp.ones((amount,), jnp.int32)
    for exponent in range(6):
        widths = widths + (in_period * 64 >= period * 2**exponent).astype(jnp.int32)
    return widths


MESH = pl.DeviceIdType.MESH
VMEM_SPEC = pl.BlockSpec(memory_space=pltpu.VMEM)
ANY_SPEC = pl.BlockSpec(memory_space=pl.ANY)


def column_peers():
    count = lax.axis_size("mp")
    me = lax.axis_index("mp")
    return [lax.rem(me + j, count) for j in range(1, count)]


def greet(devices):
    barrier = pltpu.get_barrier_semaphore()
    for device in devices:
        pl.semaphore_signal(barrier, inc=1, device_id=device, device_id_type=MESH)
    pl.semaphore_wait(barrier, len(devices))


def remote(source, target, send, recv, device):
    return pltpu.make_async_remote_copy(
        src_ref=source,
        dst_ref=target,
        send_sem=send,
        recv_sem=recv,
        device_id=device,
        device_id_type=MESH,
    )


def one_hot_columns(ids, vocabulary):
    symbols = lax.broadcasted_iota(jnp.int32, (vocabulary, ids.shape[1]), 0)
    return (symbols == ids).astype(F32).astype(BF16)


def cnn_forward_kernel(
    ids_ref,
    table_ref,
    flags_ref,
    masked_ref,
    log_positions,
    b_high,
    b_proj,
    high_ref,
    proj_ref,
    input_ref,
    state_ref,
    base_out,
    taps_out,
    peak_out,
    pooled_out,
    current_out,
    transform_out,
    gate_out,
    features_all,
    last_out,
    input_out,
    state_out,
    features,
    w_high,
    w_proj,
    raw,
    turned,
    send_sem,
    recv_sem,
    base_send,
    base_recv,
    row_send,
    row_recv,
    own_sem,
    raw_sem,
    turned_sem,
    load_sem,
    relay_send,
    relay_recv,
):
    count = lax.axis_size("mp")
    me = lax.axis_index("mp")
    section = lax.axis_index("section")
    peers = column_peers()
    depth_count, tokens, local = current_out.shape
    chunk_rows = ids_ref.shape[2]
    padded = chunk_rows // CHUNK
    half = tokens // 2
    emb = 16
    block = min(256, local)
    loads = [
        pltpu.make_async_copy(high_ref, w_high, load_sem.at[0]),
        pltpu.make_async_copy(proj_ref, w_proj, load_sem.at[1]),
    ]
    for load in loads:
        load.start()
    groups = lax.axis_size("dp")
    group = lax.axis_index("dp")
    others = [lax.rem(group + j, groups) for j in range(1, groups)]
    relayed = groups == 4
    beside = group + 1 - 2 * lax.rem(group, 2)
    across = lax.rem(group + 2, 4)
    far = 3 - group
    near = [beside, across] if relayed else others
    origin = near if relayed else others[::-1]
    greet(
        [{"mp": peer} for peer in peers]
        + [{"section": 1 - section}]
        + [{"dp": other} for other in others]
    )

    def relay_rows(depth, way, slot):
        pieces = pl.ds(way * (count // 2), count // 2)
        return remote(
            features_all.at[depth, section, slot, pieces],
            features_all.at[depth, section, slot, pieces],
            relay_send.at[depth, way],
            relay_recv.at[depth, way],
            {"dp": across if way == 0 else beside},
        )

    def pass_rows(depth):
        for j in range(len(near)):
            give_rows(depth, j, origin[j]).wait_recv()
        if relayed:
            for way in range(2):
                relay_rows(depth, way, beside if way == 0 else across).start()

    blocks = input_out.shape[2] // TURN
    units = 4 * blocks

    def fetch(unit, start):
        slot = lax.rem(unit, 2)
        d = lax.rem(unit, 2 * blocks) // blocks
        rows = pl.ds(pl.multiple_of(lax.rem(unit, blocks) * TURN, TURN), TURN)
        for which, source in enumerate((input_ref, state_ref)):

            @pl.when(unit // (2 * blocks) == which)
            def _():
                copy = pltpu.make_async_copy(source.at[d, rows], raw.at[slot], raw_sem.at[slot])
                copy.start() if start else copy.wait()

    def deliver(unit, start):
        slot = lax.rem(unit, 2)
        d = lax.rem(unit, 2 * blocks) // blocks
        rows = pl.ds(pl.multiple_of(lax.rem(unit, blocks) * TURN, TURN), TURN)
        for which, target in enumerate((input_out, state_out)):

            @pl.when(unit // (2 * blocks) == which)
            def _():
                copy = pltpu.make_async_copy(
                    turned.at[slot], target.at[d, :, rows], turned_sem.at[slot]
                )
                copy.start() if start else copy.wait()

    def turn_units(first, last):
        @pl.loop(first, last)
        def _(unit):
            slot = lax.rem(unit, 2)
            fetch(unit, False)

            @pl.when(unit + 1 < units)
            def _():
                fetch(unit + 1, True)

            @pl.when(unit >= 2)
            def _():
                deliver(unit - 2, False)

            for g in range(4):
                turned[slot, g] = raw[slot, :, g, :]
            deliver(unit, True)

    fetch(0, True)

    def own_rows(depth):
        return pltpu.make_async_copy(
            features.at[depth], features_all.at[depth, section, group], own_sem.at[depth]
        )

    def give_rows(depth, j, slot):
        return remote(
            features.at[depth],
            features_all.at[depth, section, slot],
            row_send.at[depth, j],
            row_recv.at[depth, j],
            {"dp": near[j]},
        )

    def send(depth, part, rows, start):
        for j, peer in enumerate(peers):
            copy = remote(
                features.at[depth, me, rows],
                features.at[depth, me, rows],
                send_sem.at[depth, part, j],
                recv_sem.at[depth, part, me],
                {"mp": peer},
            )
            if start:
                copy.start()
            else:
                copy.wait_send()

    def receive(depth, part):
        rows = pl.ds(part * half, half)
        for j, peer in enumerate(peers):
            remote(
                features.at[depth, peer, rows],
                features.at[depth, peer, rows],
                send_sem.at[depth, part, j],
                recv_sem.at[depth, part, peer],
                {"mp": peer},
            ).wait_recv()

    lane_group = lax.broadcasted_iota(jnp.int32, (chunk_rows, 128), 1) // emb

    def pool_chunk(c):
        hot = one_hot_columns(ids_ref[c], table_ref.shape[0])
        embedded = lax.dot_general(
            hot, table_ref[...], (((0,), (0,)), ((), ())), preferred_element_type=F32
        )
        taps = embedded + flags_ref[...]
        for offset in range(1, TAPS):
            rolled = pltpu.roll(embedded, chunk_rows - offset, 0)
            taps = jnp.where(lane_group == offset, rolled, taps)
        taps = taps.astype(BF16)
        taps_out[c] = taps
        rows = pl.ds(pl.multiple_of(c * CHUNK, CHUNK), CHUNK)
        for start in range(0, local, block):
            cols = slice(start, start + block)
            scores = jnp.dot(taps, masked_ref[:, cols], preferred_element_type=F32)
            scores = scores.reshape(CHUNK, padded, block)
            top = jnp.max(scores, axis=1, keepdims=True)
            total = jnp.sum(jnp.exp(scores - top), axis=1, keepdims=True)
            peak = top + jnp.log(total)
            peak_out[rows, :, cols] = peak
            pooled = jnp.sum(peak, axis=1) - log_positions[:, cols]
            pooled_out[rows, cols] = pooled
            current = jnp.maximum(pooled, 0.0) + jnp.log1p(jnp.exp(-jnp.abs(pooled)))
            current_out[0, rows, cols] = current
            features[0, me, rows, cols] = current.astype(BF16)
        return rows

    for part in range(2):

        @pl.loop(0, half // CHUNK)
        def _(i):
            rows = pool_chunk(part * (half // CHUNK) + i)
            send(0, part, rows, True)

    for load in loads:
        load.wait()
    stops = [2, 2, 6, 9, 13, 16]
    turned_to = [0]

    def turn_some():
        stop = units * stops[min(turn_count[0], len(stops) - 1)] // 16
        turn_count[0] += 1
        if stop > turned_to[0]:
            turn_units(turned_to[0], stop)
            turned_to[0] = stop

    turn_count = [0]
    for depth in range(depth_count):
        for part in range(2):
            rows = pl.ds(part * half, half)
            turn_some()
            receive(depth, part)
            if part == 1:
                own_rows(depth).start()
                if depth + 1 < depth_count:
                    for j in range(len(near)):
                        give_rows(depth, j, group).start()
            mixed = []
            for g in range(2):
                total = jnp.broadcast_to(b_high[depth, g : g + 1, :].astype(F32), (half, local))
                for p in range(count):
                    total = total + jnp.dot(
                        features[depth, p, rows, :],
                        w_high[depth, g, p * local : (p + 1) * local, :],
                        preferred_element_type=F32,
                    )
                mixed.append(total)
            transform = mixed[0]
            gate = jax.nn.sigmoid(mixed[1])
            transform_out[depth, rows, :] = transform
            gate_out[depth, rows, :] = gate
            current = gate * current_out[depth, rows, :] + (1.0 - gate) * (
                transform * jax.nn.sigmoid(transform)
            )
            if depth + 1 < depth_count:
                current_out[depth + 1, rows, :] = current
            else:
                last_out[rows, :] = current.astype(BF16)
            features[depth + 1, me, rows, :] = current.astype(BF16)
            send(depth + 1, part, rows, True)
        if depth >= 1:
            pass_rows(depth - 1)

    def give():
        return remote(
            base_out.at[section],
            base_out.at[section],
            base_send,
            base_recv,
            {"section": 1 - section},
        )

    for part in range(2):
        rows = pl.ds(part * half, half)
        turn_some()
        receive(depth_count, part)
        total = jnp.broadcast_to(b_proj[...].astype(F32), (half, w_proj.shape[1]))
        for p in range(count):
            total = total + jnp.dot(
                features[depth_count, p, rows, :],
                w_proj[p * local : (p + 1) * local, :],
                preferred_element_type=F32,
            )
        base_out[section, rows, :] = total
    give().start()
    turn_units(turned_to[0], units)
    for depth in range(depth_count + 1):
        for part in range(2):
            send(depth, part, pl.ds(part * half, half), False)
    give().wait_send()
    remote(
        base_out.at[1 - section],
        base_out.at[1 - section],
        base_send,
        base_recv,
        {"section": 1 - section},
    ).wait_recv()
    for depth in range(depth_count):
        own_rows(depth).wait()
        if depth + 1 < depth_count:
            for j in range(len(near)):
                give_rows(depth, j, group).wait_send()
            if relayed:
                for way in range(2):
                    relay_rows(depth, way, beside if way == 0 else across).wait_send()
                    relay_rows(depth, way, far).wait_recv()
    for unit in range(units - 2, units):
        deliver(unit, False)


def cnn_forward(ids, weights, lstm_input, lstm_state):
    table, masked, log_positions, w_high, b_high, w_proj, b_proj = weights
    chunks, _, chunk_rows = ids.shape
    tokens = chunks * CHUNK
    depth_count, _, total, local = w_high.shape
    count = lax.axis_size("mp")
    groups = lax.axis_size("dp")
    directions, in_width, gate_blocks, cell_columns = lstm_input.shape
    padded = chunk_rows // CHUNK
    position = np.tile(np.arange(padded), CHUNK)[:, None]
    lane = np.arange(128)[None, :]
    excluded = lane - 16 * TAPS
    flags = (lane == 16 * TAPS) | (
        (excluded >= 1) & (excluded <= TAPS) & (position > PER_TOKEN - excluded)
    )
    dma = pltpu.SemaphoreType.DMA
    return pl.pallas_call(
        cnn_forward_kernel,
        out_shape=(
            jax.ShapeDtypeStruct((2, tokens, w_proj.shape[1]), F32),
            jax.ShapeDtypeStruct((chunks, chunk_rows, 128), BF16),
            jax.ShapeDtypeStruct((tokens, 1, local), F32),
            jax.ShapeDtypeStruct((tokens, local), F32),
            jax.ShapeDtypeStruct((depth_count, tokens, local), F32),
            jax.ShapeDtypeStruct((depth_count, tokens, local), F32),
            jax.ShapeDtypeStruct((depth_count, tokens, local), F32),
            jax.ShapeDtypeStruct((depth_count, 2, groups, count, tokens, local), BF16),
            jax.ShapeDtypeStruct((tokens, local), BF16),
            jax.ShapeDtypeStruct((directions, gate_blocks, in_width, cell_columns), BF16),
            jax.ShapeDtypeStruct((directions, gate_blocks, in_width, cell_columns), BF16),
        ),
        in_specs=[VMEM_SPEC] * 7 + [ANY_SPEC] * 4,
        out_specs=(*[VMEM_SPEC] * 7, ANY_SPEC, VMEM_SPEC, *[ANY_SPEC] * 2),
        scratch_shapes=[
            pltpu.VMEM((depth_count + 1, count, tokens, local), BF16),
            pltpu.VMEM(w_high.shape, BF16),
            pltpu.VMEM(w_proj.shape, BF16),
            pltpu.VMEM((2, TURN, gate_blocks, cell_columns), BF16),
            pltpu.VMEM((2, gate_blocks, TURN, cell_columns), BF16),
            dma((depth_count + 1, 2, count - 1)),
            dma((depth_count + 1, 2, count)),
            dma,
            dma,
            dma((depth_count, groups - 1)),
            dma((depth_count, groups - 1)),
            dma((depth_count,)),
            dma((2,)),
            dma((2,)),
            dma((2,)),
            dma((depth_count, 2)),
            dma((depth_count, 2)),
        ],
        compiler_params=pltpu.CompilerParams(
            collective_id=1, has_side_effects=True, vmem_limit_bytes=VMEM_LIMIT
        ),
        name="cnn_forward",
    )(
        ids,
        table,
        jnp.asarray(flags.astype(np.float32)),
        masked,
        log_positions,
        b_high,
        b_proj,
        w_high,
        w_proj,
        lstm_input,
        lstm_state,
    )


def cnn_backward_kernel(
    base_ref,
    own_ref,
    current_ref,
    transform_ref,
    gate_ref,
    peak_ref,
    pooled_ref,
    masked_ref,
    masked_t,
    ids_ref,
    high_ref,
    taps_hbm,
    gates_in,
    projected_in,
    x_in,
    hidden_in,
    state_all,
    gates_all,
    projected_all,
    x_all,
    hidden_all,
    base_full,
    mixed_all,
    late_a,
    late_b,
    late_c,
    late_d,
    small_out,
    w_high,
    taps_ref,
    load_sem,
    conv_out,
    mixed_out,
    late_buf,
    base_all,
    base_rows,
    table_sum,
    table_all,
    grad_current,
    outgoing,
    incoming,
    base_send,
    base_recv,
    sum_send,
    sum_recv,
    own_sem,
    relay_send,
    relay_recv,
    lift_send,
    lift_recv,
    row_send,
    row_recv,
    full_sem,
    share_send,
    share_recv,
    table_send,
    table_recv,
    mixed_sem,
    mixed_send,
    mixed_recv,
    mixed_share,
    mixed_shared,
    late_sem,
    defer_send,
    defer_recv,
    x_buf,
    flip_sem,
):
    count = lax.axis_size("mp")
    me = lax.axis_index("mp")
    section = lax.axis_index("section")
    groups = lax.axis_size("dp")
    group = lax.axis_index("dp")
    peers = column_peers()
    depth_count, tokens, local = current_ref.shape
    steps = x_all.shape[2]
    chunks, chunk_rows, _ = taps_ref.shape
    loads = [
        pltpu.make_async_copy(high_ref, w_high, load_sem.at[0]),
        pltpu.make_async_copy(taps_hbm, taps_ref, load_sem.at[1]),
    ]
    for load in loads:
        load.start()
    padded = chunk_rows // CHUNK
    emb = 16
    vocabulary = -(-CHARS // 8) * 8
    relayed = groups == 4
    beside = group + 1 - 2 * lax.rem(group, 2)
    across = lax.rem(group + 2, 4)
    far = 3 - group
    greet(
        [{"mp": peer} for peer in peers]
        + [{"section": 1 - section, "mp": peer} for peer in [*peers, me]]
        + [{"dp": lax.rem(group + j, groups)} for j in range(1, groups)]
    )

    def lift():
        return remote(
            state_all.at[:, :, pl.ds(1, steps)],
            x_all,
            lift_send,
            lift_recv,
            {"section": 1 - section},
        )

    half_steps = steps // 2
    others = [lax.rem(group + j, groups) for j in range(1, groups)]
    near = [beside, across] if relayed else others
    origin = near if relayed else others[::-1]

    def relay(kind, way, slot):
        head = steps * 7 // 10
        if kind == 0:
            block = projected_all.at[way, slot]
        else:
            block = hidden_all.at[way, slot, pl.ds(head, steps - head)]
        return remote(
            block,
            block,
            relay_send.at[kind, way],
            relay_recv.at[kind, way],
            {"dp": across if way == 0 else beside},
        )

    def deferred(j, slot):
        return remote(
            gates_all.at[:, slot, pl.ds(0, DEFER)],
            gates_all.at[:, slot, pl.ds(0, DEFER)],
            defer_send.at[j],
            defer_recv.at[j],
            {"dp": near[j]},
        )

    for j in range(len(near)):
        deferred(j, group).start()


    late_loads, late_stores = [], []
    for i, target in enumerate((late_a, late_b, late_c, late_d)):
        d, way = i // 2, i % 2
        rows = pl.ds(way * half_steps, half_steps)
        source = gates_all.at[d, (beside, across)[way], rows]
        late_loads.append(pltpu.make_async_copy(source, late_buf.at[i], late_sem.at[i]))
        late_stores.append(pltpu.make_async_copy(late_buf.at[i], target, late_sem.at[i]))

    def spread_base(half, target_section, peer, j):
        return remote(
            base_ref.at[half],
            base_all.at[me],
            base_send.at[half, j],
            base_recv.at[me],
            {"section": target_section, "mp": peer},
        )

    everyone = [*peers, me]

    x_load = pltpu.make_async_copy(x_all.at[0], x_buf, flip_sem.at[0])

    @pl.when(section == 0)
    def _():
        x_load.start()
        for j, peer in enumerate(peers):
            spread_base(0, 0, peer, j).start()
        for j, peer in enumerate(everyone):
            spread_base(1, 1, peer, j).start()
        lift().start()
        own = pltpu.make_async_copy(base_ref.at[0], base_all.at[me], own_sem)
        own.start()
        own.wait()

    def base_arrival(source):
        return remote(
            base_ref.at[0],
            base_all.at[source],
            base_send.at[0, 0],
            base_recv.at[source],
            {"section": 1 - section},
        )

    for peer in peers:
        base_arrival(peer).wait_recv()

    @pl.when(section == 1)
    def _():
        base_arrival(me).wait_recv()

    wide = base_all.shape[2]
    for p in range(count):
        base_rows[:, p * wide : (p + 1) * wide] = base_all[p]
    keep = pltpu.make_async_copy(base_rows, base_full.at[section, group], full_sem)
    keep.start()

    def base_row(j, slot):
        return remote(
            base_rows,
            base_full.at[section, slot],
            row_send.at[j],
            row_recv.at[j],
            {"dp": others[j]},
        )

    def share_base(owner):
        return remote(
            base_full.at[owner],
            base_full.at[owner],
            share_send,
            share_recv,
            {"section": 1 - section},
        )

    for j in range(groups - 1):
        base_row(j, group).start()

    def keep_mixed(depth):
        return pltpu.make_async_copy(
            mixed_out.at[depth], mixed_all.at[depth, section, group], mixed_sem.at[depth]
        )

    def mixed_row(depth, j, slot):
        return remote(
            mixed_out.at[depth],
            mixed_all.at[depth, section, slot],
            mixed_send.at[depth, j],
            mixed_recv.at[depth, j],
            {"dp": others[j]},
        )

    def share_mixed(depth, owner):
        return remote(
            mixed_all.at[depth, owner],
            mixed_all.at[depth, owner],
            mixed_share.at[depth],
            mixed_shared.at[depth],
            {"section": 1 - section},
        )

    def collect_mixed(depth):
        keep_mixed(depth).wait()
        for j in range(groups - 1):
            mixed_row(depth, j, others[groups - 2 - j]).wait_recv()
        share_mixed(depth, section).start()

    own_rows = pl.ds(pl.multiple_of(me * local, local), local)
    total = jnp.zeros((tokens, local), F32)
    for p in range(count):
        total = total + lax.dot_general(
            base_all[p],
            own_ref[own_rows, p * wide : (p + 1) * wide],
            (((1,), (1,)), ((), ())),
            preferred_element_type=F32,
        )
    grad_current[...] = total

    def send_sum(depth, peer, j):
        return remote(
            outgoing.at[depth, j],
            incoming.at[depth, me],
            sum_send.at[depth, j],
            sum_recv.at[depth, me],
            {"mp": peer},
        )

    def back(depth, owner):
        rows = pl.ds(pl.multiple_of(owner * local, local), local)
        parts = [
            lax.dot_general(
                mixed_out[depth, :, g * local : (g + 1) * local],
                w_high[depth, g, rows, :],
                (((1,), (1,)), ((), ())),
                preferred_element_type=F32,
            )
            for g in range(2)
        ]
        return parts[0] + parts[1]

    for load in loads:
        load.wait()
    for depth in range(depth_count - 1, -1, -1):
        transform = transform_ref[depth]
        gate = gate_ref[depth]
        grad = grad_current[...]
        slope = jax.nn.sigmoid(transform)
        mixed_out[depth, :, :local] = (
            grad * (1.0 - gate) * slope * (1.0 + transform * (1.0 - slope))
        ).astype(BF16)
        mixed_out[depth, :, local:] = (
            grad * (current_ref[depth] - transform * slope) * gate * (1.0 - gate)
        ).astype(BF16)
        keep_mixed(depth).start()
        for j in range(groups - 1):
            mixed_row(depth, j, group).start()
        if relayed and depth == depth_count - 1:
            for kind in range(2):
                for way in range(2):
                    relay(kind, way, beside if way == 0 else across).start()
        for j, peer in enumerate(peers):
            outgoing[depth, j] = back(depth, peer).astype(BF16)
            send_sum(depth, peer, j).start()
        total = grad * gate + back(depth, me)
        for j, peer in enumerate(peers):
            remote(
                outgoing.at[depth, j],
                incoming.at[depth, peer],
                sum_send.at[depth, j],
                sum_recv.at[depth, peer],
                {"mp": peer},
            ).wait_recv()
            total = total + incoming[depth, peer].astype(F32)
        grad_current[...] = total

    for j in range(len(near)):
        deferred(j, group).wait_send()
        deferred(j, origin[j]).wait_recv()
    if relayed:
        for load in late_loads:
            load.start()
    for depth in range(depth_count - 1, 0, -1):
        collect_mixed(depth)
    if relayed:
        for load, store in zip(late_loads, late_stores):
            load.wait()
            store.start()
    @pl.when(section == 0)
    def _():
        x_load.wait()

        @pl.loop(0, steps)
        def _(t):
            for q in range(groups):
                pltpu.make_async_copy(
                    x_buf.at[q, t], x_all.at[1, q, steps - 1 - t], flip_sem.at[1]
                ).start()

    grad_current[...] = grad_current[...] * jax.nn.sigmoid(pooled_ref[...])
    conv_out[...] = jnp.zeros_like(conv_out)
    small_out[...] = jnp.zeros_like(small_out)
    table_sum[...] = jnp.zeros_like(table_sum)
    lane_group = lax.broadcasted_iota(jnp.int32, (chunk_rows, 128), 1) // emb

    @pl.loop(0, chunks)
    def _(c):
        rows = pl.ds(pl.multiple_of(c * CHUNK, CHUNK), CHUNK)
        taps = taps_ref[c]
        scores = jnp.dot(taps, masked_ref[...], preferred_element_type=F32)
        scores = scores.reshape(CHUNK, padded, local)
        share = jnp.exp(scores - peak_ref[rows])
        grads = share * grad_current[rows, :][:, None, :]
        grads = grads.reshape(chunk_rows, local).astype(BF16)
        conv_out[...] += lax.dot_general(
            taps, grads, (((0,), (0,)), ((), ())), preferred_element_type=F32
        )
        back_taps = jnp.dot(grads, masked_t[...], preferred_element_type=F32)
        moved = back_taps
        for offset in range(1, TAPS):
            moved = jnp.where(lane_group == offset, pltpu.roll(back_taps, offset, 0), moved)
        hot = one_hot_columns(ids_ref[c], vocabulary)
        table_sum[:vocabulary, :] += jnp.dot(
            hot, moved.astype(BF16), preferred_element_type=F32
        )

    columns = table_sum[...].T
    folded = columns[:emb]
    for offset in range(1, TAPS):
        folded = folded + columns[offset * emb : (offset + 1) * emb]
    table_all[me] = folded

    def table_copy(j, slot):
        return remote(
            table_all.at[slot],
            table_all.at[slot],
            table_send.at[j],
            table_recv.at[slot],
            {"mp": peers[j]},
        )

    for j in range(count - 1):
        table_copy(j, me).start()

    for j in range(count - 1):
        table_copy(j, peers[j]).wait_recv()
    folded = table_all[0]
    for p in range(1, count):
        folded = folded + table_all[p]
    small_out[:128, :] = conv_out[...].astype(BF16)
    span = min(local, folded.shape[1])
    for i in range(folded.shape[1] // span):
        at = 128 + i * emb
        small_out[at : at + emb, :span] = folded[:, i * span : (i + 1) * span].astype(BF16)
    for j in range(count - 1):
        table_copy(j, me).wait_send()
    keep.wait()
    for j in range(groups - 1):
        base_row(j, others[groups - 2 - j]).wait_recv()
    share_base(section).start()
    collect_mixed(0)
    for j in range(groups - 1):
        base_row(j, group).wait_send()
        for depth in range(depth_count):
            mixed_row(depth, j, group).wait_send()
    for depth in range(depth_count):
        for j, peer in enumerate(peers):
            send_sum(depth, peer, j).wait_send()

    @pl.when(section == 0)
    def _():
        for j, peer in enumerate(peers):
            spread_base(0, 0, peer, j).wait_send()
        for j, peer in enumerate(everyone):
            spread_base(1, 1, peer, j).wait_send()
        lift().wait_send()
        pltpu.make_async_copy(x_buf, x_all.at[1], flip_sem.at[1]).wait()

    @pl.when(section == 1)
    def _():
        lift().wait_recv()

    if relayed:
        for kind in range(2):
            for way in range(2):
                relay(kind, way, beside if way == 0 else across).wait_send()
                relay(kind, way, far).wait_recv()
        for copy in late_stores:
            copy.wait()

    share_base(section).wait_send()
    share_base(1 - section).wait_recv()
    for depth in range(depth_count):
        share_mixed(depth, section).wait_send()
        share_mixed(depth, 1 - section).wait_recv()


def cnn_backward(base_shards, saved, weights, rows_all):
    w_proj, w_high, masked, ids = weights
    taps, peak, pooled, current, transform, gate = saved
    gates_all, projected_all, x_all, hidden_all, state_all = rows_all
    depth_count, tokens, local = current.shape
    count = lax.axis_size("mp")
    groups = lax.axis_size("dp")
    vocabulary = -(-CHARS // 128) * 128
    half_steps = gates_all.shape[2] // 2
    late = (half_steps, *gates_all.shape[3:])
    dma = pltpu.SemaphoreType.DMA
    return pl.pallas_call(
        cnn_backward_kernel,
        out_shape=(
            jax.ShapeDtypeStruct(gates_all.shape, BF16),
            jax.ShapeDtypeStruct(projected_all.shape, BF16),
            jax.ShapeDtypeStruct(x_all.shape, BF16),
            jax.ShapeDtypeStruct(hidden_all.shape, BF16),
            jax.ShapeDtypeStruct((2, groups, tokens, count * base_shards.shape[2]), BF16),
            jax.ShapeDtypeStruct((depth_count, 2, groups, tokens, 2 * local), BF16),
            *[jax.ShapeDtypeStruct(late, BF16)] * 4,
            jax.ShapeDtypeStruct((128 + 16 * max(1, vocabulary // local), local), BF16),
        ),
        in_specs=[VMEM_SPEC] * 10 + [ANY_SPEC] * 7,
        out_specs=(*[ANY_SPEC] * 10, VMEM_SPEC),
        input_output_aliases={12: 0, 13: 1, 14: 2, 15: 3},
        scratch_shapes=[
            pltpu.VMEM(w_high.shape, BF16),
            pltpu.VMEM(taps.shape, BF16),
            dma((2,)),
            pltpu.VMEM((128, local), F32),
            pltpu.VMEM((depth_count, tokens, 2 * local), BF16),
            pltpu.VMEM((4, *late), BF16),
            pltpu.VMEM((count, tokens, base_shards.shape[2]), BF16),
            pltpu.VMEM((tokens, count * base_shards.shape[2]), BF16),
            pltpu.VMEM((vocabulary, 128), F32),
            pltpu.VMEM((count, 16, vocabulary), F32),
            pltpu.VMEM((tokens, local), F32),
            pltpu.VMEM((depth_count, count - 1, tokens, local), BF16),
            pltpu.VMEM((depth_count, count, tokens, local), BF16),
            dma((2, count)),
            dma((count,)),
            dma((depth_count, count - 1)),
            dma((depth_count, count)),
            dma,
            dma((2, 2)),
            dma((2, 2)),
            dma,
            dma,
            dma((groups - 1,)),
            dma((groups - 1,)),
            dma,
            dma,
            dma,
            dma((count - 1,)),
            dma((count,)),
            dma((depth_count,)),
            dma((depth_count, groups - 1)),
            dma((depth_count, groups - 1)),
            dma((depth_count,)),
            dma((depth_count,)),
            dma((4,)),
            dma((groups - 1,)),
            dma((groups - 1,)),
            pltpu.VMEM(x_all.shape[1:], BF16),
            dma((2,)),
        ],
        compiler_params=pltpu.CompilerParams(
            collective_id=2, has_side_effects=True, vmem_limit_bytes=VMEM_LIMIT
        ),
        name="cnn_backward",
    )(
        base_shards,
        w_proj,
        current,
        transform,
        gate,
        peak,
        pooled,
        masked,
        jnp.pad(masked[: 16 * TAPS], ((0, 128 - 16 * TAPS), (0, 0))).T,
        ids,
        w_high,
        taps,
        gates_all,
        projected_all,
        x_all,
        hidden_all,
        state_all,
    )


def recurrence_kernel(
    base_ref,
    live_ref,
    top_ref,
    bias_ref,
    proj_ref,
    in_ref,
    state_ref,
    features_in,
    x_all,
    state_all,
    hidden_all,
    gates_all,
    projected_all,
    base_out,
    features_all,
    x_out,
    state_out,
    hidden_out,
    projected_out,
    acts,
    cells,
    clips,
    pre,
    grad_cell,
    parts,
    back_parts,
    above,
    gate_buf,
    base_sem,
    send_sem,
    recv_sem,
    back_send,
    back_recv,
    x_send,
    x_recv,
    above_send,
    above_recv,
    gate_sem,
    gate_send,
    own_sem,
    row_send,
    row_recv,
    w_in,
    w_state,
    load_sem,
    w_in_t,
    w_state_t,
    proj_t,
    input_parts,
    input_sums,
    input_send,
    input_recv,
    base_sum,
    share_send,
    share_recv,
    relay_send,
    relay_recv,
    feature_send,
    feature_recv,
    hidden_send,
    hidden_recv,
):
    count = lax.axis_size("mp")
    me = lax.axis_index("mp")
    section = lax.axis_index("section")
    steps = x_out.shape[1]
    cell_count = proj_ref.shape[1]
    chunk = min(256, cell_count)
    peers = [lax.rem(me + j, count) for j in range(1, count)]
    groups = lax.axis_size("dp")
    group = lax.axis_index("dp")
    others = [lax.rem(group + j, groups) for j in range(1, groups)]
    relayed = groups == 4
    beside = group + 1 - 2 * lax.rem(group, 2)
    across = lax.rem(group + 2, 4)
    near = [beside, across] if relayed else others
    loads = [
        [pltpu.make_async_copy(source.at[d], target.at[d], load_sem.at[i, d]) for d in range(2)]
        for i, (source, target) in enumerate(((in_ref, w_in), (state_ref, w_state)))
    ]
    for d in range(2):
        loads[0][d].start()
    for d in range(2):
        loads[1][d].start()

    barrier = pltpu.get_barrier_semaphore()
    for peer in peers:
        pl.semaphore_signal(barrier, inc=1, device_id={"mp": peer}, device_id_type=MESH)
    pl.semaphore_signal(barrier, inc=1, device_id={"section": 1 - section}, device_id_type=MESH)
    for other in others:
        pl.semaphore_signal(barrier, inc=1, device_id={"dp": other}, device_id_type=MESH)
    pl.semaphore_wait(barrier, count + groups - 1)

    def share_features(owner):
        return remote(
            features_all.at[:, owner],
            features_all.at[:, owner],
            share_send,
            share_recv,
            {"section": 1 - section},
        )

    pieces = features_all.shape[3]

    last_depth = features_all.shape[0] - 1

    def give_features(j, slot):
        return remote(
            features_all.at[last_depth, section, slot],
            features_all.at[last_depth, section, slot],
            feature_send.at[j],
            feature_recv.at[j],
            {"dp": near[j]},
        )

    def relay_features(way, slot):
        half = pl.ds(way * (pieces // 2), pieces // 2)
        block = features_all.at[last_depth, section, slot, half]
        return remote(
            block,
            block,
            relay_send.at[way],
            relay_recv.at[way],
            {"dp": across if way == 0 else beside},
        )

    def start_relays():
        if relayed:
            for way in range(2):
                relay_features(way, beside if way == 0 else across).start()

    def finish_relays():
        if relayed:
            for way in range(2):
                relay_features(way, beside if way == 0 else across).wait_send()
                relay_features(way, 3 - group).wait_recv()

    for j in range(len(near)):
        give_features(j, group).start()

    def wide(values, width):
        return jnp.concatenate([values] * (width // values.shape[1]), axis=1)

    def copy_part(buffer, send, recv, d, parity, source, j, target):
        return pltpu.make_async_remote_copy(
            src_ref=buffer.at[d, parity, source],
            dst_ref=buffer.at[d, parity, source],
            send_sem=send.at[d, parity, j],
            recv_sem=recv.at[d, parity, source],
            device_id={"mp": target},
            device_id_type=MESH,
        )

    ordered = peers
    if count == 4:
        ordered = [3 - me, lax.rem(me + 2, 4), me + 1 - 2 * lax.rem(me, 2)]

    def exchange_start(buffer, send, recv, d, parity, value):
        buffer[d, parity, me] = value.astype(BF16)
        for j, peer in enumerate(ordered):
            copy_part(buffer, send, recv, d, parity, me, j, peer).start()

    def exchange_wait(buffer, send, recv, d, parity):
        for j, peer in enumerate(ordered):
            copy_part(buffer, send, recv, d, parity, peer, j, peer).wait_recv()
        total = buffer[d, parity, 0].astype(F32)
        for source in range(1, count):
            total = total + buffer[d, parity, source].astype(F32)
        for j, peer in enumerate(ordered):
            copy_part(buffer, send, recv, d, parity, me, j, peer).wait_send()
        return total

    def pass_up(d, k):
        return pltpu.make_async_remote_copy(
            src_ref=state_out.at[d, k + 1],
            dst_ref=x_out.at[d, k],
            send_sem=x_send.at[d],
            recv_sem=x_recv.at[d, k],
            device_id={"section": 1 - section},
            device_id_type=MESH,
        )

    def pass_down(d, k):
        return pltpu.make_async_remote_copy(
            src_ref=above.at[d, k],
            dst_ref=above.at[d, k],
            send_sem=above_send.at[d],
            recv_sem=above_recv.at[d, k],
            device_id={"section": 1 - section},
            device_id_type=MESH,
        )

    def gates_copy(d, k, slot):
        return pltpu.make_async_copy(
            gate_buf.at[d, slot], gates_all.at[d, group, k], gate_sem.at[d, slot]
        )

    def gates_row(d, k, slot, j, other):
        return pltpu.make_async_remote_copy(
            src_ref=gate_buf.at[d, slot],
            dst_ref=gates_all.at[d, group, k],
            send_sem=gate_send.at[d, slot, j],
            recv_sem=row_recv.at[0, j],
            device_id={"dp": other},
            device_id_type=MESH,
        )

    def row(kind, source, target, j, other):
        return pltpu.make_async_remote_copy(
            src_ref=source,
            dst_ref=target,
            send_sem=row_send.at[kind, j],
            recv_sem=row_recv.at[kind, j],
            device_id={"dp": other},
            device_id_type=MESH,
        )

    def from_peer(j, targets):
        back = len(targets) - 1 - j
        return targets[j] if relayed and len(targets) == 2 else targets[back]

    head = steps * 7 // 10

    def relay_hidden(way, slot):
        block = hidden_all.at[way, slot, pl.ds(0, head)]
        return remote(
            block,
            block,
            hidden_send.at[way],
            hidden_recv.at[way],
            {"dp": across if way == 0 else beside},
        )

    def finish_hidden(kind, some):
        for j, other in enumerate(near):
            target = hidden_all.at[:, from_peer(j, near), some]
            copy = row(kind, hidden_out.at[:, some], target, j, other)
            copy.wait_send()
            copy.wait_recv()

    def time_of(d, k):
        return k if d == 0 else steps - 1 - k

    @pl.when(section == 0)
    def _():
        part_rows = base_ref.shape[1] // steps

        @pl.loop(0, steps)
        def _(t):
            at = pl.ds(pl.multiple_of(t * part_rows, part_rows), part_rows)
            x = jnp.concatenate([base_ref[0, at, :], base_ref[1, at, :]], axis=0).astype(BF16)
            for d in range(2):
                x_out[d, time_of(d, t)] = x

        for j, other in enumerate(others):
            row(1, x_out.at[0], x_all.at[0, group], j, other).start()

    for d in range(2):
        state_out[d, 0] = jnp.zeros(state_out.shape[2:], BF16)
        cells[d, 0] = jnp.zeros(cells.shape[2:], F32)
        grad_cell[d] = jnp.zeros(grad_cell.shape[1:], F32)

    def input_part(d, k):
        @pl.when(section == 1)
        def _():
            pass_up(d, k).wait_recv()

        x = x_out[d, k]
        for block in range(4):
            for start in range(0, cell_count, chunk):
                cols = slice(block * cell_count + start, block * cell_count + start + chunk)
                bias = bias_ref[d, block : block + 1, start : start + chunk].astype(F32)
                pre[d, :, cols] = bias + jnp.dot(
                    x, w_in[d, block, :, start : start + chunk], preferred_element_type=F32
                )

    def turn_weights(unit):
        per_block = cell_count // chunk
        block = unit // per_block
        cols = pl.ds(pl.multiple_of(lax.rem(unit, per_block) * chunk, chunk), chunk)
        rows_t = pl.ds(pl.multiple_of(unit * chunk, chunk), chunk)
        for d in range(2):
            w_in_t[d, rows_t, :] = w_in[d, block, :, cols].T
            w_state_t[d, rows_t, :] = w_state[d, block, :, cols].T

    def turn_proj(unit):
        cols = pl.ds(pl.multiple_of(unit * 128, 128), 128)
        for d in range(2):
            proj_t[d, :, cols] = proj_ref[d, cols, :].T

    def forward_cells(d, k):
        state = state_out[d, k]
        live = live_ref[time_of(d, k)]
        for start in range(0, cell_count, chunk):
            raw = []
            for block in range(4):
                cols = slice(block * cell_count + start, block * cell_count + start + chunk)
                raw.append(
                    pre[d, :, cols]
                    + jnp.dot(
                        state, w_state[d, block, :, start : start + chunk], preferred_element_type=F32
                    )
                )
            own = slice(start, start + chunk)
            in_gate = jax.nn.sigmoid(raw[0])
            forget = jax.nn.sigmoid(raw[1])
            memory = jnp.tanh(raw[2])
            out_gate = jax.nn.sigmoid(raw[3])
            for block, value in enumerate((in_gate, forget, memory, out_gate)):
                acts[d, k, block, :, own] = value
            cell_new = soft_clip(in_gate * memory + forget * cells[d, k, :, own])
            cells[d, k + 1, :, own] = wide(live, chunk) * cell_new
            hidden_out[d, k, :, own] = (out_gate * jnp.tanh(cell_new)).astype(BF16)
        part = jnp.dot(hidden_out[d, k], proj_ref[d], preferred_element_type=F32)
        exchange_start(parts, send_sem, recv_sem, d, lax.rem(k, 2), part)
        for j, other in enumerate(near):
            kind = 2 + 3 * (k // head)
            row(kind, hidden_out.at[d, k], hidden_all.at[d, group, k], j, other).start()

    def forward_state(d, k):
        total = exchange_wait(parts, send_sem, recv_sem, d, lax.rem(k, 2))
        clip = jnp.tanh(total / 3.0)
        clips[d, k] = clip
        live = wide(live_ref[time_of(d, k)], clip.shape[1])
        state_out[d, k + 1] = (live * 3.0 * clip).astype(BF16)

        @pl.when(section == 0)
        def _():
            @pl.when(k > 0)
            def _():
                pass_up(d, k - 1).wait_send()

            pass_up(d, k).start()

        for j, other in enumerate(others):
            row(3, state_out.at[d, k + 1], state_all.at[d, group, k + 1], j, other).start()

    units = 4 * cell_count // chunk
    for d in range(2):
        loads[0][d].wait()
        input_part(d, 0)
    for d in range(2):
        loads[1][d].wait()
        forward_cells(d, 0)
    for d in range(2):
        input_part(d, 1)

    @pl.loop(1, steps)
    def _(k):
        for d in range(2):
            forward_state(d, k - 1)
            forward_cells(d, k)

        @pl.when(k + 1 < steps)
        def _():
            for d in range(2):
                input_part(d, k + 1)

        @pl.when(k <= units)
        def _():
            turn_weights(k - 1)

        @pl.when(k == steps - 3)
        def _():
            finish_hidden(2, pl.ds(0, head))
            if relayed:
                for way in range(2):
                    relay_hidden(way, beside if way == 0 else across).start()

        @pl.when(k == steps - 5)
        def _():
            for j in range(len(near)):
                give_features(j, group).wait_send()
                give_features(j, from_peer(j, near)).wait_recv()
            start_relays()

        @pl.when(k <= cell_count // 128)
        def _():
            turn_proj(k - 1)

    for unit in range(steps - 1, units):
        turn_weights(unit)
    for d in range(2):
        forward_state(d, steps - 1)

    @pl.when(section == 0)
    def _():
        for d in range(2):
            pass_up(d, steps - 1).wait_send()

    def back_wait(d, parity):
        return exchange_wait(back_parts, back_send, back_recv, d, parity)

    def back_start(d, parity, value):
        exchange_start(back_parts, back_send, back_recv, d, parity, value)

    def backward_cells(d, k, total):
        slot = lax.rem(k, SLOTS)
        live = live_ref[time_of(d, k)]
        clip = clips[d, k]
        grad_out = wide(live, clip.shape[1]) * (total + top_ref[d, time_of(d, k)].astype(F32))
        grad_projected = (grad_out * (1.0 - clip * clip)).astype(BF16)
        projected_out[d, k] = grad_projected

        for j, other in enumerate(near):
            row(
                4, projected_out.at[d, k], projected_all.at[d, group, k], j, other
            ).start()

        @pl.when(k < steps - SLOTS)
        def _():
            gates_copy(d, k + SLOTS, slot).wait()
            for j, other in enumerate(near):
                gates_row(d, k + SLOTS, slot, j, other).wait_send()

        for start in range(0, cell_count, chunk):
            own = slice(start, start + chunk)
            grad_hidden = jnp.dot(grad_projected, proj_t[d, :, own], preferred_element_type=F32)
            in_gate, forget, memory, out_gate = [acts[d, k, block, :, own] for block in range(4)]
            cell = cells[d, k, :, own]
            clip_raw = jnp.tanh((in_gate * memory + forget * cell) / 3.0)
            tanh_cell = jnp.tanh(3.0 * clip_raw)
            grad_new = wide(live, chunk) * grad_cell[d, :, own] + grad_hidden * out_gate * (
                1.0 - tanh_cell * tanh_cell
            )
            grad_raw = grad_new * (1.0 - clip_raw * clip_raw)
            grad_cell[d, :, own] = grad_raw * forget
            grads = (
                grad_raw * memory * in_gate * (1.0 - in_gate),
                grad_raw * cell * forget * (1.0 - forget),
                grad_raw * in_gate * (1.0 - memory * memory),
                grad_hidden * tanh_cell * out_gate * (1.0 - out_gate),
            )
            for block, value in enumerate(grads):
                cols = slice(block * cell_count + start, block * cell_count + start + chunk)
                gate_buf[d, slot, :, cols] = value.astype(BF16)
        gates_copy(d, k, slot).start()

    def gates_send(d, k):
        @pl.when(k >= DEFER)
        def _():
            for j, other in enumerate(near):
                gates_row(d, k, lax.rem(k, SLOTS), j, other).start()

    def backward_state(d, k):
        @pl.when(k > 0)
        def _():
            back = jnp.dot(gate_buf[d, lax.rem(k, SLOTS)], w_state_t[d], preferred_element_type=F32)
            pre[d, :, : back.shape[1]] = back

            @pl.when(section == 0)
            def _():
                pass_down(d, k - 1).wait_recv()
                pre[d, :, : back.shape[1]] = back + above[d, k - 1]

            back_start(d, lax.rem(k - 1, 2), pre[d, :, : back.shape[1]])

    share = base_out.shape[2]

    def input_copy(source, target, j, peer):
        return remote(source, target, input_send.at[j], input_recv.at[j], {"mp": peer})

    def backward_input(d, k):
        gates_send(d, k)
        part = jnp.dot(gate_buf[d, lax.rem(k, SLOTS)], w_in_t[d], preferred_element_type=F32)

        @pl.when(section == 1)
        def _():
            above[d, k] = part

            @pl.when(k < steps - 1)
            def _():
                pass_down(d, k + 1).wait_send()

            pass_down(d, k).start()

        @pl.when(section == 0)
        def _():
            for p in range(count):
                input_parts[d, k, p] = part[:, p * share : (p + 1) * share].astype(BF16)
            for j, peer in enumerate(peers):
                input_copy(input_parts.at[d, k, peer], input_sums.at[d, k, me], j, peer).start()

    last = steps - 1

    @pl.when(section == 0)
    def _():
        for d in range(2):
            pass_down(d, last).wait_recv()
            back_start(d, lax.rem(last, 2), above[d, last])

    for d in range(2):

        @pl.when(section == 0)
        def _():
            pre[d, :, : clips.shape[3]] = back_wait(d, lax.rem(last, 2))

        @pl.when(section == 1)
        def _():
            pre[d, :, : clips.shape[3]] = jnp.zeros(clips.shape[2:], F32)

        backward_cells(d, last, pre[d, :, : clips.shape[3]])
        backward_state(d, last)
    for d in range(2):
        backward_input(d, last)

    @pl.loop(1, steps)
    def _(tick):
        k = last - tick
        for d in range(2):
            backward_cells(d, k, back_wait(d, lax.rem(k, 2)))
            backward_state(d, k)
        for d in range(2):
            backward_input(d, k)

        @pl.when(tick == 5)
        def _():
            finish_relays()
            share_features(section).start()
            if relayed:
                for way in range(2):
                    relay_hidden(way, beside if way == 0 else across).wait_send()
                    relay_hidden(way, 3 - group).wait_recv()

    for d in range(2):
        for k in range(min(SLOTS, steps)):
            gates_copy(d, k, k % SLOTS).wait()
            for j, other in enumerate(near):
                if k >= DEFER:
                    gates_row(d, k, k % SLOTS, j, other).wait_send()

    @pl.when(section == 1)
    def _():
        for d in range(2):
            pass_down(d, 0).wait_send()

    own = [
        (hidden_out, hidden_all.at[:, group]),
        (state_out, state_all.at[:, group]),
        (projected_out, projected_all.at[:, group]),
    ]
    for other in others:
        own.append((state_out.at[:, 0], state_all.at[:, other, 0]))
    own = [
        pltpu.make_async_copy(source, target, own_sem.at[i])
        for i, (source, target) in enumerate(own)
    ]
    for copy in own:
        copy.start()

    rest = pl.ds(1, steps)
    for j, other in enumerate(others):
        source = from_peer(j, others)
        state_row = row(3, state_out.at[:, rest], state_all.at[:, source, rest], j, other)
        state_row.wait_send()
        state_row.wait_recv()

    finish_hidden(5, pl.ds(head, steps - head))

    for copy in own:
        copy.wait()

    @pl.when(section == 0)
    def _():
        mine = pltpu.make_async_copy(x_out.at[0], x_all.at[0, group], base_sem)
        mine.start()
        for j, other in enumerate(others):
            copy = row(1, x_out.at[0], x_all.at[0, from_peer(j, others)], j, other)
            copy.wait_send()
            copy.wait_recv()
        mine.wait()

    @pl.when(section == 0)
    def _():
        for j, peer in enumerate(peers):
            source = peers[count - 2 - j]
            copy = input_copy(input_parts.at[:, :, peer], input_sums.at[:, :, source], j, peer)
            copy.wait_send()
            copy.wait_recv()
        rows_half = base_out.shape[1] // steps

        @pl.loop(0, steps)
        def _(t):
            total = input_parts[0, t, me].astype(F32) + input_parts[1, steps - 1 - t, me].astype(F32)
            for peer in peers:
                total = total + input_sums[0, t, peer].astype(F32)
                total = total + input_sums[1, steps - 1 - t, peer].astype(F32)
            at = pl.ds(pl.multiple_of(t * rows_half, rows_half), rows_half)
            for half in range(2):
                base_sum[half, at, :] = total[half * rows_half : (half + 1) * rows_half]

        base_out[...] = base_sum[...].astype(BF16)

    share_features(section).wait_send()
    share_features(1 - section).wait_recv()

    for j, other in enumerate(near):
        source = from_peer(j, near)
        pltpu.make_async_remote_copy(
            src_ref=gates_all.at[:, source, pl.ds(DEFER, steps - DEFER)],
            dst_ref=gates_all.at[:, source, pl.ds(DEFER, steps - DEFER)],
            send_sem=row_send.at[0, j],
            recv_sem=row_recv.at[0, j],
            device_id={"dp": other},
            device_id_type=MESH,
        ).wait_recv()
        projected_row = row(4, projected_out, projected_all.at[:, source], j, other)
        projected_row.wait_send()
        projected_row.wait_recv()


def recurrence(base_seq, live_seq, top_seq, layer_weights, features_all):
    w_in, w_state, bias, proj = layer_weights
    _, steps, rows, width = top_seq.shape
    cell_count = proj.shape[1]
    count = lax.axis_size("mp")
    groups = lax.axis_size("dp")
    weights = (bias, proj, w_in, w_state)
    dma = pltpu.SemaphoreType.DMA
    return pl.pallas_call(
        recurrence_kernel,
        out_shape=(
            jax.ShapeDtypeStruct((2, groups, steps, rows, width), BF16),
            jax.ShapeDtypeStruct((2, groups, steps + 1, rows, width), BF16),
            jax.ShapeDtypeStruct((2, groups, steps, rows, cell_count), BF16),
            jax.ShapeDtypeStruct((2, groups, steps, rows, 4 * cell_count), BF16),
            jax.ShapeDtypeStruct((2, groups, steps, rows, width), BF16),
            jax.ShapeDtypeStruct((2, steps * rows // 2, width // count), BF16),
            jax.ShapeDtypeStruct(features_all.shape, BF16),
        ),
        in_specs=[VMEM_SPEC] * 5 + [ANY_SPEC] * 3,
        out_specs=(*[ANY_SPEC] * 5, VMEM_SPEC, ANY_SPEC),
        input_output_aliases={7: 6},
        scratch_shapes=[
            pltpu.VMEM((2, steps, rows, width), BF16),
            pltpu.VMEM((2, steps + 1, rows, width), BF16),
            pltpu.VMEM((2, steps, rows, cell_count), BF16),
            pltpu.VMEM((2, steps, rows, width), BF16),
            pltpu.VMEM((2, steps, 4, rows, cell_count), F32),
            pltpu.VMEM((2, steps + 1, rows, cell_count), F32),
            pltpu.VMEM((2, steps, rows, width), F32),
            pltpu.VMEM((2, rows, 4 * cell_count), F32),
            pltpu.VMEM((2, rows, cell_count), F32),
            pltpu.VMEM((2, 2, count, rows, width), BF16),
            pltpu.VMEM((2, 2, count, rows, width), BF16),
            pltpu.VMEM((2, steps, rows, width), F32),
            pltpu.VMEM((2, SLOTS, rows, 4 * cell_count), BF16),
            dma,
            dma((2, 2, count - 1)),
            dma((2, 2, count)),
            dma((2, 2, count - 1)),
            dma((2, 2, count)),
            dma((2,)),
            dma((2, steps)),
            dma((2,)),
            dma((2, steps)),
            dma((2, SLOTS)),
            dma((2, SLOTS, groups - 1)),
            dma((groups + 2,)),
            dma((6, groups - 1)),
            dma((6, groups - 1)),
            pltpu.VMEM(w_in.shape, BF16),
            pltpu.VMEM(w_state.shape, BF16),
            dma((2, 2)),
            pltpu.VMEM((2, 4 * cell_count, width), BF16),
            pltpu.VMEM((2, 4 * cell_count, width), BF16),
            pltpu.VMEM((2, width, cell_count), BF16),
            pltpu.VMEM((2, steps, count, rows, width // count), BF16),
            pltpu.VMEM((2, steps, count, rows, width // count), BF16),
            dma((count - 1,)),
            dma((count - 1,)),
            pltpu.VMEM((2, steps * rows // 2, width // count), F32),
            dma,
            dma,
            dma((2,)),
            dma((2,)),
            dma((groups - 1,)),
            dma((groups - 1,)),
            dma((2,)),
            dma((2,)),
        ],
        compiler_params=pltpu.CompilerParams(
            collective_id=0, has_side_effects=True, vmem_limit_bytes=VMEM_LIMIT
        ),
        name="recurrence",
    )(base_seq, live_seq, top_seq, *weights, features_all)


def weight_grads(lefts, right, parts, only=None, done=(), widen=()):
    _, outer, pieces, inner, size = lefts[0].shape
    batch = right.shape[0]
    tokens = right.shape[1]
    inner = tokens // outer
    columns = right.shape[2] // parts
    block = min(512, columns)
    blocks = columns // block
    chunk = min(512, size)
    total = size * len(lefts)
    single = parts == 1
    chosen = 1 if only is not None else batch

    def entry(b):
        return b if only is None else only

    def left_entry(left, b):
        return entry(b) if left.shape[0] == batch else 0


    def kernel(*refs):
        left_refs = refs[: len(lefts)]
        right_refs = refs[len(lefts) : len(lefts) + parts]
        outs = len(lefts) + parts + len(done) + len(widen)
        out_refs = refs[outs : outs + len(lefts)]
        bias_out = refs[outs + len(lefts)]
        turned, ones = refs[-2:]
        if widen:
            refs[outs + len(lefts) + 1][...] = refs[outs - 1][...].astype(F32)

        @pl.when(pl.program_id(2) == 0)
        def _():
            for i, left in enumerate(left_refs):
                for offset in range(0, size, chunk):
                    at = i * size + offset
                    turned[at : at + chunk, :] = (
                        left[0, :, 0, :, offset : offset + chunk].reshape(tokens, chunk).T
                    )
            ones[...] = jnp.ones_like(ones)

        for i, out in enumerate(out_refs):

            @pl.loop(0, size // chunk)
            def _(step):
                at = pl.multiple_of(i * size + step * chunk, chunk)
                own = pl.multiple_of(step * chunk, chunk)
                left = turned[pl.ds(at, chunk), :]
                for part in range(parts):
                    value = jnp.dot(left, right_refs[part][0], preferred_element_type=F32)
                    if single:
                        out[0, pl.ds(own, chunk), :] = value
                    else:
                        out[0, pl.ds(own, chunk), part, :] = value

        for part in range(parts):
            bias_out[0, part : part + 1, :] = jnp.dot(
                ones[...], right_refs[part][0], preferred_element_type=F32
            )[:1]

    outputs = 4 * chosen * pieces * total * parts * columns
    return pl.pallas_call(
        kernel,
        out_shape=(
            *[
                jax.ShapeDtypeStruct(
                    (batch, pieces * size, *((parts,) * (not single)), columns), F32
                )
                for _ in lefts
            ],
            jax.ShapeDtypeStruct((batch, parts, columns), F32),
            *[jax.ShapeDtypeStruct(item.shape, F32) for item in widen],
        ),
        grid=(chosen, pieces, blocks),
        in_specs=[
            *[
                pl.BlockSpec(
                    (1, outer, 1, inner, size),
                    functools.partial(
                        lambda left, b, p, n: (left_entry(left, b), 0, p, 0, 0), left
                    ),
                )
                for left in lefts
            ],
            *[
                pl.BlockSpec(
                    (1, tokens, block),
                    functools.partial(lambda g, b, p, n: (entry(b), 0, g * blocks + n), g),
                )
                for g in range(parts)
            ],
            *[ANY_SPEC] * len(done),
            *[
                pl.BlockSpec((item.shape[0] // blocks, item.shape[1]), lambda b, p, n: (n, 0))
                for item in widen
            ],
        ],
        input_output_aliases={len(lefts) + parts + i: i for i in range(len(done))},
        out_specs=(
            *[
                pl.BlockSpec((1, size, block), lambda b, p, n: (entry(b), p, n))
                if single
                else pl.BlockSpec((1, size, parts, block), lambda b, p, n: (entry(b), p, 0, n))
                for _ in lefts
            ],
            pl.BlockSpec((1, parts, block), lambda b, p, n: (entry(b), 0, n)),
            *[
                pl.BlockSpec((item.shape[0] // blocks, item.shape[1]), lambda b, p, n: (n, 0))
                for item in widen
            ],
        ),
        scratch_shapes=[
            pltpu.VMEM((total, tokens), BF16),
            pltpu.VMEM((16, tokens), BF16),
        ],
        compiler_params=pltpu.CompilerParams(vmem_limit_bytes=VMEM_LIMIT),
        cost_estimate=pl.CostEstimate(
            flops=2 * chosen * pieces * total * tokens * parts * columns,
            bytes_accessed=outputs + 2 * right.size + 2 * batch * pieces * total * tokens,
            transcendentals=0,
        ),
        name="weight_grads",
    )(*lefts, *[right] * parts, *done, *widen)


def merge_kernel(d, first_ref, second_ref, gates_in, gates_all, staged, sems):
    far = 3 - lax.axis_index("dp")
    late = first_ref.shape[0]
    half_steps = gates_all.shape[2] // 2
    loads, stores = [], []
    for way, source in enumerate((first_ref, second_ref)):
        rows = pl.ds((way + 1) * half_steps - late, late)
        buffer = staged.at[way]
        loads.append(pltpu.make_async_copy(source, buffer, sems.at[way]))
        stores.append(pltpu.make_async_copy(buffer, gates_all.at[d, far, rows], sems.at[way]))
    for load in loads:
        load.start()
    for load, store in zip(loads, stores):
        load.wait()
        store.start()
    for store in stores:
        store.wait()


def send_late(late):
    beside = [(i, i + 1 - 2 * (i % 2)) for i in range(4)]
    across = [(i, (i + 2) % 4) for i in range(4)]
    return lax.ppermute(late[0], "dp", across), lax.ppermute(late[1], "dp", beside)


def merge_late(d, gates_all, moved):
    return pl.pallas_call(
        functools.partial(merge_kernel, d),
        out_shape=jax.ShapeDtypeStruct(gates_all.shape, BF16),
        in_specs=[ANY_SPEC] * 3,
        out_specs=ANY_SPEC,
        input_output_aliases={2: 0},
        scratch_shapes=[pltpu.VMEM((2, *moved[0].shape), BF16), pltpu.SemaphoreType.DMA((2,))],
        compiler_params=pltpu.CompilerParams(vmem_limit_bytes=VMEM_LIMIT),
        name="merge_late",
    )(*moved, gates_all)


def on_device(
    char_ids,
    row_lengths,
    top_grad,
    char_table,
    conv_weight,
    conv_bias,
    highway_weight,
    highway_bias,
    proj_weight,
    proj_bias,
    lstm_input,
    lstm_state,
    lstm_bias,
    lstm_proj,
):
    section = lax.axis_index("section")
    rows, steps, per_token = char_ids.shape
    proj_width = proj_weight.shape[1]
    half = rows // 2
    tokens = half * steps
    local = conv_weight.shape[2]
    emb = char_table.shape[1]
    padded = -(-(per_token + TAPS - 1) // 8) * 8
    vocabulary = -(-char_table.shape[0] // 8) * 8
    chars = lax.dynamic_slice_in_dim(char_ids, section * half, half, 0)
    chars = jnp.transpose(chars, (1, 0, 2)).reshape(tokens, per_token)
    ids = jnp.pad(chars, ((0, 0), (0, padded - per_token)), constant_values=-1)
    ids = ids.reshape(tokens // CHUNK, 1, CHUNK * padded)
    table = jnp.pad(
        jnp.tile(char_table, (1, TAPS)),
        ((0, vocabulary - char_table.shape[0]), (0, 128 - TAPS * emb)),
    )
    widths = filter_widths(lax.axis_index("mp") * local, local, local * lax.axis_size("mp"))
    tap_keep = jnp.arange(TAPS, dtype=jnp.int32)[:, None] < widths[None, :]
    row = jnp.arange(128, dtype=jnp.int32)[:, None]
    taps_padded = jnp.pad(
        conv_weight.reshape(TAPS * emb, local), ((0, 128 - TAPS * emb), (0, 0))
    )
    masked = jnp.where(
        row < emb * widths[None, :],
        taps_padded,
        jnp.where(
            row == TAPS * emb,
            conv_bias[None, :],
            jnp.where(row == TAPS * emb + widths[None, :], -1e30, 0.0).astype(BF16),
        ),
    )
    log_positions = jnp.log((per_token - widths + 1).astype(F32))[None, :]
    w_high = jnp.transpose(highway_weight, (0, 2, 1, 3))
    (
        base_pair,
        taps,
        peak,
        pooled,
        current,
        transform,
        gate,
        features_all,
        last_own,
        w_input,
        w_state,
    ) = cnn_forward(
        ids,
        (table, masked, log_positions, w_high, highway_bias, proj_weight, proj_bias[None]),
        lstm_input[0],
        lstm_state[0],
    )
    depth_count = highway_weight.shape[0]

    def all_tokens(values):
        return lax.all_gather(values, ("section", "dp"), axis=values.ndim - 2, tiled=True)

    last_features = all_tokens(last_own)
    top_seq = jnp.transpose(top_grad, (2, 1, 0, 3))
    live = (jnp.arange(steps, dtype=jnp.int32)[:, None] < row_lengths[None, :]).astype(F32)
    live_seq = jnp.broadcast_to(live[..., None], (steps, rows, 128))
    layer_weights = (
        w_input,
        w_state,
        lstm_bias[0],
        lstm_proj[0],
    )
    (
        x_all,
        all_states,
        hidden_all,
        gates_all,
        projected_all,
        base_shards,
        high_features,
    ) = recurrence(base_pair, live_seq, top_seq, layer_weights, features_all)
    (
        all_gates,
        all_projected,
        all_inputs,
        all_hidden,
        base_full,
        all_mixed,
        *late,
        small,
    ) = (
        cnn_backward(
            base_shards,
            (taps, peak, pooled, current, transform, gate),
            (proj_weight, w_high, masked, ids),
            (gates_all, projected_all, x_all, hidden_all, all_states),
        )
    )
    relayed = lax.axis_size("dp") == 4
    if relayed:
        moved_first = send_late(late[:2])
        moved_second = send_late(late[2:])
    all_base = base_full.reshape(-1, proj_width)

    def flat(values):
        return values.reshape(2, -1, values.shape[4])

    def one_piece(values):
        batch, groups, _, _, width = values.shape
        return values.reshape(batch, groups, 1, -1, width)

    own_proj = dot(last_features, all_base, 0, 0).astype(BF16)
    all_mixed, own_proj = lax.optimization_barrier((all_mixed, own_proj))
    proj_weight_low = lax.all_gather(own_proj, "mp", axis=0, tiled=True)
    proj_grad = weight_grads([one_piece(all_hidden)], flat(all_projected), 1)[0]
    batch, _, groups, count, _, _ = high_features.shape
    high_grad, high_bias_grad = weight_grads(
        [high_features.reshape(batch, 2 * groups, count, tokens, local)],
        all_mixed.reshape(batch, -1, 2 * local),
        2,
    )
    small, high_grad, proj_grad = lax.optimization_barrier((small, high_grad, proj_grad))
    small = lax.all_gather(small, ("section", "dp"), axis=0)
    states = one_piece(all_states)
    inputs = one_piece(all_inputs)
    if relayed:
        moved_first, high_grad, proj_grad = lax.optimization_barrier(
            (moved_first, high_grad, proj_grad)
        )
        all_gates = merge_late(0, all_gates, moved_first)
        done = weight_grads([inputs, states], flat(all_gates), 4, only=0)
        done, moved_second, all_gates = lax.optimization_barrier((done, moved_second, all_gates))
        all_gates = merge_late(1, all_gates, moved_second)
        input_grad, state_grad, bias_grad, proj_weight_grad = weight_grads(
            [inputs, states], flat(all_gates), 4, only=1, done=done, widen=(proj_weight_low,)
        )
    else:
        input_grad, state_grad, bias_grad = weight_grads([inputs, states], flat(all_gates), 4)
        proj_weight_grad = proj_weight_low.astype(F32)
    small, bias_grad = lax.optimization_barrier((small, bias_grad))
    small = jnp.sum(small.astype(F32), axis=0)
    conv_weight_grad = jnp.where(
        tap_keep[:, None, :], small[: TAPS * emb].reshape(conv_weight.shape), 0.0
    )
    table_grad = small[128:].reshape(-1, emb, local)
    table_grad = jnp.transpose(table_grad, (0, 2, 1)).reshape(-1, emb)[: char_table.shape[0]]
    return (
        table_grad,
        conv_weight_grad,
        small[TAPS * emb],
        high_grad,
        high_bias_grad,
        proj_weight_grad,
        jnp.sum(all_base.astype(F32), axis=0),
        input_grad.reshape(lstm_input.shape),
        state_grad.reshape(lstm_state.shape),
        bias_grad.reshape(lstm_bias.shape),
        proj_grad.reshape(lstm_proj.shape),
    )


def solution(mesh):
    return jax.shard_map(
        on_device,
        mesh=mesh,
        in_specs=(
            P("dp", None, None),
            P("dp"),
            P("dp", None, None, None),
            P(),
            P(None, None, "mp"),
            P("mp"),
            P(None, None, None, "mp"),
            P(None, None, "mp"),
            P(),
            P(),
            P("section", None, None, None, "mp"),
            P("section", None, None, None, "mp"),
            P("section", None, None, "mp"),
            P("section", None, "mp", None),
        ),
        out_specs=(
            P(),
            P(None, None, "mp"),
            P("mp"),
            P(None, None, None, "mp"),
            P(None, None, "mp"),
            P(),
            P(),
            P("section", None, None, None, "mp"),
            P("section", None, None, None, "mp"),
            P("section", None, None, "mp"),
            P("section", None, "mp", None),
        ),
        check_vma=False,
    )
```

```python
import functools

import jax
import jax.numpy as jnp
import numpy as np
from jax import lax
from jax.experimental import pallas as pl
from jax.experimental.pallas import tpu as pltpu
from jax.sharding import PartitionSpec as P

F32 = jnp.float32
BF16 = jnp.bfloat16
PERIODS = 32
TAPS = 7
VMEM_LIMIT = 62 * 1024 * 1024
SLOTS = 4
DEFER = 2
CHUNK = 16
TURN = 128
PER_TOKEN = 50
CHARS = 262


def dot(left, right, left_dim, right_dim):
    return lax.dot_general(
        left, right, (((left_dim,), (right_dim,)), ((), ())), preferred_element_type=F32
    )


def soft_clip(values):
    return 3.0 * jnp.tanh(values / 3.0)


def filter_widths(offset, amount, total):
    period = total // PERIODS
    in_period = (offset + jnp.arange(amount, dtype=jnp.int32)) % period
    widths = jnp.ones((amount,), jnp.int32)
    for exponent in range(6):
        widths = widths + (in_period * 64 >= period * 2**exponent).astype(jnp.int32)
    return widths


MESH = pl.DeviceIdType.MESH
VMEM_SPEC = pl.BlockSpec(memory_space=pltpu.VMEM)
ANY_SPEC = pl.BlockSpec(memory_space=pl.ANY)


def column_peers():
    count = lax.axis_size("mp")
    me = lax.axis_index("mp")
    return [lax.rem(me + j, count) for j in range(1, count)]


def greet(devices):
    barrier = pltpu.get_barrier_semaphore()
    for device in devices:
        pl.semaphore_signal(barrier, inc=1, device_id=device, device_id_type=MESH)
    pl.semaphore_wait(barrier, len(devices))


def remote(source, target, send, recv, device):
    return pltpu.make_async_remote_copy(
        src_ref=source,
        dst_ref=target,
        send_sem=send,
        recv_sem=recv,
        device_id=device,
        device_id_type=MESH,
    )


def one_hot_columns(ids, vocabulary):
    symbols = lax.broadcasted_iota(jnp.int32, (vocabulary, ids.shape[1]), 0)
    return (symbols == ids).astype(F32).astype(BF16)


def cnn_forward_kernel(
    ids_ref,
    table_ref,
    flags_ref,
    masked_ref,
    log_positions,
    b_high,
    b_proj,
    high_ref,
    proj_ref,
    input_ref,
    state_ref,
    base_out,
    taps_out,
    peak_out,
    pooled_out,
    current_out,
    transform_out,
    gate_out,
    features_all,
    last_out,
    input_out,
    state_out,
    features,
    w_high,
    w_proj,
    raw,
    turned,
    send_sem,
    recv_sem,
    base_send,
    base_recv,
    row_send,
    row_recv,
    own_sem,
    raw_sem,
    turned_sem,
    load_sem,
    relay_send,
    relay_recv,
):
    count = lax.axis_size("mp")
    me = lax.axis_index("mp")
    section = lax.axis_index("section")
    peers = column_peers()
    depth_count, tokens, local = current_out.shape
    chunk_rows = ids_ref.shape[2]
    padded = chunk_rows // CHUNK
    half = tokens // 2
    emb = 16
    block = min(256, local)
    loads = [
        pltpu.make_async_copy(high_ref, w_high, load_sem.at[0]),
        pltpu.make_async_copy(proj_ref, w_proj, load_sem.at[1]),
    ]
    for load in loads:
        load.start()
    groups = lax.axis_size("dp")
    group = lax.axis_index("dp")
    others = [lax.rem(group + j, groups) for j in range(1, groups)]
    relayed = groups == 4
    beside = group + 1 - 2 * lax.rem(group, 2)
    across = lax.rem(group + 2, 4)
    far = 3 - group
    near = [beside, across] if relayed else others
    origin = near if relayed else others[::-1]
    greet(
        [{"mp": peer} for peer in peers]
        + [{"section": 1 - section}]
        + [{"dp": other} for other in others]
    )

    def relay_rows(depth, way, slot):
        pieces = pl.ds(way * (count // 2), count // 2)
        return remote(
            features_all.at[depth, section, slot, pieces],
            features_all.at[depth, section, slot, pieces],
            relay_send.at[depth, way],
            relay_recv.at[depth, way],
            {"dp": across if way == 0 else beside},
        )

    def pass_rows(depth):
        for j in range(len(near)):
            give_rows(depth, j, origin[j]).wait_recv()
        if relayed:
            for way in range(2):
                relay_rows(depth, way, beside if way == 0 else across).start()

    blocks = input_out.shape[2] // TURN
    units = 4 * blocks

    def fetch(unit, start):
        slot = lax.rem(unit, 2)
        d = lax.rem(unit, 2 * blocks) // blocks
        rows = pl.ds(pl.multiple_of(lax.rem(unit, blocks) * TURN, TURN), TURN)
        for which, source in enumerate((input_ref, state_ref)):

            @pl.when(unit // (2 * blocks) == which)
            def _():
                copy = pltpu.make_async_copy(source.at[d, rows], raw.at[slot], raw_sem.at[slot])
                copy.start() if start else copy.wait()

    def deliver(unit, start):
        slot = lax.rem(unit, 2)
        d = lax.rem(unit, 2 * blocks) // blocks
        rows = pl.ds(pl.multiple_of(lax.rem(unit, blocks) * TURN, TURN), TURN)
        for which, target in enumerate((input_out, state_out)):

            @pl.when(unit // (2 * blocks) == which)
            def _():
                copy = pltpu.make_async_copy(
                    turned.at[slot], target.at[d, :, rows], turned_sem.at[slot]
                )
                copy.start() if start else copy.wait()

    def turn_units(first, last):
        @pl.loop(first, last)
        def _(unit):
            slot = lax.rem(unit, 2)
            fetch(unit, False)

            @pl.when(unit + 1 < units)
            def _():
                fetch(unit + 1, True)

            @pl.when(unit >= 2)
            def _():
                deliver(unit - 2, False)

            for g in range(4):
                turned[slot, g] = raw[slot, :, g, :]
            deliver(unit, True)

    fetch(0, True)

    def own_rows(depth):
        return pltpu.make_async_copy(
            features.at[depth], features_all.at[depth, section, group], own_sem.at[depth]
        )

    def give_rows(depth, j, slot):
        return remote(
            features.at[depth],
            features_all.at[depth, section, slot],
            row_send.at[depth, j],
            row_recv.at[depth, j],
            {"dp": near[j]},
        )

    def send(depth, part, rows, start):
        for j, peer in enumerate(peers):
            copy = remote(
                features.at[depth, me, rows],
                features.at[depth, me, rows],
                send_sem.at[depth, part, j],
                recv_sem.at[depth, part, me],
                {"mp": peer},
            )
            if start:
                copy.start()
            else:
                copy.wait_send()

    def receive(depth, part):
        rows = pl.ds(part * half, half)
        for j, peer in enumerate(peers):
            remote(
                features.at[depth, peer, rows],
                features.at[depth, peer, rows],
                send_sem.at[depth, part, j],
                recv_sem.at[depth, part, peer],
                {"mp": peer},
            ).wait_recv()

    lane_group = lax.broadcasted_iota(jnp.int32, (chunk_rows, 128), 1) // emb

    def pool_chunk(c):
        hot = one_hot_columns(ids_ref[c], table_ref.shape[0])
        embedded = lax.dot_general(
            hot, table_ref[...], (((0,), (0,)), ((), ())), preferred_element_type=F32
        )
        taps = embedded + flags_ref[...]
        for offset in range(1, TAPS):
            rolled = pltpu.roll(embedded, chunk_rows - offset, 0)
            taps = jnp.where(lane_group == offset, rolled, taps)
        taps = taps.astype(BF16)
        taps_out[c] = taps
        rows = pl.ds(pl.multiple_of(c * CHUNK, CHUNK), CHUNK)
        for start in range(0, local, block):
            cols = slice(start, start + block)
            scores = jnp.dot(taps, masked_ref[:, cols], preferred_element_type=F32)
            scores = scores.reshape(CHUNK, padded, block)
            top = jnp.max(scores, axis=1, keepdims=True)
            total = jnp.sum(jnp.exp(scores - top), axis=1, keepdims=True)
            peak = top + jnp.log(total)
            peak_out[rows, :, cols] = peak
            pooled = jnp.sum(peak, axis=1) - log_positions[:, cols]
            pooled_out[rows, cols] = pooled
            current = jnp.maximum(pooled, 0.0) + jnp.log1p(jnp.exp(-jnp.abs(pooled)))
            current_out[0, rows, cols] = current
            features[0, me, rows, cols] = current.astype(BF16)
        return rows

    for part in range(2):

        @pl.loop(0, half // CHUNK)
        def _(i):
            rows = pool_chunk(part * (half // CHUNK) + i)
            send(0, part, rows, True)

    for load in loads:
        load.wait()
    stops = [2, 2, 6, 9, 13, 16]
    turned_to = [0]

    def turn_some():
        stop = units * stops[min(turn_count[0], len(stops) - 1)] // 16
        turn_count[0] += 1
        if stop > turned_to[0]:
            turn_units(turned_to[0], stop)
            turned_to[0] = stop

    turn_count = [0]
    for depth in range(depth_count):
        for part in range(2):
            rows = pl.ds(part * half, half)
            turn_some()
            receive(depth, part)
            if part == 1:
                own_rows(depth).start()
                if depth + 1 < depth_count:
                    for j in range(len(near)):
                        give_rows(depth, j, group).start()
            mixed = []
            for g in range(2):
                total = jnp.broadcast_to(b_high[depth, g : g + 1, :].astype(F32), (half, local))
                for p in range(count):
                    total = total + jnp.dot(
                        features[depth, p, rows, :],
                        w_high[depth, g, p * local : (p + 1) * local, :],
                        preferred_element_type=F32,
                    )
                mixed.append(total)
            transform = mixed[0]
            gate = jax.nn.sigmoid(mixed[1])
            transform_out[depth, rows, :] = transform
            gate_out[depth, rows, :] = gate
            current = gate * current_out[depth, rows, :] + (1.0 - gate) * (
                transform * jax.nn.sigmoid(transform)
            )
            if depth + 1 < depth_count:
                current_out[depth + 1, rows, :] = current
            else:
                last_out[rows, :] = current.astype(BF16)
            features[depth + 1, me, rows, :] = current.astype(BF16)
            send(depth + 1, part, rows, True)
        if depth >= 1:
            pass_rows(depth - 1)

    def give():
        return remote(
            base_out.at[section],
            base_out.at[section],
            base_send,
            base_recv,
            {"section": 1 - section},
        )

    for part in range(2):
        rows = pl.ds(part * half, half)
        turn_some()
        receive(depth_count, part)
        total = jnp.broadcast_to(b_proj[...].astype(F32), (half, w_proj.shape[1]))
        for p in range(count):
            total = total + jnp.dot(
                features[depth_count, p, rows, :],
                w_proj[p * local : (p + 1) * local, :],
                preferred_element_type=F32,
            )
        base_out[section, rows, :] = total
    give().start()
    turn_units(turned_to[0], units)
    for depth in range(depth_count + 1):
        for part in range(2):
            send(depth, part, pl.ds(part * half, half), False)
    give().wait_send()
    remote(
        base_out.at[1 - section],
        base_out.at[1 - section],
        base_send,
        base_recv,
        {"section": 1 - section},
    ).wait_recv()
    for depth in range(depth_count):
        own_rows(depth).wait()
        if depth + 1 < depth_count:
            for j in range(len(near)):
                give_rows(depth, j, group).wait_send()
            if relayed:
                for way in range(2):
                    relay_rows(depth, way, beside if way == 0 else across).wait_send()
                    relay_rows(depth, way, far).wait_recv()
    for unit in range(units - 2, units):
        deliver(unit, False)


def cnn_forward(ids, weights, lstm_input, lstm_state):
    table, masked, log_positions, w_high, b_high, w_proj, b_proj = weights
    chunks, _, chunk_rows = ids.shape
    tokens = chunks * CHUNK
    depth_count, _, total, local = w_high.shape
    count = lax.axis_size("mp")
    groups = lax.axis_size("dp")
    directions, in_width, gate_blocks, cell_columns = lstm_input.shape
    padded = chunk_rows // CHUNK
    position = np.tile(np.arange(padded), CHUNK)[:, None]
    lane = np.arange(128)[None, :]
    excluded = lane - 16 * TAPS
    flags = (lane == 16 * TAPS) | (
        (excluded >= 1) & (excluded <= TAPS) & (position > PER_TOKEN - excluded)
    )
    dma = pltpu.SemaphoreType.DMA
    return pl.pallas_call(
        cnn_forward_kernel,
        out_shape=(
            jax.ShapeDtypeStruct((2, tokens, w_proj.shape[1]), F32),
            jax.ShapeDtypeStruct((chunks, chunk_rows, 128), BF16),
            jax.ShapeDtypeStruct((tokens, 1, local), F32),
            jax.ShapeDtypeStruct((tokens, local), F32),
            jax.ShapeDtypeStruct((depth_count, tokens, local), F32),
            jax.ShapeDtypeStruct((depth_count, tokens, local), F32),
            jax.ShapeDtypeStruct((depth_count, tokens, local), F32),
            jax.ShapeDtypeStruct((depth_count, 2, groups, count, tokens, local), BF16),
            jax.ShapeDtypeStruct((tokens, local), BF16),
            jax.ShapeDtypeStruct((directions, gate_blocks, in_width, cell_columns), BF16),
            jax.ShapeDtypeStruct((directions, gate_blocks, in_width, cell_columns), BF16),
        ),
        in_specs=[VMEM_SPEC] * 7 + [ANY_SPEC] * 4,
        out_specs=(*[VMEM_SPEC] * 7, ANY_SPEC, VMEM_SPEC, *[ANY_SPEC] * 2),
        scratch_shapes=[
            pltpu.VMEM((depth_count + 1, count, tokens, local), BF16),
            pltpu.VMEM(w_high.shape, BF16),
            pltpu.VMEM(w_proj.shape, BF16),
            pltpu.VMEM((2, TURN, gate_blocks, cell_columns), BF16),
            pltpu.VMEM((2, gate_blocks, TURN, cell_columns), BF16),
            dma((depth_count + 1, 2, count - 1)),
            dma((depth_count + 1, 2, count)),
            dma,
            dma,
            dma((depth_count, groups - 1)),
            dma((depth_count, groups - 1)),
            dma((depth_count,)),
            dma((2,)),
            dma((2,)),
            dma((2,)),
            dma((depth_count, 2)),
            dma((depth_count, 2)),
        ],
        compiler_params=pltpu.CompilerParams(
            collective_id=1, has_side_effects=True, vmem_limit_bytes=VMEM_LIMIT
        ),
        name="cnn_forward",
    )(
        ids,
        table,
        jnp.asarray(flags.astype(np.float32)),
        masked,
        log_positions,
        b_high,
        b_proj,
        w_high,
        w_proj,
        lstm_input,
        lstm_state,
    )


def cnn_backward_kernel(
    base_ref,
    own_ref,
    current_ref,
    transform_ref,
    gate_ref,
    peak_ref,
    pooled_ref,
    masked_ref,
    masked_t,
    ids_ref,
    high_ref,
    taps_hbm,
    gates_in,
    projected_in,
    x_in,
    hidden_in,
    state_all,
    gates_all,
    projected_all,
    x_all,
    hidden_all,
    base_full,
    mixed_all,
    late_a,
    late_b,
    late_c,
    late_d,
    small_out,
    w_high,
    taps_ref,
    load_sem,
    conv_out,
    mixed_out,
    late_buf,
    base_all,
    base_rows,
    table_sum,
    table_all,
    grad_current,
    outgoing,
    incoming,
    base_send,
    base_recv,
    sum_send,
    sum_recv,
    own_sem,
    relay_send,
    relay_recv,
    lift_send,
    lift_recv,
    row_send,
    row_recv,
    full_sem,
    share_send,
    share_recv,
    table_send,
    table_recv,
    mixed_sem,
    mixed_send,
    mixed_recv,
    mixed_share,
    mixed_shared,
    late_sem,
    defer_send,
    defer_recv,
    x_buf,
    flip_sem,
):
    count = lax.axis_size("mp")
    me = lax.axis_index("mp")
    section = lax.axis_index("section")
    groups = lax.axis_size("dp")
    group = lax.axis_index("dp")
    peers = column_peers()
    depth_count, tokens, local = current_ref.shape
    steps = x_all.shape[2]
    chunks, chunk_rows, _ = taps_ref.shape
    loads = [
        pltpu.make_async_copy(high_ref, w_high, load_sem.at[0]),
        pltpu.make_async_copy(taps_hbm, taps_ref, load_sem.at[1]),
    ]
    for load in loads:
        load.start()
    padded = chunk_rows // CHUNK
    emb = 16
    vocabulary = -(-CHARS // 8) * 8
    relayed = groups == 4
    beside = group + 1 - 2 * lax.rem(group, 2)
    across = lax.rem(group + 2, 4)
    far = 3 - group
    greet(
        [{"mp": peer} for peer in peers]
        + [{"section": 1 - section, "mp": peer} for peer in [*peers, me]]
        + [{"dp": lax.rem(group + j, groups)} for j in range(1, groups)]
    )

    def lift():
        return remote(
            state_all.at[:, :, pl.ds(1, steps)],
            x_all,
            lift_send,
            lift_recv,
            {"section": 1 - section},
        )

    half_steps = steps // 2
    others = [lax.rem(group + j, groups) for j in range(1, groups)]
    near = [beside, across] if relayed else others
    origin = near if relayed else others[::-1]

    def relay(kind, way, slot):
        head = steps * 7 // 10
        if kind == 0:
            block = projected_all.at[way, slot]
        else:
            block = hidden_all.at[way, slot, pl.ds(head, steps - head)]
        return remote(
            block,
            block,
            relay_send.at[kind, way],
            relay_recv.at[kind, way],
            {"dp": across if way == 0 else beside},
        )

    def deferred(j, slot):
        return remote(
            gates_all.at[:, slot, pl.ds(0, DEFER)],
            gates_all.at[:, slot, pl.ds(0, DEFER)],
            defer_send.at[j],
            defer_recv.at[j],
            {"dp": near[j]},
        )

    for j in range(len(near)):
        deferred(j, group).start()


    late_loads, late_stores = [], []
    for i, target in enumerate((late_a, late_b, late_c, late_d)):
        d, way = i // 2, i % 2
        rows = pl.ds(way * half_steps, half_steps)
        source = gates_all.at[d, (beside, across)[way], rows]
        late_loads.append(pltpu.make_async_copy(source, late_buf.at[i], late_sem.at[i]))
        late_stores.append(pltpu.make_async_copy(late_buf.at[i], target, late_sem.at[i]))

    def spread_base(half, target_section, peer, j):
        return remote(
            base_ref.at[half],
            base_all.at[me],
            base_send.at[half, j],
            base_recv.at[me],
            {"section": target_section, "mp": peer},
        )

    everyone = [*peers, me]

    x_load = pltpu.make_async_copy(x_all.at[0], x_buf, flip_sem.at[0])

    @pl.when(section == 0)
    def _():
        x_load.start()
        for j, peer in enumerate(peers):
            spread_base(0, 0, peer, j).start()
        for j, peer in enumerate(everyone):
            spread_base(1, 1, peer, j).start()
        lift().start()
        own = pltpu.make_async_copy(base_ref.at[0], base_all.at[me], own_sem)
        own.start()
        own.wait()

    def base_arrival(source):
        return remote(
            base_ref.at[0],
            base_all.at[source],
            base_send.at[0, 0],
            base_recv.at[source],
            {"section": 1 - section},
        )

    for peer in peers:
        base_arrival(peer).wait_recv()

    @pl.when(section == 1)
    def _():
        base_arrival(me).wait_recv()

    wide = base_all.shape[2]
    for p in range(count):
        base_rows[:, p * wide : (p + 1) * wide] = base_all[p]
    keep = pltpu.make_async_copy(base_rows, base_full.at[section, group], full_sem)
    keep.start()

    def base_row(j, slot):
        return remote(
            base_rows,
            base_full.at[section, slot],
            row_send.at[j],
            row_recv.at[j],
            {"dp": others[j]},
        )

    def share_base(owner):
        return remote(
            base_full.at[owner],
            base_full.at[owner],
            share_send,
            share_recv,
            {"section": 1 - section},
        )

    for j in range(groups - 1):
        base_row(j, group).start()

    def keep_mixed(depth):
        return pltpu.make_async_copy(
            mixed_out.at[depth], mixed_all.at[depth, section, group], mixed_sem.at[depth]
        )

    def mixed_row(depth, j, slot):
        return remote(
            mixed_out.at[depth],
            mixed_all.at[depth, section, slot],
            mixed_send.at[depth, j],
            mixed_recv.at[depth, j],
            {"dp": others[j]},
        )

    def share_mixed(depth, owner):
        return remote(
            mixed_all.at[depth, owner],
            mixed_all.at[depth, owner],
            mixed_share.at[depth],
            mixed_shared.at[depth],
            {"section": 1 - section},
        )

    def collect_mixed(depth):
        keep_mixed(depth).wait()
        for j in range(groups - 1):
            mixed_row(depth, j, others[groups - 2 - j]).wait_recv()
        share_mixed(depth, section).start()

    own_rows = pl.ds(pl.multiple_of(me * local, local), local)
    total = jnp.zeros((tokens, local), F32)
    for p in range(count):
        total = total + lax.dot_general(
            base_all[p],
            own_ref[own_rows, p * wide : (p + 1) * wide],
            (((1,), (1,)), ((), ())),
            preferred_element_type=F32,
        )
    grad_current[...] = total

    def send_sum(depth, peer, j):
        return remote(
            outgoing.at[depth, j],
            incoming.at[depth, me],
            sum_send.at[depth, j],
            sum_recv.at[depth, me],
            {"mp": peer},
        )

    def back(depth, owner):
        rows = pl.ds(pl.multiple_of(owner * local, local), local)
        parts = [
            lax.dot_general(
                mixed_out[depth, :, g * local : (g + 1) * local],
                w_high[depth, g, rows, :],
                (((1,), (1,)), ((), ())),
                preferred_element_type=F32,
            )
            for g in range(2)
        ]
        return parts[0] + parts[1]

    for load in loads:
        load.wait()
    for depth in range(depth_count - 1, -1, -1):
        transform = transform_ref[depth]
        gate = gate_ref[depth]
        grad = grad_current[...]
        slope = jax.nn.sigmoid(transform)
        mixed_out[depth, :, :local] = (
            grad * (1.0 - gate) * slope * (1.0 + transform * (1.0 - slope))
        ).astype(BF16)
        mixed_out[depth, :, local:] = (
            grad * (current_ref[depth] - transform * slope) * gate * (1.0 - gate)
        ).astype(BF16)
        keep_mixed(depth).start()
        for j in range(groups - 1):
            mixed_row(depth, j, group).start()
        if relayed and depth == depth_count - 1:
            for kind in range(2):
                for way in range(2):
                    relay(kind, way, beside if way == 0 else across).start()
        for j, peer in enumerate(peers):
            outgoing[depth, j] = back(depth, peer).astype(BF16)
            send_sum(depth, peer, j).start()
        total = grad * gate + back(depth, me)
        for j, peer in enumerate(peers):
            remote(
                outgoing.at[depth, j],
                incoming.at[depth, peer],
                sum_send.at[depth, j],
                sum_recv.at[depth, peer],
                {"mp": peer},
            ).wait_recv()
            total = total + incoming[depth, peer].astype(F32)
        grad_current[...] = total

    for j in range(len(near)):
        deferred(j, group).wait_send()
        deferred(j, origin[j]).wait_recv()
    if relayed:
        for load in late_loads:
            load.start()
    for depth in range(depth_count - 1, 0, -1):
        collect_mixed(depth)
    if relayed:
        for load, store in zip(late_loads, late_stores):
            load.wait()
            store.start()
    @pl.when(section == 0)
    def _():
        x_load.wait()

        @pl.loop(0, steps)
        def _(t):
            for q in range(groups):
                pltpu.make_async_copy(
                    x_buf.at[q, t], x_all.at[1, q, steps - 1 - t], flip_sem.at[1]
                ).start()

    grad_current[...] = grad_current[...] * jax.nn.sigmoid(pooled_ref[...])
    conv_out[...] = jnp.zeros_like(conv_out)
    small_out[...] = jnp.zeros_like(small_out)
    table_sum[...] = jnp.zeros_like(table_sum)
    lane_group = lax.broadcasted_iota(jnp.int32, (chunk_rows, 128), 1) // emb

    @pl.loop(0, chunks)
    def _(c):
        rows = pl.ds(pl.multiple_of(c * CHUNK, CHUNK), CHUNK)
        taps = taps_ref[c]
        scores = jnp.dot(taps, masked_ref[...], preferred_element_type=F32)
        scores = scores.reshape(CHUNK, padded, local)
        share = jnp.exp(scores - peak_ref[rows])
        grads = share * grad_current[rows, :][:, None, :]
        grads = grads.reshape(chunk_rows, local).astype(BF16)
        conv_out[...] += lax.dot_general(
            taps, grads, (((0,), (0,)), ((), ())), preferred_element_type=F32
        )
        back_taps = jnp.dot(grads, masked_t[...], preferred_element_type=F32)
        moved = back_taps
        for offset in range(1, TAPS):
            moved = jnp.where(lane_group == offset, pltpu.roll(back_taps, offset, 0), moved)
        hot = one_hot_columns(ids_ref[c], vocabulary)
        table_sum[:vocabulary, :] += jnp.dot(
            hot, moved.astype(BF16), preferred_element_type=F32
        )

    columns = table_sum[...].T
    folded = columns[:emb]
    for offset in range(1, TAPS):
        folded = folded + columns[offset * emb : (offset + 1) * emb]
    table_all[me] = folded

    def table_copy(j, slot):
        return remote(
            table_all.at[slot],
            table_all.at[slot],
            table_send.at[j],
            table_recv.at[slot],
            {"mp": peers[j]},
        )

    for j in range(count - 1):
        table_copy(j, me).start()

    for j in range(count - 1):
        table_copy(j, peers[j]).wait_recv()
    folded = table_all[0]
    for p in range(1, count):
        folded = folded + table_all[p]
    small_out[:128, :] = conv_out[...].astype(BF16)
    span = min(local, folded.shape[1])
    for i in range(folded.shape[1] // span):
        at = 128 + i * emb
        small_out[at : at + emb, :span] = folded[:, i * span : (i + 1) * span].astype(BF16)
    for j in range(count - 1):
        table_copy(j, me).wait_send()
    keep.wait()
    for j in range(groups - 1):
        base_row(j, others[groups - 2 - j]).wait_recv()
    share_base(section).start()
    collect_mixed(0)
    for j in range(groups - 1):
        base_row(j, group).wait_send()
        for depth in range(depth_count):
            mixed_row(depth, j, group).wait_send()
    for depth in range(depth_count):
        for j, peer in enumerate(peers):
            send_sum(depth, peer, j).wait_send()

    @pl.when(section == 0)
    def _():
        for j, peer in enumerate(peers):
            spread_base(0, 0, peer, j).wait_send()
        for j, peer in enumerate(everyone):
            spread_base(1, 1, peer, j).wait_send()
        lift().wait_send()
        pltpu.make_async_copy(x_buf, x_all.at[1], flip_sem.at[1]).wait()

    @pl.when(section == 1)
    def _():
        lift().wait_recv()

    if relayed:
        for kind in range(2):
            for way in range(2):
                relay(kind, way, beside if way == 0 else across).wait_send()
                relay(kind, way, far).wait_recv()
        for copy in late_stores:
            copy.wait()

    share_base(section).wait_send()
    share_base(1 - section).wait_recv()
    for depth in range(depth_count):
        share_mixed(depth, section).wait_send()
        share_mixed(depth, 1 - section).wait_recv()


def cnn_backward(base_shards, saved, weights, rows_all):
    w_proj, w_high, masked, ids = weights
    taps, peak, pooled, current, transform, gate = saved
    gates_all, projected_all, x_all, hidden_all, state_all = rows_all
    depth_count, tokens, local = current.shape
    count = lax.axis_size("mp")
    groups = lax.axis_size("dp")
    vocabulary = -(-CHARS // 128) * 128
    half_steps = gates_all.shape[2] // 2
    late = (half_steps, *gates_all.shape[3:])
    dma = pltpu.SemaphoreType.DMA
    return pl.pallas_call(
        cnn_backward_kernel,
        out_shape=(
            jax.ShapeDtypeStruct(gates_all.shape, BF16),
            jax.ShapeDtypeStruct(projected_all.shape, BF16),
            jax.ShapeDtypeStruct(x_all.shape, BF16),
            jax.ShapeDtypeStruct(hidden_all.shape, BF16),
            jax.ShapeDtypeStruct((2, groups, tokens, count * base_shards.shape[2]), BF16),
            jax.ShapeDtypeStruct((depth_count, 2, groups, tokens, 2 * local), BF16),
            *[jax.ShapeDtypeStruct(late, BF16)] * 4,
            jax.ShapeDtypeStruct((128 + 16 * max(1, vocabulary // local), local), BF16),
        ),
        in_specs=[VMEM_SPEC] * 10 + [ANY_SPEC] * 7,
        out_specs=(*[ANY_SPEC] * 10, VMEM_SPEC),
        input_output_aliases={12: 0, 13: 1, 14: 2, 15: 3},
        scratch_shapes=[
            pltpu.VMEM(w_high.shape, BF16),
            pltpu.VMEM(taps.shape, BF16),
            dma((2,)),
            pltpu.VMEM((128, local), F32),
            pltpu.VMEM((depth_count, tokens, 2 * local), BF16),
            pltpu.VMEM((4, *late), BF16),
            pltpu.VMEM((count, tokens, base_shards.shape[2]), BF16),
            pltpu.VMEM((tokens, count * base_shards.shape[2]), BF16),
            pltpu.VMEM((vocabulary, 128), F32),
            pltpu.VMEM((count, 16, vocabulary), F32),
            pltpu.VMEM((tokens, local), F32),
            pltpu.VMEM((depth_count, count - 1, tokens, local), BF16),
            pltpu.VMEM((depth_count, count, tokens, local), BF16),
            dma((2, count)),
            dma((count,)),
            dma((depth_count, count - 1)),
            dma((depth_count, count)),
            dma,
            dma((2, 2)),
            dma((2, 2)),
            dma,
            dma,
            dma((groups - 1,)),
            dma((groups - 1,)),
            dma,
            dma,
            dma,
            dma((count - 1,)),
            dma((count,)),
            dma((depth_count,)),
            dma((depth_count, groups - 1)),
            dma((depth_count, groups - 1)),
            dma((depth_count,)),
            dma((depth_count,)),
            dma((4,)),
            dma((groups - 1,)),
            dma((groups - 1,)),
            pltpu.VMEM(x_all.shape[1:], BF16),
            dma((2,)),
        ],
        compiler_params=pltpu.CompilerParams(
            collective_id=2, has_side_effects=True, vmem_limit_bytes=VMEM_LIMIT
        ),
        name="cnn_backward",
    )(
        base_shards,
        w_proj,
        current,
        transform,
        gate,
        peak,
        pooled,
        masked,
        jnp.pad(masked[: 16 * TAPS], ((0, 128 - 16 * TAPS), (0, 0))).T,
        ids,
        w_high,
        taps,
        gates_all,
        projected_all,
        x_all,
        hidden_all,
        state_all,
    )


def recurrence_kernel(
    base_ref,
    live_ref,
    top_ref,
    bias_ref,
    proj_ref,
    in_ref,
    state_ref,
    features_in,
    x_all,
    state_all,
    hidden_all,
    gates_all,
    projected_all,
    base_out,
    features_all,
    x_out,
    state_out,
    hidden_out,
    projected_out,
    acts,
    cells,
    clips,
    pre,
    grad_cell,
    parts,
    back_parts,
    above,
    gate_buf,
    base_sem,
    send_sem,
    recv_sem,
    back_send,
    back_recv,
    x_send,
    x_recv,
    above_send,
    above_recv,
    gate_sem,
    gate_send,
    own_sem,
    row_send,
    row_recv,
    w_in,
    w_state,
    load_sem,
    w_in_t,
    w_state_t,
    proj_t,
    input_parts,
    input_sums,
    input_send,
    input_recv,
    base_sum,
    share_send,
    share_recv,
    relay_send,
    relay_recv,
    feature_send,
    feature_recv,
    hidden_send,
    hidden_recv,
):
    count = lax.axis_size("mp")
    me = lax.axis_index("mp")
    section = lax.axis_index("section")
    steps = x_out.shape[1]
    cell_count = proj_ref.shape[1]
    chunk = min(256, cell_count)
    peers = [lax.rem(me + j, count) for j in range(1, count)]
    groups = lax.axis_size("dp")
    group = lax.axis_index("dp")
    others = [lax.rem(group + j, groups) for j in range(1, groups)]
    relayed = groups == 4
    beside = group + 1 - 2 * lax.rem(group, 2)
    across = lax.rem(group + 2, 4)
    near = [beside, across] if relayed else others
    loads = [
        [pltpu.make_async_copy(source.at[d], target.at[d], load_sem.at[i, d]) for d in range(2)]
        for i, (source, target) in enumerate(((in_ref, w_in), (state_ref, w_state)))
    ]
    for d in range(2):
        loads[0][d].start()
    for d in range(2):
        loads[1][d].start()

    barrier = pltpu.get_barrier_semaphore()
    for peer in peers:
        pl.semaphore_signal(barrier, inc=1, device_id={"mp": peer}, device_id_type=MESH)
    pl.semaphore_signal(barrier, inc=1, device_id={"section": 1 - section}, device_id_type=MESH)
    for other in others:
        pl.semaphore_signal(barrier, inc=1, device_id={"dp": other}, device_id_type=MESH)
    pl.semaphore_wait(barrier, count + groups - 1)

    def share_features(owner):
        return remote(
            features_all.at[:, owner],
            features_all.at[:, owner],
            share_send,
            share_recv,
            {"section": 1 - section},
        )

    pieces = features_all.shape[3]

    last_depth = features_all.shape[0] - 1

    def give_features(j, slot):
        return remote(
            features_all.at[last_depth, section, slot],
            features_all.at[last_depth, section, slot],
            feature_send.at[j],
            feature_recv.at[j],
            {"dp": near[j]},
        )

    def relay_features(way, slot):
        half = pl.ds(way * (pieces // 2), pieces // 2)
        block = features_all.at[last_depth, section, slot, half]
        return remote(
            block,
            block,
            relay_send.at[way],
            relay_recv.at[way],
            {"dp": across if way == 0 else beside},
        )

    def start_relays():
        if relayed:
            for way in range(2):
                relay_features(way, beside if way == 0 else across).start()

    def finish_relays():
        if relayed:
            for way in range(2):
                relay_features(way, beside if way == 0 else across).wait_send()
                relay_features(way, 3 - group).wait_recv()

    for j in range(len(near)):
        give_features(j, group).start()

    def wide(values, width):
        return jnp.concatenate([values] * (width // values.shape[1]), axis=1)

    def copy_part(buffer, send, recv, d, parity, source, j, target):
        return pltpu.make_async_remote_copy(
            src_ref=buffer.at[d, parity, source],
            dst_ref=buffer.at[d, parity, source],
            send_sem=send.at[d, parity, j],
            recv_sem=recv.at[d, parity, source],
            device_id={"mp": target},
            device_id_type=MESH,
        )

    ordered = peers
    if count == 4:
        ordered = [3 - me, lax.rem(me + 2, 4), me + 1 - 2 * lax.rem(me, 2)]

    def exchange_start(buffer, send, recv, d, parity, value):
        buffer[d, parity, me] = value.astype(BF16)
        for j, peer in enumerate(ordered):
            copy_part(buffer, send, recv, d, parity, me, j, peer).start()

    def exchange_wait(buffer, send, recv, d, parity):
        for j, peer in enumerate(ordered):
            copy_part(buffer, send, recv, d, parity, peer, j, peer).wait_recv()
        total = buffer[d, parity, 0].astype(F32)
        for source in range(1, count):
            total = total + buffer[d, parity, source].astype(F32)
        for j, peer in enumerate(ordered):
            copy_part(buffer, send, recv, d, parity, me, j, peer).wait_send()
        return total

    def pass_up(d, k):
        return pltpu.make_async_remote_copy(
            src_ref=state_out.at[d, k + 1],
            dst_ref=x_out.at[d, k],
            send_sem=x_send.at[d],
            recv_sem=x_recv.at[d, k],
            device_id={"section": 1 - section},
            device_id_type=MESH,
        )

    def pass_down(d, k):
        return pltpu.make_async_remote_copy(
            src_ref=above.at[d, k],
            dst_ref=above.at[d, k],
            send_sem=above_send.at[d],
            recv_sem=above_recv.at[d, k],
            device_id={"section": 1 - section},
            device_id_type=MESH,
        )

    def gates_copy(d, k, slot):
        return pltpu.make_async_copy(
            gate_buf.at[d, slot], gates_all.at[d, group, k], gate_sem.at[d, slot]
        )

    def gates_row(d, k, slot, j, other):
        return pltpu.make_async_remote_copy(
            src_ref=gate_buf.at[d, slot],
            dst_ref=gates_all.at[d, group, k],
            send_sem=gate_send.at[d, slot, j],
            recv_sem=row_recv.at[0, j],
            device_id={"dp": other},
            device_id_type=MESH,
        )

    def row(kind, source, target, j, other):
        return pltpu.make_async_remote_copy(
            src_ref=source,
            dst_ref=target,
            send_sem=row_send.at[kind, j],
            recv_sem=row_recv.at[kind, j],
            device_id={"dp": other},
            device_id_type=MESH,
        )

    def from_peer(j, targets):
        back = len(targets) - 1 - j
        return targets[j] if relayed and len(targets) == 2 else targets[back]

    head = steps * 7 // 10

    def relay_hidden(way, slot):
        block = hidden_all.at[way, slot, pl.ds(0, head)]
        return remote(
            block,
            block,
            hidden_send.at[way],
            hidden_recv.at[way],
            {"dp": across if way == 0 else beside},
        )

    def finish_hidden(kind, some):
        for j, other in enumerate(near):
            target = hidden_all.at[:, from_peer(j, near), some]
            copy = row(kind, hidden_out.at[:, some], target, j, other)
            copy.wait_send()
            copy.wait_recv()

    def time_of(d, k):
        return k if d == 0 else steps - 1 - k

    @pl.when(section == 0)
    def _():
        part_rows = base_ref.shape[1] // steps

        @pl.loop(0, steps)
        def _(t):
            at = pl.ds(pl.multiple_of(t * part_rows, part_rows), part_rows)
            x = jnp.concatenate([base_ref[0, at, :], base_ref[1, at, :]], axis=0).astype(BF16)
            for d in range(2):
                x_out[d, time_of(d, t)] = x

        for j, other in enumerate(others):
            row(1, x_out.at[0], x_all.at[0, group], j, other).start()

    for d in range(2):
        state_out[d, 0] = jnp.zeros(state_out.shape[2:], BF16)
        cells[d, 0] = jnp.zeros(cells.shape[2:], F32)
        grad_cell[d] = jnp.zeros(grad_cell.shape[1:], F32)

    def input_part(d, k):
        @pl.when(section == 1)
        def _():
            pass_up(d, k).wait_recv()

        x = x_out[d, k]
        for block in range(4):
            for start in range(0, cell_count, chunk):
                cols = slice(block * cell_count + start, block * cell_count + start + chunk)
                bias = bias_ref[d, block : block + 1, start : start + chunk].astype(F32)
                pre[d, :, cols] = bias + jnp.dot(
                    x, w_in[d, block, :, start : start + chunk], preferred_element_type=F32
                )

    def turn_weights(unit):
        per_block = cell_count // chunk
        block = unit // per_block
        cols = pl.ds(pl.multiple_of(lax.rem(unit, per_block) * chunk, chunk), chunk)
        rows_t = pl.ds(pl.multiple_of(unit * chunk, chunk), chunk)
        for d in range(2):
            w_in_t[d, rows_t, :] = w_in[d, block, :, cols].T
            w_state_t[d, rows_t, :] = w_state[d, block, :, cols].T

    def turn_proj(unit):
        cols = pl.ds(pl.multiple_of(unit * 128, 128), 128)
        for d in range(2):
            proj_t[d, :, cols] = proj_ref[d, cols, :].T

    def forward_cells(d, k):
        state = state_out[d, k]
        live = live_ref[time_of(d, k)]
        for start in range(0, cell_count, chunk):
            raw = []
            for block in range(4):
                cols = slice(block * cell_count + start, block * cell_count + start + chunk)
                raw.append(
                    pre[d, :, cols]
                    + jnp.dot(
                        state, w_state[d, block, :, start : start + chunk], preferred_element_type=F32
                    )
                )
            own = slice(start, start + chunk)
            in_gate = jax.nn.sigmoid(raw[0])
            forget = jax.nn.sigmoid(raw[1])
            memory = jnp.tanh(raw[2])
            out_gate = jax.nn.sigmoid(raw[3])
            for block, value in enumerate((in_gate, forget, memory, out_gate)):
                acts[d, k, block, :, own] = value
            cell_new = soft_clip(in_gate * memory + forget * cells[d, k, :, own])
            cells[d, k + 1, :, own] = wide(live, chunk) * cell_new
            hidden_out[d, k, :, own] = (out_gate * jnp.tanh(cell_new)).astype(BF16)
        part = jnp.dot(hidden_out[d, k], proj_ref[d], preferred_element_type=F32)
        exchange_start(parts, send_sem, recv_sem, d, lax.rem(k, 2), part)
        for j, other in enumerate(near):
            kind = 2 + 3 * (k // head)
            row(kind, hidden_out.at[d, k], hidden_all.at[d, group, k], j, other).start()

    def forward_state(d, k):
        total = exchange_wait(parts, send_sem, recv_sem, d, lax.rem(k, 2))
        clip = jnp.tanh(total / 3.0)
        clips[d, k] = clip
        live = wide(live_ref[time_of(d, k)], clip.shape[1])
        state_out[d, k + 1] = (live * 3.0 * clip).astype(BF16)

        @pl.when(section == 0)
        def _():
            @pl.when(k > 0)
            def _():
                pass_up(d, k - 1).wait_send()

            pass_up(d, k).start()

        for j, other in enumerate(others):
            row(3, state_out.at[d, k + 1], state_all.at[d, group, k + 1], j, other).start()

    units = 4 * cell_count // chunk
    for d in range(2):
        loads[0][d].wait()
        input_part(d, 0)
    for d in range(2):
        loads[1][d].wait()
        forward_cells(d, 0)
    for d in range(2):
        input_part(d, 1)

    @pl.loop(1, steps)
    def _(k):
        for d in range(2):
            forward_state(d, k - 1)
            forward_cells(d, k)

        @pl.when(k + 1 < steps)
        def _():
            for d in range(2):
                input_part(d, k + 1)

        @pl.when(k <= units)
        def _():
            turn_weights(k - 1)

        @pl.when(k == steps - 3)
        def _():
            finish_hidden(2, pl.ds(0, head))
            if relayed:
                for way in range(2):
                    relay_hidden(way, beside if way == 0 else across).start()

        @pl.when(k == steps - 5)
        def _():
            for j in range(len(near)):
                give_features(j, group).wait_send()
                give_features(j, from_peer(j, near)).wait_recv()
            start_relays()

        @pl.when(k <= cell_count // 128)
        def _():
            turn_proj(k - 1)

    for unit in range(steps - 1, units):
        turn_weights(unit)
    for d in range(2):
        forward_state(d, steps - 1)

    @pl.when(section == 0)
    def _():
        for d in range(2):
            pass_up(d, steps - 1).wait_send()

    def back_wait(d, parity):
        return exchange_wait(back_parts, back_send, back_recv, d, parity)

    def back_start(d, parity, value):
        exchange_start(back_parts, back_send, back_recv, d, parity, value)

    def backward_cells(d, k, total):
        slot = lax.rem(k, SLOTS)
        live = live_ref[time_of(d, k)]
        clip = clips[d, k]
        grad_out = wide(live, clip.shape[1]) * (total + top_ref[d, time_of(d, k)].astype(F32))
        grad_projected = (grad_out * (1.0 - clip * clip)).astype(BF16)
        projected_out[d, k] = grad_projected

        for j, other in enumerate(near):
            row(
                4, projected_out.at[d, k], projected_all.at[d, group, k], j, other
            ).start()

        @pl.when(k < steps - SLOTS)
        def _():
            gates_copy(d, k + SLOTS, slot).wait()
            for j, other in enumerate(near):
                gates_row(d, k + SLOTS, slot, j, other).wait_send()

        for start in range(0, cell_count, chunk):
            own = slice(start, start + chunk)
            grad_hidden = jnp.dot(grad_projected, proj_t[d, :, own], preferred_element_type=F32)
            in_gate, forget, memory, out_gate = [acts[d, k, block, :, own] for block in range(4)]
            cell = cells[d, k, :, own]
            clip_raw = jnp.tanh((in_gate * memory + forget * cell) / 3.0)
            tanh_cell = jnp.tanh(3.0 * clip_raw)
            grad_new = wide(live, chunk) * grad_cell[d, :, own] + grad_hidden * out_gate * (
                1.0 - tanh_cell * tanh_cell
            )
            grad_raw = grad_new * (1.0 - clip_raw * clip_raw)
            grad_cell[d, :, own] = grad_raw * forget
            grads = (
                grad_raw * memory * in_gate * (1.0 - in_gate),
                grad_raw * cell * forget * (1.0 - forget),
                grad_raw * in_gate * (1.0 - memory * memory),
                grad_hidden * tanh_cell * out_gate * (1.0 - out_gate),
            )
            for block, value in enumerate(grads):
                cols = slice(block * cell_count + start, block * cell_count + start + chunk)
                gate_buf[d, slot, :, cols] = value.astype(BF16)
        gates_copy(d, k, slot).start()

    def gates_send(d, k):
        @pl.when(k >= DEFER)
        def _():
            for j, other in enumerate(near):
                gates_row(d, k, lax.rem(k, SLOTS), j, other).start()

    def backward_state(d, k):
        @pl.when(k > 0)
        def _():
            back = jnp.dot(gate_buf[d, lax.rem(k, SLOTS)], w_state_t[d], preferred_element_type=F32)
            pre[d, :, : back.shape[1]] = back

            @pl.when(section == 0)
            def _():
                pass_down(d, k - 1).wait_recv()
                pre[d, :, : back.shape[1]] = back + above[d, k - 1]

            back_start(d, lax.rem(k - 1, 2), pre[d, :, : back.shape[1]])

    share = base_out.shape[2]

    def input_copy(source, target, j, peer):
        return remote(source, target, input_send.at[j], input_recv.at[j], {"mp": peer})

    def backward_input(d, k):
        gates_send(d, k)
        part = jnp.dot(gate_buf[d, lax.rem(k, SLOTS)], w_in_t[d], preferred_element_type=F32)

        @pl.when(section == 1)
        def _():
            above[d, k] = part

            @pl.when(k < steps - 1)
            def _():
                pass_down(d, k + 1).wait_send()

            pass_down(d, k).start()

        @pl.when(section == 0)
        def _():
            for p in range(count):
                input_parts[d, k, p] = part[:, p * share : (p + 1) * share].astype(BF16)
            for j, peer in enumerate(peers):
                input_copy(input_parts.at[d, k, peer], input_sums.at[d, k, me], j, peer).start()

    last = steps - 1

    @pl.when(section == 0)
    def _():
        for d in range(2):
            pass_down(d, last).wait_recv()
            back_start(d, lax.rem(last, 2), above[d, last])

    for d in range(2):

        @pl.when(section == 0)
        def _():
            pre[d, :, : clips.shape[3]] = back_wait(d, lax.rem(last, 2))

        @pl.when(section == 1)
        def _():
            pre[d, :, : clips.shape[3]] = jnp.zeros(clips.shape[2:], F32)

        backward_cells(d, last, pre[d, :, : clips.shape[3]])
        backward_state(d, last)
    for d in range(2):
        backward_input(d, last)

    @pl.loop(1, steps)
    def _(tick):
        k = last - tick
        for d in range(2):
            backward_cells(d, k, back_wait(d, lax.rem(k, 2)))
            backward_state(d, k)
        for d in range(2):
            backward_input(d, k)

        @pl.when(tick == 5)
        def _():
            finish_relays()
            share_features(section).start()
            if relayed:
                for way in range(2):
                    relay_hidden(way, beside if way == 0 else across).wait_send()
                    relay_hidden(way, 3 - group).wait_recv()

    for d in range(2):
        for k in range(min(SLOTS, steps)):
            gates_copy(d, k, k % SLOTS).wait()
            for j, other in enumerate(near):
                if k >= DEFER:
                    gates_row(d, k, k % SLOTS, j, other).wait_send()

    @pl.when(section == 1)
    def _():
        for d in range(2):
            pass_down(d, 0).wait_send()

    own = [
        (hidden_out, hidden_all.at[:, group]),
        (state_out, state_all.at[:, group]),
        (projected_out, projected_all.at[:, group]),
    ]
    for other in others:
        own.append((state_out.at[:, 0], state_all.at[:, other, 0]))
    own = [
        pltpu.make_async_copy(source, target, own_sem.at[i])
        for i, (source, target) in enumerate(own)
    ]
    for copy in own:
        copy.start()

    rest = pl.ds(1, steps)
    for j, other in enumerate(others):
        source = from_peer(j, others)
        state_row = row(3, state_out.at[:, rest], state_all.at[:, source, rest], j, other)
        state_row.wait_send()
        state_row.wait_recv()

    finish_hidden(5, pl.ds(head, steps - head))

    for copy in own:
        copy.wait()

    @pl.when(section == 0)
    def _():
        mine = pltpu.make_async_copy(x_out.at[0], x_all.at[0, group], base_sem)
        mine.start()
        for j, other in enumerate(others):
            copy = row(1, x_out.at[0], x_all.at[0, from_peer(j, others)], j, other)
            copy.wait_send()
            copy.wait_recv()
        mine.wait()

    @pl.when(section == 0)
    def _():
        for j, peer in enumerate(peers):
            source = peers[count - 2 - j]
            copy = input_copy(input_parts.at[:, :, peer], input_sums.at[:, :, source], j, peer)
            copy.wait_send()
            copy.wait_recv()
        rows_half = base_out.shape[1] // steps

        @pl.loop(0, steps)
        def _(t):
            total = input_parts[0, t, me].astype(F32) + input_parts[1, steps - 1 - t, me].astype(F32)
            for peer in peers:
                total = total + input_sums[0, t, peer].astype(F32)
                total = total + input_sums[1, steps - 1 - t, peer].astype(F32)
            at = pl.ds(pl.multiple_of(t * rows_half, rows_half), rows_half)
            for half in range(2):
                base_sum[half, at, :] = total[half * rows_half : (half + 1) * rows_half]

        base_out[...] = base_sum[...].astype(BF16)

    share_features(section).wait_send()
    share_features(1 - section).wait_recv()

    for j, other in enumerate(near):
        source = from_peer(j, near)
        pltpu.make_async_remote_copy(
            src_ref=gates_all.at[:, source, pl.ds(DEFER, steps - DEFER)],
            dst_ref=gates_all.at[:, source, pl.ds(DEFER, steps - DEFER)],
            send_sem=row_send.at[0, j],
            recv_sem=row_recv.at[0, j],
            device_id={"dp": other},
            device_id_type=MESH,
        ).wait_recv()
        projected_row = row(4, projected_out, projected_all.at[:, source], j, other)
        projected_row.wait_send()
        projected_row.wait_recv()


def recurrence(base_seq, live_seq, top_seq, layer_weights, features_all):
    w_in, w_state, bias, proj = layer_weights
    _, steps, rows, width = top_seq.shape
    cell_count = proj.shape[1]
    count = lax.axis_size("mp")
    groups = lax.axis_size("dp")
    weights = (bias, proj, w_in, w_state)
    dma = pltpu.SemaphoreType.DMA
    return pl.pallas_call(
        recurrence_kernel,
        out_shape=(
            jax.ShapeDtypeStruct((2, groups, steps, rows, width), BF16),
            jax.ShapeDtypeStruct((2, groups, steps + 1, rows, width), BF16),
            jax.ShapeDtypeStruct((2, groups, steps, rows, cell_count), BF16),
            jax.ShapeDtypeStruct((2, groups, steps, rows, 4 * cell_count), BF16),
            jax.ShapeDtypeStruct((2, groups, steps, rows, width), BF16),
            jax.ShapeDtypeStruct((2, steps * rows // 2, width // count), BF16),
            jax.ShapeDtypeStruct(features_all.shape, BF16),
        ),
        in_specs=[VMEM_SPEC] * 5 + [ANY_SPEC] * 3,
        out_specs=(*[ANY_SPEC] * 5, VMEM_SPEC, ANY_SPEC),
        input_output_aliases={7: 6},
        scratch_shapes=[
            pltpu.VMEM((2, steps, rows, width), BF16),
            pltpu.VMEM((2, steps + 1, rows, width), BF16),
            pltpu.VMEM((2, steps, rows, cell_count), BF16),
            pltpu.VMEM((2, steps, rows, width), BF16),
            pltpu.VMEM((2, steps, 4, rows, cell_count), F32),
            pltpu.VMEM((2, steps + 1, rows, cell_count), F32),
            pltpu.VMEM((2, steps, rows, width), F32),
            pltpu.VMEM((2, rows, 4 * cell_count), F32),
            pltpu.VMEM((2, rows, cell_count), F32),
            pltpu.VMEM((2, 2, count, rows, width), BF16),
            pltpu.VMEM((2, 2, count, rows, width), BF16),
            pltpu.VMEM((2, steps, rows, width), F32),
            pltpu.VMEM((2, SLOTS, rows, 4 * cell_count), BF16),
            dma,
            dma((2, 2, count - 1)),
            dma((2, 2, count)),
            dma((2, 2, count - 1)),
            dma((2, 2, count)),
            dma((2,)),
            dma((2, steps)),
            dma((2,)),
            dma((2, steps)),
            dma((2, SLOTS)),
            dma((2, SLOTS, groups - 1)),
            dma((groups + 2,)),
            dma((6, groups - 1)),
            dma((6, groups - 1)),
            pltpu.VMEM(w_in.shape, BF16),
            pltpu.VMEM(w_state.shape, BF16),
            dma((2, 2)),
            pltpu.VMEM((2, 4 * cell_count, width), BF16),
            pltpu.VMEM((2, 4 * cell_count, width), BF16),
            pltpu.VMEM((2, width, cell_count), BF16),
            pltpu.VMEM((2, steps, count, rows, width // count), BF16),
            pltpu.VMEM((2, steps, count, rows, width // count), BF16),
            dma((count - 1,)),
            dma((count - 1,)),
            pltpu.VMEM((2, steps * rows // 2, width // count), F32),
            dma,
            dma,
            dma((2,)),
            dma((2,)),
            dma((groups - 1,)),
            dma((groups - 1,)),
            dma((2,)),
            dma((2,)),
        ],
        compiler_params=pltpu.CompilerParams(
            collective_id=0, has_side_effects=True, vmem_limit_bytes=VMEM_LIMIT
        ),
        name="recurrence",
    )(base_seq, live_seq, top_seq, *weights, features_all)


def weight_grads(lefts, right, parts, only=None, done=()):
    _, outer, pieces, inner, size = lefts[0].shape
    batch = right.shape[0]
    tokens = right.shape[1]
    inner = tokens // outer
    columns = right.shape[2] // parts
    block = min(512, columns)
    blocks = columns // block
    chunk = min(512, size)
    total = size * len(lefts)
    single = parts == 1
    chosen = 1 if only is not None else batch

    def entry(b):
        return b if only is None else only

    def left_entry(left, b):
        return entry(b) if left.shape[0] == batch else 0


    def kernel(*refs):
        left_refs = refs[: len(lefts)]
        right_refs = refs[len(lefts) : len(lefts) + parts]
        out_refs = refs[len(lefts) + parts + len(done) : -3]
        bias_out, turned, ones = refs[-3:]

        @pl.when(pl.program_id(2) == 0)
        def _():
            for i, left in enumerate(left_refs):
                for offset in range(0, size, chunk):
                    at = i * size + offset
                    turned[at : at + chunk, :] = (
                        left[0, :, 0, :, offset : offset + chunk].reshape(tokens, chunk).T
                    )
            ones[...] = jnp.ones_like(ones)

        for i, out in enumerate(out_refs):

            @pl.loop(0, size // chunk)
            def _(step):
                at = pl.multiple_of(i * size + step * chunk, chunk)
                own = pl.multiple_of(step * chunk, chunk)
                left = turned[pl.ds(at, chunk), :]
                for part in range(parts):
                    value = jnp.dot(left, right_refs[part][0], preferred_element_type=F32)
                    if single:
                        out[0, pl.ds(own, chunk), :] = value
                    else:
                        out[0, pl.ds(own, chunk), part, :] = value

        for part in range(parts):
            bias_out[0, part : part + 1, :] = jnp.dot(
                ones[...], right_refs[part][0], preferred_element_type=F32
            )[:1]

    outputs = 4 * chosen * pieces * total * parts * columns
    return pl.pallas_call(
        kernel,
        out_shape=(
            *[
                jax.ShapeDtypeStruct(
                    (batch, pieces * size, *((parts,) * (not single)), columns), F32
                )
                for _ in lefts
            ],
            jax.ShapeDtypeStruct((batch, parts, columns), F32),
        ),
        grid=(chosen, pieces, blocks),
        in_specs=[
            *[
                pl.BlockSpec(
                    (1, outer, 1, inner, size),
                    functools.partial(
                        lambda left, b, p, n: (left_entry(left, b), 0, p, 0, 0), left
                    ),
                )
                for left in lefts
            ],
            *[
                pl.BlockSpec(
                    (1, tokens, block),
                    functools.partial(lambda g, b, p, n: (entry(b), 0, g * blocks + n), g),
                )
                for g in range(parts)
            ],
            *[ANY_SPEC] * len(done),
        ],
        input_output_aliases={len(lefts) + parts + i: i for i in range(len(done))},
        out_specs=(
            *[
                pl.BlockSpec((1, size, block), lambda b, p, n: (entry(b), p, n))
                if single
                else pl.BlockSpec((1, size, parts, block), lambda b, p, n: (entry(b), p, 0, n))
                for _ in lefts
            ],
            pl.BlockSpec((1, parts, block), lambda b, p, n: (entry(b), 0, n)),
        ),
        scratch_shapes=[
            pltpu.VMEM((total, tokens), BF16),
            pltpu.VMEM((16, tokens), BF16),
        ],
        compiler_params=pltpu.CompilerParams(vmem_limit_bytes=VMEM_LIMIT),
        cost_estimate=pl.CostEstimate(
            flops=2 * chosen * pieces * total * tokens * parts * columns,
            bytes_accessed=outputs + 2 * right.size + 2 * batch * pieces * total * tokens,
            transcendentals=0,
        ),
        name="weight_grads",
    )(*lefts, *[right] * parts, *done)


def merge_kernel(d, first_ref, second_ref, gates_in, gates_all, staged, sems):
    far = 3 - lax.axis_index("dp")
    late = first_ref.shape[0]
    half_steps = gates_all.shape[2] // 2
    loads, stores = [], []
    for way, source in enumerate((first_ref, second_ref)):
        rows = pl.ds((way + 1) * half_steps - late, late)
        buffer = staged.at[way]
        loads.append(pltpu.make_async_copy(source, buffer, sems.at[way]))
        stores.append(pltpu.make_async_copy(buffer, gates_all.at[d, far, rows], sems.at[way]))
    for load in loads:
        load.start()
    for load, store in zip(loads, stores):
        load.wait()
        store.start()
    for store in stores:
        store.wait()


def send_late(late):
    beside = [(i, i + 1 - 2 * (i % 2)) for i in range(4)]
    across = [(i, (i + 2) % 4) for i in range(4)]
    return lax.ppermute(late[0], "dp", across), lax.ppermute(late[1], "dp", beside)


def merge_late(d, gates_all, moved):
    return pl.pallas_call(
        functools.partial(merge_kernel, d),
        out_shape=jax.ShapeDtypeStruct(gates_all.shape, BF16),
        in_specs=[ANY_SPEC] * 3,
        out_specs=ANY_SPEC,
        input_output_aliases={2: 0},
        scratch_shapes=[pltpu.VMEM((2, *moved[0].shape), BF16), pltpu.SemaphoreType.DMA((2,))],
        compiler_params=pltpu.CompilerParams(vmem_limit_bytes=VMEM_LIMIT),
        name="merge_late",
    )(*moved, gates_all)


def on_device(
    char_ids,
    row_lengths,
    top_grad,
    char_table,
    conv_weight,
    conv_bias,
    highway_weight,
    highway_bias,
    proj_weight,
    proj_bias,
    lstm_input,
    lstm_state,
    lstm_bias,
    lstm_proj,
):
    section = lax.axis_index("section")
    rows, steps, per_token = char_ids.shape
    proj_width = proj_weight.shape[1]
    half = rows // 2
    tokens = half * steps
    local = conv_weight.shape[2]
    emb = char_table.shape[1]
    padded = -(-(per_token + TAPS - 1) // 8) * 8
    vocabulary = -(-char_table.shape[0] // 8) * 8
    chars = lax.dynamic_slice_in_dim(char_ids, section * half, half, 0)
    chars = jnp.transpose(chars, (1, 0, 2)).reshape(tokens, per_token)
    ids = jnp.pad(chars, ((0, 0), (0, padded - per_token)), constant_values=-1)
    ids = ids.reshape(tokens // CHUNK, 1, CHUNK * padded)
    table = jnp.pad(
        jnp.tile(char_table, (1, TAPS)),
        ((0, vocabulary - char_table.shape[0]), (0, 128 - TAPS * emb)),
    )
    widths = filter_widths(lax.axis_index("mp") * local, local, local * lax.axis_size("mp"))
    tap_keep = jnp.arange(TAPS, dtype=jnp.int32)[:, None] < widths[None, :]
    row = jnp.arange(128, dtype=jnp.int32)[:, None]
    taps_padded = jnp.pad(
        conv_weight.reshape(TAPS * emb, local), ((0, 128 - TAPS * emb), (0, 0))
    )
    masked = jnp.where(
        row < emb * widths[None, :],
        taps_padded,
        jnp.where(
            row == TAPS * emb,
            conv_bias[None, :],
            jnp.where(row == TAPS * emb + widths[None, :], -1e30, 0.0).astype(BF16),
        ),
    )
    log_positions = jnp.log((per_token - widths + 1).astype(F32))[None, :]
    w_high = jnp.transpose(highway_weight, (0, 2, 1, 3))
    (
        base_pair,
        taps,
        peak,
        pooled,
        current,
        transform,
        gate,
        features_all,
        last_own,
        w_input,
        w_state,
    ) = cnn_forward(
        ids,
        (table, masked, log_positions, w_high, highway_bias, proj_weight, proj_bias[None]),
        lstm_input[0],
        lstm_state[0],
    )
    depth_count = highway_weight.shape[0]

    def all_tokens(values):
        return lax.all_gather(values, ("section", "dp"), axis=values.ndim - 2, tiled=True)

    last_features = all_tokens(last_own)
    top_seq = jnp.transpose(top_grad, (2, 1, 0, 3))
    live = (jnp.arange(steps, dtype=jnp.int32)[:, None] < row_lengths[None, :]).astype(F32)
    live_seq = jnp.broadcast_to(live[..., None], (steps, rows, 128))
    layer_weights = (
        w_input,
        w_state,
        lstm_bias[0],
        lstm_proj[0],
    )
    (
        x_all,
        all_states,
        hidden_all,
        gates_all,
        projected_all,
        base_shards,
        high_features,
    ) = recurrence(base_pair, live_seq, top_seq, layer_weights, features_all)
    (
        all_gates,
        all_projected,
        all_inputs,
        all_hidden,
        base_full,
        all_mixed,
        *late,
        small,
    ) = (
        cnn_backward(
            base_shards,
            (taps, peak, pooled, current, transform, gate),
            (proj_weight, w_high, masked, ids),
            (gates_all, projected_all, x_all, hidden_all, all_states),
        )
    )
    relayed = lax.axis_size("dp") == 4
    if relayed:
        moved_first = send_late(late[:2])
        moved_second = send_late(late[2:])
    small = lax.all_gather(small, ("section", "dp"), axis=0)
    small = jnp.sum(small.astype(F32), axis=0)
    conv_weight_grad = jnp.where(
        tap_keep[:, None, :], small[: TAPS * emb].reshape(conv_weight.shape), 0.0
    )
    table_grad = small[128:].reshape(-1, emb, local)
    table_grad = jnp.transpose(table_grad, (0, 2, 1)).reshape(-1, emb)[: char_table.shape[0]]
    all_base = base_full.reshape(-1, proj_width)

    def flat(values):
        return values.reshape(2, -1, values.shape[4])

    def one_piece(values):
        batch, groups, _, _, width = values.shape
        return values.reshape(batch, groups, 1, -1, width)

    proj_weight_grad = lax.all_gather(
        dot(last_features, all_base, 0, 0).astype(BF16), "mp", axis=0, tiled=True
    ).astype(F32)
    proj_grad = weight_grads([one_piece(all_hidden)], flat(all_projected), 1)[0]
    batch, _, groups, count, _, _ = high_features.shape
    high_grad, high_bias_grad = weight_grads(
        [high_features.reshape(batch, 2 * groups, count, tokens, local)],
        all_mixed.reshape(batch, -1, 2 * local),
        2,
    )
    states = one_piece(all_states)
    inputs = one_piece(all_inputs)
    if relayed:
        moved_first, high_grad, proj_grad, conv_weight_grad, table_grad = lax.optimization_barrier(
            (moved_first, high_grad, proj_grad, conv_weight_grad, table_grad)
        )
        all_gates = merge_late(0, all_gates, moved_first)
        done = weight_grads([inputs, states], flat(all_gates), 4, only=0)
        done, moved_second, all_gates = lax.optimization_barrier((done, moved_second, all_gates))
        all_gates = merge_late(1, all_gates, moved_second)
        input_grad, state_grad, bias_grad = weight_grads(
            [inputs, states], flat(all_gates), 4, only=1, done=done
        )
    else:
        input_grad, state_grad, bias_grad = weight_grads([inputs, states], flat(all_gates), 4)
    return (
        table_grad,
        conv_weight_grad,
        small[TAPS * emb],
        high_grad,
        high_bias_grad,
        proj_weight_grad,
        jnp.sum(all_base.astype(F32), axis=0),
        input_grad.reshape(lstm_input.shape),
        state_grad.reshape(lstm_state.shape),
        bias_grad.reshape(lstm_bias.shape),
        proj_grad.reshape(lstm_proj.shape),
    )


def solution(mesh):
    return jax.shard_map(
        on_device,
        mesh=mesh,
        in_specs=(
            P("dp", None, None),
            P("dp"),
            P("dp", None, None, None),
            P(),
            P(None, None, "mp"),
            P("mp"),
            P(None, None, None, "mp"),
            P(None, None, "mp"),
            P(),
            P(),
            P("section", None, None, None, "mp"),
            P("section", None, None, None, "mp"),
            P("section", None, None, "mp"),
            P("section", None, "mp", None),
        ),
        out_specs=(
            P(),
            P(None, None, "mp"),
            P("mp"),
            P(None, None, None, "mp"),
            P(None, None, "mp"),
            P(),
            P(),
            P("section", None, None, None, "mp"),
            P("section", None, None, None, "mp"),
            P("section", None, None, "mp"),
            P("section", None, "mp", None),
        ),
        check_vma=False,
    )
```
